128 devices in a mesh: dp: 32 (over z, x, core), tp: 4 (over y).
Axes of the slice: x: 4, y: 4, z: 4, core: 2. Of those that a mesh axis runs over, the one named last changes fastest.
Arguments:
- activations: bfloat16 [16384, 8192], P(('dp', 'tp')), may hold values from -6 to 6
- value_grad: bfloat16 [16384, 1024], P('dp', 'tp'), may hold values from -6 to 6
- value_weight: bfloat16 [8192, 1024], P(None, 'tp'), may hold values from -0.1875 to 0.1875
- error_prev: float32 [32, 8192, 1024], P('dp', None, 'tp'), may hold values from -96 to 96
- right_prev: float32 [1024, 32], P('tp'), may hold values from -6 to 6
Outputs:
- grad_input: bfloat16 [16384, 8192], P(('dp', 'tp'))
- error_next: float32 [32, 8192, 1024], P('dp', None, 'tp')
- left_factor: float32 [8192, 32], replicated
- right_factor: float32 [1024, 32], P('tp')
The draws below stay inside these ranges and needn't reach their ends.
All inputs are finite; a program needn't handle non-finite values.
Results may differ from the reference program's by a relative error of at most 0.019.
Values may be sent and summed in bfloat16 or wider, within the bound.
A program may use at most 128 MiB of HBM per device.

```python
import math
import jax
import jax.numpy as jnp
from jax import lax

D = 8192
KV = 1024
R = 32
TOK_DEV = 512
TOKENS = 16384
N_DP = 32
N_TP = 4


def block_scale(key, shape, cuts, smallest, largest):
    gain = 1.0
    for position, shards_of in cuts:
        heights = jax.random.uniform(jax.random.fold_in(jax.random.fold_in(key, 6), position), (shards_of,), jnp.float32, smallest / len(cuts), largest / len(cuts))
        gain = gain * jnp.repeat(jnp.exp(heights), shape[position] // shards_of).reshape((-1,) + (1,) * (len(shape) - 1 - position))
    return gain


def normal_values(own_key, extent, scale, limit, shards=(), kind=jnp.bfloat16):
    loudness = block_scale(own_key, extent, shards, -0.22, 0.18) if shards else 1.0
    result = jax.random.normal(own_key, extent, jnp.float32) * scale * loudness
    return jnp.minimum(jnp.maximum(result, -limit), limit).astype(kind)


def setup_inputs(seed: int = 0) -> dict:
    streams_of = jax.random.split(jax.random.key(seed), 6)
    activations = normal_values(streams_of[0], (TOKENS, D), 1.0, 6.0, ((0, 128),))
    value_grad = normal_values(streams_of[1], (TOKENS, KV), 1.0, 6.0, ((0, 32), (1, 4)))
    value_weight = normal_values(streams_of[2], (D, KV), KV ** -0.5, 0.1875, ((1, 4),))
    error_prev = normal_values(streams_of[3], (N_DP, D, KV), 16.0, 96.0, ((0, 32), (2, 4)), jnp.float32)
    right_prev = normal_values(streams_of[4], (KV, R), 1.0, 6.0, ((0, 4),), jnp.float32)
    return dict(activations=activations, value_grad=value_grad, value_weight=value_weight, error_prev=error_prev, right_prev=right_prev)


def orthonormal(factor):
    highest = lax.Precision.HIGHEST
    columns = []
    for number in range(factor.shape[1]):
        vector = factor[:, number]
        if columns:
            spanned = jnp.stack(columns, axis=1)
            for sweep in range(2):
                weights = jnp.dot(vector, spanned, precision=highest)
                vector = vector - jnp.dot(spanned, weights, precision=highest)
        vector = vector / jnp.sqrt(jnp.sum(vector * vector) + 1e-12)
        columns.append(vector)
    return jnp.stack(columns, axis=1)

def reference(activations, value_grad, value_weight, error_prev, right_prev):
    highest = lax.Precision.HIGHEST
    tokens = activations.reshape(N_DP, TOK_DEV, D)
    grads = value_grad.reshape(N_DP, TOK_DEV, KV)

    def merged(items):
        rows, cotangent, error = items
        grad = lax.dot_general(rows, cotangent, (((0,), (0,)), ((), ())), preferred_element_type=jnp.float32)
        return grad + error

    def left_step(total, items):
        return (total + jnp.dot(merged(items), right_prev, precision=highest), None)
    left_sum, unused = lax.scan(left_step, jnp.zeros((D, R), jnp.float32), (tokens, grads, error_prev))
    ortho = orthonormal(left_sum)

    def right_step(total, items):
        return (total + lax.dot_general(merged(items), ortho, (((0,), (0,)), ((), ())), precision=highest), None)
    right_sum, unused = lax.scan(right_step, jnp.zeros((KV, R), jnp.float32), (tokens, grads, error_prev))
    right_factor = right_sum / float(N_DP)
    approx = jnp.dot(ortho, right_factor.T, precision=highest)

    def error_step(carry, items):
        return (carry, merged(items) - approx)
    unused, error_next = lax.scan(error_step, jnp.zeros((), jnp.float32), (tokens, grads, error_prev))
    width = KV // N_TP
    total = jnp.zeros((TOKENS, D), jnp.float32)
    for group in range(N_TP):
        cotangent = value_grad[:, group * width:(group + 1) * width]
        weight = value_weight[:, group * width:(group + 1) * width]
        partial_sum = jnp.dot(cotangent, weight.T, preferred_element_type=jnp.float32).astype(jnp.bfloat16)
        partial_sum = lax.optimization_barrier(partial_sum)
        total = total + partial_sum.astype(jnp.float32)
    grad_input = total.astype(jnp.bfloat16)
    left_factor = ortho * math.sqrt(float(D))
    return (grad_input, error_next, left_factor, right_factor)
```

```python
import functools
import math

import jax
import jax.numpy as jnp
from jax import lax
from jax.experimental import pallas as pl
from jax.experimental.pallas import tpu as pltpu
from jax.sharding import PartitionSpec as P

MESH = pl.DeviceIdType.MESH
HIGHEST = lax.Precision.HIGHEST
F32 = jnp.float32
BF16 = jnp.bfloat16
BLK = 256
EPS = 1e-12
NN = (((1,), (0,)), ((), ()))
NT = (((1,), (1,)), ((), ()))
TN = (((0,), (0,)), ((), ()))
CHUNKS = 4


def mm(a, b, dims=NN, precision=None):
    return lax.dot_general(a, b, dims, precision=precision, preferred_element_type=F32)


def split2(a):
    hi = a.astype(BF16)
    lo = (a - hi.astype(F32)).astype(BF16)
    return hi, lo


def split3(a):
    hi = a.astype(BF16)
    rest = a - hi.astype(F32)
    mid = rest.astype(BF16)
    lo = (rest - mid.astype(F32)).astype(BF16)
    return hi, mid, lo


def rows3(a):
    return jnp.concatenate(split3(a), axis=0)


def fold3(a):
    n = a.shape[0] // 3
    return (a[2 * n :] + a[n : 2 * n]) + a[:n]


def gram_schmidt(gram):
    n = gram.shape[0]
    row_id = lax.broadcasted_iota(jnp.int32, (n, 1), 0)
    eye = (lax.broadcasted_iota(jnp.int32, (n, n), 0) == lax.broadcasted_iota(jnp.int32, (n, n), 1)).astype(F32)
    left, weights = gram, eye
    for j in range(n):
        s = jnp.maximum(left[j : j + 1, j : j + 1], 0.0)
        inverse = 1.0 / (s + EPS)
        c = (2.0 - s * inverse) * inverse
        f = jnp.where(row_id > j, left[:, j : j + 1] * c, 0.0)
        new_weights = weights - f * weights[j : j + 1, :]
        left = left - (f * (2.0 - c * s)) * left[j : j + 1, :]
        weights = new_weights
    s = jnp.maximum(jnp.sum(left * eye, axis=1, keepdims=True), 0.0)
    return weights / jnp.sqrt(s + EPS), eye * (s / (s + EPS))


def comm_kernel(
    geom, act, vg, w, err, rt, actfull, q_out, r_out, gi,
    act_v, vg_v, err_v, rtf, vgx, wbuf, outs, lacc, lf, rc, rx, rz, ry, q1, ptf, rs0, rs1, rr_c, rr_x, rr_z,
    local_sem, send_sem, recv_sem,
):
    nz, nx, nc, ny = geom
    nb = nc * nx * nz
    tok, d = act_v.shape
    r = rt.shape[0]
    rq = r // ny
    dp, y = lax.axis_index("dp"), lax.axis_index("tp")
    c = lax.rem(dp, nc)
    x = lax.rem(lax.div(dp, nc), nx)
    z = lax.div(dp, nc * nx)
    k = c * nx + x

    def shifted(i, by, n):
        return lax.rem(i + by, n)

    def device(zz, xx, cc, yy):
        return ((zz * nx + xx) * nc + cc, yy)

    y_peers = [(dy, shifted(y, dy, ny)) for dy in range(1, ny)]
    z_peers = [(dz, shifted(z, dz, nz)) for dz in range(1, nz)]
    x_peers = [(dx, shifted(x, dx, nx)) for dx in range(1, nx)]
    group = [
        (shifted(x, dx, nx), shifted(c, dc, nc)) for dc in range(nc) for dx in range(nx) if (dc, dx) != (0, 0)
    ]

    sent = []
    counter = [0, 0]

    def send(src, dst, to):
        i = counter[0]
        counter[0] += 1
        copy = pltpu.make_async_remote_copy(
            src_ref=src, dst_ref=dst, send_sem=send_sem.at[i], recv_sem=recv_sem.at[i], device_id=to, device_id_type=MESH
        )
        copy.start()
        sent.append(copy)
        return copy

    def fetch(src, dst):
        i = counter[1]
        counter[1] += 1
        copy = pltpu.make_async_copy(src, dst, local_sem.at[i])
        copy.start()
        return copy

    def wait_all(copies):
        for copy in copies:
            copy.wait_recv()

    load_vgx = fetch(vg.at[pl.ds(pl.multiple_of(y * tok, tok), tok)], vgx.at[k, y])
    quarter = d // nc
    load_err = [fetch(err.at[pl.ds(i * quarter, quarter)], err_v.at[pl.ds(i * quarter, quarter)]) for i in range(nc)]
    load_act = fetch(act, act_v)
    load_vg = fetch(vg, vg_v)
    load_w = [
        fetch(w.at[pl.ds(pl.multiple_of((k * nz + zz) * BLK, BLK), BLK)], wbuf.at[zz, y]) for zz in range(nz)
    ]
    keep_act = fetch(act, actfull.at[y])

    barrier = pltpu.get_barrier_semaphore()
    everyone = (
        [device(z, xx, cc, y) for xx, cc in group]
        + [device(zz, x, c, y) for _, zz in z_peers]
        + [device(z, x, c, yy) for _, yy in y_peers]
    )
    for peer in everyone:
        pl.semaphore_signal(barrier, inc=1, device_id=peer, device_id_type=MESH)
    pl.semaphore_wait(barrier, len(everyone))

    recv_rt = [send(rt, rtf.at[y], device(z, x, c, yy)) for _, yy in y_peers]
    recv_vg = [
        send(vg.at[pl.ds(pl.multiple_of(yy * tok, tok), tok)], vgx.at[k, y], device(z, x, c, yy)) for _, yy in y_peers
    ]
    recv_w = [
        send(w.at[pl.ds(pl.multiple_of((k * nz + z) * BLK, BLK), BLK)], wbuf.at[z, y], device(z, x, c, yy))
        for _, yy in y_peers
    ]
    up, down = shifted(y, 1, ny), shifted(y, ny - 1, ny)
    part = tok // CHUNKS
    half = CHUNKS // 2

    def rows(i):
        return pl.ds(i * part, part)

    from_down, from_up = {}, {}
    for i in range(CHUNKS):
        j = (i + half) % CHUNKS
        from_down[i] = send(act.at[rows(i)], actfull.at[y, rows(i)], device(z, x, c, up))
        from_up[j] = send(act.at[rows(j)], actfull.at[y, rows(j)], device(z, x, c, down))

    passed = []

    def forward(i):
        from_down[i].wait_recv()
        passed.append(send(actfull.at[down, rows(i)], actfull.at[down, rows(i)], device(z, x, c, up)))
        j = i + half
        from_up[j].wait_recv()
        passed.append(send(actfull.at[up, rows(j)], actfull.at[up, rows(j)], device(z, x, c, down)))

    rtf[y] = rt[...]
    rt3 = rows3(rt[...])
    per = nx * nz

    def columns(b):
        return pl.ds(pl.multiple_of(b * BLK, BLK), BLK)

    for cc in range(nc):
        load_err[cc].wait()

        def err_left(j, carry, cc=cc):
            hi, lo = split2(err_v[columns(cc * per + j), :])
            lacc[cc, j] = fold3(mm(rt3, lo, NT)) + fold3(mm(rt3, hi, NT))
            return carry

        lax.fori_loop(0, per, err_left, 0)

    wait_all(recv_rt)
    load_vgx.wait()
    wait_all(recv_vg)
    recv_vgx = [send(vgx.at[k], vgx.at[k], device(z, xx, cc, y)) for xx, cc in group]
    ut = jnp.zeros((r, tok), F32)
    for yy in range(ny):
        ut = ut + fold3(mm(rows3(rtf[yy]), vgx[k, yy], NT))
    ut3 = rows3(ut)
    load_act.wait()

    def act_left(cc):
        def step(j, carry):
            lacc[cc, j] += fold3(mm(ut3, act_v[:, columns(cc * per + j)]))
            return carry

        lax.fori_loop(0, per, step, 0)

    recv_c = []
    for dc in range(1, nc):
        cc = shifted(c, dc, nc)
        act_left(cc)
        recv_c.append(send(lacc.at[cc], rc, device(z, x, cc, y)))
    act_left(c)

    for copy in load_w:
        copy.wait()
    recv_wz = []
    for copy, (dy, _) in zip(recv_w, y_peers):
        copy.wait_recv()
        source = shifted(y, ny - dy, ny)
        for _, zz in z_peers:
            recv_wz.append(send(wbuf.at[z, source], wbuf.at[z, source], device(zz, x, c, y)))

    wait_all(recv_c)
    lacc[c] += rc[...]
    recv = [
        send(lacc.at[c, pl.ds(xx * nz, nz)], rx.at[dx - 1], device(z, xx, c, y)) for dx, xx in x_peers
    ]
    wait_all(recv)
    own_x = pl.ds(x * nz, nz)
    total = lacc[c, own_x]
    for dx in range(nx - 1):
        total = total + rx[dx]
    lacc[c, own_x] = total
    mine = x * nz + z
    recv = [send(lacc.at[c, x * nz + zz], rz.at[dz - 1], device(zz, x, c, y)) for dz, zz in z_peers]
    wait_all(recv)
    total = lacc[c, mine]
    for dz in range(nz - 1):
        total = total + rz[dz]
    lacc[c, mine] = total

    def strip(yy):
        return pl.ds(pl.multiple_of(yy * rq, rq), rq)

    recv = [send(lacc.at[c, mine, strip(yy)], ry.at[dy - 1], device(z, x, c, yy)) for dy, yy in y_peers]

    sent_out, kept_out = [], []

    def input_grad(i):
        xx, cc = ([(x, c)] + group)[i]
        slot = cc * nx + xx
        for zz in range(nz):
            total = None
            for yy in range(ny):
                piece = mm(vgx[slot, yy], wbuf[zz, yy], NT).astype(BF16).astype(F32)
                total = piece if total is None else total + piece
            outs[i, :, zz * BLK : (zz + 1) * BLK] = total.astype(BF16)
        place = gi.at[:, pl.ds(pl.multiple_of(k * nz * BLK, BLK), nz * BLK)]
        if i == 0:
            kept_out.append(fetch(outs.at[i], place))
        else:
            sent_out.append(send(outs.at[i], place, device(z, xx, cc, y)))

    wait_all(recv_wz)
    wait_all(recv_vgx)
    jobs = list(range(nc * nx))

    def some_jobs(n):
        for _ in range(min(n, len(jobs))):
            input_grad(jobs.pop())

    some_jobs(2)
    wait_all(recv)
    total = lacc[c, mine, strip(y)]
    for dy in range(ny - 1):
        total = total + ry[dy]
    lf[c, mine, strip(y)] = total

    own = lf.at[c, mine, strip(y)]
    recv = [send(own, own, device(z, x, c, yy)) for _, yy in y_peers]
    some_jobs(2)
    forward(0)
    wait_all(recv)
    own = lf.at[c, mine]
    recv = [send(own, own, device(zz, x, c, y)) for _, zz in z_peers]
    some_jobs(2)
    wait_all(recv)
    own = lf.at[c, own_x]
    recv = [send(own, own, device(z, xx, c, y)) for _, xx in x_peers]
    some_jobs(2)
    wait_all(recv)
    own = lf.at[c]
    recv = [send(own, own, device(z, x, shifted(c, dc, nc), y)) for dc in range(1, nc)]
    some_jobs(len(jobs))
    for i in range(1, half):
        forward(i)
    wait_all(recv)

    def gram_of(ref_of):
        def step(b, total):
            block = ref_of(b)
            return total + mm(block, block, NT, HIGHEST)

        return lax.fori_loop(0, nb, step, jnp.zeros((r, r), F32))

    def left_block(b):
        return lf[lax.div(b, per), lax.rem(b, per)]

    weights, norms = gram_schmidt(gram_of(left_block))

    def apply_first(b, total):
        block = mm(weights, left_block(b), NN, HIGHEST)
        q1[b] = block
        return total + mm(block, block, NT, HIGHEST)

    off = lax.fori_loop(0, nb, apply_first, jnp.zeros((r, r), F32)) - norms
    row_id = lax.broadcasted_iota(jnp.int32, (r, r), 0)
    col_id = lax.broadcasted_iota(jnp.int32, (r, r), 1)
    again = jnp.where(col_id < row_id, off, jnp.where(col_id == row_id, 0.5 * off, 0.0))

    def apply_second(b, total):
        block = q1[b]
        block = block - mm(again, block, NN, HIGHEST)
        q_out[b] = block
        return total + fold3(mm(rows3(block), act_v[:, columns(b)], NT))

    pt = lax.fori_loop(0, nb, apply_second, jnp.zeros((r, tok), F32))
    ptf[y] = pt
    own = ptf.at[y]
    recv = [send(own, own, device(z, x, c, yy)) for _, yy in y_peers]

    def err_right(b, total):
        hi, lo = split2(err_v[columns(b), :])
        block = rows3(q_out[b])
        return total + (mm(block, lo) + mm(block, hi))

    right = fold3(lax.fori_loop(0, nb, err_right, jnp.zeros((3 * r, err_v.shape[1]), F32)))
    load_vg.wait()
    wait_all(recv)
    for yy in range(ny):
        right = right + fold3(mm(rows3(ptf[yy]), vg_v[yy * tok : (yy + 1) * tok, :]))
    rs0[...] = right
    recv = [send(rs0, rr_c.at[dc - 1], device(z, x, shifted(c, dc, nc), y)) for dc in range(1, nc)]
    wait_all(recv)
    for dc in range(nc - 1):
        right = right + rr_c[dc]
    rs1[0] = right
    recv = [send(rs1.at[0], rr_x.at[dx - 1], device(z, xx, c, y)) for dx, xx in x_peers]
    wait_all(recv)
    for dx in range(nx - 1):
        right = right + rr_x[dx]
    rs1[1] = right
    recv = [send(rs1.at[1], rr_z.at[dz - 1], device(zz, x, c, y)) for dz, zz in z_peers]
    wait_all(recv)
    for dz in range(nz - 1):
        right = right + rr_z[dz]
    r_out[...] = right / float(nz * nx * nc)

    for i in range(half, CHUNKS):
        from_down[i].wait_recv()
    for j in range(half):
        from_up[j].wait_recv()
    wait_all(passed)
    wait_all(sent_out)
    for copy in kept_out + [keep_act]:
        copy.wait()
    for copy in sent:
        copy.wait_send()


def error_kernel(act, vg, err, q, right, out):
    ny, tok, width = act.shape
    cotangent = vg[...]
    hi, lo = split2(right[...])
    right3 = jnp.concatenate([hi, hi, lo], axis=0)
    for j in range(width // BLK):
        cols = slice(j * BLK, (j + 1) * BLK)
        tokens = act[:, :, cols].reshape(ny * tok, BLK)
        hi, lo = split2(q[j])
        approx = mm(jnp.concatenate([hi, lo, hi], axis=0), right3, TN)
        out[cols, :] = (mm(tokens, cotangent, TN) + err[cols, :]) - approx


def build(geom):
    nz, nx, nc, ny = geom

    def body(act, vg, w, err, right_prev):
        tok, d = act.shape
        kv = vg.shape[1]
        r = right_prev.shape[1]
        nb = nc * nx * nz
        assert d == nb * BLK and kv == BLK
        err = err[0]
        anywhere = pl.BlockSpec(memory_space=pl.ANY)
        vmem = pl.BlockSpec(memory_space=pltpu.VMEM)
        xc = nx * nc
        sends = 6 * (ny - 1) + 2 * CHUNKS + CHUNKS + (xc - 1) * 2 + (ny - 1) * (nz - 1) + 3 * (nc + nx + nz - 3)
        actfull, q, right, grad_input = pl.pallas_call(
            functools.partial(comm_kernel, geom),
            out_shape=(
                jax.ShapeDtypeStruct((ny, tok, d), BF16),
                jax.ShapeDtypeStruct((nb, r, BLK), F32),
                jax.ShapeDtypeStruct((r, kv), F32),
                jax.ShapeDtypeStruct((tok, d), BF16),
            ),
            in_specs=[anywhere, anywhere, anywhere, anywhere, vmem],
            out_specs=(anywhere, vmem, vmem, anywhere),
            scratch_shapes=[
                pltpu.VMEM((tok, d), BF16),
                pltpu.VMEM(vg.shape, BF16),
                pltpu.VMEM((d, kv), F32),
                pltpu.VMEM((ny, r, kv), F32),
                pltpu.VMEM((xc, ny, tok, kv), BF16),
                pltpu.VMEM((nz, ny, BLK, kv), BF16),
                pltpu.VMEM((xc, tok, nz * BLK), BF16),
                pltpu.VMEM((nc, nx * nz, r, BLK), F32),
                pltpu.VMEM((nc, nx * nz, r, BLK), F32),
                pltpu.VMEM((nx * nz, r, BLK), F32),
                pltpu.VMEM((max(nx - 1, 1), nz, r, BLK), F32),
                pltpu.VMEM((max(nz - 1, 1), r, BLK), F32),
                pltpu.VMEM((ny - 1, r // ny, BLK), F32),
                pltpu.VMEM((nb, r, BLK), F32),
                pltpu.VMEM((ny, r, tok), F32),
                pltpu.VMEM((r, kv), F32),
                pltpu.VMEM((2, r, kv), F32),
                pltpu.VMEM((max(nc - 1, 1), r, kv), F32),
                pltpu.VMEM((max(nx - 1, 1), r, kv), F32),
                pltpu.VMEM((max(nz - 1, 1), r, kv), F32),
                pltpu.SemaphoreType.DMA((8 + nz + nc,)),
                pltpu.SemaphoreType.DMA((sends,)),
                pltpu.SemaphoreType.DMA((sends,)),
            ],
            compiler_params=pltpu.CompilerParams(
                collective_id=0, has_side_effects=True, vmem_limit_bytes=48 * 1024 * 1024
            ),
        )(act, vg, w, err, right_prev.T)

        width = 2 * BLK
        error_next = pl.pallas_call(
            error_kernel,
            grid=(d // width,),
            out_shape=jax.ShapeDtypeStruct((d, kv), F32),
            in_specs=[
                pl.BlockSpec((ny, tok, width), lambda i: (0, 0, i)),
                pl.BlockSpec(vg.shape, lambda i: (0, 0)),
                pl.BlockSpec((width, kv), lambda i: (i, 0)),
                pl.BlockSpec((2, r, BLK), lambda i: (i, 0, 0)),
                pl.BlockSpec((r, kv), lambda i: (0, 0)),
            ],
            out_specs=pl.BlockSpec((width, kv), lambda i: (i, 0)),
            compiler_params=pltpu.CompilerParams(vmem_limit_bytes=32 * 1024 * 1024),
        )(actfull, vg, err, q, right)
        left_factor = (q * math.sqrt(float(d))).transpose(0, 2, 1).reshape(d, r)
        return (grad_input, error_next[None], left_factor, right.T)

    return body


def solution(mesh):
    return jax.shard_map(
        build((4, 4, 2, 4)),
        mesh=mesh,
        in_specs=(
            P(("dp", "tp"), None),
            P("dp", "tp"),
            P(None, "tp"),
            P("dp", None, "tp"),
            P("tp", None),
        ),
        out_specs=(P(("dp", "tp"), None), P("dp", None, "tp"), P(), P("tp", None)),
        check_vma=False,
    )
```

```python
import functools
import math

import jax
import jax.numpy as jnp
from jax import lax
from jax.experimental import pallas as pl
from jax.experimental.pallas import tpu as pltpu
from jax.sharding import PartitionSpec as P

MESH = pl.DeviceIdType.MESH
HIGHEST = lax.Precision.HIGHEST
F32 = jnp.float32
BF16 = jnp.bfloat16
BLK = 256
D = 8192
EPS = 1e-12
VMEM = 62 * 1024 * 1024
NN = (((1,), (0,)), ((), ()))
NT = (((1,), (1,)), ((), ()))
TN = (((0,), (0,)), ((), ()))


def mm(a, b, dims=NN, precision=None):
    return lax.dot_general(a, b, dims, precision=precision, preferred_element_type=F32)


def split2(a):
    hi = a.astype(BF16)
    lo = (a - hi.astype(F32)).astype(BF16)
    return hi, lo


def split3(a):
    hi = a.astype(BF16)
    rest = a - hi.astype(F32)
    mid = rest.astype(BF16)
    lo = (rest - mid.astype(F32)).astype(BF16)
    return hi, mid, lo


def rows3(a):
    return jnp.concatenate(split3(a), axis=0)


def fold3(a):
    n = a.shape[0] // 3
    return (a[2 * n :] + a[n : 2 * n]) + a[:n]


def gram_schmidt(gram):
    n = gram.shape[0]
    row_id = lax.broadcasted_iota(jnp.int32, (n, 1), 0)
    eye = (lax.broadcasted_iota(jnp.int32, (n, n), 0) == lax.broadcasted_iota(jnp.int32, (n, n), 1)).astype(F32)
    left, weights = gram, eye
    for j in range(n):
        s = jnp.maximum(left[j : j + 1, j : j + 1], 0.0)
        inverse = 1.0 / (s + EPS)
        c = (2.0 - s * inverse) * inverse
        f = jnp.where(row_id > j, left[:, j : j + 1] * c, 0.0)
        new_weights = weights - f * weights[j : j + 1, :]
        left = left - (f * (2.0 - c * s)) * left[j : j + 1, :]
        weights = new_weights
    s = jnp.maximum(jnp.sum(left * eye, axis=1, keepdims=True), 0.0)
    return weights / jnp.sqrt(s + EPS), eye * (s / (s + EPS))


def comm_kernel(
    geom, act, vg, w, err, rt_in, q_out, r_out, gi,
    rt, act_v, vg_v, err_v, rtf, vgx, wbuf, outs, lacc, lf, rc, rx, rz, ry, q1, ptf, rs0, rs1, rr_c, rr_x, rr_z,
    local_sem, send_sem, recv_sem,
):
    nz, nx, nc, ny = geom
    nb = nc * nx * nz
    tok, d = act_v.shape
    r = rt.shape[0]
    rq = r // ny
    dp, y = lax.axis_index("dp"), lax.axis_index("tp")
    c = lax.rem(dp, nc)
    x = lax.rem(lax.div(dp, nc), nx)
    z = lax.div(dp, nc * nx)
    k = c * nx + x

    def shifted(i, by, n):
        return lax.rem(i + by, n)

    def device(zz, xx, cc, yy):
        return ((zz * nx + xx) * nc + cc, yy)

    y_peers = [(dy, shifted(y, dy, ny)) for dy in range(1, ny)]
    z_peers = [(dz, shifted(z, dz, nz)) for dz in range(1, nz)]
    x_peers = [(dx, shifted(x, dx, nx)) for dx in range(1, nx)]
    group = [
        (shifted(x, dx, nx), shifted(c, dc, nc)) for dc in range(nc) for dx in range(nx) if (dc, dx) != (0, 0)
    ]

    sent = []
    counter = [0, 0]

    def send(src, dst, to):
        i = counter[0]
        counter[0] += 1
        copy = pltpu.make_async_remote_copy(
            src_ref=src, dst_ref=dst, send_sem=send_sem.at[i], recv_sem=recv_sem.at[i], device_id=to, device_id_type=MESH
        )
        copy.start()
        sent.append(copy)
        return copy

    def fetch(src, dst):
        i = counter[1]
        counter[1] += 1
        copy = pltpu.make_async_copy(src, dst, local_sem.at[i])
        copy.start()
        return copy

    def wait_all(copies):
        for copy in copies:
            copy.wait_recv()

    load_rt = fetch(rt_in, rt)
    load_vgx = fetch(vg.at[pl.ds(pl.multiple_of(y * tok, tok), tok)], vgx.at[k, y])
    quarter = d // nc
    load_err = [fetch(err.at[pl.ds(i * quarter, quarter)], err_v.at[pl.ds(i * quarter, quarter)]) for i in range(nc)]
    load_act = fetch(act, act_v)
    load_vg = fetch(vg, vg_v)
    load_w = [
        fetch(w.at[pl.ds(pl.multiple_of((k * nz + zz) * BLK, BLK), BLK)], wbuf.at[zz, y]) for zz in range(nz)
    ]

    barrier = pltpu.get_barrier_semaphore()
    everyone = (
        [device(z, xx, cc, y) for xx, cc in group]
        + [device(zz, x, c, y) for _, zz in z_peers]
        + [device(z, x, c, yy) for _, yy in y_peers]
    )
    for peer in everyone:
        pl.semaphore_signal(barrier, inc=1, device_id=peer, device_id_type=MESH)
    pl.semaphore_wait(barrier, len(everyone))

    recv_rt = [send(rt_in, rtf.at[y], device(z, x, c, yy)) for _, yy in y_peers]
    recv_vg = [
        send(vg.at[pl.ds(pl.multiple_of(yy * tok, tok), tok)], vgx.at[k, y], device(z, x, c, yy)) for _, yy in y_peers
    ]
    recv_w = [
        send(w.at[pl.ds(pl.multiple_of((k * nz + z) * BLK, BLK), BLK)], wbuf.at[z, y], device(z, x, c, yy))
        for _, yy in y_peers
    ]
    load_rt.wait()
    rtf[y] = rt[...]
    rt3 = rows3(rt[...])
    per = nx * nz

    def columns(b):
        return pl.ds(pl.multiple_of(b * BLK, BLK), BLK)

    for cc in range(nc):
        load_err[cc].wait()

        def err_left(j, carry, cc=cc):
            hi, lo = split2(err_v[columns(cc * per + j), :])
            lacc[cc, j] = fold3(mm(rt3, lo, NT)) + fold3(mm(rt3, hi, NT))
            return carry

        lax.fori_loop(0, per, err_left, 0)

    wait_all(recv_rt)
    load_vgx.wait()
    wait_all(recv_vg)
    recv_vgx = [send(vgx.at[k], vgx.at[k], device(z, xx, cc, y)) for xx, cc in group]
    ut = jnp.zeros((r, tok), F32)
    for yy in range(ny):
        ut = ut + fold3(mm(rows3(rtf[yy]), vgx[k, yy], NT))
    ut3 = rows3(ut)
    load_act.wait()

    def act_left(cc):
        def step(j, carry):
            lacc[cc, j] += fold3(mm(ut3, act_v[:, columns(cc * per + j)]))
            return carry

        lax.fori_loop(0, per, step, 0)

    recv_c = []
    for dc in range(1, nc):
        cc = shifted(c, dc, nc)
        act_left(cc)
        recv_c.append(send(lacc.at[cc], rc, device(z, x, cc, y)))
    act_left(c)

    for copy in load_w:
        copy.wait()
    recv_wz = []
    for copy, (dy, _) in zip(recv_w, y_peers):
        copy.wait_recv()
        source = shifted(y, ny - dy, ny)
        for _, zz in z_peers:
            recv_wz.append(send(wbuf.at[z, source], wbuf.at[z, source], device(zz, x, c, y)))

    wait_all(recv_c)
    lacc[c] += rc[...]
    recv = [
        send(lacc.at[c, pl.ds(xx * nz, nz)], rx.at[dx - 1], device(z, xx, c, y)) for dx, xx in x_peers
    ]
    wait_all(recv)
    own_x = pl.ds(x * nz, nz)
    total = lacc[c, own_x]
    for dx in range(nx - 1):
        total = total + rx[dx]
    lacc[c, own_x] = total
    mine = x * nz + z
    recv = [send(lacc.at[c, x * nz + zz], rz.at[dz - 1], device(zz, x, c, y)) for dz, zz in z_peers]
    wait_all(recv)
    total = lacc[c, mine]
    for dz in range(nz - 1):
        total = total + rz[dz]
    lacc[c, mine] = total

    def strip(yy):
        return pl.ds(pl.multiple_of(yy * rq, rq), rq)

    recv = [send(lacc.at[c, mine, strip(yy)], ry.at[dy - 1], device(z, x, c, yy)) for dy, yy in y_peers]

    sent_out, kept_out = [], []

    def input_grad(i):
        xx, cc = ([(x, c)] + group)[i]
        slot = cc * nx + xx
        for zz in range(nz):
            total = None
            for yy in range(ny):
                piece = mm(vgx[slot, yy], wbuf[zz, yy], NT).astype(BF16).astype(F32)
                total = piece if total is None else total + piece
            outs[i, :, zz * BLK : (zz + 1) * BLK] = total.astype(BF16)
        place = gi.at[:, pl.ds(pl.multiple_of(k * nz * BLK, BLK), nz * BLK)]
        if i == 0:
            kept_out.append(fetch(outs.at[i], place))
        else:
            sent_out.append(send(outs.at[i], place, device(z, xx, cc, y)))

    wait_all(recv_wz)
    wait_all(recv_vgx)
    jobs = list(range(nc * nx))

    def some_jobs(n):
        for _ in range(min(n, len(jobs))):
            input_grad(jobs.pop())

    some_jobs(2)
    wait_all(recv)
    total = lacc[c, mine, strip(y)]
    for dy in range(ny - 1):
        total = total + ry[dy]
    lf[c, mine, strip(y)] = total

    own = lf.at[c, mine, strip(y)]
    recv = [send(own, own, device(z, x, c, yy)) for _, yy in y_peers]
    some_jobs(2)
    wait_all(recv)
    own = lf.at[c, mine]
    recv = [send(own, own, device(zz, x, c, y)) for _, zz in z_peers]
    some_jobs(2)
    wait_all(recv)
    own = lf.at[c, own_x]
    recv = [send(own, own, device(z, xx, c, y)) for _, xx in x_peers]
    some_jobs(2)
    wait_all(recv)
    own = lf.at[c]
    recv = [send(own, own, device(z, x, shifted(c, dc, nc), y)) for dc in range(1, nc)]
    some_jobs(len(jobs))
    wait_all(recv)

    def gram_of(ref_of):
        def step(b, total):
            block = ref_of(b)
            return total + mm(block, block, NT, HIGHEST)

        return lax.fori_loop(0, nb, step, jnp.zeros((r, r), F32))

    def left_block(b):
        return lf[lax.div(b, per), lax.rem(b, per)]

    weights, norms = gram_schmidt(gram_of(left_block))

    def apply_first(b, total):
        block = mm(weights, left_block(b), NN, HIGHEST)
        q1[b] = block
        return total + mm(block, block, NT, HIGHEST)

    off = lax.fori_loop(0, nb, apply_first, jnp.zeros((r, r), F32)) - norms
    row_id = lax.broadcasted_iota(jnp.int32, (r, r), 0)
    col_id = lax.broadcasted_iota(jnp.int32, (r, r), 1)
    again = jnp.where(col_id < row_id, off, jnp.where(col_id == row_id, 0.5 * off, 0.0))

    def apply_second(b, total):
        block = q1[b]
        block = block - mm(again, block, NN, HIGHEST)
        q_out[b] = block
        return total + fold3(mm(rows3(block), act_v[:, columns(b)], NT))

    pt = lax.fori_loop(0, nb, apply_second, jnp.zeros((r, tok), F32))
    ptf[y] = pt
    own = ptf.at[y]
    recv = [send(own, own, device(z, x, c, yy)) for _, yy in y_peers]

    def err_right(b, total):
        hi, lo = split2(err_v[columns(b), :])
        block = rows3(q_out[b])
        return total + (mm(block, lo) + mm(block, hi))

    right = fold3(lax.fori_loop(0, nb, err_right, jnp.zeros((3 * r, err_v.shape[1]), F32)))
    load_vg.wait()
    wait_all(recv)
    for yy in range(ny):
        right = right + fold3(mm(rows3(ptf[yy]), vg_v[yy * tok : (yy + 1) * tok, :]))
    rs0[...] = right
    recv = [send(rs0, rr_c.at[dc - 1], device(z, x, shifted(c, dc, nc), y)) for dc in range(1, nc)]
    wait_all(recv)
    for dc in range(nc - 1):
        right = right + rr_c[dc]
    rs1[0] = right
    recv = [send(rs1.at[0], rr_x.at[dx - 1], device(z, xx, c, y)) for dx, xx in x_peers]
    wait_all(recv)
    for dx in range(nx - 1):
        right = right + rr_x[dx]
    rs1[1] = right
    recv = [send(rs1.at[1], rr_z.at[dz - 1], device(zz, x, c, y)) for dz, zz in z_peers]
    wait_all(recv)
    for dz in range(nz - 1):
        right = right + rr_z[dz]
    r_out[...] = right / float(nz * nx * nc)

    wait_all(sent_out)
    for copy in kept_out:
        copy.wait()
    for copy in sent:
        copy.wait_send()


def error_kernel(act, vg, err, q, right, gi_in, out, left_out, right_out, gi_out):
    ny, tok, width = act.shape
    gi_out[...] = gi_in[...]
    right_out[...] = right[...]
    scale = math.sqrt(float(D))
    cotangent = vg[...]
    hi, lo = split2(right[...])
    right3 = jnp.concatenate([hi, hi, lo], axis=0)
    for j in range(width // BLK):
        cols = slice(j * BLK, (j + 1) * BLK)
        tokens = act[:, :, cols].reshape(ny * tok, BLK)
        left_out[:, cols] = q[j] * scale
        hi, lo = split2(q[j])
        approx = mm(jnp.concatenate([hi, lo, hi], axis=0), right3, TN)
        out[cols, :] = (mm(tokens, cotangent, TN) + err[cols, :]) - approx


def build(geom):
    nz, nx, nc, ny = geom

    def body(act, vg, w, err, right_prev):
        tok, d = act.shape
        kv = vg.shape[1]
        r = right_prev.shape[1]
        nb = nc * nx * nz
        assert d == nb * BLK and kv == BLK
        err = err[0]
        hbm = pl.BlockSpec(memory_space=pltpu.HBM)
        vmem = pl.BlockSpec(memory_space=pltpu.VMEM)
        xc = nx * nc
        sends = 6 * (ny - 1) + (xc - 1) * 2 + (ny - 1) * (nz - 1) + 3 * (nc + nx + nz - 3)
        actfull = lax.all_gather(act, "tp", axis=0, tiled=False)
        q, right, grad_input = pl.pallas_call(
            functools.partial(comm_kernel, geom),
            out_shape=(
                jax.ShapeDtypeStruct((nb, r, BLK), F32),
                jax.ShapeDtypeStruct((r, kv), F32),
                jax.ShapeDtypeStruct((tok, d), BF16),
            ),
            in_specs=[hbm] * 5,
            out_specs=(vmem, vmem, hbm),
            scratch_shapes=[
                pltpu.VMEM((r, kv), F32),
                pltpu.VMEM((tok, d), BF16),
                pltpu.VMEM(vg.shape, BF16),
                pltpu.VMEM((d, kv), F32),
                pltpu.VMEM((ny, r, kv), F32),
                pltpu.VMEM((xc, ny, tok, kv), BF16),
                pltpu.VMEM((nz, ny, BLK, kv), BF16),
                pltpu.VMEM((xc, tok, nz * BLK), BF16),
                pltpu.VMEM((nc, nx * nz, r, BLK), F32),
                pltpu.VMEM((nc, nx * nz, r, BLK), F32),
                pltpu.VMEM((nx * nz, r, BLK), F32),
                pltpu.VMEM((max(nx - 1, 1), nz, r, BLK), F32),
                pltpu.VMEM((max(nz - 1, 1), r, BLK), F32),
                pltpu.VMEM((ny - 1, r // ny, BLK), F32),
                pltpu.VMEM((nb, r, BLK), F32),
                pltpu.VMEM((ny, r, tok), F32),
                pltpu.VMEM((r, kv), F32),
                pltpu.VMEM((2, r, kv), F32),
                pltpu.VMEM((max(nc - 1, 1), r, kv), F32),
                pltpu.VMEM((max(nx - 1, 1), r, kv), F32),
                pltpu.VMEM((max(nz - 1, 1), r, kv), F32),
                pltpu.SemaphoreType.DMA((8 + nz + nc,)),
                pltpu.SemaphoreType.DMA((sends,)),
                pltpu.SemaphoreType.DMA((sends,)),
            ],
            compiler_params=pltpu.CompilerParams(
                collective_id=0, has_side_effects=True, vmem_limit_bytes=VMEM
            ),
        )(act, vg, w, err, right_prev.T)

        width = 2 * BLK
        error_next, left, right, grad_input = pl.pallas_call(
            error_kernel,
            grid=(d // width,),
            out_shape=(
                jax.ShapeDtypeStruct((d, kv), F32),
                jax.ShapeDtypeStruct((r, d), F32),
                jax.ShapeDtypeStruct((r, kv), F32),
                jax.ShapeDtypeStruct((tok, d), BF16),
            ),
            in_specs=[
                pl.BlockSpec((ny, tok, width), lambda i: (0, 0, i)),
                pl.BlockSpec(vg.shape, lambda i: (0, 0)),
                pl.BlockSpec((width, kv), lambda i: (i, 0)),
                pl.BlockSpec((2, r, BLK), lambda i: (i, 0, 0)),
                pl.BlockSpec((r, kv), lambda i: (0, 0)),
                pl.BlockSpec((tok, width), lambda i: (0, i)),
            ],
            out_specs=(
                pl.BlockSpec((width, kv), lambda i: (i, 0)),
                pl.BlockSpec((r, width), lambda i: (0, i)),
                pl.BlockSpec((r, kv), lambda i: (0, 0)),
                pl.BlockSpec((tok, width), lambda i: (0, i)),
            ),
            compiler_params=pltpu.CompilerParams(vmem_limit_bytes=VMEM),
        )(actfull, vg, err, q, right, grad_input)
        return (grad_input, error_next[None], left.T, right.T)

    return body


def solution(mesh):
    return jax.shard_map(
        build((4, 4, 2, 4)),
        mesh=mesh,
        in_specs=(
            P(("dp", "tp"), None),
            P("dp", "tp"),
            P(None, "tp"),
            P("dp", None, "tp"),
            P("tp", None),
        ),
        out_specs=(P(("dp", "tp"), None), P("dp", None, "tp"), P(), P("tp", None)),
        check_vma=False,
    )
```

```python
import functools
import math

import jax
import jax.numpy as jnp
from jax import lax
from jax.experimental import pallas as pl
from jax.experimental.pallas import tpu as pltpu
from jax.sharding import PartitionSpec as P

MESH = pl.DeviceIdType.MESH
HIGHEST = lax.Precision.HIGHEST
F32 = jnp.float32
BF16 = jnp.bfloat16
BLK = 256
D = 8192
EPS = 1e-12
MIB = 1024 * 1024
WIDE = 8 * BLK
CHUNKS = 8
NN = (((1,), (0,)), ((), ()))
NT = (((1,), (1,)), ((), ()))
TN = (((0,), (0,)), ((), ()))


def mm(a, b, dims=NN, precision=None):
    return lax.dot_general(a, b, dims, precision=precision, preferred_element_type=F32)


def split2(a):
    hi = a.astype(BF16)
    lo = (a - hi.astype(F32)).astype(BF16)
    return hi, lo


def split3(a):
    hi = a.astype(BF16)
    rest = a - hi.astype(F32)
    mid = rest.astype(BF16)
    lo = (rest - mid.astype(F32)).astype(BF16)
    return hi, mid, lo


def rows3(a):
    return jnp.concatenate(split3(a), axis=0)


def fold3(a):
    n = a.shape[0] // 3
    return (a[2 * n :] + a[n : 2 * n]) + a[:n]


def self_products(total, r):
    total = fold3(total)
    return (total[:, 2 * r :] + total[:, r : 2 * r]) + total[:, :r]


def times(a, b):
    a_hi, a_mid, a_lo = (v.astype(F32) for v in split3(a))
    b_hi, b_mid, b_lo = split3(b)
    left = jnp.concatenate([a_lo, a_mid, a_hi, a_mid, a_hi, a_hi], axis=1).astype(BF16)
    return mm(left, jnp.concatenate([b_hi, b_mid, b_lo, b_hi, b_mid, b_hi], axis=0))


def gram_schmidt(gram):
    n = gram.shape[0]
    row_id = lax.broadcasted_iota(jnp.int32, (n, 1), 0)
    eye = (lax.broadcasted_iota(jnp.int32, (n, n), 0) == lax.broadcasted_iota(jnp.int32, (n, n), 1)).astype(F32)
    left, weights = gram, eye
    for j in range(n):
        column = jnp.broadcast_to(left[:, j : j + 1], (n, n))
        s = jnp.maximum(column[j : j + 1, :], 0.0)
        inverse = 1.0 / (s + EPS)
        c = (2.0 - s * inverse) * inverse
        f = jnp.where(row_id > j, column * c, 0.0)
        new_weights = weights - f * weights[j : j + 1, :]
        left = left - (f * (2.0 - c * s)) * left[j : j + 1, :]
        weights = new_weights
    s = jnp.maximum(jnp.sum(left * eye, axis=1, keepdims=True), 0.0)
    return weights / jnp.sqrt(s + EPS), eye * (s / (s + EPS))


def comm_kernel(
    geom, act, vg, w, err, rt_in, merged, q_out, r_out, gi,
    rt, actr, vg_v, err_v, rtf, vgx, wbuf, outs, lacc, lf, rc, rx, rz, ry, q1, q3, ptf, rs0, rs1, rr_c, rr_x, rr_z,
    local_sem, send_sem, recv_sem,
):
    nz, nx, nc, ny = geom
    nb = nc * nx * nz
    per = nx * nz
    _, tok, d = actr.shape
    r = rt.shape[0]
    rq = r // ny
    wide = min(WIDE, per * BLK)
    wb = wide // BLK
    pieces = d // wide
    dp, y = lax.axis_index("dp"), lax.axis_index("tp")
    c = lax.rem(dp, nc)
    x = lax.rem(lax.div(dp, nc), nx)
    z = lax.div(dp, nc * nx)
    k = c * nx + x

    def shifted(i, by, n):
        return lax.rem(i + by, n)

    def device(zz, xx, cc, yy):
        return ((zz * nx + xx) * nc + cc, yy)

    y_peers = [(dy, shifted(y, dy, ny)) for dy in range(1, ny)]
    z_peers = [(dz, shifted(z, dz, nz)) for dz in range(1, nz)]
    x_peers = [(dx, shifted(x, dx, nx)) for dx in range(1, nx)]
    group = [
        (shifted(x, dx, nx), shifted(c, dc, nc)) for dc in range(nc) for dx in range(nx) if (dc, dx) != (0, 0)
    ]
    up, down, across = shifted(y, 1, ny), shifted(y, ny - 1, ny), shifted(y, 2, ny)

    sent = []
    counter = [0, 0]

    def send(src, dst, to):
        i = counter[0]
        counter[0] += 1
        copy = pltpu.make_async_remote_copy(
            src_ref=src, dst_ref=dst, send_sem=send_sem.at[i], recv_sem=recv_sem.at[i], device_id=to, device_id_type=MESH
        )
        copy.start()
        sent.append(copy)
        return copy

    def fetch(src, dst):
        i = counter[1]
        counter[1] += 1
        copy = pltpu.make_async_copy(src, dst, local_sem.at[i])
        copy.start()
        return copy

    def wait_all(copies):
        for copy in copies:
            copy.wait_recv()

    def tokens(yy):
        return pl.ds(pl.multiple_of(yy * tok, tok), tok)

    load_rt = fetch(rt_in, rt)
    load_vgx = fetch(vg.at[tokens(y)], vgx.at[k, y])
    share = d // 4
    load_err = [fetch(err.at[pl.ds(i * share, share)], err_v.at[pl.ds(i * share, share)]) for i in range(4)]
    load_act = fetch(act, actr.at[0])
    load_vg = [fetch(vg.at[tokens(yy)], vg_v.at[i]) for i, yy in enumerate((y, down, up, across))]
    load_w = [
        fetch(w.at[pl.ds(pl.multiple_of((k * nz + zz) * BLK, BLK), BLK)], wbuf.at[zz, y]) for zz in range(nz)
    ]

    barrier = pltpu.get_barrier_semaphore()
    everyone = (
        [device(z, xx, cc, y) for xx, cc in group]
        + [device(zz, x, c, y) for _, zz in z_peers]
        + [device(z, x, c, yy) for _, yy in y_peers]
    )
    for peer in everyone:
        pl.semaphore_signal(barrier, inc=1, device_id=peer, device_id_type=MESH)
    pl.semaphore_wait(barrier, len(everyone))

    recv_rt = [send(rt_in, rtf.at[y], device(z, x, c, yy)) for _, yy in y_peers]
    recv_vg = [send(vg.at[tokens(yy)], vgx.at[k, y], device(z, x, c, yy)) for _, yy in y_peers]
    recv_w = [
        send(w.at[pl.ds(pl.multiple_of((k * nz + z) * BLK, BLK), BLK)], wbuf.at[z, y], device(z, x, c, yy))
        for _, yy in y_peers
    ]
    half = CHUNKS // 2
    part = d // CHUNKS

    def cols(i):
        return pl.ds(i * part, part)

    from_down, from_up, from_across = {}, {}, {}
    for i in range(CHUNKS):
        j = (i + half) % CHUNKS
        from_down[i] = send(act.at[:, cols(i)], actr.at[1, :, cols(i)], device(z, x, c, up))
        from_up[j] = send(act.at[:, cols(j)], actr.at[2, :, cols(j)], device(z, x, c, down))

    def forward(i):
        from_down[i].wait_recv()
        from_across[i] = send(actr.at[1, :, cols(i)], actr.at[3, :, cols(i)], device(z, x, c, up))
        j = i + half
        from_up[j].wait_recv()
        from_across[j] = send(actr.at[2, :, cols(j)], actr.at[3, :, cols(j)], device(z, x, c, down))

    load_rt.wait()
    rtf[y] = rt[...]
    rt3 = rows3(rt[...])

    def columns(p):
        return pl.ds(pl.multiple_of(p * wide, wide), wide)

    def store_left(value, cc, j0):
        for j in range(wb):
            lacc[cc, j0 + j] = value[:, j * BLK : (j + 1) * BLK]

    def load_left(ref, cc, j0):
        return jnp.concatenate([ref[cc, j0 + j] for j in range(wb)], axis=1)

    per_piece = per // wb

    for load in load_err:
        load.wait()

    def err_left(p, carry):
        hi, lo = split2(err_v[columns(p), :])
        store_left(fold3(mm(rt3, lo, NT)) + fold3(mm(rt3, hi, NT)), lax.div(p, per_piece), lax.rem(p, per_piece) * wb)
        return carry

    lax.fori_loop(0, pieces, err_left, 0)

    wait_all(recv_rt)
    load_vgx.wait()
    wait_all(recv_vg)
    recv_vgx = [send(vgx.at[k], vgx.at[k], device(z, xx, cc, y)) for xx, cc in group]
    ut = jnp.zeros((r, tok), F32)
    for yy in range(ny):
        ut = ut + fold3(mm(rows3(rtf[yy]), vgx[k, yy], NT))
    ut3 = rows3(ut)
    load_act.wait()

    def act_left(cc):
        def step(i, carry):
            value = fold3(mm(ut3, actr[0, :, columns(cc * per_piece + i)]))
            store_left(load_left(lacc, cc, i * wb) + value, cc, i * wb)
            return carry

        lax.fori_loop(0, per_piece, step, 0)

    recv_c = []
    for dc in range(1, nc):
        cc = shifted(c, dc, nc)
        act_left(cc)
        recv_c.append(send(lacc.at[cc], rc, device(z, x, cc, y)))
    act_left(c)

    for copy in load_w:
        copy.wait()
    recv_wz = []
    for copy, (dy, _) in zip(recv_w, y_peers):
        copy.wait_recv()
        source = shifted(y, ny - dy, ny)
        for _, zz in z_peers:
            recv_wz.append(send(wbuf.at[z, source], wbuf.at[z, source], device(zz, x, c, y)))

    wait_all(recv_c)
    lacc[c] += rc[...]
    recv = [
        send(lacc.at[c, pl.ds(xx * nz, nz)], rx.at[dx - 1], device(z, xx, c, y)) for dx, xx in x_peers
    ]
    wait_all(recv)
    own_x = pl.ds(x * nz, nz)
    total = lacc[c, own_x]
    for dx in range(nx - 1):
        total = total + rx[dx]
    lacc[c, own_x] = total
    mine = x * nz + z
    recv = [send(lacc.at[c, x * nz + zz], rz.at[dz - 1], device(zz, x, c, y)) for dz, zz in z_peers]
    wait_all(recv)
    total = lacc[c, mine]
    for dz in range(nz - 1):
        total = total + rz[dz]
    lacc[c, mine] = total

    def strip(yy):
        return pl.ds(pl.multiple_of(yy * rq, rq), rq)

    recv = [send(lacc.at[c, mine, strip(yy)], ry.at[dy - 1], device(z, x, c, yy)) for dy, yy in y_peers]
    forward(0)
    wait_all(recv)
    total = lacc[c, mine, strip(y)]
    for dy in range(ny - 1):
        total = total + ry[dy]
    lf[c, mine, strip(y)] = total

    own = lf.at[c, mine, strip(y)]
    recv = [send(own, own, device(z, x, c, yy)) for _, yy in y_peers]
    forward(1)
    wait_all(recv)
    own = lf.at[c, mine]
    recv = [send(own, own, device(zz, x, c, y)) for _, zz in z_peers]
    wait_all(recv)
    own = lf.at[c, own_x]
    recv = [send(own, own, device(z, xx, c, y)) for _, xx in x_peers]

    wait_all(recv_wz)
    wait_all(recv_vgx)
    xc = nc * nx
    many = min(4, xc)

    def input_grad(i, carry):
        zz, g = lax.div(i, xc // many), lax.rem(i, xc // many)
        total = None
        for yy in range(ny):
            cotangent = vgx[pl.ds(g * many, many), yy].reshape(many * tok, BLK)
            piece = mm(cotangent, wbuf[zz, yy], NT).astype(BF16).astype(F32)
            total = piece if total is None else total + piece
        outs[zz, pl.ds(g * many, many)] = total.astype(BF16).reshape(many, tok, BLK)
        return carry

    lax.fori_loop(0, nz * xc // many, input_grad, 0)

    def place(zz):
        return gi.at[:, pl.ds(pl.multiple_of((k * nz + zz) * BLK, BLK), BLK)]

    sent_out = [
        send(outs.at[zz, cc * nx + xx], place(zz), device(z, xx, cc, y)) for xx, cc in group for zz in range(nz)
    ]
    kept_out = [fetch(outs.at[zz, k], place(zz)) for zz in range(nz)]

    wait_all(recv)
    own = lf.at[c]
    recv = [send(own, own, device(z, x, shifted(c, dc, nc), y)) for dc in range(1, nc)]
    forward(2)
    wait_all(recv)

    def left_piece(p):
        return load_left(lf, lax.div(p, per_piece), lax.rem(p, per_piece) * wb)

    def first_gram(p, total):
        block = rows3(left_piece(p))
        return total + mm(block, block, NT)

    nothing = jnp.zeros((3 * r, 3 * r), F32)
    gram = self_products(lax.fori_loop(0, pieces, first_gram, nothing), r)
    weights, norms = gram_schmidt(gram)
    forward(3)

    def apply_first(p, total):
        block = times(weights, left_piece(p))
        q1[p] = block
        block = rows3(block)
        return total + mm(block, block, NT)

    off = self_products(lax.fori_loop(0, pieces, apply_first, nothing), r) - norms
    row_id = lax.broadcasted_iota(jnp.int32, (r, r), 0)
    col_id = lax.broadcasted_iota(jnp.int32, (r, r), 1)
    again = jnp.where(col_id < row_id, off, jnp.where(col_id == row_id, 0.5 * off, 0.0))

    def apply_second(p, total):
        block = q1[p]
        block = block - times(again, block)
        for j in range(wb):
            q_out[p * wb + j] = block[:, j * BLK : (j + 1) * BLK]
        block = rows3(block)
        q3[p] = block
        return total + mm(block, actr[0, :, columns(p)], NT)

    pt = fold3(lax.fori_loop(0, pieces, apply_second, jnp.zeros((3 * r, tok), F32)))
    ptf[0] = pt
    recv = [send(ptf.at[0], ptf.at[dy], device(z, x, c, yy)) for dy, yy in y_peers]

    def err_right(p, total):
        hi, lo = split2(err_v[columns(p), :])
        return total + (mm(q3[p], lo) + mm(q3[p], hi))

    right = fold3(lax.fori_loop(0, pieces, err_right, jnp.zeros((3 * r, err_v.shape[1]), F32)))
    for load in load_vg:
        load.wait()
    wait_all(recv)
    for dy, slot in enumerate((0, 1, 3, 2)):
        right = right + fold3(mm(rows3(ptf[dy]), vg_v[slot]))
    rs0[...] = right
    recv = [send(rs0, rr_c.at[dc - 1], device(z, x, shifted(c, dc, nc), y)) for dc in range(1, nc)]

    for i in range(CHUNKS):
        if i >= half:
            from_down[i].wait_recv()
        else:
            from_up[i].wait_recv()
    near = vg_v[1:3].reshape(2 * tok, BLK)

    def merge_near(i, carry):
        at = pl.ds(pl.multiple_of(i * BLK, BLK), BLK)
        block = actr[1:3, :, at].reshape(2 * tok, BLK)
        merged[at, :] = err_v[at, :] + mm(block, near, TN)
        return carry

    def some_near(p, of):
        lax.fori_loop(p * nb // of, (p + 1) * nb // of, merge_near, 0)

    some_near(0, 4)
    wait_all(recv)
    for dc in range(nc - 1):
        right = right + rr_c[dc]
    rs1[0] = right
    recv = [send(rs1.at[0], rr_x.at[dx - 1], device(z, xx, c, y)) for dx, xx in x_peers]
    some_near(1, 4)
    wait_all(recv)
    for dx in range(nx - 1):
        right = right + rr_x[dx]
    rs1[1] = right
    recv = [send(rs1.at[1], rr_z.at[dz - 1], device(zz, x, c, y)) for dz, zz in z_peers]
    some_near(2, 4)
    some_near(3, 4)
    wait_all(recv)
    for dz in range(nz - 1):
        right = right + rr_z[dz]
    r_out[...] = right / float(nz * nx * nc)

    far = jnp.concatenate([vg_v[0], vg_v[3]], axis=0)

    def merge_far(i, carry):
        at = pl.ds(pl.multiple_of(i * BLK, BLK), BLK)
        block = jnp.concatenate([actr[0, :, at], actr[3, :, at]], axis=0)
        merged[at, :] += mm(block, far, TN)
        return carry

    for i in range(half):
        for j in (i, i + half):
            from_across[j].wait_recv()
            lax.fori_loop(j * part // BLK, (j + 1) * part // BLK, merge_far, 0)

    wait_all(sent_out)
    for copy in kept_out:
        copy.wait()
    for copy in sent:
        copy.wait_send()


def error_kernel(merged, q, right, gi_in, out, left_out, right_out, gi_out):
    gi_out[...] = gi_in[...]
    right_out[...] = right[...]
    scale = math.sqrt(float(D))
    hi, lo = split2(right[...])
    right3 = jnp.concatenate([hi, hi, lo], axis=0)
    for j in range(q.shape[0]):
        cols = slice(j * BLK, (j + 1) * BLK)
        left_out[:, cols] = q[j] * scale
        hi, lo = split2(q[j])
        approx = mm(jnp.concatenate([hi, lo, hi], axis=0), right3, TN)
        out[cols, :] = merged[cols, :] - approx


def build(geom):
    nz, nx, nc, ny = geom

    def body(act, vg, w, err, right_prev):
        tok, d = act.shape
        kv = vg.shape[1]
        r = right_prev.shape[1]
        nb = nc * nx * nz
        per = nx * nz
        wide = min(WIDE, per * BLK)
        assert d == nb * BLK and kv == BLK and per * BLK % wide == 0
        xc = nx * nc
        sends = 6 * (ny - 1) + 3 * CHUNKS + (xc - 1) * (nz + 1) + (ny - 1) * (nz - 1) + 3 * (nc + nx + nz - 3)
        inputs = [
            pltpu.with_memory_space_constraint(a, pltpu.HBM) for a in (act, vg, w, err[0], right_prev.T)
        ]
        hbm = pl.BlockSpec(memory_space=pltpu.HBM)
        vmem = pl.BlockSpec(memory_space=pltpu.VMEM)
        merged, q, right, grad_input = pl.pallas_call(
            functools.partial(comm_kernel, geom),
            out_shape=(
                pltpu.VMEM((d, kv), F32),
                pltpu.VMEM((nb, r, BLK), F32),
                pltpu.VMEM((r, kv), F32),
                pltpu.VMEM((tok, d), BF16),
            ),
            in_specs=[hbm] * 5,
            out_specs=(vmem, vmem, vmem, vmem),
            scratch_shapes=[
                pltpu.VMEM((r, kv), F32),
                pltpu.VMEM((ny, tok, d), BF16),
                pltpu.VMEM((ny, tok, kv), BF16),
                pltpu.VMEM((d, kv), F32),
                pltpu.VMEM((ny, r, kv), F32),
                pltpu.VMEM((xc, ny, tok, kv), BF16),
                pltpu.VMEM((nz, ny, BLK, kv), BF16),
                pltpu.VMEM((nz, xc, tok, BLK), BF16),
                pltpu.VMEM((nc, per, r, BLK), F32),
                pltpu.VMEM((nc, per, r, BLK), F32),
                pltpu.VMEM((per, r, BLK), F32),
                pltpu.VMEM((max(nx - 1, 1), nz, r, BLK), F32),
                pltpu.VMEM((max(nz - 1, 1), r, BLK), F32),
                pltpu.VMEM((ny - 1, r // ny, BLK), F32),
                pltpu.VMEM((d // wide, r, wide), F32),
                pltpu.VMEM((d // wide, 3 * r, wide), BF16),
                pltpu.VMEM((ny, r, tok), F32),
                pltpu.VMEM((r, kv), F32),
                pltpu.VMEM((2, r, kv), F32),
                pltpu.VMEM((max(nc - 1, 1), r, kv), F32),
                pltpu.VMEM((max(nx - 1, 1), r, kv), F32),
                pltpu.VMEM((max(nz - 1, 1), r, kv), F32),
                pltpu.SemaphoreType.DMA((1 + 1 + 4 + 1 + ny + 2 * nz,)),
                pltpu.SemaphoreType.DMA((sends,)),
                pltpu.SemaphoreType.DMA((sends,)),
            ],
            compiler_params=pltpu.CompilerParams(
                collective_id=0, has_side_effects=True, vmem_limit_bytes=44 * MIB
            ),
        )(*inputs)

        blocks = min(4, nb)
        width = blocks * BLK
        error_next, left, right, grad_input = pl.pallas_call(
            error_kernel,
            grid=(d // width,),
            out_shape=(
                jax.ShapeDtypeStruct((d, kv), F32),
                jax.ShapeDtypeStruct((r, d), F32),
                jax.ShapeDtypeStruct((r, kv), F32),
                jax.ShapeDtypeStruct((tok, d), BF16),
            ),
            in_specs=[
                pl.BlockSpec((width, kv), lambda i: (i, 0)),
                pl.BlockSpec((blocks, r, BLK), lambda i: (i, 0, 0)),
                pl.BlockSpec((r, kv), lambda i: (0, 0)),
                pl.BlockSpec((tok, width), lambda i: (0, i)),
            ],
            out_specs=(
                pl.BlockSpec((width, kv), lambda i: (i, 0)),
                pl.BlockSpec((r, width), lambda i: (0, i)),
                pl.BlockSpec((r, kv), lambda i: (0, 0)),
                pl.BlockSpec((tok, width), lambda i: (0, i)),
            ),
            compiler_params=pltpu.CompilerParams(vmem_limit_bytes=20 * MIB),
        )(merged, q, right, grad_input)
        return (grad_input, error_next[None], left.T, right.T)

    return body


def solution(mesh):
    return jax.shard_map(
        build((4, 4, 2, 4)),
        mesh=mesh,
        in_specs=(
            P(("dp", "tp"), None),
            P("dp", "tp"),
            P(None, "tp"),
            P("dp", None, "tp"),
            P("tp", None),
        ),
        out_specs=(P(("dp", "tp"), None), P("dp", None, "tp"), P(), P("tp", None)),
        check_vma=False,
    )
```

```python
import functools
import math

import jax
import jax.numpy as jnp
from jax import lax
from jax.experimental import pallas as pl
from jax.experimental.pallas import tpu as pltpu
from jax.sharding import PartitionSpec as P

MESH = pl.DeviceIdType.MESH
F32 = jnp.float32
BF16 = jnp.bfloat16
BLK = 256
EPS = 1e-12
MIB = 1024 * 1024
WIDE = 8 * BLK
CHUNKS = 8
NN = (((1,), (0,)), ((), ()))
NT = (((1,), (1,)), ((), ()))
TN = (((0,), (0,)), ((), ()))


def mm(a, b, dims=NN):
    return lax.dot_general(a, b, dims, preferred_element_type=F32)


def split2(a):
    hi = a.astype(BF16)
    lo = (a - hi.astype(F32)).astype(BF16)
    return hi, lo


def split3(a):
    hi = a.astype(BF16)
    rest = a - hi.astype(F32)
    mid = rest.astype(BF16)
    lo = (rest - mid.astype(F32)).astype(BF16)
    return hi, mid, lo


def rows3(a):
    return jnp.concatenate(split3(a), axis=0)


def fold3(a):
    n = a.shape[0] // 3
    return (a[2 * n :] + a[n : 2 * n]) + a[:n]


def self_products(total, r):
    total = fold3(total)
    return (total[:, 2 * r :] + total[:, r : 2 * r]) + total[:, :r]


def times(a, b):
    a_hi, a_mid, a_lo = (v.astype(F32) for v in split3(a))
    b_hi, b_mid, b_lo = split3(b)
    left = jnp.concatenate([a_lo, a_mid, a_hi, a_mid, a_hi, a_hi], axis=1).astype(BF16)
    return mm(left, jnp.concatenate([b_hi, b_mid, b_lo, b_hi, b_mid, b_hi], axis=0))


def eye_like(n):
    return (lax.broadcasted_iota(jnp.int32, (n, n), 0) == lax.broadcasted_iota(jnp.int32, (n, n), 1)).astype(F32)


def gram_schmidt_steps(state, steps):
    left, weights = state
    n = left.shape[0]
    row_id = lax.broadcasted_iota(jnp.int32, (n, 1), 0)
    for j in steps:
        column = jnp.broadcast_to(left[:, j : j + 1], (n, n))
        s = jnp.maximum(column[j : j + 1, :], 0.0)
        inverse = 1.0 / (s + EPS)
        c = (2.0 - s * inverse) * inverse
        f = jnp.where(row_id > j, column * c, 0.0)
        new_weights = weights - f * weights[j : j + 1, :]
        left = left - (f * (2.0 - c * s)) * left[j : j + 1, :]
        weights = new_weights
    return left, weights


def unit_weights(state):
    left, weights = state
    eye = eye_like(left.shape[0])
    s = jnp.maximum(jnp.sum(left * eye, axis=1, keepdims=True), 0.0)
    return weights / jnp.sqrt(s + EPS), eye * (s / (s + EPS))


def comm_kernel(
    geom, act, vg, w, err, rt_in, error_out, left_out, r_out, gi,
    rt, actr, vg_v, err_v, rtf, vgx, wbuf, outs, lacc, lf, rc, rxz, ysum, q1, q3, zout, zin, tz,
    local_sem, send_sem, recv_sem,
):
    nz, nx, nc, ny = geom
    nb = nc * nx * nz
    per = nx * nz
    _, tok, d = actr.shape
    r = rt.shape[0]
    wide = min(WIDE, per * BLK)
    wb = wide // BLK
    pieces = d // wide
    per_piece = per // wb
    dp, y = lax.axis_index("dp"), lax.axis_index("tp")
    c = lax.rem(dp, nc)
    x = lax.rem(lax.div(dp, nc), nx)
    z = lax.div(dp, nc * nx)
    k = c * nx + x
    mine = x * nz + z

    def shifted(i, by, n):
        return lax.rem(i + by, n)

    def device(zz, xx, cc, yy):
        return ((zz * nx + xx) * nc + cc, yy)

    y_peers = [(dy, shifted(y, dy, ny)) for dy in range(1, ny)]
    z_peers = [(dz, shifted(z, dz, nz)) for dz in range(1, nz)]
    x_peers = [(dx, shifted(x, dx, nx)) for dx in range(1, nx)]
    plane = [
        (shifted(x, dx, nx), shifted(z, dz, nz)) for dx in range(nx) for dz in range(nz) if (dx, dz) != (0, 0)
    ]
    group = [
        (shifted(x, dx, nx), shifted(c, dc, nc)) for dc in range(nc) for dx in range(nx) if (dc, dx) != (0, 0)
    ]
    cores = [shifted(c, dc, nc) for dc in range(1, nc)]
    up, down, across = shifted(y, 1, ny), shifted(y, ny - 1, ny), shifted(y, 2, ny)

    sent = []
    counter = [0, 0]

    def send(src, dst, to):
        i = counter[0]
        counter[0] += 1
        copy = pltpu.make_async_remote_copy(
            src_ref=src, dst_ref=dst, send_sem=send_sem.at[i], recv_sem=recv_sem.at[i], device_id=to, device_id_type=MESH
        )
        copy.start()
        sent.append(copy)
        return copy

    def fetch(src, dst):
        i = counter[1]
        counter[1] += 1
        copy = pltpu.make_async_copy(src, dst, local_sem.at[i])
        copy.start()
        return copy

    def wait_all(copies):
        for copy in copies:
            copy.wait_recv()

    def tokens(yy):
        return pl.ds(pl.multiple_of(yy * tok, tok), tok)

    def weight_rows(zz):
        return pl.ds(pl.multiple_of((k * nz + zz) * BLK, BLK), BLK)

    load_rt = fetch(rt_in, rt)
    load_vgx = fetch(vg.at[tokens(y)], vgx.at[k, y])
    share = d // 4
    load_err = [fetch(err.at[pl.ds(i * share, share)], err_v.at[pl.ds(i * share, share)]) for i in range(4)]
    load_act = fetch(act, actr.at[0])
    load_vg = [fetch(vg.at[tokens(yy)], vg_v.at[i]) for i, yy in enumerate((y, down, up, across))]
    load_w = [fetch(w.at[weight_rows(zz)], wbuf.at[zz, y]) for zz in range(nz)]

    barrier = pltpu.get_barrier_semaphore()
    everyone = (
        [device(z, xx, cc, y) for xx, cc in group]
        + [device(zz, shifted(x, dx, nx), c, y) for dx in range(nx) for _, zz in z_peers]
        + [device(z, x, cc, yy) for _, yy in y_peers for cc in [c] + cores]
    )
    for peer in everyone:
        pl.semaphore_signal(barrier, inc=1, device_id=peer, device_id_type=MESH)
    pl.semaphore_wait(barrier, len(everyone))

    recv_rt = [send(rt_in, rtf.at[y], device(z, x, c, yy)) for _, yy in y_peers]
    recv_vg = [send(vg.at[tokens(yy)], vgx.at[k, y], device(z, x, c, yy)) for _, yy in y_peers]
    half = CHUNKS // 2
    part = d // CHUNKS

    def cols(i):
        return pl.ds(i * part, part)

    from_down, from_up, from_across = {}, {}, {}

    def direct(*numbers):
        for i in numbers:
            j = (i + half) % CHUNKS
            from_down[i] = send(act.at[:, cols(i)], actr.at[1, :, cols(i)], device(z, x, c, up))
            from_up[j] = send(act.at[:, cols(j)], actr.at[2, :, cols(j)], device(z, x, c, down))

    def forward(*numbers):
        for i in numbers:
            from_down[i].wait_recv()
            from_across[i] = send(actr.at[1, :, cols(i)], actr.at[3, :, cols(i)], device(z, x, c, up))
            j = i + half
            from_up[j].wait_recv()
            from_across[j] = send(actr.at[2, :, cols(j)], actr.at[3, :, cols(j)], device(z, x, c, down))

    direct(0, 1, 2)

    load_rt.wait()
    rtf[y] = rt[...]
    rt3 = rows3(rt[...])

    def columns(p):
        return pl.ds(pl.multiple_of(p * wide, wide), wide)

    def store_left(value, cc, j0):
        for j in range(wb):
            lacc[cc, j0 + j] = value[:, j * BLK : (j + 1) * BLK]

    def load_left(ref, cc, j0):
        return jnp.concatenate([ref[cc, j0 + j] for j in range(wb)], axis=1)

    for load in load_err:
        load.wait()

    def err_left(p, carry):
        hi, lo = split2(err_v[columns(p), :])
        store_left(fold3(mm(rt3, lo, NT)) + fold3(mm(rt3, hi, NT)), lax.div(p, per_piece), lax.rem(p, per_piece) * wb)
        return carry

    lax.fori_loop(0, pieces, err_left, 0)

    wait_all(recv_rt)
    load_vgx.wait()
    wait_all(recv_vg)
    recv_vgx = [send(vgx.at[k], vgx.at[k], device(z, xx, c, y)) for _, xx in x_peers]
    relayed = [send(vgx.at[k], vgx.at[k], device(z, x, cc, y)) for cc in cores]
    ut = jnp.zeros((r, tok), F32)
    for yy in range(ny):
        ut = ut + fold3(mm(rows3(rtf[yy]), vgx[k, yy], NT))
    ut3 = rows3(ut)
    load_act.wait()

    def act_left(cc):
        def step(i, carry):
            value = fold3(mm(ut3, actr[0, :, columns(cc * per_piece + i)]))
            store_left(load_left(lacc, cc, i * wb) + value, cc, i * wb)
            return carry

        lax.fori_loop(0, per_piece, step, 0)

    recv = []
    for cc in cores:
        act_left(cc)
        recv.append(send(lacc.at[cc], rc, device(z, x, cc, y)))
    act_left(c)

    wait_all(recv)
    lacc[c] += rc[...]
    recv = [
        send(lacc.at[c, xx * nz + zz], rxz.at[i], device(zz, xx, c, y)) for i, (xx, zz) in enumerate(plane)
    ]
    direct(3)
    recv_w = [send(w.at[weight_rows(z)], wbuf.at[z, y], device(z, x, c, yy)) for _, yy in y_peers]
    wait_all(recv)
    total = lacc[c, mine]
    for i in range(len(plane)):
        total = total + rxz[i]
    ysum[y] = total
    own = ysum.at[y]
    recv = [send(own, own, device(z, x, c, yy)) for _, yy in y_peers]
    direct(4)
    wait_all(recv)
    total = ysum[0]
    for yy in range(1, ny):
        total = total + ysum[yy]
    lf[c, mine] = total
    own = lf.at[c, mine]
    recv = [send(own, own, device(zz, xx, c, y)) for xx, zz in plane]
    direct(5)
    wait_all(recv)
    own = lf.at[c]
    recv = [send(own, own, device(z, x, cc, y)) for cc in cores]

    for copy in load_w:
        copy.wait()
    recv_wz = []
    for copy, (dy, _) in zip(recv_w, y_peers):
        copy.wait_recv()
        source = shifted(y, ny - dy, ny)
        for _, zz in z_peers:
            recv_wz.append(send(wbuf.at[z, source], wbuf.at[z, source], device(zz, x, c, y)))
    for copy, (dx, _) in zip(recv_vgx, x_peers):
        copy.wait_recv()
        slot = c * nx + shifted(x, nx - dx, nx)
        relayed += [send(vgx.at[slot], vgx.at[slot], device(z, x, cc, y)) for cc in cores]
    direct(6)
    wait_all(recv)

    def products(p, carry):
        gram, by_act, by_err = carry
        block = rows3(load_left(lf, lax.div(p, per_piece), lax.rem(p, per_piece) * wb))
        hi, lo = split2(err_v[columns(p), :])
        by_act = by_act + mm(block, actr[0, :, columns(p)], NT)
        by_err = by_err + (mm(block, lo) + mm(block, hi))
        return gram + mm(block, block, NT), by_act, by_err

    gram, by_act, by_err = lax.fori_loop(
        0,
        pieces,
        products,
        (jnp.zeros((3 * r, 3 * r), F32), jnp.zeros((3 * r, tok), F32), jnp.zeros((3 * r, err_v.shape[1]), F32)),
    )
    by_act = rows3(fold3(by_act))
    for yy in range(ny):
        zout[yy] = fold3(mm(by_act, vgx[k, yy]))
    zout[y] += fold3(by_err)
    zin[c, y] = zout[y]
    recv = [
        send(zout.at[yy], zin.at[c, y], device(z, x, cc, yy))
        for yy, cc in [(yy, cc) for _, yy in y_peers for cc in [c] + cores] + [(y, cc) for cc in cores]
    ]
    direct(7)
    forward(0)

    state = self_products(gram, r), eye_like(r)
    state = gram_schmidt_steps(state, range(r // 2))
    wait_all(recv)
    total = None
    for cc in range(nc):
        for yy in range(ny):
            total = zin[cc, yy] if total is None else total + zin[cc, yy]
    tz[mine] = total
    own = tz.at[mine]
    recv = [send(own, own, device(zz, xx, c, y)) for xx, zz in plane]
    forward(1)
    state = gram_schmidt_steps(state, range(r // 2, r))
    weights, norms = unit_weights(state)

    def apply_first(p, total):
        block = times(weights, load_left(lf, lax.div(p, per_piece), lax.rem(p, per_piece) * wb))
        q1[p] = block
        block = rows3(block)
        return total + mm(block, block, NT)

    off = self_products(lax.fori_loop(0, pieces, apply_first, jnp.zeros((3 * r, 3 * r), F32)), r) - norms
    row_id = lax.broadcasted_iota(jnp.int32, (r, r), 0)
    col_id = lax.broadcasted_iota(jnp.int32, (r, r), 1)
    again = jnp.where(col_id < row_id, off, jnp.where(col_id == row_id, 0.5 * off, 0.0))
    weights = weights - times(again, weights)
    scale = math.sqrt(float(d))

    def apply_second(p, carry):
        block = q1[p]
        block = block - times(again, block)
        left_out[:, columns(p)] = block * scale
        hi, lo = split2(block)
        q3[p] = jnp.concatenate([hi, lo, hi], axis=0)
        return carry

    lax.fori_loop(0, pieces, apply_second, 0)
    forward(2)

    wait_all(recv_wz)
    wait_all(relayed)
    xc = nc * nx
    many = min(4, xc)

    def input_grad(i, carry):
        zz, g = lax.div(i, xc // many), lax.rem(i, xc // many)
        total = None
        for yy in range(ny):
            cotangent = vgx[pl.ds(g * many, many), yy].reshape(many * tok, BLK)
            piece = mm(cotangent, wbuf[zz, yy], NT).astype(BF16).astype(F32)
            total = piece if total is None else total + piece
        outs[zz, pl.ds(g * many, many)] = total.astype(BF16).reshape(many, tok, BLK)
        return carry

    lax.fori_loop(0, nz * xc // many, input_grad, 0)

    def place(zz):
        return gi.at[:, pl.ds(pl.multiple_of((k * nz + zz) * BLK, BLK), BLK)]

    sent_out = [
        send(outs.at[zz, cc * nx + xx], place(zz), device(z, xx, cc, y)) for xx, cc in group for zz in range(nz)
    ]
    kept_out = [fetch(outs.at[zz, k], place(zz)) for zz in range(nz)]
    forward(3)

    wait_all(recv)
    total = tz[0]
    for i in range(1, per):
        total = total + tz[i]
    right = times(weights, total) / float(nb)
    r_out[...] = right
    hi, lo = split2(right)
    right3 = jnp.concatenate([hi, hi, lo], axis=0)

    for load in load_vg:
        load.wait()
    for i in range(CHUNKS):
        if i >= half:
            from_down[i].wait_recv()
        else:
            from_up[i].wait_recv()
    near = vg_v[0:3].reshape(3 * tok, BLK)
    far = vg_v[3]

    def error_near(i, carry):
        at = pl.ds(pl.multiple_of(i * BLK, BLK), BLK)
        block = actr[0:3, :, at].reshape(3 * tok, BLK)
        inside = pl.ds(pl.multiple_of(lax.rem(i, wb) * BLK, BLK), BLK)
        approx = mm(q3[lax.div(i, wb), :, inside], right3, TN)
        error_out[at, :] = (err_v[at, :] - approx) + mm(block, near, TN)
        return carry

    lax.fori_loop(0, nb, error_near, 0)

    def error_far(i, carry):
        at = pl.ds(pl.multiple_of(i * BLK, BLK), BLK)
        error_out[at, :] += mm(actr[3, :, at], far, TN)
        return carry

    for i in range(half):
        for j in (i, i + half):
            from_across[j].wait_recv()
            lax.fori_loop(j * part // BLK, (j + 1) * part // BLK, error_far, 0)

    wait_all(sent_out)
    for copy in kept_out:
        copy.wait()
    for copy in sent:
        copy.wait_send()


def store_kernel(error_in, left_in, right_in, gi_in, error_out, left_out, right_out, gi_out, sem):
    n = 8
    rows = error_in.shape[0] // n
    pairs = [(error_in.at[pl.ds(i * rows, rows)], error_out.at[pl.ds(i * rows, rows)]) for i in range(n)]
    pairs += [(left_in, left_out), (right_in, right_out), (gi_in, gi_out)]
    copies = [pltpu.make_async_copy(a, b, sem.at[i]) for i, (a, b) in enumerate(pairs)]
    for copy in copies:
        copy.start()
    for copy in copies:
        copy.wait()


def build(geom):
    nz, nx, nc, ny = geom

    def body(act, vg, w, err, right_prev):
        tok, d = act.shape
        kv = vg.shape[1]
        r = right_prev.shape[1]
        nb = nc * nx * nz
        per = nx * nz
        wide = min(WIDE, per * BLK)
        assert d == nb * BLK and kv == BLK and per * BLK % wide == 0
        xc = nx * nc
        sends = (
            4 * (ny - 1) + 3 * CHUNKS + (nx - 1) + nx * (nc - 1) + (xc - 1) * nz + (ny - 1) * (nz - 1)
            + 3 * (per - 1) + 2 * (nc - 1) + (ny * nc - 1)
        )
        inputs = [
            pltpu.with_memory_space_constraint(a, pltpu.HBM) for a in (act, vg, w, err[0], right_prev.T)
        ]
        hbm = pl.BlockSpec(memory_space=pltpu.HBM)
        vmem = pl.BlockSpec(memory_space=pltpu.VMEM)
        anywhere = pl.BlockSpec(memory_space=pl.ANY)
        results = (((d, kv), F32), ((r, d), F32), ((r, kv), F32), ((tok, d), BF16))
        made = pl.pallas_call(
            functools.partial(comm_kernel, geom),
            out_shape=tuple(pltpu.VMEM(*shape) for shape in results),
            in_specs=[hbm] * 5,
            out_specs=(vmem,) * 4,
            scratch_shapes=[
                pltpu.VMEM((r, kv), F32),
                pltpu.VMEM((ny, tok, d), BF16),
                pltpu.VMEM((ny, tok, kv), BF16),
                pltpu.VMEM((d, kv), F32),
                pltpu.VMEM((ny, r, kv), F32),
                pltpu.VMEM((xc, ny, tok, kv), BF16),
                pltpu.VMEM((nz, ny, BLK, kv), BF16),
                pltpu.VMEM((nz, xc, tok, BLK), BF16),
                pltpu.VMEM((nc, per, r, BLK), F32),
                pltpu.VMEM((nc, per, r, BLK), F32),
                pltpu.VMEM((per, r, BLK), F32),
                pltpu.VMEM((per - 1, r, BLK), F32),
                pltpu.VMEM((ny, r, BLK), F32),
                pltpu.VMEM((d // wide, r, wide), F32),
                pltpu.VMEM((d // wide, 3 * r, wide), BF16),
                pltpu.VMEM((ny, r, kv), F32),
                pltpu.VMEM((nc, ny, r, kv), F32),
                pltpu.VMEM((per, r, kv), F32),
                pltpu.SemaphoreType.DMA((1 + 1 + 4 + 1 + ny + 2 * nz,)),
                pltpu.SemaphoreType.DMA((sends,)),
                pltpu.SemaphoreType.DMA((sends,)),
            ],
            compiler_params=pltpu.CompilerParams(
                collective_id=0, has_side_effects=True, vmem_limit_bytes=44 * MIB
            ),
        )(*inputs)

        error_next, left, right, grad_input = pl.pallas_call(
            store_kernel,
            out_shape=tuple(jax.ShapeDtypeStruct(*shape) for shape in results),
            in_specs=[anywhere] * 4,
            out_specs=(anywhere,) * 4,
            scratch_shapes=[pltpu.SemaphoreType.DMA((11,))],
            compiler_params=pltpu.CompilerParams(vmem_limit_bytes=4 * MIB),
        )(*made)
        return (grad_input, error_next[None], left.T, right.T)

    return body


def solution(mesh):
    return jax.shard_map(
        build((4, 4, 2, 4)),
        mesh=mesh,
        in_specs=(
            P(("dp", "tp"), None),
            P("dp", "tp"),
            P(None, "tp"),
            P("dp", None, "tp"),
            P("tp", None),
        ),
        out_specs=(P(("dp", "tp"), None), P("dp", None, "tp"), P(), P("tp", None)),
        check_vma=False,
    )
```

```python
import functools
import math

import jax
import jax.numpy as jnp
from jax import lax
from jax.experimental import pallas as pl
from jax.experimental.pallas import tpu as pltpu
from jax.sharding import PartitionSpec as P

MESH = pl.DeviceIdType.MESH
F32 = jnp.float32
BF16 = jnp.bfloat16
BLK = 256
EPS = 1e-12
MIB = 1024 * 1024
WIDE = 8 * BLK
CHUNKS = 8
NN = (((1,), (0,)), ((), ()))
NT = (((1,), (1,)), ((), ()))
TN = (((0,), (0,)), ((), ()))


def mm(a, b, dims=NN):
    return lax.dot_general(a, b, dims, preferred_element_type=F32)


def split2(a):
    hi = a.astype(BF16)
    lo = (a - hi.astype(F32)).astype(BF16)
    return hi, lo


def split3(a):
    hi = a.astype(BF16)
    rest = a - hi.astype(F32)
    mid = rest.astype(BF16)
    lo = (rest - mid.astype(F32)).astype(BF16)
    return hi, mid, lo


def rows3(a):
    return jnp.concatenate(split3(a), axis=0)


def fold3(a):
    n = a.shape[0] // 3
    return (a[2 * n :] + a[n : 2 * n]) + a[:n]


def rows2(a):
    return jnp.concatenate(split2(a), axis=0)


def fold2(a):
    n = a.shape[0] // 2
    return a[n:] + a[:n]


def self_products(total, r):
    total = fold3(total)
    return (total[:, 2 * r :] + total[:, r : 2 * r]) + total[:, :r]


def times(a, b):
    a_hi, a_mid, a_lo = (v.astype(F32) for v in split3(a))
    b_hi, b_mid, b_lo = split3(b)
    left = jnp.concatenate([a_lo, a_mid, a_hi, a_mid, a_hi, a_hi], axis=1).astype(BF16)
    return mm(left, jnp.concatenate([b_hi, b_mid, b_lo, b_hi, b_mid, b_hi], axis=0))


def eye_like(n):
    return (lax.broadcasted_iota(jnp.int32, (n, n), 0) == lax.broadcasted_iota(jnp.int32, (n, n), 1)).astype(F32)


def gram_schmidt(gram):
    n = gram.shape[0]
    left, weights = gram, eye_like(n)
    row_id = lax.broadcasted_iota(jnp.int32, (n, 1), 0)
    m = 4
    for j in range(0, n, m):
        columns = [jnp.broadcast_to(left[:, i : i + 1], (n, n)) for i in range(j, j + m)]
        rows = [left[i : i + 1, :] for i in range(j, j + m)]
        given = [weights[i : i + 1, :] for i in range(j, j + m)]
        off_left, off_weights = jnp.zeros((n, n), F32), jnp.zeros((n, n), F32)
        for i in range(m):
            at = j + i
            s = jnp.maximum(columns[i][at : at + 1, :], 0.0)
            inverse = 1.0 / (s + EPS)
            c = (2.0 - s * inverse) * inverse
            f = jnp.where(row_id > at, columns[i] * c, 0.0)
            h = f * (2.0 - c * s)
            for later in range(i + 1, m):
                to = j + later
                columns[later] = columns[later] - h * columns[later][at : at + 1, :]
                rows[later] = rows[later] - h[to : to + 1, :] * rows[i]
                given[later] = given[later] - f[to : to + 1, :] * given[i]
            off_left = off_left + h * rows[i]
            off_weights = off_weights + f * given[i]
        left, weights = left - off_left, weights - off_weights
    return left, weights


def unit_weights(state):
    left, weights = state
    eye = eye_like(left.shape[0])
    s = jnp.maximum(jnp.sum(left * eye, axis=1, keepdims=True), 0.0)
    return weights / jnp.sqrt(s + EPS), eye * (s / (s + EPS))


def comm_kernel(
    geom, act, vg, w, err, rt_in, error_out, left_out, r_out, gi,
    rt, actr, vg_v, err_v, rtf, vgx, wbuf, outs, lacc, lf, rc, rxz, ysum, q1, q3, zout, zin, tz,
    local_sem, send_sem, recv_sem,
):
    nz, nx, nc, ny = geom
    nb = nc * nx * nz
    per = nx * nz
    _, tok, d = actr.shape
    r = rt.shape[0]
    wide = min(WIDE, per * BLK)
    wb = wide // BLK
    pieces = d // wide
    per_piece = per // wb
    dp, y = lax.axis_index("dp"), lax.axis_index("tp")
    c = lax.rem(dp, nc)
    x = lax.rem(lax.div(dp, nc), nx)
    z = lax.div(dp, nc * nx)
    k = c * nx + x
    mine = x * nz + z

    def shifted(i, by, n):
        return lax.rem(i + by, n)

    def device(zz, xx, cc, yy):
        return ((zz * nx + xx) * nc + cc, yy)

    y_peers = [(dy, shifted(y, dy, ny)) for dy in range(1, ny)]
    z_peers = [(dz, shifted(z, dz, nz)) for dz in range(1, nz)]
    x_peers = [(dx, shifted(x, dx, nx)) for dx in range(1, nx)]
    plane = [
        (shifted(x, dx, nx), shifted(z, dz, nz)) for dx in range(nx) for dz in range(nz) if (dx, dz) != (0, 0)
    ]
    group = [
        (shifted(x, dx, nx), shifted(c, dc, nc)) for dc in range(nc) for dx in range(nx) if (dc, dx) != (0, 0)
    ]
    cores = [shifted(c, dc, nc) for dc in range(1, nc)]
    up, down, across = shifted(y, 1, ny), shifted(y, ny - 1, ny), shifted(y, 2, ny)

    sent = []
    counter = [0, 0]

    def send(src, dst, to):
        i = counter[0]
        counter[0] += 1
        copy = pltpu.make_async_remote_copy(
            src_ref=src, dst_ref=dst, send_sem=send_sem.at[i], recv_sem=recv_sem.at[i], device_id=to, device_id_type=MESH
        )
        copy.start()
        sent.append(copy)
        return copy

    def fetch(src, dst):
        i = counter[1]
        counter[1] += 1
        copy = pltpu.make_async_copy(src, dst, local_sem.at[i])
        copy.start()
        return copy

    def wait_all(copies):
        for copy in copies:
            copy.wait_recv()

    def tokens(yy):
        return pl.ds(pl.multiple_of(yy * tok, tok), tok)

    def weight_rows(zz):
        return pl.ds(pl.multiple_of((k * nz + zz) * BLK, BLK), BLK)

    load_rt = fetch(rt_in, rt)
    load_vgx = fetch(vg.at[tokens(y)], vgx.at[k, y])
    share = d // 4
    load_err = [fetch(err.at[pl.ds(i * share, share)], err_v.at[pl.ds(i * share, share)]) for i in range(4)]
    load_act = fetch(act, actr.at[0])
    load_vg = [fetch(vg.at[tokens(yy)], vg_v.at[i]) for i, yy in enumerate((y, down, up, across))]
    load_w = [fetch(w.at[weight_rows(zz)], wbuf.at[zz, y]) for zz in range(nz)]

    barrier = pltpu.get_barrier_semaphore()
    everyone = (
        [device(z, xx, cc, y) for xx, cc in group]
        + [device(zz, shifted(x, dx, nx), c, y) for dx in range(nx) for _, zz in z_peers]
        + [device(z, x, cc, yy) for _, yy in y_peers for cc in [c] + cores]
    )
    for peer in everyone:
        pl.semaphore_signal(barrier, inc=1, device_id=peer, device_id_type=MESH)
    pl.semaphore_wait(barrier, len(everyone))

    recv_rt = [send(rt_in, rtf.at[y], device(z, x, c, yy)) for _, yy in y_peers]
    recv_vg = [send(vg.at[tokens(yy)], vgx.at[k, y], device(z, x, c, yy)) for _, yy in y_peers]
    recv_w = [send(w.at[weight_rows(z)], wbuf.at[z, y], device(z, x, c, yy)) for _, yy in y_peers]
    half = CHUNKS // 2
    part = d // CHUNKS

    def cols(i):
        return pl.ds(i * part, part)

    from_down, from_up, from_across = {}, {}, {}

    def direct(*numbers):
        for i in numbers:
            j = (i + half) % CHUNKS
            from_down[i] = send(act.at[:, cols(i)], actr.at[1, :, cols(i)], device(z, x, c, up))
            from_up[j] = send(act.at[:, cols(j)], actr.at[2, :, cols(j)], device(z, x, c, down))

    def forward(*numbers):
        for i in numbers:
            from_down[i].wait_recv()
            from_across[i] = send(actr.at[1, :, cols(i)], actr.at[3, :, cols(i)], device(z, x, c, up))
            j = i + half
            from_up[j].wait_recv()
            from_across[j] = send(actr.at[2, :, cols(j)], actr.at[3, :, cols(j)], device(z, x, c, down))

    direct(0, 1, 2)

    load_rt.wait()
    rtf[y] = rt[...]
    rt2 = rows2(rt[...])

    def columns(p):
        return pl.ds(pl.multiple_of(p * wide, wide), wide)

    def store_left(value, cc, j0):
        for j in range(wb):
            lacc[cc, j0 + j] = value[:, j * BLK : (j + 1) * BLK]

    def load_left(ref, cc, j0):
        return jnp.concatenate([ref[cc, j0 + j] for j in range(wb)], axis=1)

    for load in load_err:
        load.wait()

    def err_left(p, carry):
        hi, lo = split2(err_v[columns(p), :])
        store_left(fold2(mm(rt2, lo, NT) + mm(rt2, hi, NT)), lax.div(p, per_piece), lax.rem(p, per_piece) * wb)
        return carry

    lax.fori_loop(0, pieces, err_left, 0)

    wait_all(recv_rt)
    load_vgx.wait()
    wait_all(recv_vg)
    recv_vgx = [send(vgx.at[k], vgx.at[k], device(z, xx, c, y)) for _, xx in x_peers]
    relayed = [send(vgx.at[k], vgx.at[k], device(z, x, cc, y)) for cc in cores]
    ut = jnp.zeros((r, tok), F32)
    for yy in range(ny):
        ut = ut + fold3(mm(rows3(rtf[yy]), vgx[k, yy], NT))
    ut3 = rows3(ut)
    load_act.wait()

    def act_left(cc):
        def step(i, carry):
            value = fold3(mm(ut3, actr[0, :, columns(cc * per_piece + i)]))
            store_left(load_left(lacc, cc, i * wb) + value, cc, i * wb)
            return carry

        lax.fori_loop(0, per_piece, step, 0)

    recv = []
    for cc in cores:
        act_left(cc)
        recv.append(send(lacc.at[cc], rc, device(z, x, cc, y)))
    act_left(c)

    wait_all(recv)
    lacc[c] += rc[...]
    recv = [
        send(lacc.at[c, xx * nz + zz], rxz.at[i], device(zz, xx, c, y)) for i, (xx, zz) in enumerate(plane)
    ]
    direct(3)
    for copy in load_w:
        copy.wait()
    recv_wz = []
    for copy, (dy, _) in zip(recv_w, y_peers):
        copy.wait_recv()
        source = shifted(y, ny - dy, ny)
        for _, zz in z_peers:
            recv_wz.append(send(wbuf.at[z, source], wbuf.at[z, source], device(zz, x, c, y)))
    wait_all(recv)
    total = lacc[c, mine]
    for i in range(len(plane)):
        total = total + rxz[i]
    ysum[y] = total
    own = ysum.at[y]
    recv = [send(own, own, device(z, x, c, yy)) for _, yy in y_peers]
    direct(4)
    wait_all(recv)
    total = ysum[0]
    for yy in range(1, ny):
        total = total + ysum[yy]
    lf[c, mine] = total
    own = lf.at[c, mine]
    recv = [send(own, own, device(zz, xx, c, y)) for xx, zz in plane]
    direct(5)
    wait_all(recv)
    own = lf.at[c]
    recv = [send(own, own, device(z, x, cc, y)) for cc in cores]

    for copy, (dx, _) in zip(recv_vgx, x_peers):
        copy.wait_recv()
        slot = c * nx + shifted(x, nx - dx, nx)
        relayed += [send(vgx.at[slot], vgx.at[slot], device(z, x, cc, y)) for cc in cores]
    direct(6)
    wait_all(recv)

    def products(p, carry):
        gram, by_act, by_err = carry
        block = rows3(load_left(lf, lax.div(p, per_piece), lax.rem(p, per_piece) * wb))
        hi, lo = split2(err_v[columns(p), :])
        top = block[: 2 * r]
        by_act = by_act + mm(top, actr[0, :, columns(p)], NT)
        by_err = by_err + (mm(top, lo) + mm(top, hi))
        return gram + mm(block, block, NT), by_act, by_err

    gram, by_act, by_err = lax.fori_loop(
        0,
        pieces,
        products,
        (jnp.zeros((3 * r, 3 * r), F32), jnp.zeros((2 * r, tok), F32), jnp.zeros((2 * r, err_v.shape[1]), F32)),
    )
    by_act = rows3(fold2(by_act))
    for yy in range(ny):
        zout[yy] = fold3(mm(by_act, vgx[k, yy]))
    zout[y] += fold2(by_err)
    zin[c, y] = zout[y]
    recv = [
        send(zout.at[yy], zin.at[c, y], device(z, x, cc, yy))
        for yy, cc in [(yy, cc) for _, yy in y_peers for cc in [c] + cores] + [(y, cc) for cc in cores]
    ]
    direct(7)
    forward(0)

    wait_all(recv_wz)
    wait_all(relayed)
    xc = nc * nx
    many = min(4, xc)

    def place(zz):
        return gi.at[:, pl.ds(pl.multiple_of((k * nz + zz) * BLK, BLK), BLK)]

    sent_out, kept_out = [], []
    for zz in range(nz):

        def input_grad(g, carry, zz=zz):
            total = None
            for yy in range(ny):
                cotangent = vgx[pl.ds(g * many, many), yy].reshape(many * tok, BLK)
                piece = mm(cotangent, wbuf[zz, yy], NT).astype(BF16).astype(F32)
                total = piece if total is None else total + piece
            outs[zz, pl.ds(g * many, many)] = total.astype(BF16).reshape(many, tok, BLK)
            return carry

        lax.fori_loop(0, xc // many, input_grad, 0)
        sent_out += [send(outs.at[zz, cc * nx + xx], place(zz), device(z, xx, cc, y)) for xx, cc in group]
        kept_out.append(fetch(outs.at[zz, k], place(zz)))

    wait_all(recv)
    total = None
    for cc in range(nc):
        for yy in range(ny):
            total = zin[cc, yy] if total is None else total + zin[cc, yy]
    tz[mine] = total
    own = tz.at[mine]
    recv = [send(own, own, device(zz, xx, c, y)) for xx, zz in plane]
    forward(1)
    weights, norms = unit_weights(gram_schmidt(self_products(gram, r)))

    def apply_first(p, total):
        block = times(weights, load_left(lf, lax.div(p, per_piece), lax.rem(p, per_piece) * wb))
        q1[p] = block
        block = rows3(block)
        return total + mm(block, block, NT)

    off = self_products(lax.fori_loop(0, pieces, apply_first, jnp.zeros((3 * r, 3 * r), F32)), r) - norms
    row_id = lax.broadcasted_iota(jnp.int32, (r, r), 0)
    col_id = lax.broadcasted_iota(jnp.int32, (r, r), 1)
    again = jnp.where(col_id < row_id, off, jnp.where(col_id == row_id, 0.5 * off, 0.0))
    weights = weights - times(again, weights)
    scale = math.sqrt(float(d))

    def apply_second(p, carry):
        block = q1[p]
        block = block - times(again, block)
        left_out[:, columns(p)] = block * scale
        hi, lo = split2(block)
        q3[p] = jnp.concatenate([hi, lo, hi], axis=0)
        return carry

    lax.fori_loop(0, pieces, apply_second, 0)
    forward(2)

    forward(3)

    wait_all(recv)
    total = tz[0]
    for i in range(1, per):
        total = total + tz[i]
    right = times(weights, total) / float(nb)
    r_out[...] = right
    hi, lo = split2(right)
    hi, lo = hi.astype(F32), lo.astype(F32)
    low_rank = jnp.concatenate([hi, hi, lo], axis=0).T.astype(BF16)

    for load in load_vg:
        load.wait()
    for i in range(CHUNKS):
        if i >= half:
            from_down[i].wait_recv()
        else:
            from_up[i].wait_recv()
    cotangent = vg_v[...].reshape(ny * tok, BLK).astype(F32).T.astype(BF16)

    def new_error(i, carry):
        at = pl.ds(pl.multiple_of(i * BLK, BLK), BLK)
        inside = pl.ds(pl.multiple_of(lax.rem(i, wb) * BLK, BLK), BLK)
        block = mm(cotangent, actr[:, :, at].reshape(ny * tok, BLK)) - mm(low_rank, q3[lax.div(i, wb), :, inside])
        error_out[at, :] = err_v[at, :] + block.T
        return carry

    for i in range(half):
        for j in (i, i + half):
            from_across[j].wait_recv()
            lax.fori_loop(j * part // BLK, (j + 1) * part // BLK, new_error, 0)

    wait_all(sent_out)
    for copy in kept_out:
        copy.wait()
    for copy in sent:
        copy.wait_send()


def store_kernel(error_in, left_in, right_in, gi_in, error_out, left_out, right_out, gi_out, sem):
    n = 8
    rows = error_in.shape[0] // n
    pairs = [(error_in.at[pl.ds(i * rows, rows)], error_out.at[pl.ds(i * rows, rows)]) for i in range(n)]
    pairs += [(left_in, left_out), (right_in, right_out), (gi_in, gi_out)]
    copies = [pltpu.make_async_copy(a, b, sem.at[i]) for i, (a, b) in enumerate(pairs)]
    for copy in copies:
        copy.start()
    for copy in copies:
        copy.wait()


def build(geom):
    nz, nx, nc, ny = geom

    def body(act, vg, w, err, right_prev):
        tok, d = act.shape
        kv = vg.shape[1]
        r = right_prev.shape[1]
        nb = nc * nx * nz
        per = nx * nz
        wide = min(WIDE, per * BLK)
        assert d == nb * BLK and kv == BLK and per * BLK % wide == 0
        xc = nx * nc
        sends = (
            4 * (ny - 1) + 3 * CHUNKS + (nx - 1) + nx * (nc - 1) + (xc - 1) * nz + (ny - 1) * (nz - 1)
            + 3 * (per - 1) + 2 * (nc - 1) + (ny * nc - 1)
        )
        inputs = [
            pltpu.with_memory_space_constraint(a, pltpu.HBM) for a in (act, vg, w, err[0], right_prev.T)
        ]
        hbm = pl.BlockSpec(memory_space=pltpu.HBM)
        vmem = pl.BlockSpec(memory_space=pltpu.VMEM)
        anywhere = pl.BlockSpec(memory_space=pl.ANY)
        results = (((d, kv), F32), ((r, d), F32), ((r, kv), F32), ((tok, d), BF16))
        made = pl.pallas_call(
            functools.partial(comm_kernel, geom),
            out_shape=tuple(pltpu.VMEM(*shape) for shape in results),
            in_specs=[hbm] * 5,
            out_specs=(vmem,) * 4,
            scratch_shapes=[
                pltpu.VMEM((r, kv), F32),
                pltpu.VMEM((ny, tok, d), BF16),
                pltpu.VMEM((ny, tok, kv), BF16),
                pltpu.VMEM((d, kv), F32),
                pltpu.VMEM((ny, r, kv), F32),
                pltpu.VMEM((xc, ny, tok, kv), BF16),
                pltpu.VMEM((nz, ny, BLK, kv), BF16),
                pltpu.VMEM((nz, xc, tok, BLK), BF16),
                pltpu.VMEM((nc, per, r, BLK), F32),
                pltpu.VMEM((nc, per, r, BLK), F32),
                pltpu.VMEM((per, r, BLK), F32),
                pltpu.VMEM((per - 1, r, BLK), F32),
                pltpu.VMEM((ny, r, BLK), F32),
                pltpu.VMEM((d // wide, r, wide), F32),
                pltpu.VMEM((d // wide, 3 * r, wide), BF16),
                pltpu.VMEM((ny, r, kv), F32),
                pltpu.VMEM((nc, ny, r, kv), F32),
                pltpu.VMEM((per, r, kv), F32),
                pltpu.SemaphoreType.DMA((1 + 1 + 4 + 1 + ny + 2 * nz,)),
                pltpu.SemaphoreType.DMA((sends,)),
                pltpu.SemaphoreType.DMA((sends,)),
            ],
            compiler_params=pltpu.CompilerParams(
                collective_id=0, has_side_effects=True, vmem_limit_bytes=44 * MIB
            ),
        )(*inputs)

        error_next, left, right, grad_input = pl.pallas_call(
            store_kernel,
            out_shape=tuple(jax.ShapeDtypeStruct(*shape) for shape in results),
            in_specs=[anywhere] * 4,
            out_specs=(anywhere,) * 4,
            scratch_shapes=[pltpu.SemaphoreType.DMA((11,))],
            compiler_params=pltpu.CompilerParams(vmem_limit_bytes=4 * MIB),
        )(*made)
        return (grad_input, error_next[None], left.T, right.T)

    return body


def solution(mesh):
    return jax.shard_map(
        build((4, 4, 2, 4)),
        mesh=mesh,
        in_specs=(
            P(("dp", "tp"), None),
            P("dp", "tp"),
            P(None, "tp"),
            P("dp", None, "tp"),
            P("tp", None),
        ),
        out_specs=(P(("dp", "tp"), None), P("dp", None, "tp"), P(), P("tp", None)),
        check_vma=False,
    )
```

```python
import functools
import math

import jax
import jax.numpy as jnp
from jax import lax
from jax.experimental import pallas as pl
from jax.experimental.pallas import tpu as pltpu
from jax.sharding import PartitionSpec as P

MESH = pl.DeviceIdType.MESH
F32 = jnp.float32
BF16 = jnp.bfloat16
BLK = 256
EPS = 1e-12
MIB = 1024 * 1024
WIDE = 8 * BLK
CHUNKS = 8
NN = (((1,), (0,)), ((), ()))
NT = (((1,), (1,)), ((), ()))
TN = (((0,), (0,)), ((), ()))


def mm(a, b, dims=NN):
    return lax.dot_general(a, b, dims, preferred_element_type=F32)


def split2(a):
    hi = a.astype(BF16)
    lo = (a - hi.astype(F32)).astype(BF16)
    return hi, lo


def split3(a):
    hi = a.astype(BF16)
    rest = a - hi.astype(F32)
    mid = rest.astype(BF16)
    lo = (rest - mid.astype(F32)).astype(BF16)
    return hi, mid, lo


def rows3(a):
    return jnp.concatenate(split3(a), axis=0)


def fold3(a):
    n = a.shape[0] // 3
    return (a[2 * n :] + a[n : 2 * n]) + a[:n]


def rows2(a):
    return jnp.concatenate(split2(a), axis=0)


def fold2(a):
    n = a.shape[0] // 2
    return a[n:] + a[:n]


def self_products(total, r):
    total = fold3(total)
    return (total[:, 2 * r :] + total[:, r : 2 * r]) + total[:, :r]


def times(a, b):
    a_hi, a_mid, a_lo = (v.astype(F32) for v in split3(a))
    b_hi, b_mid, b_lo = split3(b)
    left = jnp.concatenate([a_lo, a_mid, a_hi, a_mid, a_hi, a_hi], axis=1).astype(BF16)
    return mm(left, jnp.concatenate([b_hi, b_mid, b_lo, b_hi, b_mid, b_hi], axis=0))


def eye_like(n):
    return (lax.broadcasted_iota(jnp.int32, (n, n), 0) == lax.broadcasted_iota(jnp.int32, (n, n), 1)).astype(F32)


def gram_schmidt(gram):
    n = gram.shape[0]
    left, weights = gram, eye_like(n)
    row_id = lax.broadcasted_iota(jnp.int32, (n, 1), 0)
    m = 4
    for j in range(0, n, m):
        columns = [jnp.broadcast_to(left[:, i : i + 1], (n, n)) for i in range(j, j + m)]
        rows = [left[i : i + 1, :] for i in range(j, j + m)]
        given = [weights[i : i + 1, :] for i in range(j, j + m)]
        off_left, off_weights = jnp.zeros((n, n), F32), jnp.zeros((n, n), F32)
        for i in range(m):
            at = j + i
            s = jnp.maximum(columns[i][at : at + 1, :], 0.0)
            inverse = 1.0 / (s + EPS)
            c = (2.0 - s * inverse) * inverse
            f = jnp.where(row_id > at, columns[i] * c, 0.0)
            h = f * (2.0 - c * s)
            for later in range(i + 1, m):
                to = j + later
                columns[later] = columns[later] - h * columns[later][at : at + 1, :]
                rows[later] = rows[later] - h[to : to + 1, :] * rows[i]
                given[later] = given[later] - f[to : to + 1, :] * given[i]
            off_left = off_left + h * rows[i]
            off_weights = off_weights + f * given[i]
        left, weights = left - off_left, weights - off_weights
    return left, weights


def unit_weights(state):
    left, weights = state
    eye = eye_like(left.shape[0])
    s = jnp.maximum(jnp.sum(left * eye, axis=1, keepdims=True), 0.0)
    return weights / jnp.sqrt(s + EPS), eye * (s / (s + EPS))


def comm_kernel(
    geom, act, vg, w, err, rt_in, error_out, left_out, r_out, gi,
    rt, actr, vg_v, err_v, uout, uin, vgx, wbuf, outs, lacc, lf, rc, rxz, ysum, q1, q3, zout, zin, zsum, tz,
    local_sem, send_sem, recv_sem,
):
    nz, nx, nc, ny = geom
    nb = nc * nx * nz
    per = nx * nz
    _, _, tok, part = actr.shape
    d = part * CHUNKS
    half = CHUNKS // 2
    r = rt.shape[0]
    wide = min(WIDE, per * BLK)
    wb = wide // BLK
    pieces = d // wide
    per_piece = per // wb
    dp, y = lax.axis_index("dp"), lax.axis_index("tp")
    c = lax.rem(dp, nc)
    x = lax.rem(lax.div(dp, nc), nx)
    z = lax.div(dp, nc * nx)
    k = c * nx + x
    mine = x * nz + z

    def shifted(i, by, n):
        return lax.rem(i + by, n)

    def device(zz, xx, cc, yy):
        return ((zz * nx + xx) * nc + cc, yy)

    y_peers = [(dy, shifted(y, dy, ny)) for dy in range(1, ny)]
    z_peers = [(dz, shifted(z, dz, nz)) for dz in range(1, nz)]
    x_peers = [(dx, shifted(x, dx, nx)) for dx in range(1, nx)]
    plane = [
        (shifted(x, dx, nx), shifted(z, dz, nz)) for dx in range(nx) for dz in range(nz) if (dx, dz) != (0, 0)
    ]
    group = [
        (shifted(x, dx, nx), shifted(c, dc, nc)) for dc in range(nc) for dx in range(nx) if (dc, dx) != (0, 0)
    ]
    cores = [shifted(c, dc, nc) for dc in range(1, nc)]
    up, down, across = shifted(y, 1, ny), shifted(y, ny - 1, ny), shifted(y, 2, ny)

    sent = []
    counter = [0, 0]

    def send(src, dst, to):
        i = counter[0]
        counter[0] += 1
        copy = pltpu.make_async_remote_copy(
            src_ref=src, dst_ref=dst, send_sem=send_sem.at[i], recv_sem=recv_sem.at[i], device_id=to, device_id_type=MESH
        )
        copy.start()
        sent.append(copy)
        return copy

    def fetch(src, dst):
        i = counter[1]
        counter[1] += 1
        copy = pltpu.make_async_copy(src, dst, local_sem.at[i])
        copy.start()
        return copy

    def wait_all(copies):
        for copy in copies:
            copy.wait_recv()

    def tokens(yy):
        return pl.ds(pl.multiple_of(yy * tok, tok), tok)

    def weight_rows(zz):
        return pl.ds(pl.multiple_of((k * nz + zz) * BLK, BLK), BLK)

    load_rt = fetch(rt_in, rt)
    load_vg = [fetch(vg.at[tokens(yy)], vg_v.at[i]) for i, yy in enumerate((y, up, across, down))]
    load_vgx = fetch(vg.at[tokens(y)], vgx.at[k, y])
    load_act = [fetch(act.at[:, pl.ds(i * part, part)], actr.at[0, i]) for i in range(CHUNKS)]
    share = d // 4
    load_err = [fetch(err.at[pl.ds(i * share, share)], err_v.at[pl.ds(i * share, share)]) for i in range(4)]
    load_w = [fetch(w.at[weight_rows(zz)], wbuf.at[zz, y]) for zz in range(nz)]

    barrier = pltpu.get_barrier_semaphore()
    everyone = (
        [device(z, xx, cc, y) for xx, cc in group]
        + [device(zz, shifted(x, dx, nx), c, y) for dx in range(nx) for _, zz in z_peers]
        + [device(z, x, c, yy) for _, yy in y_peers]
    )
    for peer in everyone:
        pl.semaphore_signal(barrier, inc=1, device_id=peer, device_id_type=MESH)
    pl.semaphore_wait(barrier, len(everyone))

    load_rt.wait()
    rt3 = rows3(rt[...])
    for load in load_vg:
        load.wait()
    for dy in range(ny):
        uout[dy] = fold3(mm(rt3, vg_v[dy], NT))
    recv_u = [send(uout.at[dy], uin.at[dy - 1], device(z, x, c, yy)) for dy, yy in y_peers]

    from_down, from_up, from_across = {}, {}, {}

    def direct(*numbers):
        for i in numbers:
            j = (i + half) % CHUNKS
            for piece in (i, j):
                if piece in load_act:
                    load_act.pop(piece).wait()
            from_down[i] = send(actr.at[0, i], actr.at[3, i], device(z, x, c, up))
            from_up[j] = send(actr.at[0, j], actr.at[1, j], device(z, x, c, down))

    def forward(*numbers):
        for i in numbers:
            from_down[i].wait_recv()
            from_across[i] = send(actr.at[3, i], actr.at[2, i], device(z, x, c, up))
            j = i + half
            from_up[j].wait_recv()
            from_across[j] = send(actr.at[1, j], actr.at[2, j], device(z, x, c, down))

    load_act = dict(enumerate(load_act))
    direct(0)
    recv_vg = [send(vg.at[tokens(yy)], vgx.at[k, y], device(z, x, c, yy)) for _, yy in y_peers]
    own_w = w.at[weight_rows(z)]
    w_from_down = send(own_w, wbuf.at[z, y], device(z, x, c, up))
    w_from_up = send(own_w, wbuf.at[z, y], device(z, x, c, down))
    direct(1, 2)

    rt2 = rt3[: 2 * r]

    def columns(p):
        return pl.ds(pl.multiple_of(p * wide, wide), wide)

    def store_left(value, cc, j0):
        for j in range(wb):
            lacc[cc, j0 + j] = value[:, j * BLK : (j + 1) * BLK]

    def load_left(ref, cc, j0):
        return jnp.concatenate([ref[cc, j0 + j] for j in range(wb)], axis=1)

    for load in load_err:
        load.wait()

    def err_left(p, carry):
        hi, lo = split2(err_v[columns(p), :])
        store_left(fold2(mm(rt2, lo, NT) + mm(rt2, hi, NT)), lax.div(p, per_piece), lax.rem(p, per_piece) * wb)
        return carry

    lax.fori_loop(0, pieces, err_left, 0)

    wait_all(recv_u)
    ut = uout[0]
    for dy in range(ny - 1):
        ut = ut + uin[dy]
    ut3 = rows3(ut)
    for load in load_act.values():
        load.wait()
    load_act = {}

    def own_act(p):
        n = wide // part
        if n >= 1:
            return jnp.concatenate([actr[0, p * n + i] for i in range(n)], axis=1)
        n = part // wide
        inside = pl.ds(pl.multiple_of(lax.rem(p, n) * wide, wide), wide)
        return actr[0, lax.div(p, n), :, inside]

    def act_left(cc):
        def step(i, carry):
            value = fold3(mm(ut3, own_act(cc * per_piece + i)))
            store_left(load_left(lacc, cc, i * wb) + value, cc, i * wb)
            return carry

        lax.fori_loop(0, per_piece, step, 0)

    recv = []
    for cc in cores:
        act_left(cc)
        recv.append(send(lacc.at[cc], rc, device(z, x, cc, y)))
    act_left(c)

    wait_all(recv)
    lacc[c] += rc[...]
    recv = [
        send(lacc.at[c, xx * nz + zz], rxz.at[i], device(zz, xx, c, y)) for i, (xx, zz) in enumerate(plane)
    ]
    direct(3)

    load_vgx.wait()
    wait_all(recv_vg)
    recv_vgx = [send(vgx.at[k], vgx.at[k], device(z, xx, c, y)) for _, xx in x_peers]
    relayed = [send(vgx.at[k], vgx.at[k], device(z, x, cc, y)) for cc in cores]
    for copy in load_w:
        copy.wait()
    first, second = pl.ds(0, BLK // 2), pl.ds(BLK // 2, BLK // 2)
    w_from_down.wait_recv()
    w_halves = [send(wbuf.at[z, down, first], wbuf.at[z, down, first], device(z, x, c, up))]
    w_from_up.wait_recv()
    w_halves.append(send(wbuf.at[z, up, second], wbuf.at[z, up, second], device(z, x, c, down)))
    recv_wz = []

    def weights_on(source):
        for _, zz in z_peers:
            recv_wz.append(send(wbuf.at[z, source], wbuf.at[z, source], device(zz, x, c, y)))

    weights_on(down)
    weights_on(up)
    wait_all(recv)
    total = lacc[c, mine]
    for i in range(len(plane)):
        total = total + rxz[i]
    ysum[y] = total
    own = ysum.at[y]
    recv = [send(own, own, device(z, x, c, yy)) for _, yy in y_peers]
    direct(4)
    wait_all(w_halves)
    weights_on(across)
    wait_all(recv)
    total = ysum[0]
    for yy in range(1, ny):
        total = total + ysum[yy]
    lf[c, mine] = total
    own = lf.at[c, mine]
    recv = [send(own, own, device(zz, xx, c, y)) for xx, zz in plane]
    direct(5)
    wait_all(recv)
    own = lf.at[c]
    recv = [send(own, own, device(z, x, cc, y)) for cc in cores]

    for copy, (dx, _) in zip(recv_vgx, x_peers):
        copy.wait_recv()
        slot = c * nx + shifted(x, nx - dx, nx)
        relayed += [send(vgx.at[slot], vgx.at[slot], device(z, x, cc, y)) for cc in cores]
    direct(6)
    wait_all(recv)

    def products(p, carry):
        gram, by_act, by_err = carry
        block = rows3(load_left(lf, lax.div(p, per_piece), lax.rem(p, per_piece) * wb))
        hi, lo = split2(err_v[columns(p), :])
        top = block[: 2 * r]
        by_act = by_act + mm(top, own_act(p), NT)
        by_err = by_err + (mm(top, lo) + mm(top, hi))
        return gram + mm(block, block, NT), by_act, by_err

    gram, by_act, by_err = lax.fori_loop(
        0,
        pieces,
        products,
        (jnp.zeros((3 * r, 3 * r), F32), jnp.zeros((2 * r, tok), F32), jnp.zeros((2 * r, err_v.shape[1]), F32)),
    )
    by_act = rows3(fold2(by_act))
    for yy in range(ny):
        zout[yy] = fold3(mm(by_act, vgx[k, yy]))
    zout[y] += fold2(by_err)
    recv = [send(zout.at[yy], zin.at[dy - 1], device(z, x, c, yy)) for dy, yy in y_peers]
    direct(7)
    forward(0)

    wait_all(recv_wz)
    wait_all(relayed)
    xc = nc * nx
    many = min(4, xc)

    def place(zz):
        return gi.at[:, pl.ds(pl.multiple_of((k * nz + zz) * BLK, BLK), BLK)]

    sent_out, kept_out = [], []
    for zz in range(nz):

        def input_grad(g, carry, zz=zz):
            total = None
            for yy in range(ny):
                cotangent = vgx[pl.ds(g * many, many), yy].reshape(many * tok, BLK)
                piece = mm(cotangent, wbuf[zz, yy], NT).astype(BF16).astype(F32)
                total = piece if total is None else total + piece
            outs[zz, pl.ds(g * many, many)] = total.astype(BF16).reshape(many, tok, BLK)
            return carry

        lax.fori_loop(0, xc // many, input_grad, 0)
        sent_out += [send(outs.at[zz, cc * nx + xx], place(zz), device(z, xx, cc, y)) for xx, cc in group]
        kept_out.append(fetch(outs.at[zz, k], place(zz)))

    wait_all(recv)
    total = zout[y]
    for dy in range(ny - 1):
        total = total + zin[dy]
    zsum[0] = total
    recv = [send(zsum.at[0], zsum.at[dc], device(z, x, cc, y)) for dc, cc in enumerate(cores, 1)]
    forward(1)
    wait_all(recv)
    for dc in range(1, nc):
        total = total + zsum[dc]
    tz[mine] = total
    own = tz.at[mine]
    recv = [send(own, own, device(zz, xx, c, y)) for xx, zz in plane]
    weights, norms = unit_weights(gram_schmidt(self_products(gram, r)))

    def apply_first(p, total):
        block = times(weights, load_left(lf, lax.div(p, per_piece), lax.rem(p, per_piece) * wb))
        q1[p] = block
        block = rows3(block)
        return total + mm(block, block, NT)

    off = self_products(lax.fori_loop(0, pieces, apply_first, jnp.zeros((3 * r, 3 * r), F32)), r) - norms
    row_id = lax.broadcasted_iota(jnp.int32, (r, r), 0)
    col_id = lax.broadcasted_iota(jnp.int32, (r, r), 1)
    again = jnp.where(col_id < row_id, off, jnp.where(col_id == row_id, 0.5 * off, 0.0))
    weights = weights - times(again, weights)
    scale = math.sqrt(float(d))

    def apply_second(p, carry):
        block = q1[p]
        block = block - times(again, block)
        left_out[:, columns(p)] = block * scale
        hi, lo = split2(block)
        q3[p] = jnp.concatenate([hi, lo, hi], axis=0)
        return carry

    lax.fori_loop(0, pieces, apply_second, 0)
    forward(2)

    forward(3)

    wait_all(recv)
    total = tz[0]
    for i in range(1, per):
        total = total + tz[i]
    right = times(weights, total) / float(nb)
    r_out[...] = right
    hi, lo = split2(right)
    hi, lo = hi.astype(F32), lo.astype(F32)
    low_rank = jnp.concatenate([hi, hi, lo], axis=0).T.astype(BF16)

    for i in range(CHUNKS):
        if i >= half:
            from_down[i].wait_recv()
        else:
            from_up[i].wait_recv()
    cotangent = vg_v[...].reshape(ny * tok, BLK).astype(F32).T.astype(BF16)

    def new_error(i, carry):
        at = pl.ds(pl.multiple_of(i * BLK, BLK), BLK)
        inside = pl.ds(pl.multiple_of(lax.rem(i, wb) * BLK, BLK), BLK)
        n = part // BLK
        piece = pl.ds(pl.multiple_of(lax.rem(i, n) * BLK, BLK), BLK)
        block = actr[:, lax.div(i, n), :, piece].reshape(ny * tok, BLK)
        block = mm(cotangent, block) - mm(low_rank, q3[lax.div(i, wb), :, inside])
        error_out[at, :] = err_v[at, :] + block.T
        return carry

    for i in range(half):
        for j in (i, i + half):
            from_across[j].wait_recv()
            lax.fori_loop(j * part // BLK, (j + 1) * part // BLK, new_error, 0)

    wait_all(sent_out)
    for copy in kept_out:
        copy.wait()
    for copy in sent:
        copy.wait_send()


def store_kernel(error_in, left_in, right_in, gi_in, error_out, left_out, right_out, gi_out, sem):
    n = 8
    rows = error_in.shape[0] // n
    pairs = [(error_in.at[pl.ds(i * rows, rows)], error_out.at[pl.ds(i * rows, rows)]) for i in range(n)]
    pairs += [(left_in, left_out), (right_in, right_out), (gi_in, gi_out)]
    copies = [pltpu.make_async_copy(a, b, sem.at[i]) for i, (a, b) in enumerate(pairs)]
    for copy in copies:
        copy.start()
    for copy in copies:
        copy.wait()


def build(geom):
    nz, nx, nc, ny = geom

    def body(act, vg, w, err, right_prev):
        tok, d = act.shape
        kv = vg.shape[1]
        r = right_prev.shape[1]
        nb = nc * nx * nz
        per = nx * nz
        wide = min(WIDE, per * BLK)
        assert d == nb * BLK and kv == BLK and per * BLK % wide == 0
        xc = nx * nc
        sends = (
            4 * (ny - 1) + 4 + 3 * CHUNKS + (nx - 1) + nx * (nc - 1) + (xc - 1) * nz + (ny - 1) * (nz - 1)
            + 3 * (per - 1) + 3 * (nc - 1)
        )
        inputs = [
            pltpu.with_memory_space_constraint(a, pltpu.HBM) for a in (act, vg, w, err[0], right_prev.T)
        ]
        hbm = pl.BlockSpec(memory_space=pltpu.HBM)
        vmem = pl.BlockSpec(memory_space=pltpu.VMEM)
        anywhere = pl.BlockSpec(memory_space=pl.ANY)
        results = (((d, kv), F32), ((r, d), F32), ((r, kv), F32), ((tok, d), BF16))
        made = pl.pallas_call(
            functools.partial(comm_kernel, geom),
            out_shape=tuple(pltpu.VMEM(*shape) for shape in results),
            in_specs=[hbm] * 5,
            out_specs=(vmem,) * 4,
            scratch_shapes=[
                pltpu.VMEM((r, kv), F32),
                pltpu.VMEM((ny, CHUNKS, tok, d // CHUNKS), BF16),
                pltpu.VMEM((ny, tok, kv), BF16),
                pltpu.VMEM((d, kv), F32),
                pltpu.VMEM((ny, r, tok), F32),
                pltpu.VMEM((ny - 1, r, tok), F32),
                pltpu.VMEM((xc, ny, tok, kv), BF16),
                pltpu.VMEM((nz, ny, BLK, kv), BF16),
                pltpu.VMEM((nz, xc, tok, BLK), BF16),
                pltpu.VMEM((nc, per, r, BLK), F32),
                pltpu.VMEM((nc, per, r, BLK), F32),
                pltpu.VMEM((per, r, BLK), F32),
                pltpu.VMEM((per - 1, r, BLK), F32),
                pltpu.VMEM((ny, r, BLK), F32),
                pltpu.VMEM((d // wide, r, wide), F32),
                pltpu.VMEM((d // wide, 3 * r, wide), BF16),
                pltpu.VMEM((ny, r, kv), F32),
                pltpu.VMEM((ny - 1, r, kv), F32),
                pltpu.VMEM((nc, r, kv), F32),
                pltpu.VMEM((per, r, kv), F32),
                pltpu.SemaphoreType.DMA((1 + 1 + 4 + CHUNKS + ny + 2 * nz,)),
                pltpu.SemaphoreType.DMA((sends,)),
                pltpu.SemaphoreType.DMA((sends,)),
            ],
            compiler_params=pltpu.CompilerParams(
                collective_id=0, has_side_effects=True, vmem_limit_bytes=44 * MIB
            ),
        )(*inputs)

        error_next, left, right, grad_input = pl.pallas_call(
            store_kernel,
            out_shape=tuple(jax.ShapeDtypeStruct(*shape) for shape in results),
            in_specs=[anywhere] * 4,
            out_specs=(anywhere,) * 4,
            scratch_shapes=[pltpu.SemaphoreType.DMA((11,))],
            compiler_params=pltpu.CompilerParams(vmem_limit_bytes=4 * MIB),
        )(*made)
        return (grad_input, error_next[None], left.T, right.T)

    return body


def solution(mesh):
    return jax.shard_map(
        build((4, 4, 2, 4)),
        mesh=mesh,
        in_specs=(
            P(("dp", "tp"), None),
            P("dp", "tp"),
            P(None, "tp"),
            P("dp", None, "tp"),
            P("tp", None),
        ),
        out_specs=(P(("dp", "tp"), None), P("dp", None, "tp"), P(), P("tp", None)),
        check_vma=False,
    )
```

```python
import functools
import math

import jax
import jax.numpy as jnp
from jax import lax
from jax.experimental import pallas as pl
from jax.experimental.pallas import tpu as pltpu
from jax.sharding import PartitionSpec as P

MESH = pl.DeviceIdType.MESH
F32 = jnp.float32
BF16 = jnp.bfloat16
BLK = 256
EPS = 1e-12
MIB = 1024 * 1024
WIDE = 8 * BLK
CHUNKS = 8
NN = (((1,), (0,)), ((), ()))
NT = (((1,), (1,)), ((), ()))
TN = (((0,), (0,)), ((), ()))


def mm(a, b, dims=NN):
    return lax.dot_general(a, b, dims, preferred_element_type=F32)


def split2(a):
    hi = a.astype(BF16)
    lo = (a - hi.astype(F32)).astype(BF16)
    return hi, lo


def split3(a):
    hi = a.astype(BF16)
    rest = a - hi.astype(F32)
    mid = rest.astype(BF16)
    lo = (rest - mid.astype(F32)).astype(BF16)
    return hi, mid, lo


def rows3(a):
    return jnp.concatenate(split3(a), axis=0)


def fold3(a):
    n = a.shape[0] // 3
    return (a[2 * n :] + a[n : 2 * n]) + a[:n]


def rows2(a):
    return jnp.concatenate(split2(a), axis=0)


def fold2(a):
    n = a.shape[0] // 2
    return a[n:] + a[:n]


def self_products(total, r):
    total = fold3(total)
    return (total[:, 2 * r :] + total[:, r : 2 * r]) + total[:, :r]


def times(a, b):
    a_hi, a_mid, a_lo = (v.astype(F32) for v in split3(a))
    b_hi, b_mid, b_lo = split3(b)
    left = jnp.concatenate([a_lo, a_mid, a_hi, a_mid, a_hi, a_hi], axis=1).astype(BF16)
    return mm(left, jnp.concatenate([b_hi, b_mid, b_lo, b_hi, b_mid, b_hi], axis=0))


def eye_like(n):
    return (lax.broadcasted_iota(jnp.int32, (n, n), 0) == lax.broadcasted_iota(jnp.int32, (n, n), 1)).astype(F32)


def gram_schmidt(gram):
    n = gram.shape[0]
    left, weights = gram, eye_like(n)
    row_id = lax.broadcasted_iota(jnp.int32, (n, 1), 0)
    m = 4
    for j in range(0, n, m):
        columns = [jnp.broadcast_to(left[:, i : i + 1], (n, n)) for i in range(j, j + m)]
        rows = [left[i : i + 1, :] for i in range(j, j + m)]
        given = [weights[i : i + 1, :] for i in range(j, j + m)]
        off_left, off_weights = jnp.zeros((n, n), F32), jnp.zeros((n, n), F32)
        for i in range(m):
            at = j + i
            s = jnp.maximum(columns[i][at : at + 1, :], 0.0)
            inverse = 1.0 / (s + EPS)
            c = (2.0 - s * inverse) * inverse
            f = jnp.where(row_id > at, columns[i] * c, 0.0)
            h = f * (2.0 - c * s)
            for later in range(i + 1, m):
                to = j + later
                columns[later] = columns[later] - h * columns[later][at : at + 1, :]
                rows[later] = rows[later] - h[to : to + 1, :] * rows[i]
                given[later] = given[later] - f[to : to + 1, :] * given[i]
            off_left = off_left + h * rows[i]
            off_weights = off_weights + f * given[i]
        left, weights = left - off_left, weights - off_weights
    return left, weights


def unit_weights(state):
    left, weights = state
    eye = eye_like(left.shape[0])
    s = jnp.maximum(jnp.sum(left * eye, axis=1, keepdims=True), 0.0)
    return weights / jnp.sqrt(s + EPS), eye * (s / (s + EPS))


def comm_kernel(
    geom, act, vg, w, err, rt_in, merged, left_out, r_out, gi,
    rt, actr, vg_v, err_v, uout, uin, vgx, wbuf, outs, lacc, lf, rc, rxz, ysum, q1, zout, zin, zsum, tz,
    local_sem, send_sem, recv_sem,
):
    nz, nx, nc, ny = geom
    nb = nc * nx * nz
    per = nx * nz
    _, _, tok, part = actr.shape
    d = part * CHUNKS
    half = CHUNKS // 2
    r = rt.shape[0]
    wide = min(WIDE, per * BLK)
    wb = wide // BLK
    pieces = d // wide
    per_piece = per // wb
    dp, y = lax.axis_index("dp"), lax.axis_index("tp")
    c = lax.rem(dp, nc)
    x = lax.rem(lax.div(dp, nc), nx)
    z = lax.div(dp, nc * nx)
    k = c * nx + x
    mine = x * nz + z

    def shifted(i, by, n):
        return lax.rem(i + by, n)

    def device(zz, xx, cc, yy):
        return ((zz * nx + xx) * nc + cc, yy)

    y_peers = [(dy, shifted(y, dy, ny)) for dy in range(1, ny)]
    z_peers = [(dz, shifted(z, dz, nz)) for dz in range(1, nz)]
    x_peers = [(dx, shifted(x, dx, nx)) for dx in range(1, nx)]
    plane = [
        (shifted(x, dx, nx), shifted(z, dz, nz)) for dx in range(nx) for dz in range(nz) if (dx, dz) != (0, 0)
    ]
    group = [
        (shifted(x, dx, nx), shifted(c, dc, nc)) for dc in range(nc) for dx in range(nx) if (dc, dx) != (0, 0)
    ]
    cores = [shifted(c, dc, nc) for dc in range(1, nc)]
    up, down, across = shifted(y, 1, ny), shifted(y, ny - 1, ny), shifted(y, 2, ny)

    sent, settled = [], []
    counter = [0, 0]

    def send(src, dst, to):
        i = counter[0]
        counter[0] += 1
        copy = pltpu.make_async_remote_copy(
            src_ref=src, dst_ref=dst, send_sem=send_sem.at[i], recv_sem=recv_sem.at[i], device_id=to, device_id_type=MESH
        )
        copy.start()
        sent.append(copy)
        return copy

    def fetch(src, dst):
        i = counter[1]
        counter[1] += 1
        copy = pltpu.make_async_copy(src, dst, local_sem.at[i])
        copy.start()
        return copy

    def wait_all(copies):
        for copy in copies:
            copy.wait_recv()

    def settle(copies):
        for copy in copies:
            copy.wait_send()
        settled.extend(id(copy) for copy in copies)

    def tokens(yy):
        return pl.ds(pl.multiple_of(yy * tok, tok), tok)

    def weight_rows(zz):
        return pl.ds(pl.multiple_of((k * nz + zz) * BLK, BLK), BLK)

    load_rt = fetch(rt_in, rt)
    load_vg = [fetch(vg.at[tokens(yy)], vg_v.at[i]) for i, yy in enumerate((y, up, across, down))]
    load_vgx = fetch(vg.at[tokens(y)], vgx.at[k, y])
    load_act = [fetch(act.at[:, pl.ds(i * part, part)], actr.at[0, i]) for i in range(CHUNKS)]
    share = d // 4
    load_err = [fetch(err.at[pl.ds(i * share, share)], err_v.at[pl.ds(i * share, share)]) for i in range(4)]
    load_w = [fetch(w.at[weight_rows(zz)], wbuf.at[zz, y]) for zz in range(nz)]

    barrier = pltpu.get_barrier_semaphore()
    everyone = (
        [device(z, xx, cc, y) for xx, cc in group]
        + [device(zz, shifted(x, dx, nx), c, y) for dx in range(nx) for _, zz in z_peers]
        + [device(z, x, c, yy) for _, yy in y_peers]
    )
    for peer in everyone:
        pl.semaphore_signal(barrier, inc=1, device_id=peer, device_id_type=MESH)
    pl.semaphore_wait(barrier, len(everyone))

    load_rt.wait()
    rt3 = rows3(rt[...])
    for load in load_vg:
        load.wait()
    for dy in range(ny):
        uout[dy] = fold3(mm(rt3, vg_v[dy], NT))
    recv_u = [send(uout.at[dy], uin.at[dy - 1], device(z, x, c, yy)) for dy, yy in y_peers]

    from_down, from_up, from_across = {}, {}, {}

    def direct(*numbers):
        for i in numbers:
            j = (i + half) % CHUNKS
            for piece in (i, j):
                if piece in load_act:
                    load_act.pop(piece).wait()
            from_down[i] = send(actr.at[0, i], actr.at[3, i], device(z, x, c, up))
            from_up[j] = send(actr.at[0, j], actr.at[1, j], device(z, x, c, down))

    def forward(*numbers):
        for i in numbers:
            from_down[i].wait_recv()
            from_across[i] = send(actr.at[3, i], actr.at[2, i], device(z, x, c, up))
            j = i + half
            from_up[j].wait_recv()
            from_across[j] = send(actr.at[1, j], actr.at[2, j], device(z, x, c, down))

    load_act = dict(enumerate(load_act))
    recv_vg = [send(vg.at[tokens(yy)], vgx.at[k, y], device(z, x, c, yy)) for _, yy in y_peers]
    direct(0)
    own_w = w.at[weight_rows(z)]
    w_from_down = send(own_w, wbuf.at[z, y], device(z, x, c, up))
    w_from_up = send(own_w, wbuf.at[z, y], device(z, x, c, down))
    direct(1, 2)

    rt2 = rt3[: 2 * r]

    def columns(p):
        return pl.ds(pl.multiple_of(p * wide, wide), wide)

    def store_left(value, cc, j0):
        for j in range(wb):
            lacc[cc, j0 + j] = value[:, j * BLK : (j + 1) * BLK]

    def load_left(ref, cc, j0):
        return jnp.concatenate([ref[cc, j0 + j] for j in range(wb)], axis=1)

    for load in load_err:
        load.wait()

    def err_left(p, carry):
        hi, lo = split2(err_v[columns(p), :])
        store_left(fold2(mm(rt2, lo, NT) + mm(rt2, hi, NT)), lax.div(p, per_piece), lax.rem(p, per_piece) * wb)
        return carry

    lax.fori_loop(0, pieces, err_left, 0)

    wait_all(recv_u)
    ut = uout[0]
    for dy in range(ny - 1):
        ut = ut + uin[dy]
    ut3 = rows3(ut)
    for load in load_act.values():
        load.wait()
    load_act = {}

    def own_act(p):
        n = wide // part
        if n >= 1:
            return jnp.concatenate([actr[0, p * n + i] for i in range(n)], axis=1)
        n = part // wide
        inside = pl.ds(pl.multiple_of(lax.rem(p, n) * wide, wide), wide)
        return actr[0, lax.div(p, n), :, inside]

    def act_left(cc):
        def step(i, carry):
            value = fold3(mm(ut3, own_act(cc * per_piece + i)))
            store_left(load_left(lacc, cc, i * wb) + value, cc, i * wb)
            return carry

        lax.fori_loop(0, per_piece, step, 0)

    recv = []
    for cc in cores:
        act_left(cc)
        recv.append(send(lacc.at[cc], rc, device(z, x, cc, y)))
    act_left(c)

    recv_core = recv
    direct(3)
    load_vgx.wait()
    wait_all(recv_vg)
    recv_vgx = [send(vgx.at[k], vgx.at[k], device(z, xx, c, y)) for _, xx in x_peers]
    relayed = [send(vgx.at[k], vgx.at[k], device(z, x, cc, y)) for cc in cores]
    wait_all(recv)
    lacc[c] += rc[...]
    recv = [
        send(lacc.at[c, xx * nz + zz], rxz.at[i], device(zz, xx, c, y)) for i, (xx, zz) in enumerate(plane)
    ]
    settle(recv_u + recv_core)
    recv_rs = recv
    wait_all(recv)
    total = lacc[c, mine]
    for i in range(len(plane)):
        total = total + rxz[i]
    ysum[y] = total
    own = ysum.at[y]
    recv = [send(own, own, device(z, x, c, yy)) for _, yy in y_peers]
    direct(4, 5)
    for copy in load_w:
        copy.wait()
    first, second = pl.ds(0, BLK // 2), pl.ds(BLK // 2, BLK // 2)
    w_from_down.wait_recv()
    w_halves = [send(wbuf.at[z, down, first], wbuf.at[z, down, first], device(z, x, c, up))]
    w_from_up.wait_recv()
    w_halves.append(send(wbuf.at[z, up, second], wbuf.at[z, up, second], device(z, x, c, down)))
    recv_wz = []

    def weights_on(source):
        for _, zz in z_peers:
            recv_wz.append(send(wbuf.at[z, source], wbuf.at[z, source], device(zz, x, c, y)))

    settle(recv_rs)
    wait_all(recv)
    total = ysum[0]
    for yy in range(1, ny):
        total = total + ysum[yy]
    lf[c, mine] = total
    own = lf.at[c, mine]
    recv_y = recv
    recv = [send(own, own, device(zz, xx, c, y)) for xx, zz in plane]
    weights_on(down)
    weights_on(up)
    direct(6, 7)
    settle(recv_y)
    wait_all(recv)
    recv_ag = recv
    own = lf.at[c]
    recv = [send(own, own, device(z, x, cc, y)) for cc in cores]
    wait_all(w_halves)
    weights_on(across)
    settle(recv_ag)

    for copy, (dx, _) in zip(recv_vgx, x_peers):
        copy.wait_recv()
        slot = c * nx + shifted(x, nx - dx, nx)
        relayed += [send(vgx.at[slot], vgx.at[slot], device(z, x, cc, y)) for cc in cores]
    forward(0, 1)
    wait_all(recv)

    def products(p, carry):
        gram, by_act, by_err = carry
        block = rows3(load_left(lf, lax.div(p, per_piece), lax.rem(p, per_piece) * wb))
        hi, lo = split2(err_v[columns(p), :])
        top = block[: 2 * r]
        by_act = by_act + mm(top, own_act(p), NT)
        by_err = by_err + (mm(top, lo) + mm(top, hi))
        return gram + mm(block, block, NT), by_act, by_err

    gram, by_act, by_err = lax.fori_loop(
        0,
        pieces,
        products,
        (jnp.zeros((3 * r, 3 * r), F32), jnp.zeros((2 * r, tok), F32), jnp.zeros((2 * r, err_v.shape[1]), F32)),
    )
    by_act = rows3(fold2(by_act))
    for yy in range(ny):
        zout[yy] = fold3(mm(by_act, vgx[k, yy]))
    zout[y] += fold2(by_err)
    recv = [send(zout.at[yy], zin.at[dy - 1], device(z, x, c, yy)) for dy, yy in y_peers]
    forward(2, 3)

    wait_all(recv_wz)
    wait_all(relayed)
    xc = nc * nx
    many = min(4, xc)

    def input_grad(i, carry):
        zz, g = lax.div(i, xc // many), lax.rem(i, xc // many)
        total = None
        for yy in range(ny):
            cotangent = vgx[pl.ds(g * many, many), yy].reshape(many * tok, BLK)
            piece = mm(cotangent, wbuf[zz, yy], NT).astype(BF16).astype(F32)
            total = piece if total is None else total + piece
        at = pl.ds(pl.multiple_of(zz * BLK, BLK), BLK)
        outs[pl.ds(g * many, many), :, at] = total.astype(BF16).reshape(many, tok, BLK)
        return carry

    lax.fori_loop(0, nz * xc // many, input_grad, 0)
    place = gi.at[:, pl.ds(pl.multiple_of(k * nz * BLK, BLK), nz * BLK)]
    sent_out = [send(outs.at[cc * nx + xx], place, device(z, xx, cc, y)) for xx, cc in group]
    kept_out = [fetch(outs.at[k], place)]

    wait_all(recv)
    total = zout[y]
    for dy in range(ny - 1):
        total = total + zin[dy]
    zsum[0] = total
    recv = [send(zsum.at[0], zsum.at[dc], device(z, x, cc, y)) for dc, cc in enumerate(cores, 1)]
    wait_all(recv)
    for dc in range(1, nc):
        total = total + zsum[dc]
    tz[mine] = total
    own = tz.at[mine]
    recv = [send(own, own, device(zz, xx, c, y)) for xx, zz in plane]
    weights, norms = unit_weights(gram_schmidt(self_products(gram, r)))

    def apply_first(p, total):
        block = times(weights, load_left(lf, lax.div(p, per_piece), lax.rem(p, per_piece) * wb))
        q1[p] = block
        block = rows3(block)
        return total + mm(block, block, NT)

    off = self_products(lax.fori_loop(0, pieces, apply_first, jnp.zeros((3 * r, 3 * r), F32)), r) - norms
    row_id = lax.broadcasted_iota(jnp.int32, (r, r), 0)
    col_id = lax.broadcasted_iota(jnp.int32, (r, r), 1)
    again = jnp.where(col_id < row_id, off, jnp.where(col_id == row_id, 0.5 * off, 0.0))
    weights = weights - times(again, weights)
    scale = math.sqrt(float(d))

    def apply_second(p, carry):
        block = q1[p]
        block = block - times(again, block)
        left_out[:, columns(p)] = block * scale
        return carry

    lax.fori_loop(0, pieces, apply_second, 0)


    for i in range(CHUNKS):
        if i >= half:
            from_down[i].wait_recv()
        else:
            from_up[i].wait_recv()
    cotangent = vg_v[...].reshape(ny * tok, BLK).astype(F32).T.astype(BF16)

    def merge(i, carry):
        at = pl.ds(pl.multiple_of(i * BLK, BLK), BLK)
        n = part // BLK
        piece = pl.ds(pl.multiple_of(lax.rem(i, n) * BLK, BLK), BLK)
        block = mm(cotangent, actr[:, lax.div(i, n), :, piece].reshape(ny * tok, BLK))
        merged[at, :] = err_v[at, :] + block.T
        return carry

    for i in range(half):
        for j in (i, i + half):
            from_across[j].wait_recv()
            lax.fori_loop(j * part // BLK, (j + 1) * part // BLK, merge, 0)

    wait_all(recv)
    total = tz[0]
    for i in range(1, per):
        total = total + tz[i]
    r_out[...] = times(weights, total) / float(nb)

    wait_all(sent_out)
    for copy in kept_out:
        copy.wait()
    settle([copy for copy in sent if id(copy) not in settled])


def error_kernel(merged, left, right, gi, error_out, left_out, right_out, gi_out, error, sem):
    d = merged.shape[0]
    pieces = error.shape[0]
    rows = d // pieces
    copies = [
        pltpu.make_async_copy(a, b, sem.at[pieces + i])
        for i, (a, b) in enumerate([(gi, gi_out), (left, left_out), (right, right_out)])
    ]
    for copy in copies:
        copy.start()
    hi, lo = split2(right[...] / math.sqrt(float(d)))
    right3 = jnp.concatenate([hi, hi, lo], axis=0)
    for i in range(pieces):
        at = pl.ds(i * rows, rows)
        hi, lo = split2(left[:, at])
        error[i] = merged[at, :] - mm(jnp.concatenate([hi, lo, hi], axis=0), right3, TN)
        copies.append(pltpu.make_async_copy(error.at[i], error_out.at[at], sem.at[i]))
        copies[-1].start()
    for copy in copies:
        copy.wait()


def build(geom):
    nz, nx, nc, ny = geom

    def body(act, vg, w, err, right_prev):
        tok, d = act.shape
        kv = vg.shape[1]
        r = right_prev.shape[1]
        nb = nc * nx * nz
        per = nx * nz
        wide = min(WIDE, per * BLK)
        assert d == nb * BLK and kv == BLK and per * BLK % wide == 0
        xc = nx * nc
        sends = (
            4 * (ny - 1) + 4 + 3 * CHUNKS + (nx - 1) + nx * (nc - 1) + (xc - 1) + (ny - 1) * (nz - 1)
            + 3 * (per - 1) + 3 * (nc - 1)
        )
        inputs = [
            pltpu.with_memory_space_constraint(a, pltpu.HBM) for a in (act, vg, w, err[0], right_prev.T)
        ]
        hbm = pl.BlockSpec(memory_space=pltpu.HBM)
        vmem = pl.BlockSpec(memory_space=pltpu.VMEM)
        anywhere = pl.BlockSpec(memory_space=pl.ANY)
        results = (((d, kv), F32), ((r, d), F32), ((r, kv), F32), ((tok, d), BF16))
        made = pl.pallas_call(
            functools.partial(comm_kernel, geom),
            out_shape=tuple(pltpu.VMEM(*shape) for shape in results),
            in_specs=[hbm] * 5,
            out_specs=(vmem,) * 4,
            scratch_shapes=[
                pltpu.VMEM((r, kv), F32),
                pltpu.VMEM((ny, CHUNKS, tok, d // CHUNKS), BF16),
                pltpu.VMEM((ny, tok, kv), BF16),
                pltpu.VMEM((d, kv), F32),
                pltpu.VMEM((ny, r, tok), F32),
                pltpu.VMEM((ny - 1, r, tok), F32),
                pltpu.VMEM((xc, ny, tok, kv), BF16),
                pltpu.VMEM((nz, ny, BLK, kv), BF16),
                pltpu.VMEM((xc, tok, nz * BLK), BF16),
                pltpu.VMEM((nc, per, r, BLK), F32),
                pltpu.VMEM((nc, per, r, BLK), F32),
                pltpu.VMEM((per, r, BLK), F32),
                pltpu.VMEM((per - 1, r, BLK), F32),
                pltpu.VMEM((ny, r, BLK), F32),
                pltpu.VMEM((d // wide, r, wide), F32),
                pltpu.VMEM((ny, r, kv), F32),
                pltpu.VMEM((ny - 1, r, kv), F32),
                pltpu.VMEM((nc, r, kv), F32),
                pltpu.VMEM((per, r, kv), F32),
                pltpu.SemaphoreType.DMA((1 + 1 + 4 + CHUNKS + ny + nz + 1,)),
                pltpu.SemaphoreType.DMA((sends,)),
                pltpu.SemaphoreType.DMA((sends,)),
            ],
            compiler_params=pltpu.CompilerParams(
                collective_id=0, has_side_effects=True, vmem_limit_bytes=44 * MIB
            ),
        )(*inputs)

        pieces = 16
        error_next, left, right, grad_input = pl.pallas_call(
            error_kernel,
            out_shape=tuple(jax.ShapeDtypeStruct(*shape) for shape in results),
            in_specs=[vmem] * 4,
            out_specs=(anywhere,) * 4,
            scratch_shapes=[pltpu.VMEM((pieces, d // pieces, kv), F32), pltpu.SemaphoreType.DMA((pieces + 3,))],
            compiler_params=pltpu.CompilerParams(vmem_limit_bytes=24 * MIB),
        )(*made)
        return (grad_input, error_next[None], left.T, right.T)

    return body


def solution(mesh):
    return jax.shard_map(
        build((4, 4, 2, 4)),
        mesh=mesh,
        in_specs=(
            P(("dp", "tp"), None),
            P("dp", "tp"),
            P(None, "tp"),
            P("dp", None, "tp"),
            P("tp", None),
        ),
        out_specs=(P(("dp", "tp"), None), P("dp", None, "tp"), P(), P("tp", None)),
        check_vma=False,
    )
```

```python
import functools
import math

import jax
import jax.numpy as jnp
from jax import lax
from jax.experimental import pallas as pl
from jax.experimental.pallas import tpu as pltpu
from jax.sharding import PartitionSpec as P

MESH = pl.DeviceIdType.MESH
F32 = jnp.float32
BF16 = jnp.bfloat16
BLK = 256
EPS = 1e-12
MIB = 1024 * 1024
WIDE = 8 * BLK
CHUNKS = 8
NN = (((1,), (0,)), ((), ()))
NT = (((1,), (1,)), ((), ()))
TN = (((0,), (0,)), ((), ()))


def mm(a, b, dims=NN):
    return lax.dot_general(a, b, dims, preferred_element_type=F32)


def split2(a):
    hi = a.astype(BF16)
    lo = (a - hi.astype(F32)).astype(BF16)
    return hi, lo


def split3(a):
    hi = a.astype(BF16)
    rest = a - hi.astype(F32)
    mid = rest.astype(BF16)
    lo = (rest - mid.astype(F32)).astype(BF16)
    return hi, mid, lo


def rows3(a):
    return jnp.concatenate(split3(a), axis=0)


def fold3(a):
    n = a.shape[0] // 3
    return (a[2 * n :] + a[n : 2 * n]) + a[:n]


def rows2(a):
    return jnp.concatenate(split2(a), axis=0)


def fold2(a):
    n = a.shape[0] // 2
    return a[n:] + a[:n]


def self_products(total, r):
    total = fold3(total)
    return (total[:, 2 * r :] + total[:, r : 2 * r]) + total[:, :r]


def times(a, b):
    a_hi, a_mid, a_lo = (v.astype(F32) for v in split3(a))
    b_hi, b_mid, b_lo = split3(b)
    left = jnp.concatenate([a_lo, a_mid, a_hi, a_mid, a_hi, a_hi], axis=1).astype(BF16)
    return mm(left, jnp.concatenate([b_hi, b_mid, b_lo, b_hi, b_mid, b_hi], axis=0))


def eye_like(n):
    return (lax.broadcasted_iota(jnp.int32, (n, n), 0) == lax.broadcasted_iota(jnp.int32, (n, n), 1)).astype(F32)


def gram_schmidt(gram):
    n = gram.shape[0]
    left, weights = gram, eye_like(n)
    row_id = lax.broadcasted_iota(jnp.int32, (n, 1), 0)
    m = 4
    for j in range(0, n, m):
        columns = [jnp.broadcast_to(left[:, i : i + 1], (n, n)) for i in range(j, j + m)]
        rows = [left[i : i + 1, :] for i in range(j, j + m)]
        given = [weights[i : i + 1, :] for i in range(j, j + m)]
        off_left, off_weights = jnp.zeros((n, n), F32), jnp.zeros((n, n), F32)
        for i in range(m):
            at = j + i
            s = jnp.maximum(columns[i][at : at + 1, :], 0.0)
            inverse = 1.0 / (s + EPS)
            c = (2.0 - s * inverse) * inverse
            f = jnp.where(row_id > at, columns[i] * c, 0.0)
            h = f * (2.0 - c * s)
            for later in range(i + 1, m):
                to = j + later
                columns[later] = columns[later] - h * columns[later][at : at + 1, :]
                rows[later] = rows[later] - h[to : to + 1, :] * rows[i]
                given[later] = given[later] - f[to : to + 1, :] * given[i]
            off_left = off_left + h * rows[i]
            off_weights = off_weights + f * given[i]
        left, weights = left - off_left, weights - off_weights
    return left, weights


def unit_weights(state):
    left, weights = state
    eye = eye_like(left.shape[0])
    s = jnp.maximum(jnp.sum(left * eye, axis=1, keepdims=True), 0.0)
    return weights / jnp.sqrt(s + EPS), eye * (s / (s + EPS))


def comm_kernel(
    geom, act, vg, w, err, rt_in, merged, left_out, r_out, gi,
    rt, actr, vg_v, err_v, uout, uin, vgx, wbuf, outs, lacc, lf, rc, rxz, ysum, q1, aout, ain, zsum, tz,
    local_sem, send_sem, recv_sem,
):
    nz, nx, nc, ny = geom
    nb = nc * nx * nz
    per = nx * nz
    _, _, tok, part = actr.shape
    d = part * CHUNKS
    half = CHUNKS // 2
    r = rt.shape[0]
    wide = min(WIDE, per * BLK)
    wb = wide // BLK
    pieces = d // wide
    per_piece = per // wb
    dp, y = lax.axis_index("dp"), lax.axis_index("tp")
    c = lax.rem(dp, nc)
    x = lax.rem(lax.div(dp, nc), nx)
    z = lax.div(dp, nc * nx)
    k = c * nx + x
    mine = x * nz + z

    def shifted(i, by, n):
        return lax.rem(i + by, n)

    def device(zz, xx, cc, yy):
        return ((zz * nx + xx) * nc + cc, yy)

    y_peers = [(dy, shifted(y, dy, ny)) for dy in range(1, ny)]
    z_peers = [(dz, shifted(z, dz, nz)) for dz in range(1, nz)]
    x_peers = [(dx, shifted(x, dx, nx)) for dx in range(1, nx)]
    plane = [
        (shifted(x, dx, nx), shifted(z, dz, nz)) for dx in range(nx) for dz in range(nz) if (dx, dz) != (0, 0)
    ]
    group = [
        (shifted(x, dx, nx), shifted(c, dc, nc)) for dc in range(nc) for dx in range(nx) if (dc, dx) != (0, 0)
    ]
    cores = [shifted(c, dc, nc) for dc in range(1, nc)]
    up, down, across = shifted(y, 1, ny), shifted(y, ny - 1, ny), shifted(y, 2, ny)

    sent, settled = [], []
    counter = [0, 0]

    def send(src, dst, to):
        i = counter[0]
        counter[0] += 1
        copy = pltpu.make_async_remote_copy(
            src_ref=src, dst_ref=dst, send_sem=send_sem.at[i], recv_sem=recv_sem.at[i], device_id=to, device_id_type=MESH
        )
        copy.start()
        sent.append(copy)
        return copy

    def fetch(src, dst):
        i = counter[1]
        counter[1] += 1
        copy = pltpu.make_async_copy(src, dst, local_sem.at[i])
        copy.start()
        return copy

    def wait_all(copies):
        for copy in copies:
            copy.wait_recv()

    def settle(copies):
        for copy in copies:
            copy.wait_send()
        settled.extend(id(copy) for copy in copies)

    def tokens(yy):
        return pl.ds(pl.multiple_of(yy * tok, tok), tok)

    def weight_rows(zz):
        return pl.ds(pl.multiple_of((k * nz + zz) * BLK, BLK), BLK)

    load_rt = fetch(rt_in, rt)
    load_vg = [fetch(vg.at[tokens(yy)], vg_v.at[i]) for i, yy in enumerate((y, up, across, down))]
    load_vgx = fetch(vg.at[tokens(y)], vgx.at[k, y])
    load_act = [fetch(act.at[:, pl.ds(i * part, part)], actr.at[0, i]) for i in range(CHUNKS)]
    share = d // 4
    load_err = [fetch(err.at[pl.ds(i * share, share)], err_v.at[pl.ds(i * share, share)]) for i in range(4)]
    load_w = [fetch(w.at[weight_rows(zz)], wbuf.at[zz, y]) for zz in range(nz)]

    barrier = pltpu.get_barrier_semaphore()
    everyone = (
        [device(z, xx, cc, y) for xx, cc in group]
        + [device(zz, shifted(x, dx, nx), c, y) for dx in range(nx) for _, zz in z_peers]
        + [device(z, x, c, yy) for _, yy in y_peers]
    )
    for peer in everyone:
        pl.semaphore_signal(barrier, inc=1, device_id=peer, device_id_type=MESH)
    pl.semaphore_wait(barrier, len(everyone))

    from_down, from_up, from_across = {}, {}, {}

    def direct(*numbers):
        for i in numbers:
            j = (i + half) % CHUNKS
            for piece in (i, j):
                if piece in load_act:
                    load_act.pop(piece).wait()
            from_down[i] = send(actr.at[0, i], actr.at[3, i], device(z, x, c, up))
            from_up[j] = send(actr.at[0, j], actr.at[1, j], device(z, x, c, down))

    def forward(*numbers):
        for i in numbers:
            from_down[i].wait_recv()
            from_across[i] = send(actr.at[3, i], actr.at[2, i], device(z, x, c, up))
            j = i + half
            from_up[j].wait_recv()
            from_across[j] = send(actr.at[1, j], actr.at[2, j], device(z, x, c, down))

    load_act = dict(enumerate(load_act))
    direct(0)

    load_rt.wait()
    rt3 = rows3(rt[...])
    for load in load_vg:
        load.wait()
    for dy in range(ny):
        uout[dy] = fold3(mm(rt3, vg_v[dy], NT))
    recv_u = [send(uout.at[dy], uin.at[dy - 1], device(z, x, c, yy)) for dy, yy in y_peers]

    recv_vg = [send(vg.at[tokens(yy)], vgx.at[k, y], device(z, x, c, yy)) for _, yy in y_peers]
    own_w = w.at[weight_rows(z)]
    w_from_down = send(own_w, wbuf.at[z, y], device(z, x, c, up))
    w_from_up = send(own_w, wbuf.at[z, y], device(z, x, c, down))
    direct(1)

    rt2 = rt3[: 2 * r]

    def columns(p):
        return pl.ds(pl.multiple_of(p * wide, wide), wide)

    def store_left(value, cc, j0):
        for j in range(wb):
            lacc[cc, j0 + j] = value[:, j * BLK : (j + 1) * BLK]

    def load_left(ref, cc, j0):
        return jnp.concatenate([ref[cc, j0 + j] for j in range(wb)], axis=1)

    for load in load_err:
        load.wait()

    def err_left(p, carry):
        hi, lo = split2(err_v[columns(p), :])
        store_left(fold2(mm(rt2, lo, NT) + mm(rt2, hi, NT)), lax.div(p, per_piece), lax.rem(p, per_piece) * wb)
        return carry

    lax.fori_loop(0, pieces, err_left, 0)

    wait_all(recv_u)
    ut = uout[0]
    for dy in range(ny - 1):
        ut = ut + uin[dy]
    ut3 = rows3(ut)
    for load in load_act.values():
        load.wait()
    load_act = {}

    def own_act(p):
        n = wide // part
        if n >= 1:
            return jnp.concatenate([actr[0, p * n + i] for i in range(n)], axis=1)
        n = part // wide
        inside = pl.ds(pl.multiple_of(lax.rem(p, n) * wide, wide), wide)
        return actr[0, lax.div(p, n), :, inside]

    def act_left(cc):
        def step(i, carry):
            value = fold3(mm(ut3, own_act(cc * per_piece + i)))
            store_left(load_left(lacc, cc, i * wb) + value, cc, i * wb)
            return carry

        lax.fori_loop(0, per_piece, step, 0)

    recv = []
    for cc in cores:
        act_left(cc)
        recv.append(send(lacc.at[cc], rc, device(z, x, cc, y)))
    act_left(c)

    recv_core = recv
    direct(2)
    load_vgx.wait()
    wait_all(recv_vg)
    recv_vgx = [send(vgx.at[k], vgx.at[k], device(z, xx, c, y)) for _, xx in x_peers]
    relayed = [send(vgx.at[k], vgx.at[k], device(z, x, cc, y)) for cc in cores]
    wait_all(recv)
    lacc[c] += rc[...]
    recv = [
        send(lacc.at[c, xx * nz + zz], rxz.at[i], device(zz, xx, c, y)) for i, (xx, zz) in enumerate(plane)
    ]
    settle(recv_u + recv_core)
    recv_rs = recv
    wait_all(recv)
    total = lacc[c, mine]
    for i in range(len(plane)):
        total = total + rxz[i]
    ysum[y] = total
    own = ysum.at[y]
    recv = [send(own, own, device(z, x, c, yy)) for _, yy in y_peers]
    direct(3, 4)
    for copy in load_w:
        copy.wait()
    first, second = pl.ds(0, BLK // 2), pl.ds(BLK // 2, BLK // 2)
    w_from_down.wait_recv()
    w_halves = [send(wbuf.at[z, down, first], wbuf.at[z, down, first], device(z, x, c, up))]
    w_from_up.wait_recv()
    w_halves.append(send(wbuf.at[z, up, second], wbuf.at[z, up, second], device(z, x, c, down)))
    recv_wz = []

    def weights_on(source):
        for _, zz in z_peers:
            recv_wz.append(send(wbuf.at[z, source], wbuf.at[z, source], device(zz, x, c, y)))

    settle(recv_rs)
    wait_all(recv)
    total = ysum[0]
    for yy in range(1, ny):
        total = total + ysum[yy]
    lf[c, mine] = total
    own = lf.at[c, mine]
    recv_y = recv
    recv = [send(own, own, device(zz, xx, c, y)) for xx, zz in plane]
    weights_on(down)
    weights_on(up)
    direct(5)
    settle(recv_y)
    wait_all(recv)
    recv_ag = recv
    own = lf.at[c]
    recv = [send(own, own, device(z, x, cc, y)) for cc in cores]
    wait_all(w_halves)
    weights_on(across)
    settle(recv_ag)

    for copy, (dx, _) in zip(recv_vgx, x_peers):
        copy.wait_recv()
        slot = c * nx + shifted(x, nx - dx, nx)
        relayed += [send(vgx.at[slot], vgx.at[slot], device(z, x, cc, y)) for cc in cores]
    direct(6)
    wait_all(recv)

    def left_piece(p):
        return rows3(load_left(lf, lax.div(p, per_piece), lax.rem(p, per_piece) * wb))

    def products(p, carry):
        gram, by_act = carry
        block = left_piece(p)
        return gram + mm(block, block, NT), by_act + mm(block[: 2 * r], own_act(p), NT)

    gram, by_act = lax.fori_loop(
        0, pieces, products, (jnp.zeros((3 * r, 3 * r), F32), jnp.zeros((2 * r, tok), F32))
    )
    aout[...] = fold2(by_act)
    recv_a = [send(aout, ain.at[dy - 1], device(z, x, c, yy)) for dy, yy in y_peers]
    direct(7)
    forward(0, 1, 2, 3)

    def error_product(p, total):
        hi, lo = split2(err_v[columns(p), :])
        block = left_piece(p)[: 2 * r]
        return total + (mm(block, lo) + mm(block, hi))

    total = fold2(lax.fori_loop(0, pieces, error_product, jnp.zeros((2 * r, err_v.shape[1]), F32)))
    wait_all(recv_a)
    for slot in range(ny):
        total = total + fold3(mm(rows3(aout[...] if slot == 0 else ain[ny - slot - 1]), vg_v[slot]))
    zsum[0] = total
    recv = [send(zsum.at[0], zsum.at[dc], device(z, x, cc, y)) for dc, cc in enumerate(cores, 1)]

    wait_all(recv_wz)
    wait_all(relayed)
    xc = nc * nx
    many = min(4, xc)

    def input_grad(i, carry):
        zz, g = lax.div(i, xc // many), lax.rem(i, xc // many)
        total = None
        for yy in range(ny):
            cotangent = vgx[pl.ds(g * many, many), yy].reshape(many * tok, BLK)
            piece = mm(cotangent, wbuf[zz, yy], NT).astype(BF16).astype(F32)
            total = piece if total is None else total + piece
        at = pl.ds(pl.multiple_of(zz * BLK, BLK), BLK)
        outs[pl.ds(g * many, many), :, at] = total.astype(BF16).reshape(many, tok, BLK)
        return carry

    lax.fori_loop(0, nz * xc // many, input_grad, 0)
    place = gi.at[:, pl.ds(pl.multiple_of(k * nz * BLK, BLK), nz * BLK)]
    sent_out = [send(outs.at[cc * nx + xx], place, device(z, xx, cc, y)) for xx, cc in group]
    kept_out = [fetch(outs.at[k], place)]

    wait_all(recv)
    for dc in range(1, nc):
        total = total + zsum[dc]
    tz[mine] = total
    own = tz.at[mine]
    recv = [send(own, own, device(zz, xx, c, y)) for xx, zz in plane]
    weights, norms = unit_weights(gram_schmidt(self_products(gram, r)))

    def apply_first(p, total):
        block = times(weights, load_left(lf, lax.div(p, per_piece), lax.rem(p, per_piece) * wb))
        q1[p] = block
        block = rows3(block)
        return total + mm(block, block, NT)

    off = self_products(lax.fori_loop(0, pieces, apply_first, jnp.zeros((3 * r, 3 * r), F32)), r) - norms
    row_id = lax.broadcasted_iota(jnp.int32, (r, r), 0)
    col_id = lax.broadcasted_iota(jnp.int32, (r, r), 1)
    again = jnp.where(col_id < row_id, off, jnp.where(col_id == row_id, 0.5 * off, 0.0))
    weights = weights - times(again, weights)
    scale = math.sqrt(float(d))

    def apply_second(p, carry):
        block = q1[p]
        block = block - times(again, block)
        left_out[:, columns(p)] = block * scale
        return carry

    lax.fori_loop(0, pieces, apply_second, 0)


    for i in range(CHUNKS):
        if i >= half:
            from_down[i].wait_recv()
        else:
            from_up[i].wait_recv()
    cotangent = vg_v[...].reshape(ny * tok, BLK).astype(F32).T.astype(BF16)

    def merge(i, carry):
        at = pl.ds(pl.multiple_of(i * BLK, BLK), BLK)
        n = part // BLK
        piece = pl.ds(pl.multiple_of(lax.rem(i, n) * BLK, BLK), BLK)
        block = mm(cotangent, actr[:, lax.div(i, n), :, piece].reshape(ny * tok, BLK))
        merged[at, :] = err_v[at, :] + block.T
        return carry

    for i in range(half):
        for j in (i, i + half):
            from_across[j].wait_recv()
            lax.fori_loop(j * part // BLK, (j + 1) * part // BLK, merge, 0)

    wait_all(recv)
    total = tz[0]
    for i in range(1, per):
        total = total + tz[i]
    r_out[...] = times(weights, total) / float(nb)

    wait_all(sent_out)
    for copy in kept_out:
        copy.wait()
    settle([copy for copy in sent if id(copy) not in settled])


def error_kernel(merged, left, right, gi, error_out, left_out, right_out, gi_out, error, sem):
    d = merged.shape[0]
    pieces = error.shape[0]
    rows = d // pieces
    copies = [
        pltpu.make_async_copy(a, b, sem.at[pieces + i])
        for i, (a, b) in enumerate([(gi, gi_out), (left, left_out), (right, right_out)])
    ]
    for copy in copies:
        copy.start()
    hi, lo = split2(right[...] / math.sqrt(float(d)))
    right3 = jnp.concatenate([hi, hi, lo], axis=0)
    for i in range(pieces):
        at = pl.ds(i * rows, rows)
        hi, lo = split2(left[:, at])
        error[i] = merged[at, :] - mm(jnp.concatenate([hi, lo, hi], axis=0), right3, TN)
        copies.append(pltpu.make_async_copy(error.at[i], error_out.at[at], sem.at[i]))
        copies[-1].start()
    for copy in copies:
        copy.wait()


def build(geom):
    nz, nx, nc, ny = geom

    def body(act, vg, w, err, right_prev):
        tok, d = act.shape
        kv = vg.shape[1]
        r = right_prev.shape[1]
        nb = nc * nx * nz
        per = nx * nz
        wide = min(WIDE, per * BLK)
        assert d == nb * BLK and kv == BLK and per * BLK % wide == 0
        xc = nx * nc
        sends = (
            4 * (ny - 1) + 4 + 3 * CHUNKS + (nx - 1) + nx * (nc - 1) + (xc - 1) + (ny - 1) * (nz - 1)
            + 3 * (per - 1) + 3 * (nc - 1)
        )
        inputs = [
            pltpu.with_memory_space_constraint(a, pltpu.HBM) for a in (act, vg, w, err[0], right_prev.T)
        ]
        hbm = pl.BlockSpec(memory_space=pltpu.HBM)
        vmem = pl.BlockSpec(memory_space=pltpu.VMEM)
        anywhere = pl.BlockSpec(memory_space=pl.ANY)
        results = (((d, kv), F32), ((r, d), F32), ((r, kv), F32), ((tok, d), BF16))
        made = pl.pallas_call(
            functools.partial(comm_kernel, geom),
            out_shape=tuple(pltpu.VMEM(*shape) for shape in results),
            in_specs=[hbm] * 5,
            out_specs=(vmem,) * 4,
            scratch_shapes=[
                pltpu.VMEM((r, kv), F32),
                pltpu.VMEM((ny, CHUNKS, tok, d // CHUNKS), BF16),
                pltpu.VMEM((ny, tok, kv), BF16),
                pltpu.VMEM((d, kv), F32),
                pltpu.VMEM((ny, r, tok), F32),
                pltpu.VMEM((ny - 1, r, tok), F32),
                pltpu.VMEM((xc, ny, tok, kv), BF16),
                pltpu.VMEM((nz, ny, BLK, kv), BF16),
                pltpu.VMEM((xc, tok, nz * BLK), BF16),
                pltpu.VMEM((nc, per, r, BLK), F32),
                pltpu.VMEM((nc, per, r, BLK), F32),
                pltpu.VMEM((per, r, BLK), F32),
                pltpu.VMEM((per - 1, r, BLK), F32),
                pltpu.VMEM((ny, r, BLK), F32),
                pltpu.VMEM((d // wide, r, wide), F32),
                pltpu.VMEM((r, tok), F32),
                pltpu.VMEM((ny - 1, r, tok), F32),
                pltpu.VMEM((nc, r, kv), F32),
                pltpu.VMEM((per, r, kv), F32),
                pltpu.SemaphoreType.DMA((1 + 1 + 4 + CHUNKS + ny + nz + 1,)),
                pltpu.SemaphoreType.DMA((sends,)),
                pltpu.SemaphoreType.DMA((sends,)),
            ],
            compiler_params=pltpu.CompilerParams(
                collective_id=0, has_side_effects=True, vmem_limit_bytes=44 * MIB
            ),
        )(*inputs)

        pieces = 16
        error_next, left, right, grad_input = pl.pallas_call(
            error_kernel,
            out_shape=tuple(jax.ShapeDtypeStruct(*shape) for shape in results),
            in_specs=[vmem] * 4,
            out_specs=(anywhere,) * 4,
            scratch_shapes=[pltpu.VMEM((pieces, d // pieces, kv), F32), pltpu.SemaphoreType.DMA((pieces + 3,))],
            compiler_params=pltpu.CompilerParams(vmem_limit_bytes=24 * MIB),
        )(*made)
        return (grad_input, error_next[None], left.T, right.T)

    return body


def solution(mesh):
    return jax.shard_map(
        build((4, 4, 2, 4)),
        mesh=mesh,
        in_specs=(
            P(("dp", "tp"), None),
            P("dp", "tp"),
            P(None, "tp"),
            P("dp", None, "tp"),
            P("tp", None),
        ),
        out_specs=(P(("dp", "tp"), None), P("dp", None, "tp"), P(), P("tp", None)),
        check_vma=False,
    )
```

```python
import functools
import math

import jax
import jax.numpy as jnp
from jax import lax
from jax.experimental import pallas as pl
from jax.experimental.pallas import tpu as pltpu
from jax.sharding import PartitionSpec as P

MESH = pl.DeviceIdType.MESH
F32 = jnp.float32
BF16 = jnp.bfloat16
BLK = 256
EPS = 1e-12
MIB = 1024 * 1024
WIDE = 8 * BLK
CHUNKS = 8
NN = (((1,), (0,)), ((), ()))
NT = (((1,), (1,)), ((), ()))
TN = (((0,), (0,)), ((), ()))


def mm(a, b, dims=NN):
    return lax.dot_general(a, b, dims, preferred_element_type=F32)


def split2(a):
    hi = a.astype(BF16)
    lo = (a - hi.astype(F32)).astype(BF16)
    return hi, lo


def split3(a):
    hi = a.astype(BF16)
    rest = a - hi.astype(F32)
    mid = rest.astype(BF16)
    lo = (rest - mid.astype(F32)).astype(BF16)
    return hi, mid, lo


def rows3(a):
    return jnp.concatenate(split3(a), axis=0)


def fold3(a):
    n = a.shape[0] // 3
    return (a[2 * n :] + a[n : 2 * n]) + a[:n]


def rows2(a):
    return jnp.concatenate(split2(a), axis=0)


def fold2(a):
    n = a.shape[0] // 2
    return a[n:] + a[:n]


def self_products(total, r):
    total = fold3(total)
    return (total[:, 2 * r :] + total[:, r : 2 * r]) + total[:, :r]


def times(a, b):
    a_hi, a_mid, a_lo = (v.astype(F32) for v in split3(a))
    b_hi, b_mid, b_lo = split3(b)
    left = jnp.concatenate([a_lo, a_mid, a_hi, a_mid, a_hi, a_hi], axis=1).astype(BF16)
    return mm(left, jnp.concatenate([b_hi, b_mid, b_lo, b_hi, b_mid, b_hi], axis=0))


def eye_like(n):
    return (lax.broadcasted_iota(jnp.int32, (n, n), 0) == lax.broadcasted_iota(jnp.int32, (n, n), 1)).astype(F32)


def gram_schmidt(gram):
    n = gram.shape[0]
    left, weights = gram, eye_like(n)
    row_id = lax.broadcasted_iota(jnp.int32, (n, 1), 0)
    m = 4
    for j in range(0, n, m):
        columns = [jnp.broadcast_to(left[:, i : i + 1], (n, n)) for i in range(j, j + m)]
        rows = [left[i : i + 1, :] for i in range(j, j + m)]
        given = [weights[i : i + 1, :] for i in range(j, j + m)]
        off_left, off_weights = jnp.zeros((n, n), F32), jnp.zeros((n, n), F32)
        for i in range(m):
            at = j + i
            s = jnp.maximum(columns[i][at : at + 1, :], 0.0)
            inverse = 1.0 / (s + EPS)
            c = (2.0 - s * inverse) * inverse
            f = jnp.where(row_id > at, columns[i] * c, 0.0)
            h = f * (2.0 - c * s)
            for later in range(i + 1, m):
                to = j + later
                columns[later] = columns[later] - h * columns[later][at : at + 1, :]
                rows[later] = rows[later] - h[to : to + 1, :] * rows[i]
                given[later] = given[later] - f[to : to + 1, :] * given[i]
            off_left = off_left + h * rows[i]
            off_weights = off_weights + f * given[i]
        left, weights = left - off_left, weights - off_weights
    return left, weights


def unit_weights(state):
    left, weights = state
    eye = eye_like(left.shape[0])
    s = jnp.maximum(jnp.sum(left * eye, axis=1, keepdims=True), 0.0)
    return weights / jnp.sqrt(s + EPS), eye * (s / (s + EPS))


def comm_kernel(
    geom, act, vg, w, err, rt_in, merged, left_out, r_out, gi,
    rt, actr, vg_v, err_v, uout, uin, vgx, wbuf, outs, lacc, lf, rc, rxz, ysum, q1, aout, ain, zsum, tz,
    local_sem, send_sem, recv_sem,
):
    nz, nx, nc, ny = geom
    nb = nc * nx * nz
    per = nx * nz
    _, _, tok, part = actr.shape
    d = part * CHUNKS
    half = CHUNKS // 2
    r = rt.shape[0]
    wide = min(WIDE, per * BLK)
    wb = wide // BLK
    pieces = d // wide
    per_piece = per // wb
    dp, y = lax.axis_index("dp"), lax.axis_index("tp")
    c = lax.rem(dp, nc)
    x = lax.rem(lax.div(dp, nc), nx)
    z = lax.div(dp, nc * nx)
    mine = x * nz + z

    def shifted(i, by, n):
        return lax.rem(i + by, n)

    def device(zz, xx, cc, yy):
        return ((zz * nx + xx) * nc + cc, yy)

    y_peers = [(dy, shifted(y, dy, ny)) for dy in range(1, ny)]
    plane = [
        (shifted(x, dx, nx), shifted(z, dz, nz)) for dx in range(nx) for dz in range(nz) if (dx, dz) != (0, 0)
    ]
    cores = [shifted(c, dc, nc) for dc in range(1, nc)]
    up, down, across = shifted(y, 1, ny), shifted(y, ny - 1, ny), shifted(y, 2, ny)

    sent, settled = [], []
    counter = [0, 0]

    def send(src, dst, to):
        i = counter[0]
        counter[0] += 1
        copy = pltpu.make_async_remote_copy(
            src_ref=src, dst_ref=dst, send_sem=send_sem.at[i], recv_sem=recv_sem.at[i], device_id=to, device_id_type=MESH
        )
        copy.start()
        sent.append(copy)
        return copy

    def fetch(src, dst):
        i = counter[1]
        counter[1] += 1
        copy = pltpu.make_async_copy(src, dst, local_sem.at[i])
        copy.start()
        return copy

    def wait_all(copies):
        for copy in copies:
            copy.wait_recv()

    def settle(copies):
        for copy in copies:
            copy.wait_send()
        settled.extend(id(copy) for copy in copies)

    def tokens(yy):
        return pl.ds(pl.multiple_of(yy * tok, tok), tok)

    load_rt = fetch(rt_in, rt)
    load_vg = [fetch(vg.at[tokens(yy)], vg_v.at[i]) for i, yy in enumerate((y, up, across, down))]
    load_vgx = fetch(vg.at[tokens(y)], vgx.at[0, 0])
    load_act = [fetch(act.at[:, pl.ds(i * part, part)], actr.at[0, i]) for i in range(CHUNKS)]
    share = d // 4
    load_err = [fetch(err.at[pl.ds(i * share, share)], err_v.at[pl.ds(i * share, share)]) for i in range(4)]
    load_w = fetch(w.at[c], wbuf.at[:, :, :, 0])

    barrier = pltpu.get_barrier_semaphore()
    everyone = (
        [device(z, x, cc, y) for cc in cores]
        + [device(zz, xx, c, y) for xx, zz in plane]
        + [device(z, x, c, yy) for _, yy in y_peers]
    )
    for peer in everyone:
        pl.semaphore_signal(barrier, inc=1, device_id=peer, device_id_type=MESH)
    pl.semaphore_wait(barrier, len(everyone))

    from_down, from_up, from_across = {}, {}, {}

    def direct(*numbers):
        for i in numbers:
            j = (i + half) % CHUNKS
            for piece in (i, j):
                if piece in load_act:
                    load_act.pop(piece).wait()
            from_down[i] = send(actr.at[0, i], actr.at[3, i], device(z, x, c, up))
            from_up[j] = send(actr.at[0, j], actr.at[1, j], device(z, x, c, down))

    def forward(*numbers):
        for i in numbers:
            from_down[i].wait_recv()
            from_across[i] = send(actr.at[3, i], actr.at[2, i], device(z, x, c, up))
            j = i + half
            from_up[j].wait_recv()
            from_across[j] = send(actr.at[1, j], actr.at[2, j], device(z, x, c, down))

    load_act = dict(enumerate(load_act))
    direct(0)

    load_rt.wait()
    rt3 = rows3(rt[...])
    for load in load_vg:
        load.wait()
    for dy in range(ny):
        uout[dy] = fold3(mm(rt3, vg_v[dy], NT))
    recv_u = [send(uout.at[dy], uin.at[dy - 1], device(z, x, c, yy)) for dy, yy in y_peers]

    recv_vg = [send(vg.at[tokens(yy)], vgx.at[0, ny - dy], device(z, x, c, yy)) for dy, yy in y_peers]
    own_w = w.at[c, x, z]
    w_from_down = send(own_w, wbuf.at[x, z, :, 3], device(z, x, c, up))
    w_from_up = send(own_w, wbuf.at[x, z, :, 1], device(z, x, c, down))
    direct(1)

    def place(h, a, b):
        return (a, b) if h == 0 else (b, a)

    def piece(h, first, second):
        zz, xx = place(h, first, second)
        return wbuf.at[xx, zz, h, 1:ny]

    def neighbour(h, stage, way):
        n = (nz if h == 0 else nx) if stage == 0 else (nx if h == 0 else nz)
        first, second = place(h, z, x)
        if stage == 0:
            first = shifted(first, way % n, n)
        else:
            second = shifted(second, way % n, n)
        zz, xx = place(h, first, second)
        return device(zz, xx, c, y)

    half_here = [(place(h, z, x), place(h, nz, nx)) for h in range(2)]
    stage_one, stage_one_across, stage_two, stage_two_across = {}, {}, {}, {}

    def weights_first():
        for h in range(2):
            (first, second), _ = half_here[h]
            own = piece(h, first, second)
            for way in (1, -1):
                stage_one[h, way] = send(own, own, neighbour(h, 0, way))

    def weights_across():
        for h in range(2):
            (first, second), (n, _) = half_here[h]
            way = 1 - 2 * h
            stage_one[h, way].wait_recv()
            came = piece(h, shifted(first, -way % n, n), second)
            stage_one_across[h] = send(came, came, neighbour(h, 0, way))

    def weights_second(i):
        for h in range(2):
            (first, second), (n, _) = half_here[h]
            if i in (1, 2):
                way = 3 - 2 * i
                if way != 1 - 2 * h:
                    stage_one[h, way].wait_recv()
                first = shifted(first, -way % n, n)
            elif i == 3:
                stage_one_across[h].wait_recv()
                first = shifted(first, 2, n)
            for way in (1, -1):
                stage_two[h, i, way] = send(piece(h, first, second), piece(h, first, second), neighbour(h, 1, way))

    def weights_second_across(i):
        for h in range(2):
            (first, second), (n, m) = half_here[h]
            first = shifted(first, (0, n - 1, 1, 2)[i], n)
            way = (1, -1, 1, -1)[i]
            stage_two[h, i, way].wait_recv()
            came = piece(h, first, shifted(second, -way % m, m))
            stage_two_across[h, i] = send(came, came, neighbour(h, 1, way))

    rt2 = rt3[: 2 * r]

    def columns(p):
        return pl.ds(pl.multiple_of(p * wide, wide), wide)

    def store_left(value, cc, j0):
        for j in range(wb):
            lacc[cc, j0 + j] = value[:, j * BLK : (j + 1) * BLK]

    def load_left(ref, cc, j0):
        return jnp.concatenate([ref[cc, j0 + j] for j in range(wb)], axis=1)

    for load in load_err:
        load.wait()

    def err_left(p, carry):
        hi, lo = split2(err_v[columns(p), :])
        store_left(fold2(mm(rt2, lo, NT) + mm(rt2, hi, NT)), lax.div(p, per_piece), lax.rem(p, per_piece) * wb)
        return carry

    lax.fori_loop(0, pieces, err_left, 0)

    wait_all(recv_u)
    ut = uout[0]
    for dy in range(ny - 1):
        ut = ut + uin[dy]
    ut3 = rows3(ut)
    for load in load_act.values():
        load.wait()
    load_act = {}

    def own_act(p):
        n = wide // part
        if n >= 1:
            return jnp.concatenate([actr[0, p * n + i] for i in range(n)], axis=1)
        n = part // wide
        inside = pl.ds(pl.multiple_of(lax.rem(p, n) * wide, wide), wide)
        return actr[0, lax.div(p, n), :, inside]

    def act_left(cc):
        def step(i, carry):
            value = fold3(mm(ut3, own_act(cc * per_piece + i)))
            store_left(load_left(lacc, cc, i * wb) + value, cc, i * wb)
            return carry

        lax.fori_loop(0, per_piece, step, 0)

    recv = []
    for cc in cores:
        act_left(cc)
        recv.append(send(lacc.at[cc], rc, device(z, x, cc, y)))
    act_left(c)

    recv_core = recv
    direct(2)
    load_vgx.wait()
    wait_all(recv_vg)
    recv_vgx = [send(vgx.at[0], vgx.at[dc], device(z, x, cc, y)) for dc, cc in enumerate(cores, 1)]
    wait_all(recv)
    lacc[c] += rc[...]
    recv = [
        send(lacc.at[c, xx * nz + zz], rxz.at[i], device(zz, xx, c, y)) for i, (xx, zz) in enumerate(plane)
    ]
    load_w.wait()
    w_from_down.wait_recv()
    w_halves = [send(wbuf.at[x, z, 0, 3], wbuf.at[x, z, 0, 2], device(z, x, c, up))]
    w_from_up.wait_recv()
    w_halves.append(send(wbuf.at[x, z, 1, 1], wbuf.at[x, z, 1, 2], device(z, x, c, down)))
    settle(recv_u + recv_core)
    recv_rs = recv
    wait_all(recv)
    total = lacc[c, mine]
    for i in range(len(plane)):
        total = total + rxz[i]
    ysum[y] = total
    own = ysum.at[y]
    recv = [send(own, own, device(z, x, c, yy)) for _, yy in y_peers]
    direct(3, 4)
    wait_all(w_halves)
    weights_first()
    weights_second(0)
    settle(recv_rs)
    wait_all(recv)
    total = ysum[0]
    for yy in range(1, ny):
        total = total + ysum[yy]
    lf[c, mine] = total
    own = lf.at[c, mine]
    recv_y = recv
    recv = [send(own, own, device(zz, xx, c, y)) for xx, zz in plane]
    direct(5)
    weights_across()
    weights_second(1)
    weights_second(2)
    settle(recv_y)
    wait_all(recv)
    recv_ag = recv
    own = lf.at[c]
    recv = [send(own, own, device(z, x, cc, y)) for cc in cores]
    weights_second(3)
    weights_second_across(0)
    settle(recv_ag)

    direct(6)
    wait_all(recv)

    def left_piece(p):
        return rows3(load_left(lf, lax.div(p, per_piece), lax.rem(p, per_piece) * wb))

    def products(p, carry):
        gram, by_act = carry
        block = left_piece(p)
        return gram + mm(block, block, NT), by_act + mm(block[: 2 * r], own_act(p), NT)

    gram, by_act = lax.fori_loop(
        0, pieces, products, (jnp.zeros((3 * r, 3 * r), F32), jnp.zeros((2 * r, tok), F32))
    )
    aout[...] = fold2(by_act)
    recv_a = [send(aout, ain.at[dy - 1], device(z, x, c, yy)) for dy, yy in y_peers]
    direct(7)
    forward(0, 1, 2, 3)
    weights_second_across(1)
    weights_second_across(2)

    def error_product(p, total):
        hi, lo = split2(err_v[columns(p), :])
        block = left_piece(p)[: 2 * r]
        return total + (mm(block, lo) + mm(block, hi))

    total = fold2(lax.fori_loop(0, pieces, error_product, jnp.zeros((2 * r, err_v.shape[1]), F32)))
    wait_all(recv_a)
    for slot in range(ny):
        total = total + fold3(mm(rows3(aout[...] if slot == 0 else ain[ny - slot - 1]), vg_v[slot]))
    zsum[0] = total
    recv = [send(zsum.at[0], zsum.at[dc], device(z, x, cc, y)) for dc, cc in enumerate(cores, 1)]

    weights_second_across(3)

    wait_all(recv)
    for dc in range(1, nc):
        total = total + zsum[dc]
    tz[mine] = total
    own = tz.at[mine]
    recv = [send(own, own, device(zz, xx, c, y)) for xx, zz in plane]
    weights, norms = unit_weights(gram_schmidt(self_products(gram, r)))

    def apply_first(p, total):
        block = times(weights, load_left(lf, lax.div(p, per_piece), lax.rem(p, per_piece) * wb))
        q1[p] = block
        block = rows3(block)
        return total + mm(block, block, NT)

    off = self_products(lax.fori_loop(0, pieces, apply_first, jnp.zeros((3 * r, 3 * r), F32)), r) - norms
    row_id = lax.broadcasted_iota(jnp.int32, (r, r), 0)
    col_id = lax.broadcasted_iota(jnp.int32, (r, r), 1)
    again = jnp.where(col_id < row_id, off, jnp.where(col_id == row_id, 0.5 * off, 0.0))
    weights = weights - times(again, weights)
    scale = math.sqrt(float(d))

    def apply_second(p, carry):
        block = q1[p]
        block = block - times(again, block)
        left_out[:, columns(p)] = block * scale
        return carry

    lax.fori_loop(0, pieces, apply_second, 0)


    for i in range(4):
        for h in range(2):
            stage_two[h, i, (-1, 1, -1, 1)[i]].wait_recv()
            stage_two_across[h, i].wait_recv()
    wait_all(recv_vgx)

    def input_grad(i, carry):
        total = None
        for slot in range(ny):
            weight = wbuf[lax.div(i, nz), lax.rem(i, nz), :, slot].reshape(BLK, BLK)
            part_sum = mm(vgx[:, slot].reshape(nc * tok, BLK), weight, NT).astype(BF16).astype(F32)
            total = part_sum if total is None else total + part_sum
        total = total.astype(BF16).reshape(nc, tok, BLK)
        gi[:, pl.ds(pl.multiple_of((c * per + i) * BLK, BLK), BLK)] = total[0]
        for dc in range(1, nc):
            outs[dc - 1, :, pl.ds(pl.multiple_of(i * BLK, BLK), BLK)] = total[dc]
        return carry

    lax.fori_loop(0, per, input_grad, 0)
    share_of = gi.at[:, pl.ds(pl.multiple_of(c * per * BLK, BLK), per * BLK)]
    sent_out = [send(outs.at[nc - 1 - dc], share_of, device(z, x, cc, y)) for dc, cc in enumerate(cores, 1)]

    for i in range(CHUNKS):
        if i >= half:
            from_down[i].wait_recv()
        else:
            from_up[i].wait_recv()
    cotangent = vg_v[...].reshape(ny * tok, BLK).astype(F32).T.astype(BF16)

    def merge(i, carry):
        at = pl.ds(pl.multiple_of(i * BLK, BLK), BLK)
        n = part // BLK
        piece = pl.ds(pl.multiple_of(lax.rem(i, n) * BLK, BLK), BLK)
        block = mm(cotangent, actr[:, lax.div(i, n), :, piece].reshape(ny * tok, BLK))
        merged[at, :] = err_v[at, :] + block.T
        return carry

    for i in range(half):
        for j in (i, i + half):
            from_across[j].wait_recv()
            lax.fori_loop(j * part // BLK, (j + 1) * part // BLK, merge, 0)

    wait_all(recv)
    total = tz[0]
    for i in range(1, per):
        total = total + tz[i]
    r_out[...] = times(weights, total) / float(nb)

    wait_all(sent_out)
    settle([copy for copy in sent if id(copy) not in settled])
    assert counter == [send_sem.shape[0], local_sem.shape[0]], counter


def error_kernel(merged, left, right, gi, error_out, left_out, right_out, gi_out, error, sem):
    d = merged.shape[0]
    pieces = error.shape[0]
    rows = d // pieces
    copies = [
        pltpu.make_async_copy(a, b, sem.at[pieces + i])
        for i, (a, b) in enumerate([(gi, gi_out), (left, left_out), (right, right_out)])
    ]
    for copy in copies:
        copy.start()
    hi, lo = split2(right[...] / math.sqrt(float(d)))
    right3 = jnp.concatenate([hi, hi, lo], axis=0)
    for i in range(pieces):
        at = pl.ds(i * rows, rows)
        hi, lo = split2(left[:, at])
        error[i] = merged[at, :] - mm(jnp.concatenate([hi, lo, hi], axis=0), right3, TN)
        copies.append(pltpu.make_async_copy(error.at[i], error_out.at[at], sem.at[i]))
        copies[-1].start()
    for copy in copies:
        copy.wait()


def build(geom):
    nz, nx, nc, ny = geom

    def body(act, vg, w, err, right_prev):
        tok, d = act.shape
        kv = vg.shape[1]
        r = right_prev.shape[1]
        nb = nc * nx * nz
        per = nx * nz
        wide = min(WIDE, per * BLK)
        assert d == nb * BLK and kv == BLK and per * BLK % wide == 0
        sends = 4 * (ny - 1) + 4 + 3 * CHUNKS + 30 + 3 * (per - 1) + 5 * (nc - 1)
        pieces = w.reshape(nc, nx, nz, 2, BLK // 2, kv)
        inputs = [
            pltpu.with_memory_space_constraint(a, pltpu.HBM) for a in (act, vg, pieces, err[0], right_prev.T)
        ]
        hbm = pl.BlockSpec(memory_space=pltpu.HBM)
        vmem = pl.BlockSpec(memory_space=pltpu.VMEM)
        anywhere = pl.BlockSpec(memory_space=pl.ANY)
        results = (((d, kv), F32), ((r, d), F32), ((r, kv), F32), ((tok, d), BF16))
        made = pl.pallas_call(
            functools.partial(comm_kernel, geom),
            out_shape=tuple(pltpu.VMEM(*shape) for shape in results),
            in_specs=[hbm] * 5,
            out_specs=(vmem,) * 4,
            scratch_shapes=[
                pltpu.VMEM((r, kv), F32),
                pltpu.VMEM((ny, CHUNKS, tok, d // CHUNKS), BF16),
                pltpu.VMEM((ny, tok, kv), BF16),
                pltpu.VMEM((d, kv), F32),
                pltpu.VMEM((ny, r, tok), F32),
                pltpu.VMEM((ny - 1, r, tok), F32),
                pltpu.VMEM((nc, ny, tok, kv), BF16),
                pltpu.VMEM((nx, nz, 2, ny, BLK // 2, kv), BF16),
                pltpu.VMEM((max(nc - 1, 1), tok, per * BLK), BF16),
                pltpu.VMEM((nc, per, r, BLK), F32),
                pltpu.VMEM((nc, per, r, BLK), F32),
                pltpu.VMEM((per, r, BLK), F32),
                pltpu.VMEM((per - 1, r, BLK), F32),
                pltpu.VMEM((ny, r, BLK), F32),
                pltpu.VMEM((d // wide, r, wide), F32),
                pltpu.VMEM((r, tok), F32),
                pltpu.VMEM((ny - 1, r, tok), F32),
                pltpu.VMEM((nc, r, kv), F32),
                pltpu.VMEM((per, r, kv), F32),
                pltpu.SemaphoreType.DMA((1 + 1 + 4 + CHUNKS + ny + 1,)),
                pltpu.SemaphoreType.DMA((sends,)),
                pltpu.SemaphoreType.DMA((sends,)),
            ],
            compiler_params=pltpu.CompilerParams(
                collective_id=0, has_side_effects=True, vmem_limit_bytes=44 * MIB
            ),
        )(*inputs)

        pieces = 16
        error_next, left, right, grad_input = pl.pallas_call(
            error_kernel,
            out_shape=tuple(jax.ShapeDtypeStruct(*shape) for shape in results),
            in_specs=[vmem] * 4,
            out_specs=(anywhere,) * 4,
            scratch_shapes=[pltpu.VMEM((pieces, d // pieces, kv), F32), pltpu.SemaphoreType.DMA((pieces + 3,))],
            compiler_params=pltpu.CompilerParams(vmem_limit_bytes=24 * MIB),
        )(*made)
        return (grad_input, error_next[None], left.T, right.T)

    return body


def solution(mesh):
    return jax.shard_map(
        build((4, 4, 2, 4)),
        mesh=mesh,
        in_specs=(
            P(("dp", "tp"), None),
            P("dp", "tp"),
            P(None, "tp"),
            P("dp", None, "tp"),
            P("tp", None),
        ),
        out_specs=(P(("dp", "tp"), None), P("dp", None, "tp"), P(), P("tp", None)),
        check_vma=False,
    )
```

```python
import functools
import math

import jax
import jax.numpy as jnp
from jax import lax
from jax.experimental import pallas as pl
from jax.experimental.pallas import tpu as pltpu
from jax.sharding import PartitionSpec as P

MESH = pl.DeviceIdType.MESH
F32 = jnp.float32
BF16 = jnp.bfloat16
BLK = 256
EPS = 1e-12
MIB = 1024 * 1024
WIDE = 8 * BLK
CHUNKS = 8
NN = (((1,), (0,)), ((), ()))
NT = (((1,), (1,)), ((), ()))
TN = (((0,), (0,)), ((), ()))


def mm(a, b, dims=NN):
    return lax.dot_general(a, b, dims, preferred_element_type=F32)


def split2(a):
    hi = a.astype(BF16)
    lo = (a - hi.astype(F32)).astype(BF16)
    return hi, lo


def split3(a):
    hi = a.astype(BF16)
    rest = a - hi.astype(F32)
    mid = rest.astype(BF16)
    lo = (rest - mid.astype(F32)).astype(BF16)
    return hi, mid, lo


def rows3(a):
    return jnp.concatenate(split3(a), axis=0)


def fold3(a):
    n = a.shape[0] // 3
    return (a[2 * n :] + a[n : 2 * n]) + a[:n]


def rows2(a):
    return jnp.concatenate(split2(a), axis=0)


def fold2(a):
    n = a.shape[0] // 2
    return a[n:] + a[:n]


def self_products(total, r):
    total = fold3(total)
    return (total[:, 2 * r :] + total[:, r : 2 * r]) + total[:, :r]


def times(a, b):
    a_hi, a_mid, a_lo = (v.astype(F32) for v in split3(a))
    b_hi, b_mid, b_lo = split3(b)
    left = jnp.concatenate([a_lo, a_mid, a_hi, a_mid, a_hi, a_hi], axis=1).astype(BF16)
    return mm(left, jnp.concatenate([b_hi, b_mid, b_lo, b_hi, b_mid, b_hi], axis=0))


def eye_like(n):
    return (lax.broadcasted_iota(jnp.int32, (n, n), 0) == lax.broadcasted_iota(jnp.int32, (n, n), 1)).astype(F32)


def gram_schmidt(gram):
    n = gram.shape[0]
    left, weights = gram, eye_like(n)
    row_id = lax.broadcasted_iota(jnp.int32, (n, 1), 0)
    m = 4
    for j in range(0, n, m):
        columns = [jnp.broadcast_to(left[:, i : i + 1], (n, n)) for i in range(j, j + m)]
        rows = [left[i : i + 1, :] for i in range(j, j + m)]
        given = [weights[i : i + 1, :] for i in range(j, j + m)]
        off_left, off_weights = jnp.zeros((n, n), F32), jnp.zeros((n, n), F32)
        for i in range(m):
            at = j + i
            s = jnp.maximum(columns[i][at : at + 1, :], 0.0)
            inverse = 1.0 / (s + EPS)
            c = (2.0 - s * inverse) * inverse
            f = jnp.where(row_id > at, columns[i] * c, 0.0)
            h = f * (2.0 - c * s)
            for later in range(i + 1, m):
                to = j + later
                columns[later] = columns[later] - h * columns[later][at : at + 1, :]
                rows[later] = rows[later] - h[to : to + 1, :] * rows[i]
                given[later] = given[later] - f[to : to + 1, :] * given[i]
            off_left = off_left + h * rows[i]
            off_weights = off_weights + f * given[i]
        left, weights = left - off_left, weights - off_weights
        yield left, weights


def unit_weights(state):
    left, weights = state
    eye = eye_like(left.shape[0])
    s = jnp.maximum(jnp.sum(left * eye, axis=1, keepdims=True), 0.0)
    return weights / jnp.sqrt(s + EPS), eye * (s / (s + EPS))


def comm_kernel(
    geom, act, vg, w, err, rt_in, merged, left_out, r_out, gi,
    rt, actr, vg_v, err_v, uout, uin, vgx, wbuf, outs, lacc, lf, rc, rxz, ysum, q1, aout, ain, zsum, tz,
    local_sem, send_sem, recv_sem,
):
    nz, nx, nc, ny = geom
    nb = nc * nx * nz
    per = nx * nz
    _, _, tok, part = actr.shape
    d = part * CHUNKS
    half = CHUNKS // 2
    r = rt.shape[0]
    wide = min(WIDE, per * BLK)
    wb = wide // BLK
    pieces = d // wide
    per_piece = per // wb
    dp, y = lax.axis_index("dp"), lax.axis_index("tp")
    c = lax.rem(dp, nc)
    x = lax.rem(lax.div(dp, nc), nx)
    z = lax.div(dp, nc * nx)
    mine = x * nz + z

    def shifted(i, by, n):
        return lax.rem(i + by, n)

    def device(zz, xx, cc, yy):
        return ((zz * nx + xx) * nc + cc, yy)

    y_peers = [(dy, shifted(y, dy, ny)) for dy in range(1, ny)]
    plane = [
        (shifted(x, dx, nx), shifted(z, dz, nz)) for dx in range(nx) for dz in range(nz) if (dx, dz) != (0, 0)
    ]
    cores = [shifted(c, dc, nc) for dc in range(1, nc)]
    up, down, across = shifted(y, 1, ny), shifted(y, ny - 1, ny), shifted(y, 2, ny)

    sent, settled = [], []
    counter = [0, 0]

    def send(src, dst, to):
        i = counter[0]
        counter[0] += 1
        copy = pltpu.make_async_remote_copy(
            src_ref=src, dst_ref=dst, send_sem=send_sem.at[i], recv_sem=recv_sem.at[i], device_id=to, device_id_type=MESH
        )
        copy.start()
        sent.append(copy)
        return copy

    def fetch(src, dst):
        i = counter[1]
        counter[1] += 1
        copy = pltpu.make_async_copy(src, dst, local_sem.at[i])
        copy.start()
        return copy

    def wait_all(copies):
        for copy in copies:
            copy.wait_recv()

    def settle(copies):
        for copy in copies:
            copy.wait_send()
        settled.extend(id(copy) for copy in copies)

    def tokens(yy):
        return pl.ds(pl.multiple_of(yy * tok, tok), tok)

    load_rt = fetch(rt_in, rt)
    load_vg = [fetch(vg.at[tokens(yy)], vg_v.at[i]) for i, yy in enumerate((y, up, across, down))]
    load_vgx = fetch(vg.at[tokens(y)], vgx.at[0, 0])
    load_act = [fetch(act.at[:, pl.ds(i * part, part)], actr.at[0, i]) for i in range(CHUNKS)]
    share = d // 4
    load_err = [fetch(err.at[pl.ds(i * share, share)], err_v.at[pl.ds(i * share, share)]) for i in range(4)]
    load_w = fetch(w.at[c], wbuf.at[:, :, :, 0])

    barrier = pltpu.get_barrier_semaphore()
    everyone = (
        [device(z, x, cc, y) for cc in cores]
        + [device(zz, xx, c, y) for xx, zz in plane]
        + [device(z, x, c, yy) for _, yy in y_peers]
    )
    for peer in everyone:
        pl.semaphore_signal(barrier, inc=1, device_id=peer, device_id_type=MESH)
    pl.semaphore_wait(barrier, len(everyone))

    from_down, from_up, from_across = {}, {}, {}

    def direct(*numbers):
        for i in numbers:
            j = (i + half) % CHUNKS
            for piece in (i, j):
                if piece in load_act:
                    load_act.pop(piece).wait()
            from_down[i] = send(actr.at[0, i], actr.at[3, i], device(z, x, c, up))
            from_up[j] = send(actr.at[0, j], actr.at[1, j], device(z, x, c, down))

    def forward(*numbers):
        for i in numbers:
            from_down[i].wait_recv()
            from_across[i] = send(actr.at[3, i], actr.at[2, i], device(z, x, c, up))
            j = i + half
            from_up[j].wait_recv()
            from_across[j] = send(actr.at[1, j], actr.at[2, j], device(z, x, c, down))

    load_act = dict(enumerate(load_act))
    direct(0)

    load_rt.wait()
    rt3 = rows3(rt[...])
    for load in load_vg:
        load.wait()
    for dy in range(ny):
        uout[dy] = fold3(mm(rt3, vg_v[dy], NT))
    recv_u = [send(uout.at[dy], uin.at[dy - 1], device(z, x, c, yy)) for dy, yy in y_peers]

    recv_vg = [send(vg.at[tokens(yy)], vgx.at[0, ny - dy], device(z, x, c, yy)) for dy, yy in y_peers]
    own_w = w.at[c, x, z]
    w_from_down = send(own_w, wbuf.at[x, z, :, 3], device(z, x, c, up))
    w_from_up = send(own_w, wbuf.at[x, z, :, 1], device(z, x, c, down))
    direct(1, 2, 3)

    def place(h, a, b):
        return (a, b) if h == 0 else (b, a)

    def piece(h, first, second):
        zz, xx = place(h, first, second)
        return wbuf.at[xx, zz, h, 1:ny]

    def neighbour(h, stage, way):
        n = (nz if h == 0 else nx) if stage == 0 else (nx if h == 0 else nz)
        first, second = place(h, z, x)
        if stage == 0:
            first = shifted(first, way % n, n)
        else:
            second = shifted(second, way % n, n)
        zz, xx = place(h, first, second)
        return device(zz, xx, c, y)

    half_here = [(place(h, z, x), place(h, nz, nx)) for h in range(2)]
    stage_one, stage_one_across, stage_two, stage_two_across = {}, {}, {}, {}

    def weights_first():
        for h in range(2):
            (first, second), _ = half_here[h]
            own = piece(h, first, second)
            for way in (1, -1):
                stage_one[h, way] = send(own, own, neighbour(h, 0, way))

    def weights_across():
        for h in range(2):
            (first, second), (n, _) = half_here[h]
            way = 1 - 2 * h
            stage_one[h, way].wait_recv()
            came = piece(h, shifted(first, -way % n, n), second)
            stage_one_across[h] = send(came, came, neighbour(h, 0, way))

    def weights_second(i):
        for h in range(2):
            (first, second), (n, _) = half_here[h]
            if i in (1, 2):
                way = 3 - 2 * i
                if way != 1 - 2 * h:
                    stage_one[h, way].wait_recv()
                first = shifted(first, -way % n, n)
            elif i == 3:
                stage_one_across[h].wait_recv()
                first = shifted(first, 2, n)
            for way in (1, -1):
                stage_two[h, i, way] = send(piece(h, first, second), piece(h, first, second), neighbour(h, 1, way))

    def weights_second_across(i):
        for h in range(2):
            (first, second), (n, m) = half_here[h]
            first = shifted(first, (0, n - 1, 1, 2)[i], n)
            way = (1, -1, 1, -1)[i]
            stage_two[h, i, way].wait_recv()
            came = piece(h, first, shifted(second, -way % m, m))
            stage_two_across[h, i] = send(came, came, neighbour(h, 1, way))

    rt2 = rt3[: 2 * r]

    def columns(p):
        return pl.ds(pl.multiple_of(p * wide, wide), wide)

    def store_left(value, cc, j0):
        for j in range(wb):
            lacc[cc, j0 + j] = value[:, j * BLK : (j + 1) * BLK]

    def load_left(ref, cc, j0):
        return jnp.concatenate([ref[cc, j0 + j] for j in range(wb)], axis=1)

    for load in load_err:
        load.wait()

    def err_left(p, carry):
        hi, lo = split2(err_v[columns(p), :])
        store_left(fold2(mm(rt2, lo, NT) + mm(rt2, hi, NT)), lax.div(p, per_piece), lax.rem(p, per_piece) * wb)
        return carry

    lax.fori_loop(0, pieces, err_left, 0)

    wait_all(recv_u)
    ut = uout[0]
    for dy in range(ny - 1):
        ut = ut + uin[dy]
    ut3 = rows3(ut)
    for load in load_act.values():
        load.wait()
    load_act = {}

    def own_act(p):
        n = wide // part
        if n >= 1:
            return jnp.concatenate([actr[0, p * n + i] for i in range(n)], axis=1)
        n = part // wide
        inside = pl.ds(pl.multiple_of(lax.rem(p, n) * wide, wide), wide)
        return actr[0, lax.div(p, n), :, inside]

    def act_left(cc):
        def step(i, carry):
            value = fold3(mm(ut3, own_act(cc * per_piece + i)))
            store_left(load_left(lacc, cc, i * wb) + value, cc, i * wb)
            return carry

        lax.fori_loop(0, per_piece, step, 0)

    recv = []
    for cc in cores:
        act_left(cc)
        recv.append(send(lacc.at[cc], rc, device(z, x, cc, y)))
    act_left(c)

    recv_core = recv
    direct(4, 5)
    load_vgx.wait()
    wait_all(recv_vg)
    recv_vgx = [send(vgx.at[0], vgx.at[dc], device(z, x, cc, y)) for dc, cc in enumerate(cores, 1)]
    wait_all(recv)
    lacc[c] += rc[...]
    recv = [
        send(lacc.at[c, xx * nz + zz], rxz.at[i], device(zz, xx, c, y)) for i, (xx, zz) in enumerate(plane)
    ]
    load_w.wait()
    w_from_down.wait_recv()
    w_halves = [send(wbuf.at[x, z, 0, 3], wbuf.at[x, z, 0, 2], device(z, x, c, up))]
    w_from_up.wait_recv()
    w_halves.append(send(wbuf.at[x, z, 1, 1], wbuf.at[x, z, 1, 2], device(z, x, c, down)))
    settle(recv_u + recv_core)
    recv_rs = recv
    wait_all(recv)
    total = lacc[c, mine]
    for i in range(len(plane)):
        total = total + rxz[i]
    ysum[y] = total
    own = ysum.at[y]
    recv = [send(own, own, device(z, x, c, yy)) for _, yy in y_peers]
    direct(6, 7)
    forward(0)
    wait_all(w_halves)
    weights_first()
    weights_second(0)
    settle(recv_rs)
    wait_all(recv)
    total = ysum[0]
    for yy in range(1, ny):
        total = total + ysum[yy]
    lf[c, mine] = total
    own = lf.at[c, mine]
    recv_y = recv
    recv = [send(own, own, device(zz, xx, c, y)) for xx, zz in plane]
    forward(1)
    weights_across()
    weights_second(1)
    weights_second(2)
    settle(recv_y)
    wait_all(recv)
    recv_ag = recv
    own = lf.at[c]
    recv = [send(own, own, device(z, x, cc, y)) for cc in cores]
    weights_second(3)
    weights_second_across(0)
    settle(recv_ag)

    forward(2, 3)
    settle(recv_vg + recv_vgx + [w_from_down, w_from_up] + w_halves + list(stage_one.values()))
    wait_all(recv)

    def left_piece(p):
        return rows3(load_left(lf, lax.div(p, per_piece), lax.rem(p, per_piece) * wb))

    def products(p, carry):
        gram, by_act = carry
        block = left_piece(p)
        return gram + mm(block, block, NT), by_act + mm(block[: 2 * r], own_act(p), NT)

    gram, by_act = lax.fori_loop(
        0, pieces, products, (jnp.zeros((3 * r, 3 * r), F32), jnp.zeros((2 * r, tok), F32))
    )
    aout[...] = fold2(by_act)
    recv_a = [send(aout, ain.at[dy - 1], device(z, x, c, yy)) for dy, yy in y_peers]
    weights_second_across(1)
    weights_second_across(2)

    total = jnp.zeros((2 * r, err_v.shape[1]), F32)
    count = nb // (r // 4)
    for i, state in enumerate(gram_schmidt(self_products(gram, r))):
        block = jnp.concatenate([lf[(i * count + j) // per, (i * count + j) % per] for j in range(count)], axis=1)
        hi, lo = split2(err_v[i * count * BLK : (i + 1) * count * BLK, :])
        block = rows2(block)
        total = total + (mm(block, lo) + mm(block, hi))
    total = fold2(total)
    weights, norms = unit_weights(state)

    wait_all(recv_a)
    for slot in range(ny):
        total = total + fold3(mm(rows3(aout[...] if slot == 0 else ain[ny - slot - 1]), vg_v[slot]))
    zsum[0] = total
    recv = [send(zsum.at[0], zsum.at[dc], device(z, x, cc, y)) for dc, cc in enumerate(cores, 1)]

    weights_second_across(3)

    def apply_first(p, gram):
        block = times(weights, load_left(lf, lax.div(p, per_piece), lax.rem(p, per_piece) * wb))
        q1[p] = block
        block = rows3(block)
        return gram + mm(block, block, NT)

    off = self_products(lax.fori_loop(0, pieces, apply_first, jnp.zeros((3 * r, 3 * r), F32)), r) - norms
    row_id = lax.broadcasted_iota(jnp.int32, (r, r), 0)
    col_id = lax.broadcasted_iota(jnp.int32, (r, r), 1)
    wait_all(recv)
    for dc in range(1, nc):
        total = total + zsum[dc]
    tz[mine] = total
    own = tz.at[mine]
    recv = [send(own, own, device(zz, xx, c, y)) for xx, zz in plane]
    again = jnp.where(col_id < row_id, off, jnp.where(col_id == row_id, 0.5 * off, 0.0))
    weights = weights - times(again, weights)
    scale = math.sqrt(float(d))

    def apply_second(p, carry):
        block = q1[p]
        block = block - times(again, block)
        left_out[:, columns(p)] = block * scale
        return carry

    lax.fori_loop(0, pieces, apply_second, 0)


    for i in range(4):
        for h in range(2):
            stage_two[h, i, (-1, 1, -1, 1)[i]].wait_recv()
            stage_two_across[h, i].wait_recv()
    wait_all(recv_vgx)

    def input_grad(i, carry):
        total = None
        for slot in range(ny):
            weight = wbuf[lax.div(i, nz), lax.rem(i, nz), :, slot].reshape(BLK, BLK)
            part_sum = mm(vgx[:, slot].reshape(nc * tok, BLK), weight, NT).astype(BF16).astype(F32)
            total = part_sum if total is None else total + part_sum
        total = total.astype(BF16).reshape(nc, tok, BLK)
        gi[:, pl.ds(pl.multiple_of((c * per + i) * BLK, BLK), BLK)] = total[0]
        for dc in range(1, nc):
            outs[dc - 1, :, pl.ds(pl.multiple_of(i * BLK, BLK), BLK)] = total[dc]
        return carry

    lax.fori_loop(0, per, input_grad, 0)
    share_of = gi.at[:, pl.ds(pl.multiple_of(c * per * BLK, BLK), per * BLK)]
    sent_out = [send(outs.at[nc - 1 - dc], share_of, device(z, x, cc, y)) for dc, cc in enumerate(cores, 1)]

    for i in range(CHUNKS):
        if i >= half:
            from_down[i].wait_recv()
        else:
            from_up[i].wait_recv()
    cotangent = vg_v[...].reshape(ny * tok, BLK).astype(F32).T.astype(BF16)

    def merge(i, carry):
        at = pl.ds(pl.multiple_of(i * BLK, BLK), BLK)
        n = part // BLK
        piece = pl.ds(pl.multiple_of(lax.rem(i, n) * BLK, BLK), BLK)
        block = mm(cotangent, actr[:, lax.div(i, n), :, piece].reshape(ny * tok, BLK))
        merged[at, :] = err_v[at, :] + block.T
        return carry

    for i in range(half):
        for j in (i, i + half):
            from_across[j].wait_recv()
            lax.fori_loop(j * part // BLK, (j + 1) * part // BLK, merge, 0)

    wait_all(recv)
    total = tz[0]
    for i in range(1, per):
        total = total + tz[i]
    r_out[...] = times(weights, total) / float(nb)

    wait_all(sent_out)
    settle([copy for copy in sent if id(copy) not in settled])
    assert counter == [send_sem.shape[0], local_sem.shape[0]], counter


def error_kernel(merged, left, right, gi, error_out, left_out, right_out, gi_out, error, sem):
    d = merged.shape[0]
    pieces = error.shape[0]
    rows = d // pieces
    copies = [
        pltpu.make_async_copy(a, b, sem.at[pieces + i])
        for i, (a, b) in enumerate([(gi, gi_out), (left, left_out), (right, right_out)])
    ]
    for copy in copies:
        copy.start()
    hi, lo = split2(right[...] / math.sqrt(float(d)))
    right3 = jnp.concatenate([hi, hi, lo], axis=0)
    for i in range(pieces):
        at = pl.ds(i * rows, rows)
        hi, lo = split2(left[:, at])
        error[i] = merged[at, :] - mm(jnp.concatenate([hi, lo, hi], axis=0), right3, TN)
        copies.append(pltpu.make_async_copy(error.at[i], error_out.at[at], sem.at[i]))
        copies[-1].start()
    for copy in copies:
        copy.wait()


def build(geom):
    nz, nx, nc, ny = geom

    def body(act, vg, w, err, right_prev):
        tok, d = act.shape
        kv = vg.shape[1]
        r = right_prev.shape[1]
        nb = nc * nx * nz
        per = nx * nz
        wide = min(WIDE, per * BLK)
        assert d == nb * BLK and kv == BLK and per * BLK % wide == 0
        sends = 4 * (ny - 1) + 4 + 3 * CHUNKS + 30 + 3 * (per - 1) + 5 * (nc - 1)
        pieces = w.reshape(nc, nx, nz, 2, BLK // 2, kv)
        inputs = [
            pltpu.with_memory_space_constraint(a, pltpu.HBM) for a in (act, vg, pieces, err[0], right_prev.T)
        ]
        hbm = pl.BlockSpec(memory_space=pltpu.HBM)
        vmem = pl.BlockSpec(memory_space=pltpu.VMEM)
        anywhere = pl.BlockSpec(memory_space=pl.ANY)
        results = (((d, kv), F32), ((r, d), F32), ((r, kv), F32), ((tok, d), BF16))
        made = pl.pallas_call(
            functools.partial(comm_kernel, geom),
            out_shape=tuple(pltpu.VMEM(*shape) for shape in results),
            in_specs=[hbm] * 5,
            out_specs=(vmem,) * 4,
            scratch_shapes=[
                pltpu.VMEM((r, kv), F32),
                pltpu.VMEM((ny, CHUNKS, tok, d // CHUNKS), BF16),
                pltpu.VMEM((ny, tok, kv), BF16),
                pltpu.VMEM((d, kv), F32),
                pltpu.VMEM((ny, r, tok), F32),
                pltpu.VMEM((ny - 1, r, tok), F32),
                pltpu.VMEM((nc, ny, tok, kv), BF16),
                pltpu.VMEM((nx, nz, 2, ny, BLK // 2, kv), BF16),
                pltpu.VMEM((max(nc - 1, 1), tok, per * BLK), BF16),
                pltpu.VMEM((nc, per, r, BLK), F32),
                pltpu.VMEM((nc, per, r, BLK), F32),
                pltpu.VMEM((per, r, BLK), F32),
                pltpu.VMEM((per - 1, r, BLK), F32),
                pltpu.VMEM((ny, r, BLK), F32),
                pltpu.VMEM((d // wide, r, wide), F32),
                pltpu.VMEM((r, tok), F32),
                pltpu.VMEM((ny - 1, r, tok), F32),
                pltpu.VMEM((nc, r, kv), F32),
                pltpu.VMEM((per, r, kv), F32),
                pltpu.SemaphoreType.DMA((1 + 1 + 4 + CHUNKS + ny + 1,)),
                pltpu.SemaphoreType.DMA((sends,)),
                pltpu.SemaphoreType.DMA((sends,)),
            ],
            compiler_params=pltpu.CompilerParams(
                collective_id=0, has_side_effects=True, vmem_limit_bytes=44 * MIB
            ),
        )(*inputs)

        pieces = 16
        error_next, left, right, grad_input = pl.pallas_call(
            error_kernel,
            out_shape=tuple(jax.ShapeDtypeStruct(*shape) for shape in results),
            in_specs=[vmem] * 4,
            out_specs=(anywhere,) * 4,
            scratch_shapes=[pltpu.VMEM((pieces, d // pieces, kv), F32), pltpu.SemaphoreType.DMA((pieces + 3,))],
            compiler_params=pltpu.CompilerParams(vmem_limit_bytes=24 * MIB),
        )(*made)
        return (grad_input, error_next[None], left.T, right.T)

    return body


def solution(mesh):
    return jax.shard_map(
        build((4, 4, 2, 4)),
        mesh=mesh,
        in_specs=(
            P(("dp", "tp"), None),
            P("dp", "tp"),
            P(None, "tp"),
            P("dp", None, "tp"),
            P("tp", None),
        ),
        out_specs=(P(("dp", "tp"), None), P("dp", None, "tp"), P(), P("tp", None)),
        check_vma=False,
    )
```

```python
import functools
import math

import jax
import jax.numpy as jnp
from jax import lax
from jax.experimental import pallas as pl
from jax.experimental.pallas import tpu as pltpu
from jax.sharding import PartitionSpec as P

MESH = pl.DeviceIdType.MESH
F32 = jnp.float32
BF16 = jnp.bfloat16
BLK = 256
EPS = 1e-12
MIB = 1024 * 1024
WIDE = 8 * BLK
CHUNKS = 16
NN = (((1,), (0,)), ((), ()))
NT = (((1,), (1,)), ((), ()))
TN = (((0,), (0,)), ((), ()))


def mm(a, b, dims=NN):
    return lax.dot_general(a, b, dims, preferred_element_type=F32)


def split2(a):
    hi = a.astype(BF16)
    lo = (a - hi.astype(F32)).astype(BF16)
    return hi, lo


def split3(a):
    hi = a.astype(BF16)
    rest = a - hi.astype(F32)
    mid = rest.astype(BF16)
    lo = (rest - mid.astype(F32)).astype(BF16)
    return hi, mid, lo


def rows3(a):
    return jnp.concatenate(split3(a), axis=0)


def fold3(a):
    n = a.shape[0] // 3
    return (a[2 * n :] + a[n : 2 * n]) + a[:n]


def rows2(a):
    return jnp.concatenate(split2(a), axis=0)


def fold2(a):
    n = a.shape[0] // 2
    return a[n:] + a[:n]


def self_products(total, r):
    total = fold3(total)
    return (total[:, 2 * r :] + total[:, r : 2 * r]) + total[:, :r]


def times(a, b):
    a_hi, a_mid, a_lo = (v.astype(F32) for v in split3(a))
    b_hi, b_mid, b_lo = split3(b)
    left = jnp.concatenate([a_lo, a_mid, a_hi, a_mid, a_hi, a_hi], axis=1).astype(BF16)
    return mm(left, jnp.concatenate([b_hi, b_mid, b_lo, b_hi, b_mid, b_hi], axis=0))


def eye_like(n):
    return (lax.broadcasted_iota(jnp.int32, (n, n), 0) == lax.broadcasted_iota(jnp.int32, (n, n), 1)).astype(F32)


def gram_schmidt(gram):
    n = gram.shape[0]
    left, weights = gram, eye_like(n)
    row_id = lax.broadcasted_iota(jnp.int32, (n, 1), 0)
    m = 4
    for j in range(0, n, m):
        columns = [jnp.broadcast_to(left[:, i : i + 1], (n, n)) for i in range(j, j + m)]
        rows = [left[i : i + 1, :] for i in range(j, j + m)]
        given = [weights[i : i + 1, :] for i in range(j, j + m)]
        off_left, off_weights = jnp.zeros((n, n), F32), jnp.zeros((n, n), F32)
        for i in range(m):
            at = j + i
            s = jnp.maximum(columns[i][at : at + 1, :], 0.0)
            inverse = 1.0 / (s + EPS)
            c = (2.0 - s * inverse) * inverse
            f = jnp.where(row_id > at, columns[i] * c, 0.0)
            h = f * (2.0 - c * s)
            for later in range(i + 1, m):
                to = j + later
                columns[later] = columns[later] - h * columns[later][at : at + 1, :]
                rows[later] = rows[later] - h[to : to + 1, :] * rows[i]
                given[later] = given[later] - f[to : to + 1, :] * given[i]
            off_left = off_left + h * rows[i]
            off_weights = off_weights + f * given[i]
        left, weights = left - off_left, weights - off_weights
        yield left, weights


def unit_weights(state):
    left, weights = state
    eye = eye_like(left.shape[0])
    s = jnp.maximum(jnp.sum(left * eye, axis=1, keepdims=True), 0.0)
    return weights / jnp.sqrt(s + EPS), eye * (s / (s + EPS))


def comm_kernel(
    geom, act, vg, w, err, rt_in, merged, left_out, r_out, gi,
    rt, actr, vg_v, err_v, uout, uin, vstage, vgx, wbuf, outs, lacc, lf, rc, rxz, ysum, q1, aout, ain, zsum, tz,
    local_sem, send_sem, recv_sem,
):
    nz, nx, nc, ny = geom
    nb = nc * nx * nz
    per = nx * nz
    _, _, tok, part = actr.shape
    d = part * CHUNKS
    half = CHUNKS // 2
    r = rt.shape[0]
    wide = min(WIDE, per * BLK)
    wb = wide // BLK
    pieces = d // wide
    per_piece = per // wb
    dp, y = lax.axis_index("dp"), lax.axis_index("tp")
    c = lax.rem(dp, nc)
    x = lax.rem(lax.div(dp, nc), nx)
    z = lax.div(dp, nc * nx)
    mine = x * nz + z

    def shifted(i, by, n):
        return lax.rem(i + by, n)

    def device(zz, xx, cc, yy):
        return ((zz * nx + xx) * nc + cc, yy)

    y_peers = [(dy, shifted(y, dy, ny)) for dy in range(1, ny)]
    plane = [
        (shifted(x, dx, nx), shifted(z, dz, nz)) for dx in range(nx) for dz in range(nz) if (dx, dz) != (0, 0)
    ]
    cores = [shifted(c, dc, nc) for dc in range(1, nc)]
    up, down, across = shifted(y, 1, ny), shifted(y, ny - 1, ny), shifted(y, 2, ny)

    sent, settled = [], []
    counter = [0, 0]

    def send(src, dst, to):
        i = counter[0]
        counter[0] += 1
        copy = pltpu.make_async_remote_copy(
            src_ref=src, dst_ref=dst, send_sem=send_sem.at[i], recv_sem=recv_sem.at[i], device_id=to, device_id_type=MESH
        )
        copy.start()
        sent.append(copy)
        return copy

    def fetch(src, dst):
        i = counter[1]
        counter[1] += 1
        copy = pltpu.make_async_copy(src, dst, local_sem.at[i])
        copy.start()
        return copy

    def wait_all(copies):
        for copy in copies:
            copy.wait_recv()

    def settle(copies):
        for copy in copies:
            copy.wait_send()
        settled.extend(id(copy) for copy in copies)

    def tokens(yy):
        return pl.ds(pl.multiple_of(yy * tok, tok), tok)

    load_rt = fetch(rt_in, rt)
    load_vg = [fetch(vg.at[tokens(yy)], vg_v.at[i]) for i, yy in enumerate((y, up, across, down))]
    load_vgx = fetch(vg.at[tokens(y)], vgx.at[0, 0])
    load_act = [fetch(act.at[:, pl.ds(i * part, part)], actr.at[0, i]) for i in range(CHUNKS)]
    share = d // 4
    load_err = [fetch(err.at[pl.ds(i * share, share)], err_v.at[pl.ds(i * share, share)]) for i in range(4)]
    load_w = fetch(w.at[c], wbuf.at[:, :, :, 0])

    barrier = pltpu.get_barrier_semaphore()
    everyone = (
        [device(z, x, cc, y) for cc in cores]
        + [device(zz, xx, c, y) for xx, zz in plane]
        + [device(z, x, c, yy) for _, yy in y_peers]
    )
    for peer in everyone:
        pl.semaphore_signal(barrier, inc=1, device_id=peer, device_id_type=MESH)
    pl.semaphore_wait(barrier, len(everyone))

    from_down, from_up, from_across = {}, {}, {}

    def direct(*numbers):
        for i in numbers:
            j = (i + half) % CHUNKS
            for piece in (i, j):
                if piece in load_act:
                    load_act.pop(piece).wait()
            from_down[i] = send(actr.at[0, i], actr.at[3, i], device(z, x, c, up))
            from_up[j] = send(actr.at[0, j], actr.at[1, j], device(z, x, c, down))

    def forward(*numbers):
        for i in numbers:
            from_down[i].wait_recv()
            from_across[i] = send(actr.at[3, i], actr.at[2, i], device(z, x, c, up))
            j = i + half
            from_up[j].wait_recv()
            from_across[j] = send(actr.at[1, j], actr.at[2, j], device(z, x, c, down))

    load_act = dict(enumerate(load_act))

    load_rt.wait()
    rt3 = rows3(rt[...])
    for load in load_vg:
        load.wait()
    for dy in range(ny):
        uout[dy] = fold3(mm(rt3, vg_v[dy], NT))
    recv_u = [send(uout.at[dy], uin.at[dy - 1], device(z, x, c, yy)) for dy, yy in y_peers]

    recv_vg = [send(vg.at[tokens(up)], vgx.at[0, 3], device(z, x, c, up))]
    recv_vg.append(send(vg.at[tokens(down)], vgx.at[0, 1], device(z, x, c, down)))
    few = tok // 2
    ways = (up, down)
    vg_passing = [
        send(vg.at[pl.ds(pl.multiple_of(across * tok + h * few, few), few)], vstage.at[h], device(z, x, c, ways[h]))
        for h in range(2)
    ]
    direct(0)
    own_w = w.at[c, x, z]
    w_from_down = send(own_w, wbuf.at[x, z, :, 3], device(z, x, c, up))
    w_from_up = send(own_w, wbuf.at[x, z, :, 1], device(z, x, c, down))
    direct(1, 2)

    def place(h, a, b):
        return (a, b) if h == 0 else (b, a)

    def piece(h, first, second):
        zz, xx = place(h, first, second)
        return wbuf.at[xx, zz, h, 1:ny]

    def neighbour(h, stage, way):
        n = (nz if h == 0 else nx) if stage == 0 else (nx if h == 0 else nz)
        first, second = place(h, z, x)
        if stage == 0:
            first = shifted(first, way % n, n)
        else:
            second = shifted(second, way % n, n)
        zz, xx = place(h, first, second)
        return device(zz, xx, c, y)

    half_here = [(place(h, z, x), place(h, nz, nx)) for h in range(2)]
    stage_one, stage_one_across, stage_two, stage_two_across = {}, {}, {}, {}

    def weights_first():
        for h in range(2):
            (first, second), _ = half_here[h]
            own = piece(h, first, second)
            for way in (1, -1):
                stage_one[h, way] = send(own, own, neighbour(h, 0, way))

    def weights_across():
        for h in range(2):
            (first, second), (n, _) = half_here[h]
            way = 1 - 2 * h
            stage_one[h, way].wait_recv()
            came = piece(h, shifted(first, -way % n, n), second)
            stage_one_across[h] = send(came, came, neighbour(h, 0, way))

    def weights_second(i):
        for h in range(2):
            (first, second), (n, _) = half_here[h]
            if i in (1, 2):
                way = 3 - 2 * i
                if way != 1 - 2 * h:
                    stage_one[h, way].wait_recv()
                first = shifted(first, -way % n, n)
            elif i == 3:
                stage_one_across[h].wait_recv()
                first = shifted(first, 2, n)
            for way in (1, -1):
                stage_two[h, i, way] = send(piece(h, first, second), piece(h, first, second), neighbour(h, 1, way))

    def weights_second_across(i):
        for h in range(2):
            (first, second), (n, m) = half_here[h]
            first = shifted(first, (0, n - 1, 1, 2)[i], n)
            way = (1, -1, 1, -1)[i]
            stage_two[h, i, way].wait_recv()
            came = piece(h, first, shifted(second, -way % m, m))
            stage_two_across[h, i] = send(came, came, neighbour(h, 1, way))

    rt2 = rt3[: 2 * r]

    def columns(p):
        return pl.ds(pl.multiple_of(p * wide, wide), wide)

    def store_left(value, cc, j0):
        for j in range(wb):
            lacc[cc, j0 + j] = value[:, j * BLK : (j + 1) * BLK]

    def load_left(ref, cc, j0):
        return jnp.concatenate([ref[cc, j0 + j] for j in range(wb)], axis=1)

    for load in load_err:
        load.wait()

    def err_left(p, carry):
        hi, lo = split2(err_v[columns(p), :])
        store_left(fold2(mm(rt2, lo, NT) + mm(rt2, hi, NT)), lax.div(p, per_piece), lax.rem(p, per_piece) * wb)
        return carry

    lax.fori_loop(0, pieces, err_left, 0)

    wait_all(recv_u)
    ut = uout[0]
    for dy in range(ny - 1):
        ut = ut + uin[dy]
    ut3 = rows3(ut)
    for load in load_act.values():
        load.wait()
    load_act = {}

    def own_act(p):
        n = wide // part
        if n >= 1:
            return jnp.concatenate([actr[0, p * n + i] for i in range(n)], axis=1)
        n = part // wide
        inside = pl.ds(pl.multiple_of(lax.rem(p, n) * wide, wide), wide)
        return actr[0, lax.div(p, n), :, inside]

    def act_left(cc):
        def step(i, carry):
            value = fold3(mm(ut3, own_act(cc * per_piece + i)))
            store_left(load_left(lacc, cc, i * wb) + value, cc, i * wb)
            return carry

        lax.fori_loop(0, per_piece, step, 0)

    recv = []
    for cc in cores:
        act_left(cc)
        recv.append(send(lacc.at[cc], rc, device(z, x, cc, y)))
    act_left(c)

    recv_core = recv
    direct(3)
    load_vgx.wait()
    for h in range(2):
        vg_passing[h].wait_recv()
        recv_vg.append(send(vstage.at[h], vgx.at[0, 2, h * few : (h + 1) * few], device(z, x, c, ways[h])))
    wait_all(recv)
    lacc[c] += rc[...]
    recv = [
        send(lacc.at[c, xx * nz + zz], rxz.at[i], device(zz, xx, c, y)) for i, (xx, zz) in enumerate(plane)
    ]
    load_w.wait()
    w_from_down.wait_recv()
    w_halves = [send(wbuf.at[x, z, 0, 3], wbuf.at[x, z, 0, 2], device(z, x, c, up))]
    w_from_up.wait_recv()
    w_halves.append(send(wbuf.at[x, z, 1, 1], wbuf.at[x, z, 1, 2], device(z, x, c, down)))
    settle(recv_u + recv_core)
    recv_rs = recv
    wait_all(recv)
    total = lacc[c, mine]
    for i in range(len(plane)):
        total = total + rxz[i]
    ysum[y] = total
    own = ysum.at[y]
    recv = [send(own, own, device(z, x, c, yy)) for _, yy in y_peers]
    direct(4, 5, 6, 7)
    wait_all(w_halves)
    weights_first()
    weights_second(0)
    settle(recv_rs)
    wait_all(recv)
    total = ysum[0]
    for yy in range(1, ny):
        total = total + ysum[yy]
    lf[c, mine] = total
    own = lf.at[c, mine]
    recv_y = recv
    recv = [send(own, own, device(zz, xx, c, y)) for xx, zz in plane]
    direct(8)
    weights_across()
    weights_second(1)
    weights_second(2)
    settle(recv_y)
    wait_all(recv)
    recv_ag = recv
    own = lf.at[c]
    recv = [send(own, own, device(z, x, cc, y)) for cc in cores]
    weights_second(3)
    weights_second_across(0)
    settle(recv_ag)

    direct(9)
    wait_all(recv_vg)
    recv_vgx = [send(vgx.at[0], vgx.at[dc], device(z, x, cc, y)) for dc, cc in enumerate(cores, 1)]
    settle(vg_passing + recv_vg + [w_from_down, w_from_up] + w_halves + list(stage_one.values()))
    wait_all(recv)

    def left_piece(p):
        return rows3(load_left(lf, lax.div(p, per_piece), lax.rem(p, per_piece) * wb))

    def products(p, carry):
        gram, by_act = carry
        block = left_piece(p)
        return gram + mm(block, block, NT), by_act + mm(block[: 2 * r], own_act(p), NT)

    gram, by_act = lax.fori_loop(
        0, pieces, products, (jnp.zeros((3 * r, 3 * r), F32), jnp.zeros((2 * r, tok), F32))
    )
    aout[...] = fold2(by_act)
    recv_a = [send(aout, ain.at[dy - 1], device(z, x, c, yy)) for dy, yy in y_peers]
    direct(*range(10, CHUNKS))
    forward(*range(half))
    weights_second_across(1)
    weights_second_across(2)

    total = jnp.zeros((2 * r, err_v.shape[1]), F32)
    count = nb // (r // 4)
    for i, state in enumerate(gram_schmidt(self_products(gram, r))):
        block = jnp.concatenate([lf[(i * count + j) // per, (i * count + j) % per] for j in range(count)], axis=1)
        hi, lo = split2(err_v[i * count * BLK : (i + 1) * count * BLK, :])
        block = rows2(block)
        total = total + (mm(block, lo) + mm(block, hi))
    total = fold2(total)
    weights, norms = unit_weights(state)

    wait_all(recv_a)
    for slot in range(ny):
        total = total + fold3(mm(rows3(aout[...] if slot == 0 else ain[ny - slot - 1]), vg_v[slot]))
    zsum[0] = total
    recv = [send(zsum.at[0], zsum.at[dc], device(z, x, cc, y)) for dc, cc in enumerate(cores, 1)]

    weights_second_across(3)

    def apply_first(p, gram):
        block = times(weights, load_left(lf, lax.div(p, per_piece), lax.rem(p, per_piece) * wb))
        q1[p] = block
        block = rows3(block)
        return gram + mm(block, block, NT)

    off = self_products(lax.fori_loop(0, pieces, apply_first, jnp.zeros((3 * r, 3 * r), F32)), r) - norms
    row_id = lax.broadcasted_iota(jnp.int32, (r, r), 0)
    col_id = lax.broadcasted_iota(jnp.int32, (r, r), 1)
    wait_all(recv)
    for dc in range(1, nc):
        total = total + zsum[dc]
    tz[mine] = total
    own = tz.at[mine]
    recv = [send(own, own, device(zz, xx, c, y)) for xx, zz in plane]
    again = jnp.where(col_id < row_id, off, jnp.where(col_id == row_id, 0.5 * off, 0.0))
    weights = weights - times(again, weights)
    scale = math.sqrt(float(d))

    def apply_second(p, carry):
        block = q1[p]
        block = block - times(again, block)
        left_out[:, columns(p)] = block * scale
        return carry

    lax.fori_loop(0, pieces, apply_second, 0)


    for i in range(4):
        for h in range(2):
            stage_two[h, i, (-1, 1, -1, 1)[i]].wait_recv()
            stage_two_across[h, i].wait_recv()
    wait_all(recv_vgx)

    def input_grad(i, carry):
        total = None
        for slot in range(ny):
            weight = wbuf[lax.div(i, nz), lax.rem(i, nz), :, slot].reshape(BLK, BLK)
            part_sum = mm(vgx[:, slot].reshape(nc * tok, BLK), weight, NT).astype(BF16).astype(F32)
            total = part_sum if total is None else total + part_sum
        total = total.astype(BF16).reshape(nc, tok, BLK)
        gi[:, pl.ds(pl.multiple_of((c * per + i) * BLK, BLK), BLK)] = total[0]
        for dc in range(1, nc):
            outs[dc - 1, :, pl.ds(pl.multiple_of(i * BLK, BLK), BLK)] = total[dc]
        return carry

    lax.fori_loop(0, per, input_grad, 0)
    share_of = gi.at[:, pl.ds(pl.multiple_of(c * per * BLK, BLK), per * BLK)]
    sent_out = [send(outs.at[nc - 1 - dc], share_of, device(z, x, cc, y)) for dc, cc in enumerate(cores, 1)]

    for i in range(CHUNKS):
        if i >= half:
            from_down[i].wait_recv()
        else:
            from_up[i].wait_recv()
    cotangent = vg_v[...].reshape(ny * tok, BLK).astype(F32).T.astype(BF16)

    def merge(j):
        from_across[j].wait_recv()
        at = pl.ds(j * part, part)
        merged[at, :] = err_v[at, :] + mm(cotangent, actr[:, j].reshape(ny * tok, part)).T

    for i in range(half - 2):
        merge(i)
        merge(i + half)

    wait_all(recv)
    total = tz[0]
    for i in range(1, per):
        total = total + tz[i]
    r_out[...] = times(weights, total) / float(nb)
    last = [id(from_across[i + h]) for i in range(half - 2, half) for h in (0, half)]
    settle([copy for copy in sent if id(copy) not in settled + last])

    for i in range(half - 2, half):
        merge(i)
        merge(i + half)

    wait_all(sent_out)
    settle([copy for copy in sent if id(copy) not in settled])
    assert counter == [send_sem.shape[0], local_sem.shape[0]], counter


def error_kernel(merged, left, right, gi, error_out, left_out, right_out, gi_out, error, sem):
    d = merged.shape[0]
    pieces = error.shape[0]
    rows = d // pieces
    copies = [
        pltpu.make_async_copy(a, b, sem.at[pieces + i])
        for i, (a, b) in enumerate([(gi, gi_out), (left, left_out), (right, right_out)])
    ]
    for copy in copies:
        copy.start()
    hi, lo = split2(right[...] / math.sqrt(float(d)))
    right3 = jnp.concatenate([hi, hi, lo], axis=0)
    for i in range(pieces):
        at = pl.ds(i * rows, rows)
        hi, lo = split2(left[:, at])
        error[i] = merged[at, :] - mm(jnp.concatenate([hi, lo, hi], axis=0), right3, TN)
        copies.append(pltpu.make_async_copy(error.at[i], error_out.at[at], sem.at[i]))
        copies[-1].start()
    for copy in copies:
        copy.wait()


def build(geom):
    nz, nx, nc, ny = geom

    def body(act, vg, w, err, right_prev):
        tok, d = act.shape
        kv = vg.shape[1]
        r = right_prev.shape[1]
        nb = nc * nx * nz
        per = nx * nz
        wide = min(WIDE, per * BLK)
        assert d == nb * BLK and kv == BLK and per * BLK % wide == 0
        sends = 3 * (ny - 1) + 6 + 4 + 3 * CHUNKS + 30 + 3 * (per - 1) + 5 * (nc - 1)
        pieces = w.reshape(nc, nx, nz, 2, BLK // 2, kv)
        inputs = [
            pltpu.with_memory_space_constraint(a, pltpu.HBM) for a in (act, vg, pieces, err[0], right_prev.T)
        ]
        hbm = pl.BlockSpec(memory_space=pltpu.HBM)
        vmem = pl.BlockSpec(memory_space=pltpu.VMEM)
        anywhere = pl.BlockSpec(memory_space=pl.ANY)
        results = (((d, kv), F32), ((r, d), F32), ((r, kv), F32), ((tok, d), BF16))
        made = pl.pallas_call(
            functools.partial(comm_kernel, geom),
            out_shape=tuple(pltpu.VMEM(*shape) for shape in results),
            in_specs=[hbm] * 5,
            out_specs=(vmem,) * 4,
            scratch_shapes=[
                pltpu.VMEM((r, kv), F32),
                pltpu.VMEM((ny, CHUNKS, tok, d // CHUNKS), BF16),
                pltpu.VMEM((ny, tok, kv), BF16),
                pltpu.VMEM((d, kv), F32),
                pltpu.VMEM((ny, r, tok), F32),
                pltpu.VMEM((ny - 1, r, tok), F32),
                pltpu.VMEM((2, tok // 2, kv), BF16),
                pltpu.VMEM((nc, ny, tok, kv), BF16),
                pltpu.VMEM((nx, nz, 2, ny, BLK // 2, kv), BF16),
                pltpu.VMEM((max(nc - 1, 1), tok, per * BLK), BF16),
                pltpu.VMEM((nc, per, r, BLK), F32),
                pltpu.VMEM((nc, per, r, BLK), F32),
                pltpu.VMEM((per, r, BLK), F32),
                pltpu.VMEM((per - 1, r, BLK), F32),
                pltpu.VMEM((ny, r, BLK), F32),
                pltpu.VMEM((d // wide, r, wide), F32),
                pltpu.VMEM((r, tok), F32),
                pltpu.VMEM((ny - 1, r, tok), F32),
                pltpu.VMEM((nc, r, kv), F32),
                pltpu.VMEM((per, r, kv), F32),
                pltpu.SemaphoreType.DMA((1 + 1 + 4 + CHUNKS + ny + 1,)),
                pltpu.SemaphoreType.DMA((sends,)),
                pltpu.SemaphoreType.DMA((sends,)),
            ],
            compiler_params=pltpu.CompilerParams(
                collective_id=0, has_side_effects=True, vmem_limit_bytes=44 * MIB
            ),
        )(*inputs)

        pieces = 16
        error_next, left, right, grad_input = pl.pallas_call(
            error_kernel,
            out_shape=tuple(jax.ShapeDtypeStruct(*shape) for shape in results),
            in_specs=[vmem] * 4,
            out_specs=(anywhere,) * 4,
            scratch_shapes=[pltpu.VMEM((pieces, d // pieces, kv), F32), pltpu.SemaphoreType.DMA((pieces + 3,))],
            compiler_params=pltpu.CompilerParams(vmem_limit_bytes=24 * MIB),
        )(*made)
        return (grad_input, error_next[None], left.T, right.T)

    return body


def solution(mesh):
    return jax.shard_map(
        build((4, 4, 2, 4)),
        mesh=mesh,
        in_specs=(
            P(("dp", "tp"), None),
            P("dp", "tp"),
            P(None, "tp"),
            P("dp", None, "tp"),
            P("tp", None),
        ),
        out_specs=(P(("dp", "tp"), None), P("dp", None, "tp"), P(), P("tp", None)),
        check_vma=False,
    )
```

```python
import functools
import math

import jax
import jax.numpy as jnp
from jax import lax
from jax.experimental import pallas as pl
from jax.experimental.pallas import tpu as pltpu
from jax.sharding import PartitionSpec as P

MESH = pl.DeviceIdType.MESH
F32 = jnp.float32
BF16 = jnp.bfloat16
BLK = 256
EPS = 1e-12
MIB = 1024 * 1024
WIDE = 8 * BLK
CHUNKS = 16
NN = (((1,), (0,)), ((), ()))
NT = (((1,), (1,)), ((), ()))
TN = (((0,), (0,)), ((), ()))


def mm(a, b, dims=NN):
    return lax.dot_general(a, b, dims, preferred_element_type=F32)


def split2(a):
    hi = a.astype(BF16)
    lo = (a - hi.astype(F32)).astype(BF16)
    return hi, lo


def split3(a):
    hi = a.astype(BF16)
    rest = a - hi.astype(F32)
    mid = rest.astype(BF16)
    lo = (rest - mid.astype(F32)).astype(BF16)
    return hi, mid, lo


def rows3(a):
    return jnp.concatenate(split3(a), axis=0)


def fold3(a):
    n = a.shape[0] // 3
    return (a[2 * n :] + a[n : 2 * n]) + a[:n]


def rows2(a):
    return jnp.concatenate(split2(a), axis=0)


def fold2(a):
    n = a.shape[0] // 2
    return a[n:] + a[:n]


def self_products(total, r):
    total = fold3(total)
    return (total[:, 2 * r :] + total[:, r : 2 * r]) + total[:, :r]


def times(a, b):
    a_hi, a_mid, a_lo = (v.astype(F32) for v in split3(a))
    b_hi, b_mid, b_lo = split3(b)
    left = jnp.concatenate([a_lo, a_mid, a_hi, a_mid, a_hi, a_hi], axis=1).astype(BF16)
    return mm(left, jnp.concatenate([b_hi, b_mid, b_lo, b_hi, b_mid, b_hi], axis=0))


def eye_like(n):
    return (lax.broadcasted_iota(jnp.int32, (n, n), 0) == lax.broadcasted_iota(jnp.int32, (n, n), 1)).astype(F32)


def gram_schmidt(gram):
    n = gram.shape[0]
    left, weights = gram, eye_like(n)
    row_id = lax.broadcasted_iota(jnp.int32, (n, 1), 0)
    m = 4
    for j in range(0, n, m):
        columns = [jnp.broadcast_to(left[:, i : i + 1], (n, n)) for i in range(j, j + m)]
        rows = [left[i : i + 1, :] for i in range(j, j + m)]
        given = [weights[i : i + 1, :] for i in range(j, j + m)]
        off_left, off_weights = jnp.zeros((n, n), F32), jnp.zeros((n, n), F32)
        for i in range(m):
            at = j + i
            s = jnp.maximum(columns[i][at : at + 1, :], 0.0)
            inverse = 1.0 / (s + EPS)
            c = (2.0 - s * inverse) * inverse
            f = jnp.where(row_id > at, columns[i] * c, 0.0)
            h = f * (2.0 - c * s)
            for later in range(i + 1, m):
                to = j + later
                columns[later] = columns[later] - h * columns[later][at : at + 1, :]
                rows[later] = rows[later] - h[to : to + 1, :] * rows[i]
                given[later] = given[later] - f[to : to + 1, :] * given[i]
            off_left = off_left + h * rows[i]
            off_weights = off_weights + f * given[i]
        left, weights = left - off_left, weights - off_weights
        yield left, weights


def unit_weights(state):
    left, weights = state
    eye = eye_like(left.shape[0])
    s = jnp.maximum(jnp.sum(left * eye, axis=1, keepdims=True), 0.0)
    return weights / jnp.sqrt(s + EPS), eye * (s / (s + EPS))


def comm_kernel(
    geom, act, vg, w, err, rt_in, merged, left_out, r_out, gi,
    rt, actr, vg_v, err_v, uout, uin, vstage, vgx, wbuf, outs, lacc, lf, rc, rxz, ysum, q1, aout, ain, zsum, tz,
    local_sem, send_sem, recv_sem,
):
    nz, nx, nc, ny = geom
    nb = nc * nx * nz
    per = nx * nz
    _, _, tok, part = actr.shape
    d = part * CHUNKS
    half = CHUNKS // 2
    r = rt.shape[0]
    wide = min(WIDE, per * BLK)
    wb = wide // BLK
    pieces = d // wide
    per_piece = per // wb
    dp, y = lax.axis_index("dp"), lax.axis_index("tp")
    c = lax.rem(dp, nc)
    x = lax.rem(lax.div(dp, nc), nx)
    z = lax.div(dp, nc * nx)
    mine = x * nz + z

    def shifted(i, by, n):
        return lax.rem(i + by, n)

    def device(zz, xx, cc, yy):
        return ((zz * nx + xx) * nc + cc, yy)

    y_peers = [(dy, shifted(y, dy, ny)) for dy in range(1, ny)]
    plane = [
        (shifted(x, dx, nx), shifted(z, dz, nz)) for dx in range(nx) for dz in range(nz) if (dx, dz) != (0, 0)
    ]
    cores = [shifted(c, dc, nc) for dc in range(1, nc)]
    up, down, across = shifted(y, 1, ny), shifted(y, ny - 1, ny), shifted(y, 2, ny)

    sent, settled = [], []
    counter = [0, 0]

    def send(src, dst, to):
        i = counter[0]
        counter[0] += 1
        copy = pltpu.make_async_remote_copy(
            src_ref=src, dst_ref=dst, send_sem=send_sem.at[i], recv_sem=recv_sem.at[i], device_id=to, device_id_type=MESH
        )
        copy.start()
        sent.append(copy)
        return copy

    def fetch(src, dst):
        i = counter[1]
        counter[1] += 1
        copy = pltpu.make_async_copy(src, dst, local_sem.at[i])
        copy.start()
        return copy

    def wait_all(copies):
        for copy in copies:
            copy.wait_recv()

    def settle(copies):
        for copy in copies:
            copy.wait_send()
        settled.extend(id(copy) for copy in copies)

    def tokens(yy):
        return pl.ds(pl.multiple_of(yy * tok, tok), tok)

    load_rt = fetch(rt_in, rt)
    load_vg = [fetch(vg.at[tokens(yy)], vg_v.at[i]) for i, yy in enumerate((y, up, across, down))]
    load_vgx = fetch(vg.at[tokens(y)], vgx.at[0, 0])
    load_act = [fetch(act.at[:, pl.ds(i * part, part)], actr.at[0, i]) for i in range(CHUNKS)]
    share = d // 4
    load_err = [fetch(err.at[pl.ds(i * share, share)], err_v.at[pl.ds(i * share, share)]) for i in range(4)]
    load_w = fetch(w.at[c], wbuf.at[:, :, :, 0])

    barrier = pltpu.get_barrier_semaphore()
    everyone = (
        [device(z, x, cc, y) for cc in cores]
        + [device(zz, xx, c, y) for xx, zz in plane]
        + [device(z, x, c, yy) for _, yy in y_peers]
    )
    for peer in everyone:
        pl.semaphore_signal(barrier, inc=1, device_id=peer, device_id_type=MESH)
    pl.semaphore_wait(barrier, len(everyone))

    from_down, from_up, from_across = {}, {}, {}

    def direct(*numbers):
        for i in numbers:
            j = (i + half) % CHUNKS
            for piece in (i, j):
                if piece in load_act:
                    load_act.pop(piece).wait()
            from_down[i] = send(actr.at[0, i], actr.at[3, i], device(z, x, c, up))
            from_up[j] = send(actr.at[0, j], actr.at[1, j], device(z, x, c, down))

    def forward(*numbers):
        for i in numbers:
            from_down[i].wait_recv()
            from_across[i] = send(actr.at[3, i], actr.at[2, i], device(z, x, c, up))
            j = i + half
            from_up[j].wait_recv()
            from_across[j] = send(actr.at[1, j], actr.at[2, j], device(z, x, c, down))

    load_act = dict(enumerate(load_act))

    load_rt.wait()
    rt3 = rows3(rt[...])
    for load in load_vg:
        load.wait()
    for dy in range(ny):
        uout[dy] = fold3(mm(rt3, vg_v[dy], NT))
    recv_u = [send(uout.at[dy], uin.at[dy - 1], device(z, x, c, yy)) for dy, yy in y_peers]

    recv_vg = [send(vg.at[tokens(up)], vgx.at[0, 3], device(z, x, c, up))]
    recv_vg.append(send(vg.at[tokens(down)], vgx.at[0, 1], device(z, x, c, down)))
    few = tok // 2
    ways = (up, down)
    vg_passing = [
        send(vg.at[pl.ds(pl.multiple_of(across * tok + h * few, few), few)], vstage.at[h], device(z, x, c, ways[h]))
        for h in range(2)
    ]
    direct(0)
    own_w = w.at[c, x, z]
    w_from_down = send(own_w, wbuf.at[x, z, :, 3], device(z, x, c, up))
    w_from_up = send(own_w, wbuf.at[x, z, :, 1], device(z, x, c, down))
    direct(1, 2)

    def place(h, a, b):
        return (a, b) if h == 0 else (b, a)

    def piece(h, first, second):
        zz, xx = place(h, first, second)
        return wbuf.at[xx, zz, h, 1:ny]

    def neighbour(h, stage, way):
        n = (nz if h == 0 else nx) if stage == 0 else (nx if h == 0 else nz)
        first, second = place(h, z, x)
        if stage == 0:
            first = shifted(first, way % n, n)
        else:
            second = shifted(second, way % n, n)
        zz, xx = place(h, first, second)
        return device(zz, xx, c, y)

    half_here = [(place(h, z, x), place(h, nz, nx)) for h in range(2)]
    stage_one, stage_one_across, stage_two, stage_two_across = {}, {}, {}, {}

    def weights_first():
        for h in range(2):
            (first, second), _ = half_here[h]
            own = piece(h, first, second)
            for way in (1, -1):
                stage_one[h, way] = send(own, own, neighbour(h, 0, way))

    def weights_across():
        for h in range(2):
            (first, second), (n, _) = half_here[h]
            way = 1 - 2 * h
            stage_one[h, way].wait_recv()
            came = piece(h, shifted(first, -way % n, n), second)
            stage_one_across[h] = send(came, came, neighbour(h, 0, way))

    def weights_second(i):
        for h in range(2):
            (first, second), (n, _) = half_here[h]
            if i in (1, 2):
                way = 3 - 2 * i
                if way != 1 - 2 * h:
                    stage_one[h, way].wait_recv()
                first = shifted(first, -way % n, n)
            elif i == 3:
                stage_one_across[h].wait_recv()
                first = shifted(first, 2, n)
            for way in (1, -1):
                stage_two[h, i, way] = send(piece(h, first, second), piece(h, first, second), neighbour(h, 1, way))

    def weights_second_across(i):
        for h in range(2):
            (first, second), (n, m) = half_here[h]
            first = shifted(first, (0, n - 1, 1, 2)[i], n)
            way = (1, -1, 1, -1)[i]
            stage_two[h, i, way].wait_recv()
            came = piece(h, first, shifted(second, -way % m, m))
            stage_two_across[h, i] = send(came, came, neighbour(h, 1, way))

    rt2 = rt3[: 2 * r]

    def columns(p):
        return pl.ds(pl.multiple_of(p * wide, wide), wide)

    def store_left(value, cc, j0):
        for j in range(wb):
            lacc[cc, j0 + j] = value[:, j * BLK : (j + 1) * BLK]

    def load_left(ref, cc, j0):
        return jnp.concatenate([ref[cc, j0 + j] for j in range(wb)], axis=1)

    for load in load_err:
        load.wait()

    def err_left(p, carry):
        hi, lo = split2(err_v[columns(p), :])
        store_left(fold2(mm(rt2, lo, NT) + mm(rt2, hi, NT)), lax.div(p, per_piece), lax.rem(p, per_piece) * wb)
        return carry

    lax.fori_loop(0, pieces, err_left, 0)

    wait_all(recv_u)
    ut = uout[0]
    for dy in range(ny - 1):
        ut = ut + uin[dy]
    ut3 = rows3(ut)
    for load in load_act.values():
        load.wait()
    load_act = {}

    def own_act(p):
        n = wide // part
        if n >= 1:
            return jnp.concatenate([actr[0, p * n + i] for i in range(n)], axis=1)
        n = part // wide
        inside = pl.ds(pl.multiple_of(lax.rem(p, n) * wide, wide), wide)
        return actr[0, lax.div(p, n), :, inside]

    def act_left(cc):
        def step(i, carry):
            value = fold3(mm(ut3, own_act(cc * per_piece + i)))
            store_left(load_left(lacc, cc, i * wb) + value, cc, i * wb)
            return carry

        lax.fori_loop(0, per_piece, step, 0)

    recv = []
    for cc in cores:
        act_left(cc)
        recv.append(send(lacc.at[cc], rc, device(z, x, cc, y)))
    act_left(c)

    recv_core = recv
    direct(3)
    load_vgx.wait()
    for h in range(2):
        vg_passing[h].wait_recv()
        recv_vg.append(send(vstage.at[h], vgx.at[0, 2, h * few : (h + 1) * few], device(z, x, c, ways[h])))
    wait_all(recv)
    lacc[c] += rc[...]
    recv = [
        send(lacc.at[c, xx * nz + zz], rxz.at[i], device(zz, xx, c, y)) for i, (xx, zz) in enumerate(plane)
    ]
    load_w.wait()
    w_from_down.wait_recv()
    w_halves = [send(wbuf.at[x, z, 0, 3], wbuf.at[x, z, 0, 2], device(z, x, c, up))]
    w_from_up.wait_recv()
    w_halves.append(send(wbuf.at[x, z, 1, 1], wbuf.at[x, z, 1, 2], device(z, x, c, down)))
    settle(recv_u + recv_core)
    recv_rs = recv
    wait_all(recv)
    total = lacc[c, mine]
    for i in range(len(plane)):
        total = total + rxz[i]
    ysum[y] = total
    own = ysum.at[y]
    recv = [send(own, own, device(z, x, c, yy)) for _, yy in y_peers]
    direct(*range(4, 12))
    wait_all(w_halves)
    weights_first()
    weights_second(0)
    settle(recv_rs)
    wait_all(recv)
    total = ysum[0]
    for yy in range(1, ny):
        total = total + ysum[yy]
    lf[c, mine] = total
    own = lf.at[c, mine]
    recv_y = recv
    recv = [send(own, own, device(zz, xx, c, y)) for xx, zz in plane]
    weights_across()
    weights_second(1)
    weights_second(2)
    settle(recv_y)
    wait_all(recv)
    recv_ag = recv
    own = lf.at[c]
    recv = [send(own, own, device(z, x, cc, y)) for cc in cores]
    weights_second(3)
    weights_second_across(0)
    settle(recv_ag)

    wait_all(recv_vg)
    recv_vgx = [send(vgx.at[0], vgx.at[dc], device(z, x, cc, y)) for dc, cc in enumerate(cores, 1)]
    settle(vg_passing + recv_vg + [w_from_down, w_from_up] + w_halves + list(stage_one.values()))
    wait_all(recv)

    def left_piece(p):
        return rows3(load_left(lf, lax.div(p, per_piece), lax.rem(p, per_piece) * wb))

    def products(p, carry):
        gram, by_act = carry
        block = left_piece(p)
        return gram + mm(block, block, NT), by_act + mm(block[: 2 * r], own_act(p), NT)

    gram, by_act = lax.fori_loop(
        0, pieces, products, (jnp.zeros((3 * r, 3 * r), F32), jnp.zeros((2 * r, tok), F32))
    )
    aout[...] = fold2(by_act)
    recv_a = [send(aout, ain.at[dy - 1], device(z, x, c, yy)) for dy, yy in y_peers]
    direct(*range(12, CHUNKS))
    forward(*range(half))
    weights_second_across(1)
    weights_second_across(2)

    total = jnp.zeros((2 * r, err_v.shape[1]), F32)
    count = nb // (r // 4)
    for i, state in enumerate(gram_schmidt(self_products(gram, r))):
        block = jnp.concatenate([lf[(i * count + j) // per, (i * count + j) % per] for j in range(count)], axis=1)
        hi, lo = split2(err_v[i * count * BLK : (i + 1) * count * BLK, :])
        block = rows2(block)
        total = total + (mm(block, lo) + mm(block, hi))
    total = fold2(total)
    weights, norms = unit_weights(state)

    def apply_first(p, gram):
        block = times(weights, load_left(lf, lax.div(p, per_piece), lax.rem(p, per_piece) * wb))
        q1[p] = block
        block = rows3(block)
        return gram + mm(block, block, NT)

    off = self_products(lax.fori_loop(0, pieces, apply_first, jnp.zeros((3 * r, 3 * r), F32)), r) - norms
    row_id = lax.broadcasted_iota(jnp.int32, (r, r), 0)
    col_id = lax.broadcasted_iota(jnp.int32, (r, r), 1)
    again = jnp.where(col_id < row_id, off, jnp.where(col_id == row_id, 0.5 * off, 0.0))
    weights = weights - times(again, weights)
    scale = math.sqrt(float(d))

    def apply_second(p, carry):
        block = q1[p]
        block = block - times(again, block)
        left_out[:, columns(p)] = block * scale
        return carry

    lax.fori_loop(0, pieces, apply_second, 0)


    wait_all(recv_a)
    for slot in range(ny):
        total = total + fold3(mm(rows3(aout[...] if slot == 0 else ain[ny - slot - 1]), vg_v[slot]))
    zsum[0] = total
    recv = [send(zsum.at[0], zsum.at[dc], device(z, x, cc, y)) for dc, cc in enumerate(cores, 1)]
    weights_second_across(3)

    for i in range(4):
        for h in range(2):
            stage_two[h, i, (-1, 1, -1, 1)[i]].wait_recv()
            stage_two_across[h, i].wait_recv()
    wait_all(recv_vgx)

    def input_grad(i, carry):
        total = None
        for slot in range(ny):
            weight = wbuf[lax.div(i, nz), lax.rem(i, nz), :, slot].reshape(BLK, BLK)
            part_sum = mm(vgx[:, slot].reshape(nc * tok, BLK), weight, NT).astype(BF16).astype(F32)
            total = part_sum if total is None else total + part_sum
        total = total.astype(BF16).reshape(nc, tok, BLK)
        gi[:, pl.ds(pl.multiple_of((c * per + i) * BLK, BLK), BLK)] = total[0]
        for dc in range(1, nc):
            outs[dc - 1, :, pl.ds(pl.multiple_of(i * BLK, BLK), BLK)] = total[dc]
        return carry

    lax.fori_loop(0, per, input_grad, 0)
    share_of = gi.at[:, pl.ds(pl.multiple_of(c * per * BLK, BLK), per * BLK)]
    sent_out = [send(outs.at[nc - 1 - dc], share_of, device(z, x, cc, y)) for dc, cc in enumerate(cores, 1)]

    wait_all(recv)
    for dc in range(1, nc):
        total = total + zsum[dc]
    tz[mine] = total
    own = tz.at[mine]
    recv = [send(own, own, device(zz, xx, c, y)) for xx, zz in plane]

    for i in range(CHUNKS):
        if i >= half:
            from_down[i].wait_recv()
        else:
            from_up[i].wait_recv()
    cotangent = vg_v[...].reshape(ny * tok, BLK).astype(F32).T.astype(BF16)

    def merge(j):
        from_across[j].wait_recv()
        at = pl.ds(j * part, part)
        merged[at, :] = err_v[at, :] + mm(cotangent, actr[:, j].reshape(ny * tok, part)).T

    for i in range(half - 2):
        merge(i)
        merge(i + half)

    wait_all(recv)
    total = tz[0]
    for i in range(1, per):
        total = total + tz[i]
    r_out[...] = times(weights, total) / float(nb)
    last = [id(from_across[i + h]) for i in range(half - 2, half) for h in (0, half)]
    settle([copy for copy in sent if id(copy) not in settled + last])

    for i in range(half - 2, half):
        merge(i)
        merge(i + half)

    wait_all(sent_out)
    settle([copy for copy in sent if id(copy) not in settled])
    assert counter == [send_sem.shape[0], local_sem.shape[0]], counter


def error_kernel(merged, left, right, gi, error_out, left_out, right_out, gi_out, error, sem):
    d = merged.shape[0]
    pieces = error.shape[0]
    rows = d // pieces
    copies = [
        pltpu.make_async_copy(a, b, sem.at[pieces + i])
        for i, (a, b) in enumerate([(gi, gi_out), (left, left_out), (right, right_out)])
    ]
    for copy in copies:
        copy.start()
    hi, lo = split2(right[...] / math.sqrt(float(d)))
    right3 = jnp.concatenate([hi, hi, lo], axis=0)
    for i in range(pieces):
        at = pl.ds(i * rows, rows)
        hi, lo = split2(left[:, at])
        error[i] = merged[at, :] - mm(jnp.concatenate([hi, lo, hi], axis=0), right3, TN)
        copies.append(pltpu.make_async_copy(error.at[i], error_out.at[at], sem.at[i]))
        copies[-1].start()
    for copy in copies:
        copy.wait()


def build(geom):
    nz, nx, nc, ny = geom

    def body(act, vg, w, err, right_prev):
        tok, d = act.shape
        kv = vg.shape[1]
        r = right_prev.shape[1]
        nb = nc * nx * nz
        per = nx * nz
        wide = min(WIDE, per * BLK)
        assert d == nb * BLK and kv == BLK and per * BLK % wide == 0
        sends = 3 * (ny - 1) + 6 + 4 + 3 * CHUNKS + 30 + 3 * (per - 1) + 5 * (nc - 1)
        pieces = w.reshape(nc, nx, nz, 2, BLK // 2, kv)
        inputs = [
            pltpu.with_memory_space_constraint(a, pltpu.HBM) for a in (act, vg, pieces, err[0], right_prev.T)
        ]
        hbm = pl.BlockSpec(memory_space=pltpu.HBM)
        vmem = pl.BlockSpec(memory_space=pltpu.VMEM)
        anywhere = pl.BlockSpec(memory_space=pl.ANY)
        results = (((d, kv), F32), ((r, d), F32), ((r, kv), F32), ((tok, d), BF16))
        made = pl.pallas_call(
            functools.partial(comm_kernel, geom),
            out_shape=tuple(pltpu.VMEM(*shape) for shape in results),
            in_specs=[hbm] * 5,
            out_specs=(vmem,) * 4,
            scratch_shapes=[
                pltpu.VMEM((r, kv), F32),
                pltpu.VMEM((ny, CHUNKS, tok, d // CHUNKS), BF16),
                pltpu.VMEM((ny, tok, kv), BF16),
                pltpu.VMEM((d, kv), F32),
                pltpu.VMEM((ny, r, tok), F32),
                pltpu.VMEM((ny - 1, r, tok), F32),
                pltpu.VMEM((2, tok // 2, kv), BF16),
                pltpu.VMEM((nc, ny, tok, kv), BF16),
                pltpu.VMEM((nx, nz, 2, ny, BLK // 2, kv), BF16),
                pltpu.VMEM((max(nc - 1, 1), tok, per * BLK), BF16),
                pltpu.VMEM((nc, per, r, BLK), F32),
                pltpu.VMEM((nc, per, r, BLK), F32),
                pltpu.VMEM((per, r, BLK), F32),
                pltpu.VMEM((per - 1, r, BLK), F32),
                pltpu.VMEM((ny, r, BLK), F32),
                pltpu.VMEM((d // wide, r, wide), F32),
                pltpu.VMEM((r, tok), F32),
                pltpu.VMEM((ny - 1, r, tok), F32),
                pltpu.VMEM((nc, r, kv), F32),
                pltpu.VMEM((per, r, kv), F32),
                pltpu.SemaphoreType.DMA((1 + 1 + 4 + CHUNKS + ny + 1,)),
                pltpu.SemaphoreType.DMA((sends,)),
                pltpu.SemaphoreType.DMA((sends,)),
            ],
            compiler_params=pltpu.CompilerParams(
                collective_id=0, has_side_effects=True, vmem_limit_bytes=44 * MIB
            ),
        )(*inputs)

        pieces = 16
        error_next, left, right, grad_input = pl.pallas_call(
            error_kernel,
            out_shape=tuple(jax.ShapeDtypeStruct(*shape) for shape in results),
            in_specs=[vmem] * 4,
            out_specs=(anywhere,) * 4,
            scratch_shapes=[pltpu.VMEM((pieces, d // pieces, kv), F32), pltpu.SemaphoreType.DMA((pieces + 3,))],
            compiler_params=pltpu.CompilerParams(vmem_limit_bytes=24 * MIB),
        )(*made)
        return (grad_input, error_next[None], left.T, right.T)

    return body


def solution(mesh):
    return jax.shard_map(
        build((4, 4, 2, 4)),
        mesh=mesh,
        in_specs=(
            P(("dp", "tp"), None),
            P("dp", "tp"),
            P(None, "tp"),
            P("dp", None, "tp"),
            P("tp", None),
        ),
        out_specs=(P(("dp", "tp"), None), P("dp", None, "tp"), P(), P("tp", None)),
        check_vma=False,
    )
```

```python
import functools
import math

import jax
import jax.numpy as jnp
from jax import lax
from jax.experimental import pallas as pl
from jax.experimental.pallas import tpu as pltpu
from jax.sharding import PartitionSpec as P

MESH = pl.DeviceIdType.MESH
F32 = jnp.float32
BF16 = jnp.bfloat16
BLK = 256
EPS = 1e-12
MIB = 1024 * 1024
WIDE = 8 * BLK
CHUNKS = 16
NN = (((1,), (0,)), ((), ()))
NT = (((1,), (1,)), ((), ()))
TN = (((0,), (0,)), ((), ()))


def mm(a, b, dims=NN):
    return lax.dot_general(a, b, dims, preferred_element_type=F32)


def split2(a):
    hi = a.astype(BF16)
    lo = (a - hi.astype(F32)).astype(BF16)
    return hi, lo


def split3(a):
    hi = a.astype(BF16)
    rest = a - hi.astype(F32)
    mid = rest.astype(BF16)
    lo = (rest - mid.astype(F32)).astype(BF16)
    return hi, mid, lo


def rows3(a):
    return jnp.concatenate(split3(a), axis=0)


def fold3(a):
    n = a.shape[0] // 3
    return (a[2 * n :] + a[n : 2 * n]) + a[:n]


def rows2(a):
    return jnp.concatenate(split2(a), axis=0)


def fold2(a):
    n = a.shape[0] // 2
    return a[n:] + a[:n]


def self_products(total, r):
    total = fold3(total)
    return (total[:, 2 * r :] + total[:, r : 2 * r]) + total[:, :r]


def times(a, b):
    a_hi, a_mid, a_lo = (v.astype(F32) for v in split3(a))
    b_hi, b_mid, b_lo = split3(b)
    left = jnp.concatenate([a_lo, a_mid, a_hi, a_mid, a_hi, a_hi], axis=1).astype(BF16)
    return mm(left, jnp.concatenate([b_hi, b_mid, b_lo, b_hi, b_mid, b_hi], axis=0))


def eye_like(n):
    return (lax.broadcasted_iota(jnp.int32, (n, n), 0) == lax.broadcasted_iota(jnp.int32, (n, n), 1)).astype(F32)


def gram_schmidt(gram):
    n = gram.shape[0]
    left, weights = gram, eye_like(n)
    row_id = lax.broadcasted_iota(jnp.int32, (n, 1), 0)
    m = 4
    for j in range(0, n, m):
        columns = [jnp.broadcast_to(left[:, i : i + 1], (n, n)) for i in range(j, j + m)]
        rows = [left[i : i + 1, :] for i in range(j, j + m)]
        given = [weights[i : i + 1, :] for i in range(j, j + m)]
        off_left, off_weights = jnp.zeros((n, n), F32), jnp.zeros((n, n), F32)
        for i in range(m):
            at = j + i
            s = jnp.maximum(columns[i][at : at + 1, :], 0.0)
            inverse = 1.0 / (s + EPS)
            c = (2.0 - s * inverse) * inverse
            f = jnp.where(row_id > at, columns[i] * c, 0.0)
            h = f * (2.0 - c * s)
            for later in range(i + 1, m):
                to = j + later
                columns[later] = columns[later] - h * columns[later][at : at + 1, :]
                rows[later] = rows[later] - h[to : to + 1, :] * rows[i]
                given[later] = given[later] - f[to : to + 1, :] * given[i]
            off_left = off_left + h * rows[i]
            off_weights = off_weights + f * given[i]
        left, weights = left - off_left, weights - off_weights
        yield left, weights


def unit_weights(state):
    left, weights = state
    eye = eye_like(left.shape[0])
    s = jnp.maximum(jnp.sum(left * eye, axis=1, keepdims=True), 0.0)
    return weights / jnp.sqrt(s + EPS), eye * (s / (s + EPS))


def comm_kernel(
    geom, act, vg, w, err, rt_in, merged, left_out, r_out, gi,
    rt, actr, vg_v, err_v, uout, uin, vstage, vgx, wbuf, outs, lacc, lf, rc, rxz, ysum, q1, aout, ain, zsum, tz,
    local_sem, send_sem, recv_sem,
):
    nz, nx, nc, ny = geom
    nb = nc * nx * nz
    per = nx * nz
    _, _, tok, part = actr.shape
    d = part * CHUNKS
    half = CHUNKS // 2
    r = rt.shape[0]
    wide = min(WIDE, per * BLK)
    wb = wide // BLK
    pieces = d // wide
    per_piece = per // wb
    dp, y = lax.axis_index("dp"), lax.axis_index("tp")
    c = lax.rem(dp, nc)
    x = lax.rem(lax.div(dp, nc), nx)
    z = lax.div(dp, nc * nx)
    mine = x * nz + z

    def shifted(i, by, n):
        return lax.rem(i + by, n)

    def device(zz, xx, cc, yy):
        return ((zz * nx + xx) * nc + cc, yy)

    y_peers = [(dy, shifted(y, dy, ny)) for dy in range(1, ny)]
    plane = [
        (shifted(x, dx, nx), shifted(z, dz, nz)) for dx in range(nx) for dz in range(nz) if (dx, dz) != (0, 0)
    ]
    cores = [shifted(c, dc, nc) for dc in range(1, nc)]
    up, down, across = shifted(y, 1, ny), shifted(y, ny - 1, ny), shifted(y, 2, ny)

    sent, settled = [], []
    counter = [0, 0]

    def send(src, dst, to):
        i = counter[0]
        counter[0] += 1
        copy = pltpu.make_async_remote_copy(
            src_ref=src, dst_ref=dst, send_sem=send_sem.at[i], recv_sem=recv_sem.at[i], device_id=to, device_id_type=MESH
        )
        copy.start()
        sent.append(copy)
        return copy

    def fetch(src, dst):
        i = counter[1]
        counter[1] += 1
        copy = pltpu.make_async_copy(src, dst, local_sem.at[i])
        copy.start()
        return copy

    def wait_all(copies):
        for copy in copies:
            copy.wait_recv()

    def settle(copies):
        for copy in copies:
            copy.wait_send()
        settled.extend(id(copy) for copy in copies)

    def tokens(yy):
        return pl.ds(pl.multiple_of(yy * tok, tok), tok)

    barrier = pltpu.get_barrier_semaphore()
    everyone = (
        [device(z, x, cc, y) for cc in cores]
        + [device(zz, xx, c, y) for xx, zz in plane]
        + [device(z, x, c, yy) for _, yy in y_peers]
    )
    for peer in everyone:
        pl.semaphore_signal(barrier, inc=1, device_id=peer, device_id_type=MESH)

    load_rt = fetch(rt_in, rt)
    load_vg = [fetch(vg.at[tokens(yy)], vg_v.at[i]) for i, yy in enumerate((y, up, across, down))]
    share = d // 4
    load_err = [fetch(err.at[pl.ds(i * share, share)], err_v.at[pl.ds(i * share, share)]) for i in range(4)]
    pl.semaphore_wait(barrier, len(everyone))

    from_down, from_up, from_across = {}, {}, {}

    def cols(i):
        return pl.ds(i * part, part)

    def direct(*numbers):
        for i in numbers:
            j = (i + half) % CHUNKS
            from_down[i] = send(act.at[:, cols(i)], actr.at[3, i], device(z, x, c, up))
            from_up[j] = send(act.at[:, cols(j)], actr.at[1, j], device(z, x, c, down))

    def forward(*numbers):
        for i in numbers:
            from_down[i].wait_recv()
            from_across[i] = send(actr.at[3, i], actr.at[2, i], device(z, x, c, up))
            j = i + half
            from_up[j].wait_recv()
            from_across[j] = send(actr.at[1, j], actr.at[2, j], device(z, x, c, down))


    recv_vg = [send(vg.at[tokens(up)], vgx.at[0, 3], device(z, x, c, up))]
    recv_vg.append(send(vg.at[tokens(down)], vgx.at[0, 1], device(z, x, c, down)))
    few = tok // 2
    ways = (up, down)
    vg_passing = [
        send(vg.at[pl.ds(pl.multiple_of(across * tok + h * few, few), few)], vstage.at[h], device(z, x, c, ways[h]))
        for h in range(2)
    ]
    direct(0)
    load_act = {
        i: fetch(act.at[:, cols(i)], actr.at[0, i]) for j in range(half) for i in (j, j + half)
    }
    load_vgx = fetch(vg.at[tokens(y)], vgx.at[0, 0])
    load_w = fetch(w.at[c], wbuf.at[:, :, :, 0])

    load_rt.wait()
    rt3 = rows3(rt[...])
    for load in load_vg:
        load.wait()
    for dy in range(ny):
        uout[dy] = fold3(mm(rt3, vg_v[dy], NT))
    recv_u = [send(uout.at[dy], uin.at[dy - 1], device(z, x, c, yy)) for dy, yy in y_peers]

    own_w = w.at[c, x, z]
    w_from_down = send(own_w, wbuf.at[x, z, :, 3], device(z, x, c, up))
    w_from_up = send(own_w, wbuf.at[x, z, :, 1], device(z, x, c, down))
    direct(1, 2)

    def place(h, a, b):
        return (a, b) if h == 0 else (b, a)

    def piece(h, first, second):
        zz, xx = place(h, first, second)
        return wbuf.at[xx, zz, h, 1:ny]

    def neighbour(h, stage, way):
        n = (nz if h == 0 else nx) if stage == 0 else (nx if h == 0 else nz)
        first, second = place(h, z, x)
        if stage == 0:
            first = shifted(first, way % n, n)
        else:
            second = shifted(second, way % n, n)
        zz, xx = place(h, first, second)
        return device(zz, xx, c, y)

    half_here = [(place(h, z, x), place(h, nz, nx)) for h in range(2)]
    stage_one, stage_one_across, stage_two, stage_two_across = {}, {}, {}, {}

    def weights_first():
        for h in range(2):
            (first, second), _ = half_here[h]
            own = piece(h, first, second)
            for way in (1, -1):
                stage_one[h, way] = send(own, own, neighbour(h, 0, way))

    def weights_across():
        for h in range(2):
            (first, second), (n, _) = half_here[h]
            way = 1 - 2 * h
            stage_one[h, way].wait_recv()
            came = piece(h, shifted(first, -way % n, n), second)
            stage_one_across[h] = send(came, came, neighbour(h, 0, way))

    def weights_second(i):
        for h in range(2):
            (first, second), (n, _) = half_here[h]
            if i in (1, 2):
                way = 3 - 2 * i
                if way != 1 - 2 * h:
                    stage_one[h, way].wait_recv()
                first = shifted(first, -way % n, n)
            elif i == 3:
                stage_one_across[h].wait_recv()
                first = shifted(first, 2, n)
            for way in (1, -1):
                stage_two[h, i, way] = send(piece(h, first, second), piece(h, first, second), neighbour(h, 1, way))

    def weights_second_across(i):
        for h in range(2):
            (first, second), (n, m) = half_here[h]
            first = shifted(first, (0, n - 1, 1, 2)[i], n)
            way = (1, -1, 1, -1)[i]
            stage_two[h, i, way].wait_recv()
            came = piece(h, first, shifted(second, -way % m, m))
            stage_two_across[h, i] = send(came, came, neighbour(h, 1, way))

    rt2 = rt3[: 2 * r]

    def columns(p):
        return pl.ds(pl.multiple_of(p * wide, wide), wide)

    def store_left(value, cc, j0):
        for j in range(wb):
            lacc[cc, j0 + j] = value[:, j * BLK : (j + 1) * BLK]

    def load_left(ref, cc, j0):
        return jnp.concatenate([ref[cc, j0 + j] for j in range(wb)], axis=1)

    for load in load_err:
        load.wait()

    def err_left(p, carry):
        hi, lo = split2(err_v[columns(p), :])
        store_left(fold2(mm(rt2, lo, NT) + mm(rt2, hi, NT)), lax.div(p, per_piece), lax.rem(p, per_piece) * wb)
        return carry

    lax.fori_loop(0, pieces, err_left, 0)

    wait_all(recv_u)
    ut = uout[0]
    for dy in range(ny - 1):
        ut = ut + uin[dy]
    ut3 = rows3(ut)
    for load in load_act.values():
        load.wait()

    def own_act(p):
        n = wide // part
        if n >= 1:
            return jnp.concatenate([actr[0, p * n + i] for i in range(n)], axis=1)
        n = part // wide
        inside = pl.ds(pl.multiple_of(lax.rem(p, n) * wide, wide), wide)
        return actr[0, lax.div(p, n), :, inside]

    def act_left(cc):
        def step(i, carry):
            value = fold3(mm(ut3, own_act(cc * per_piece + i)))
            store_left(load_left(lacc, cc, i * wb) + value, cc, i * wb)
            return carry

        lax.fori_loop(0, per_piece, step, 0)

    recv = []
    for cc in cores:
        act_left(cc)
        recv.append(send(lacc.at[cc], rc, device(z, x, cc, y)))
    act_left(c)

    recv_core = recv
    direct(3)
    load_vgx.wait()
    for h in range(2):
        vg_passing[h].wait_recv()
        recv_vg.append(send(vstage.at[h], vgx.at[0, 2, h * few : (h + 1) * few], device(z, x, c, ways[h])))
    wait_all(recv)
    lacc[c] += rc[...]
    recv = [
        send(lacc.at[c, xx * nz + zz], rxz.at[i], device(zz, xx, c, y)) for i, (xx, zz) in enumerate(plane)
    ]
    load_w.wait()
    w_from_down.wait_recv()
    w_halves = [send(wbuf.at[x, z, 0, 3], wbuf.at[x, z, 0, 2], device(z, x, c, up))]
    w_from_up.wait_recv()
    w_halves.append(send(wbuf.at[x, z, 1, 1], wbuf.at[x, z, 1, 2], device(z, x, c, down)))
    direct(4)
    settle(recv_u + recv_core)
    recv_rs = recv
    wait_all(recv)
    total = lacc[c, mine]
    for i in range(len(plane)):
        total = total + rxz[i]
    ysum[y] = total
    own = ysum.at[y]
    recv = [send(own, own, device(z, x, c, yy)) for _, yy in y_peers]
    direct(*range(5, 12))
    wait_all(w_halves)
    weights_first()
    weights_second(0)
    settle(recv_rs)
    wait_all(recv)
    total = ysum[0]
    for yy in range(1, ny):
        total = total + ysum[yy]
    lf[c, mine] = total
    own = lf.at[c, mine]
    recv_y = recv
    recv = [send(own, own, device(zz, xx, c, y)) for xx, zz in plane]
    weights_across()
    weights_second(1)
    weights_second(2)
    settle(recv_y)
    wait_all(recv)
    recv_ag = recv
    own = lf.at[c]
    recv = [send(own, own, device(z, x, cc, y)) for cc in cores]
    weights_second(3)
    weights_second_across(0)
    settle(recv_ag)

    wait_all(recv_vg)
    recv_vgx = [send(vgx.at[0], vgx.at[dc], device(z, x, cc, y)) for dc, cc in enumerate(cores, 1)]
    settle(vg_passing + recv_vg + [w_from_down, w_from_up] + w_halves + list(stage_one.values()))
    wait_all(recv)

    def left_piece(p):
        return rows3(load_left(lf, lax.div(p, per_piece), lax.rem(p, per_piece) * wb))

    def products(p, carry):
        gram, by_act = carry
        block = left_piece(p)
        return gram + mm(block, block, NT), by_act + mm(block[: 2 * r], own_act(p), NT)

    gram, by_act = lax.fori_loop(
        0, pieces, products, (jnp.zeros((3 * r, 3 * r), F32), jnp.zeros((2 * r, tok), F32))
    )
    aout[...] = fold2(by_act)
    recv_a = [send(aout, ain.at[dy - 1], device(z, x, c, yy)) for dy, yy in y_peers]
    direct(*range(12, CHUNKS))
    forward(*range(half))
    weights_second_across(1)
    weights_second_across(2)

    total = jnp.zeros((2 * r, err_v.shape[1]), F32)
    count = nb // (r // 4)
    for i, state in enumerate(gram_schmidt(self_products(gram, r))):
        block = jnp.concatenate([lf[(i * count + j) // per, (i * count + j) % per] for j in range(count)], axis=1)
        hi, lo = split2(err_v[i * count * BLK : (i + 1) * count * BLK, :])
        block = rows2(block)
        total = total + (mm(block, lo) + mm(block, hi))
    total = fold2(total)
    weights, norms = unit_weights(state)

    def apply_first(p, gram):
        block = times(weights, load_left(lf, lax.div(p, per_piece), lax.rem(p, per_piece) * wb))
        q1[p] = block
        block = rows3(block)
        return gram + mm(block, block, NT)

    off = self_products(lax.fori_loop(0, pieces, apply_first, jnp.zeros((3 * r, 3 * r), F32)), r) - norms
    row_id = lax.broadcasted_iota(jnp.int32, (r, r), 0)
    col_id = lax.broadcasted_iota(jnp.int32, (r, r), 1)
    again = jnp.where(col_id < row_id, off, jnp.where(col_id == row_id, 0.5 * off, 0.0))
    weights = weights - times(again, weights)
    scale = math.sqrt(float(d))

    def apply_second(p, carry):
        block = q1[p]
        block = block - times(again, block)
        left_out[:, columns(p)] = block * scale
        return carry

    lax.fori_loop(0, pieces, apply_second, 0)


    wait_all(recv_a)
    for slot in range(ny):
        total = total + fold3(mm(rows3(aout[...] if slot == 0 else ain[ny - slot - 1]), vg_v[slot]))
    zsum[0] = total
    recv = [send(zsum.at[0], zsum.at[dc], device(z, x, cc, y)) for dc, cc in enumerate(cores, 1)]
    weights_second_across(3)

    for i in range(4):
        for h in range(2):
            stage_two[h, i, (-1, 1, -1, 1)[i]].wait_recv()
            stage_two_across[h, i].wait_recv()
    wait_all(recv_vgx)

    def input_grad(i, carry):
        total = None
        for slot in range(ny):
            weight = wbuf[lax.div(i, nz), lax.rem(i, nz), :, slot].reshape(BLK, BLK)
            part_sum = mm(vgx[:, slot].reshape(nc * tok, BLK), weight, NT).astype(BF16).astype(F32)
            total = part_sum if total is None else total + part_sum
        total = total.astype(BF16).reshape(nc, tok, BLK)
        gi[:, pl.ds(pl.multiple_of((c * per + i) * BLK, BLK), BLK)] = total[0]
        for dc in range(1, nc):
            outs[dc - 1, :, pl.ds(pl.multiple_of(i * BLK, BLK), BLK)] = total[dc]
        return carry

    lax.fori_loop(0, per, input_grad, 0)
    share_of = gi.at[:, pl.ds(pl.multiple_of(c * per * BLK, BLK), per * BLK)]
    sent_out = [send(outs.at[nc - 1 - dc], share_of, device(z, x, cc, y)) for dc, cc in enumerate(cores, 1)]

    wait_all(recv)
    for dc in range(1, nc):
        total = total + zsum[dc]
    tz[mine] = total
    own = tz.at[mine]
    recv = [send(own, own, device(zz, xx, c, y)) for xx, zz in plane]

    for i in range(CHUNKS):
        if i >= half:
            from_down[i].wait_recv()
        else:
            from_up[i].wait_recv()
    cotangent = vg_v[...].reshape(ny * tok, BLK).astype(F32).T.astype(BF16)

    def merge(j):
        from_across[j].wait_recv()
        at = pl.ds(j * part, part)
        merged[at, :] = err_v[at, :] + mm(cotangent, actr[:, j].reshape(ny * tok, part)).T

    for i in range(half - 2):
        merge(i)
        merge(i + half)

    wait_all(recv)
    total = tz[0]
    for i in range(1, per):
        total = total + tz[i]
    r_out[...] = times(weights, total) / float(nb)
    last = [id(from_across[i + h]) for i in range(half - 2, half) for h in (0, half)]
    settle([copy for copy in sent if id(copy) not in settled + last])

    for i in range(half - 2, half):
        merge(i)
        merge(i + half)

    wait_all(sent_out)
    settle([copy for copy in sent if id(copy) not in settled])
    assert counter == [send_sem.shape[0], local_sem.shape[0]], counter


def error_kernel(merged, left, right, gi, error_out, left_out, right_out, gi_out, error, sem):
    d = merged.shape[0]
    pieces = error.shape[0]
    rows = d // pieces
    copies = [
        pltpu.make_async_copy(a, b, sem.at[pieces + i])
        for i, (a, b) in enumerate([(gi, gi_out), (left, left_out), (right, right_out)])
    ]
    for copy in copies:
        copy.start()
    hi, lo = split2(right[...] / math.sqrt(float(d)))
    right3 = jnp.concatenate([hi, hi, lo], axis=0)
    for i in range(pieces):
        at = pl.ds(i * rows, rows)
        hi, lo = split2(left[:, at])
        error[i] = merged[at, :] - mm(jnp.concatenate([hi, lo, hi], axis=0), right3, TN)
        copies.append(pltpu.make_async_copy(error.at[i], error_out.at[at], sem.at[i]))
        copies[-1].start()
    for copy in copies:
        copy.wait()


def build(geom):
    nz, nx, nc, ny = geom

    def body(act, vg, w, err, right_prev):
        tok, d = act.shape
        kv = vg.shape[1]
        r = right_prev.shape[1]
        nb = nc * nx * nz
        per = nx * nz
        wide = min(WIDE, per * BLK)
        assert d == nb * BLK and kv == BLK and per * BLK % wide == 0
        sends = 3 * (ny - 1) + 6 + 4 + 3 * CHUNKS + 30 + 3 * (per - 1) + 5 * (nc - 1)
        pieces = w.reshape(nc, nx, nz, 2, BLK // 2, kv)
        inputs = [
            pltpu.with_memory_space_constraint(a, pltpu.HBM) for a in (act, vg, pieces, err[0], right_prev.T)
        ]
        hbm = pl.BlockSpec(memory_space=pltpu.HBM)
        vmem = pl.BlockSpec(memory_space=pltpu.VMEM)
        anywhere = pl.BlockSpec(memory_space=pl.ANY)
        results = (((d, kv), F32), ((r, d), F32), ((r, kv), F32), ((tok, d), BF16))
        made = pl.pallas_call(
            functools.partial(comm_kernel, geom),
            out_shape=tuple(pltpu.VMEM(*shape) for shape in results),
            in_specs=[hbm] * 5,
            out_specs=(vmem,) * 4,
            scratch_shapes=[
                pltpu.VMEM((r, kv), F32),
                pltpu.VMEM((ny, CHUNKS, tok, d // CHUNKS), BF16),
                pltpu.VMEM((ny, tok, kv), BF16),
                pltpu.VMEM((d, kv), F32),
                pltpu.VMEM((ny, r, tok), F32),
                pltpu.VMEM((ny - 1, r, tok), F32),
                pltpu.VMEM((2, tok // 2, kv), BF16),
                pltpu.VMEM((nc, ny, tok, kv), BF16),
                pltpu.VMEM((nx, nz, 2, ny, BLK // 2, kv), BF16),
                pltpu.VMEM((max(nc - 1, 1), tok, per * BLK), BF16),
                pltpu.VMEM((nc, per, r, BLK), F32),
                pltpu.VMEM((nc, per, r, BLK), F32),
                pltpu.VMEM((per, r, BLK), F32),
                pltpu.VMEM((per - 1, r, BLK), F32),
                pltpu.VMEM((ny, r, BLK), F32),
                pltpu.VMEM((d // wide, r, wide), F32),
                pltpu.VMEM((r, tok), F32),
                pltpu.VMEM((ny - 1, r, tok), F32),
                pltpu.VMEM((nc, r, kv), F32),
                pltpu.VMEM((per, r, kv), F32),
                pltpu.SemaphoreType.DMA((1 + 1 + 4 + CHUNKS + ny + 1,)),
                pltpu.SemaphoreType.DMA((sends,)),
                pltpu.SemaphoreType.DMA((sends,)),
            ],
            compiler_params=pltpu.CompilerParams(
                collective_id=0, has_side_effects=True, vmem_limit_bytes=44 * MIB
            ),
        )(*inputs)

        pieces = 16
        error_next, left, right, grad_input = pl.pallas_call(
            error_kernel,
            out_shape=tuple(jax.ShapeDtypeStruct(*shape) for shape in results),
            in_specs=[vmem] * 4,
            out_specs=(anywhere,) * 4,
            scratch_shapes=[pltpu.VMEM((pieces, d // pieces, kv), F32), pltpu.SemaphoreType.DMA((pieces + 3,))],
            compiler_params=pltpu.CompilerParams(vmem_limit_bytes=24 * MIB),
        )(*made)
        return (grad_input, error_next[None], left.T, right.T)

    return body


def solution(mesh):
    return jax.shard_map(
        build((4, 4, 2, 4)),
        mesh=mesh,
        in_specs=(
            P(("dp", "tp"), None),
            P("dp", "tp"),
            P(None, "tp"),
            P("dp", None, "tp"),
            P("tp", None),
        ),
        out_specs=(P(("dp", "tp"), None), P("dp", None, "tp"), P(), P("tp", None)),
        check_vma=False,
    )
```

```python
import functools
import math

import jax
import jax.numpy as jnp
from jax import lax
from jax.experimental import pallas as pl
from jax.experimental.pallas import tpu as pltpu
from jax.sharding import PartitionSpec as P

MESH = pl.DeviceIdType.MESH
F32 = jnp.float32
BF16 = jnp.bfloat16
BLK = 256
EPS = 1e-12
MIB = 1024 * 1024
WIDE = 8 * BLK
CHUNKS = 16
NN = (((1,), (0,)), ((), ()))
NT = (((1,), (1,)), ((), ()))
TN = (((0,), (0,)), ((), ()))


def mm(a, b, dims=NN):
    return lax.dot_general(a, b, dims, preferred_element_type=F32)


def split2(a):
    hi = a.astype(BF16)
    lo = (a - hi.astype(F32)).astype(BF16)
    return hi, lo


def split3(a):
    hi = a.astype(BF16)
    rest = a - hi.astype(F32)
    mid = rest.astype(BF16)
    lo = (rest - mid.astype(F32)).astype(BF16)
    return hi, mid, lo


def rows3(a):
    return jnp.concatenate(split3(a), axis=0)


def fold3(a):
    n = a.shape[0] // 3
    return (a[2 * n :] + a[n : 2 * n]) + a[:n]


def rows2(a):
    return jnp.concatenate(split2(a), axis=0)


def fold2(a):
    n = a.shape[0] // 2
    return a[n:] + a[:n]


def self_products(total, r):
    total = fold3(total)
    return (total[:, 2 * r :] + total[:, r : 2 * r]) + total[:, :r]


def times(a, b):
    a_hi, a_mid, a_lo = (v.astype(F32) for v in split3(a))
    b_hi, b_mid, b_lo = split3(b)
    left = jnp.concatenate([a_lo, a_mid, a_hi, a_mid, a_hi, a_hi], axis=1).astype(BF16)
    return mm(left, jnp.concatenate([b_hi, b_mid, b_lo, b_hi, b_mid, b_hi], axis=0))


def eye_like(n):
    return (lax.broadcasted_iota(jnp.int32, (n, n), 0) == lax.broadcasted_iota(jnp.int32, (n, n), 1)).astype(F32)


def gram_schmidt(gram):
    n = gram.shape[0]
    left, weights = gram, eye_like(n)
    row_id = lax.broadcasted_iota(jnp.int32, (n, 1), 0)
    m = 4
    for j in range(0, n, m):
        columns = [jnp.broadcast_to(left[:, i : i + 1], (n, n)) for i in range(j, j + m)]
        rows = [left[i : i + 1, :] for i in range(j, j + m)]
        given = [weights[i : i + 1, :] for i in range(j, j + m)]
        off_left, off_weights = jnp.zeros((n, n), F32), jnp.zeros((n, n), F32)
        for i in range(m):
            at = j + i
            s = jnp.maximum(columns[i][at : at + 1, :], 0.0)
            inverse = 1.0 / (s + EPS)
            c = (2.0 - s * inverse) * inverse
            f = jnp.where(row_id > at, columns[i] * c, 0.0)
            h = f * (2.0 - c * s)
            for later in range(i + 1, m):
                to = j + later
                columns[later] = columns[later] - h * columns[later][at : at + 1, :]
                rows[later] = rows[later] - h[to : to + 1, :] * rows[i]
                given[later] = given[later] - f[to : to + 1, :] * given[i]
            off_left = off_left + h * rows[i]
            off_weights = off_weights + f * given[i]
        left, weights = left - off_left, weights - off_weights
        yield left, weights


def unit_weights(state):
    left, weights = state
    eye = eye_like(left.shape[0])
    s = jnp.maximum(jnp.sum(left * eye, axis=1, keepdims=True), 0.0)
    return weights / jnp.sqrt(s + EPS), eye * (s / (s + EPS))


def comm_kernel(
    geom, act, vg, w, err, rt_in, merged, left_out, r_out, gi,
    rt, actr, vg_v, err_v, uout, uin, vstage, vgx, wbuf, outs, lacc, lf, rc, rxz, ysum, q1, aout, ain, zsum, tz,
    local_sem, send_sem, recv_sem,
):
    nz, nx, nc, ny = geom
    nb = nc * nx * nz
    per = nx * nz
    _, _, tok, part = actr.shape
    d = part * CHUNKS
    half = CHUNKS // 2
    r = rt.shape[0]
    wide = min(WIDE, per * BLK)
    wb = wide // BLK
    pieces = d // wide
    per_piece = per // wb
    dp, y = lax.axis_index("dp"), lax.axis_index("tp")
    c = lax.rem(dp, nc)
    x = lax.rem(lax.div(dp, nc), nx)
    z = lax.div(dp, nc * nx)
    mine = x * nz + z

    def shifted(i, by, n):
        return lax.rem(i + by, n)

    def device(zz, xx, cc, yy):
        return ((zz * nx + xx) * nc + cc, yy)

    y_peers = [(dy, shifted(y, dy, ny)) for dy in range(1, ny)]
    plane = [
        (shifted(x, dx, nx), shifted(z, dz, nz)) for dx in range(nx) for dz in range(nz) if (dx, dz) != (0, 0)
    ]
    cores = [shifted(c, dc, nc) for dc in range(1, nc)]
    up, down, across = shifted(y, 1, ny), shifted(y, ny - 1, ny), shifted(y, 2, ny)

    sent, settled = [], []
    counter = [0, 0]

    def describe(src, dst, to):
        i = counter[0]
        counter[0] += 1
        copy = pltpu.make_async_remote_copy(
            src_ref=src, dst_ref=dst, send_sem=send_sem.at[i], recv_sem=recv_sem.at[i], device_id=to, device_id_type=MESH
        )
        sent.append(copy)
        return copy

    def send(src, dst, to):
        copy = describe(src, dst, to)
        copy.start()
        return copy

    def send_both(one, other):
        one, other = describe(*one), describe(*other)

        @pl.when(c == 0)
        def _():
            one.start()
            other.start()

        @pl.when(c != 0)
        def _():
            other.start()
            one.start()

        return one, other

    def fetch(src, dst):
        i = counter[1]
        counter[1] += 1
        copy = pltpu.make_async_copy(src, dst, local_sem.at[i])
        copy.start()
        return copy

    def wait_all(copies):
        for copy in copies:
            copy.wait_recv()

    def settle(copies):
        for copy in copies:
            copy.wait_send()
        settled.extend(id(copy) for copy in copies)

    def tokens(yy):
        return pl.ds(pl.multiple_of(yy * tok, tok), tok)

    barrier = pltpu.get_barrier_semaphore()
    everyone = (
        [device(z, x, cc, y) for cc in cores]
        + [device(zz, xx, c, y) for xx, zz in plane]
        + [device(z, x, c, yy) for _, yy in y_peers]
    )
    for peer in everyone:
        pl.semaphore_signal(barrier, inc=1, device_id=peer, device_id_type=MESH)

    load_rt = fetch(rt_in, rt)
    load_vg = [fetch(vg.at[tokens(yy)], vg_v.at[i]) for i, yy in enumerate((y, up, across, down))]
    share = d // 4
    load_err = [fetch(err.at[pl.ds(i * share, share)], err_v.at[pl.ds(i * share, share)]) for i in range(4)]
    pl.semaphore_wait(barrier, len(everyone))

    from_down, from_up, from_across = {}, {}, {}

    def cols(i):
        return pl.ds(i * part, part)

    def direct(*numbers):
        for i in numbers:
            j = (i + half) % CHUNKS
            from_down[i], from_up[j] = send_both(
                (act.at[:, cols(i)], actr.at[3, i], device(z, x, c, up)),
                (act.at[:, cols(j)], actr.at[1, j], device(z, x, c, down)),
            )

    def forward(*numbers):
        for i in numbers:
            j = i + half
            from_down[i].wait_recv()
            from_up[j].wait_recv()
            from_across[i], from_across[j] = send_both(
                (actr.at[3, i], actr.at[2, i], device(z, x, c, up)),
                (actr.at[1, j], actr.at[2, j], device(z, x, c, down)),
            )


    recv_vg = [send(vg.at[tokens(up)], vgx.at[0, 3], device(z, x, c, up))]
    recv_vg.append(send(vg.at[tokens(down)], vgx.at[0, 1], device(z, x, c, down)))
    few = tok // 2
    ways = (up, down)
    vg_passing = [
        send(vg.at[pl.ds(pl.multiple_of(across * tok + h * few, few), few)], vstage.at[h], device(z, x, c, ways[h]))
        for h in range(2)
    ]
    direct(0)
    load_act = {
        i: fetch(act.at[:, cols(i)], actr.at[0, i]) for j in range(half) for i in (j, j + half)
    }
    load_vgx = fetch(vg.at[tokens(y)], vgx.at[0, 0])
    load_w = fetch(w.at[c], wbuf.at[:, :, :, 0])

    load_rt.wait()
    rt3 = rows3(rt[...])
    for load in load_vg:
        load.wait()
    for dy in range(ny):
        uout[dy] = fold3(mm(rt3, vg_v[dy], NT))
    recv_u = [send(uout.at[dy], uin.at[dy - 1], device(z, x, c, yy)) for dy, yy in y_peers]

    own_w = w.at[c, x, z]
    w_from_down, w_from_up = send_both(
        (own_w, wbuf.at[x, z, :, 3], device(z, x, c, up)), (own_w, wbuf.at[x, z, :, 1], device(z, x, c, down))
    )
    direct(1, 2)

    def place(h, a, b):
        return (a, b) if h == 0 else (b, a)

    def piece(h, first, second):
        zz, xx = place(h, first, second)
        return wbuf.at[xx, zz, h, 1:ny]

    def neighbour(h, stage, way):
        n = (nz if h == 0 else nx) if stage == 0 else (nx if h == 0 else nz)
        first, second = place(h, z, x)
        if stage == 0:
            first = shifted(first, way % n, n)
        else:
            second = shifted(second, way % n, n)
        zz, xx = place(h, first, second)
        return device(zz, xx, c, y)

    half_here = [(place(h, z, x), place(h, nz, nx)) for h in range(2)]
    stage_one, stage_one_across, stage_two, stage_two_across = {}, {}, {}, {}

    def weights_first():
        for h in range(2):
            (first, second), _ = half_here[h]
            own = piece(h, first, second)
            stage_one[h, 1], stage_one[h, -1] = send_both(
                (own, own, neighbour(h, 0, 1)), (own, own, neighbour(h, 0, -1))
            )

    def weights_across():
        for h in range(2):
            (first, second), (n, _) = half_here[h]
            way = 1 - 2 * h
            stage_one[h, way].wait_recv()
            came = piece(h, shifted(first, -way % n, n), second)
            stage_one_across[h] = send(came, came, neighbour(h, 0, way))

    def weights_second(i):
        for h in range(2):
            (first, second), (n, _) = half_here[h]
            if i in (1, 2):
                way = 3 - 2 * i
                if way != 1 - 2 * h:
                    stage_one[h, way].wait_recv()
                first = shifted(first, -way % n, n)
            elif i == 3:
                stage_one_across[h].wait_recv()
                first = shifted(first, 2, n)
            here = piece(h, first, second)
            stage_two[h, i, 1], stage_two[h, i, -1] = send_both(
                (here, here, neighbour(h, 1, 1)), (here, here, neighbour(h, 1, -1))
            )

    def weights_second_across(i):
        for h in range(2):
            (first, second), (n, m) = half_here[h]
            first = shifted(first, (0, n - 1, 1, 2)[i], n)
            way = (1, -1, 1, -1)[i]
            stage_two[h, i, way].wait_recv()
            came = piece(h, first, shifted(second, -way % m, m))
            stage_two_across[h, i] = send(came, came, neighbour(h, 1, way))

    rt2 = rt3[: 2 * r]

    def columns(p):
        return pl.ds(pl.multiple_of(p * wide, wide), wide)

    def store_left(value, cc, j0):
        for j in range(wb):
            lacc[cc, j0 + j] = value[:, j * BLK : (j + 1) * BLK]

    def load_left(ref, cc, j0):
        return jnp.concatenate([ref[cc, j0 + j] for j in range(wb)], axis=1)

    for load in load_err:
        load.wait()

    def err_left(p, carry):
        hi, lo = split2(err_v[columns(p), :])
        store_left(fold2(mm(rt2, lo, NT) + mm(rt2, hi, NT)), lax.div(p, per_piece), lax.rem(p, per_piece) * wb)
        return carry

    lax.fori_loop(0, pieces, err_left, 0)

    wait_all(recv_u)
    ut = uout[0]
    for dy in range(ny - 1):
        ut = ut + uin[dy]
    ut3 = rows3(ut)
    for load in load_act.values():
        load.wait()

    def own_act(p):
        n = wide // part
        if n >= 1:
            return jnp.concatenate([actr[0, p * n + i] for i in range(n)], axis=1)
        n = part // wide
        inside = pl.ds(pl.multiple_of(lax.rem(p, n) * wide, wide), wide)
        return actr[0, lax.div(p, n), :, inside]

    def act_left(cc):
        def step(i, carry):
            value = fold3(mm(ut3, own_act(cc * per_piece + i)))
            store_left(load_left(lacc, cc, i * wb) + value, cc, i * wb)
            return carry

        lax.fori_loop(0, per_piece, step, 0)

    recv = []
    for cc in cores:
        act_left(cc)
        recv.append(send(lacc.at[cc], rc, device(z, x, cc, y)))
    act_left(c)

    recv_core = recv
    direct(3)
    load_vgx.wait()
    for h in range(2):
        vg_passing[h].wait_recv()
        recv_vg.append(send(vstage.at[h], vgx.at[0, 2, h * few : (h + 1) * few], device(z, x, c, ways[h])))
    wait_all(recv)
    lacc[c] += rc[...]
    recv = [
        send(lacc.at[c, xx * nz + zz], rxz.at[i], device(zz, xx, c, y)) for i, (xx, zz) in enumerate(plane)
    ]
    load_w.wait()
    w_from_down.wait_recv()
    w_halves = [send(wbuf.at[x, z, 0, 3], wbuf.at[x, z, 0, 2], device(z, x, c, up))]
    w_from_up.wait_recv()
    w_halves.append(send(wbuf.at[x, z, 1, 1], wbuf.at[x, z, 1, 2], device(z, x, c, down)))
    direct(4)
    settle(recv_u + recv_core)
    recv_rs = recv
    wait_all(recv)
    total = lacc[c, mine]
    for i in range(len(plane)):
        total = total + rxz[i]
    ysum[y] = total
    own = ysum.at[y]
    recv = [send(own, own, device(z, x, c, yy)) for _, yy in y_peers]
    direct(*range(5, 12))
    wait_all(w_halves)
    weights_first()
    weights_second(0)
    settle(recv_rs)
    wait_all(recv)
    total = ysum[0]
    for yy in range(1, ny):
        total = total + ysum[yy]
    lf[c, mine] = total
    own = lf.at[c, mine]
    recv_y = recv
    recv = [send(own, own, device(zz, xx, c, y)) for xx, zz in plane]
    weights_across()
    weights_second(1)
    weights_second(2)
    settle(recv_y)
    wait_all(recv)
    recv_ag = recv
    own = lf.at[c]
    recv = [send(own, own, device(z, x, cc, y)) for cc in cores]
    weights_second(3)
    weights_second_across(0)
    settle(recv_ag)

    wait_all(recv_vg)
    recv_vgx = [send(vgx.at[0], vgx.at[dc], device(z, x, cc, y)) for dc, cc in enumerate(cores, 1)]
    settle(vg_passing + recv_vg + [w_from_down, w_from_up] + w_halves + list(stage_one.values()))
    wait_all(recv)

    def left_piece(p):
        return rows3(load_left(lf, lax.div(p, per_piece), lax.rem(p, per_piece) * wb))

    def products(p, carry):
        gram, by_act = carry
        block = left_piece(p)
        return gram + mm(block, block, NT), by_act + mm(block[: 2 * r], own_act(p), NT)

    gram, by_act = lax.fori_loop(
        0, pieces, products, (jnp.zeros((3 * r, 3 * r), F32), jnp.zeros((2 * r, tok), F32))
    )
    aout[...] = fold2(by_act)
    recv_a = [send(aout, ain.at[dy - 1], device(z, x, c, yy)) for dy, yy in y_peers]
    direct(*range(12, CHUNKS))
    forward(*range(half))
    weights_second_across(1)
    weights_second_across(2)

    total = jnp.zeros((2 * r, err_v.shape[1]), F32)
    count = nb // (r // 4)
    for i, state in enumerate(gram_schmidt(self_products(gram, r))):
        block = jnp.concatenate([lf[(i * count + j) // per, (i * count + j) % per] for j in range(count)], axis=1)
        hi, lo = split2(err_v[i * count * BLK : (i + 1) * count * BLK, :])
        block = rows2(block)
        total = total + (mm(block, lo) + mm(block, hi))
    total = fold2(total)
    weights, norms = unit_weights(state)

    def apply_first(p, gram):
        block = times(weights, load_left(lf, lax.div(p, per_piece), lax.rem(p, per_piece) * wb))
        q1[p] = block
        block = rows3(block)
        return gram + mm(block, block, NT)

    off = self_products(lax.fori_loop(0, pieces, apply_first, jnp.zeros((3 * r, 3 * r), F32)), r) - norms
    row_id = lax.broadcasted_iota(jnp.int32, (r, r), 0)
    col_id = lax.broadcasted_iota(jnp.int32, (r, r), 1)
    again = jnp.where(col_id < row_id, off, jnp.where(col_id == row_id, 0.5 * off, 0.0))
    weights = weights - times(again, weights)
    scale = math.sqrt(float(d))

    def apply_second(p, carry):
        block = q1[p]
        block = block - times(again, block)
        left_out[:, columns(p)] = block * scale
        return carry

    lax.fori_loop(0, pieces, apply_second, 0)


    wait_all(recv_a)
    for slot in range(ny):
        total = total + fold3(mm(rows3(aout[...] if slot == 0 else ain[ny - slot - 1]), vg_v[slot]))
    zsum[0] = total
    recv = [send(zsum.at[0], zsum.at[dc], device(z, x, cc, y)) for dc, cc in enumerate(cores, 1)]
    weights_second_across(3)

    for i in range(4):
        for h in range(2):
            stage_two[h, i, (-1, 1, -1, 1)[i]].wait_recv()
            stage_two_across[h, i].wait_recv()
    wait_all(recv_vgx)

    def input_grad(i, carry):
        total = None
        for slot in range(ny):
            weight = wbuf[lax.div(i, nz), lax.rem(i, nz), :, slot].reshape(BLK, BLK)
            part_sum = mm(vgx[:, slot].reshape(nc * tok, BLK), weight, NT).astype(BF16).astype(F32)
            total = part_sum if total is None else total + part_sum
        total = total.astype(BF16).reshape(nc, tok, BLK)
        gi[:, pl.ds(pl.multiple_of((c * per + i) * BLK, BLK), BLK)] = total[0]
        for dc in range(1, nc):
            outs[dc - 1, :, pl.ds(pl.multiple_of(i * BLK, BLK), BLK)] = total[dc]
        return carry

    lax.fori_loop(0, per, input_grad, 0)
    share_of = gi.at[:, pl.ds(pl.multiple_of(c * per * BLK, BLK), per * BLK)]
    sent_out = [send(outs.at[nc - 1 - dc], share_of, device(z, x, cc, y)) for dc, cc in enumerate(cores, 1)]

    wait_all(recv)
    for dc in range(1, nc):
        total = total + zsum[dc]
    tz[mine] = total
    own = tz.at[mine]
    recv = [send(own, own, device(zz, xx, c, y)) for xx, zz in plane]

    for i in range(CHUNKS):
        if i >= half:
            from_down[i].wait_recv()
        else:
            from_up[i].wait_recv()
    cotangent = vg_v[...].reshape(ny * tok, BLK).astype(F32).T.astype(BF16)

    def merge(j):
        from_across[j].wait_recv()
        at = pl.ds(j * part, part)
        merged[at, :] = err_v[at, :] + mm(cotangent, actr[:, j].reshape(ny * tok, part)).T

    for i in range(half - 2):
        merge(i)
        merge(i + half)

    wait_all(recv)
    total = tz[0]
    for i in range(1, per):
        total = total + tz[i]
    r_out[...] = times(weights, total) / float(nb)
    last = [id(from_across[i + h]) for i in range(half - 2, half) for h in (0, half)]
    settle([copy for copy in sent if id(copy) not in settled + last])

    for i in range(half - 2, half):
        merge(i)
        merge(i + half)

    wait_all(sent_out)
    settle([copy for copy in sent if id(copy) not in settled])
    assert counter == [send_sem.shape[0], local_sem.shape[0]], counter


def error_kernel(merged, left, right, gi, error_out, left_out, right_out, gi_out, error, sem):
    d = merged.shape[0]
    pieces = error.shape[0]
    rows = d // pieces
    copies = [
        pltpu.make_async_copy(a, b, sem.at[pieces + i])
        for i, (a, b) in enumerate([(gi, gi_out), (left, left_out), (right, right_out)])
    ]
    for copy in copies:
        copy.start()
    hi, lo = split2(right[...] / math.sqrt(float(d)))
    right3 = jnp.concatenate([hi, hi, lo], axis=0)
    for i in range(pieces):
        at = pl.ds(i * rows, rows)
        hi, lo = split2(left[:, at])
        error[i] = merged[at, :] - mm(jnp.concatenate([hi, lo, hi], axis=0), right3, TN)
        copies.append(pltpu.make_async_copy(error.at[i], error_out.at[at], sem.at[i]))
        copies[-1].start()
    for copy in copies:
        copy.wait()


def build(geom):
    nz, nx, nc, ny = geom

    def body(act, vg, w, err, right_prev):
        tok, d = act.shape
        kv = vg.shape[1]
        r = right_prev.shape[1]
        nb = nc * nx * nz
        per = nx * nz
        wide = min(WIDE, per * BLK)
        assert d == nb * BLK and kv == BLK and per * BLK % wide == 0
        sends = 3 * (ny - 1) + 6 + 4 + 3 * CHUNKS + 30 + 3 * (per - 1) + 5 * (nc - 1)
        pieces = w.reshape(nc, nx, nz, 2, BLK // 2, kv)
        inputs = [
            pltpu.with_memory_space_constraint(a, pltpu.HBM) for a in (act, vg, pieces, err[0], right_prev.T)
        ]
        hbm = pl.BlockSpec(memory_space=pltpu.HBM)
        vmem = pl.BlockSpec(memory_space=pltpu.VMEM)
        anywhere = pl.BlockSpec(memory_space=pl.ANY)
        results = (((d, kv), F32), ((r, d), F32), ((r, kv), F32), ((tok, d), BF16))
        made = pl.pallas_call(
            functools.partial(comm_kernel, geom),
            out_shape=tuple(pltpu.VMEM(*shape) for shape in results),
            in_specs=[hbm] * 5,
            out_specs=(vmem,) * 4,
            scratch_shapes=[
                pltpu.VMEM((r, kv), F32),
                pltpu.VMEM((ny, CHUNKS, tok, d // CHUNKS), BF16),
                pltpu.VMEM((ny, tok, kv), BF16),
                pltpu.VMEM((d, kv), F32),
                pltpu.VMEM((ny, r, tok), F32),
                pltpu.VMEM((ny - 1, r, tok), F32),
                pltpu.VMEM((2, tok // 2, kv), BF16),
                pltpu.VMEM((nc, ny, tok, kv), BF16),
                pltpu.VMEM((nx, nz, 2, ny, BLK // 2, kv), BF16),
                pltpu.VMEM((max(nc - 1, 1), tok, per * BLK), BF16),
                pltpu.VMEM((nc, per, r, BLK), F32),
                pltpu.VMEM((nc, per, r, BLK), F32),
                pltpu.VMEM((per, r, BLK), F32),
                pltpu.VMEM((per - 1, r, BLK), F32),
                pltpu.VMEM((ny, r, BLK), F32),
                pltpu.VMEM((d // wide, r, wide), F32),
                pltpu.VMEM((r, tok), F32),
                pltpu.VMEM((ny - 1, r, tok), F32),
                pltpu.VMEM((nc, r, kv), F32),
                pltpu.VMEM((per, r, kv), F32),
                pltpu.SemaphoreType.DMA((1 + 1 + 4 + CHUNKS + ny + 1,)),
                pltpu.SemaphoreType.DMA((sends,)),
                pltpu.SemaphoreType.DMA((sends,)),
            ],
            compiler_params=pltpu.CompilerParams(
                collective_id=0, has_side_effects=True, vmem_limit_bytes=44 * MIB
            ),
        )(*inputs)

        pieces = 16
        error_next, left, right, grad_input = pl.pallas_call(
            error_kernel,
            out_shape=tuple(jax.ShapeDtypeStruct(*shape) for shape in results),
            in_specs=[vmem] * 4,
            out_specs=(anywhere,) * 4,
            scratch_shapes=[pltpu.VMEM((pieces, d // pieces, kv), F32), pltpu.SemaphoreType.DMA((pieces + 3,))],
            compiler_params=pltpu.CompilerParams(vmem_limit_bytes=24 * MIB),
        )(*made)
        return (grad_input, error_next[None], left.T, right.T)

    return body


def solution(mesh):
    return jax.shard_map(
        build((4, 4, 2, 4)),
        mesh=mesh,
        in_specs=(
            P(("dp", "tp"), None),
            P("dp", "tp"),
            P(None, "tp"),
            P("dp", None, "tp"),
            P("tp", None),
        ),
        out_specs=(P(("dp", "tp"), None), P("dp", None, "tp"), P(), P("tp", None)),
        check_vma=False,
    )
```

```python
import functools
import math

import jax
import jax.numpy as jnp
from jax import lax
from jax.experimental import pallas as pl
from jax.experimental.pallas import tpu as pltpu
from jax.sharding import PartitionSpec as P

MESH = pl.DeviceIdType.MESH
F32 = jnp.float32
BF16 = jnp.bfloat16
BLK = 256
EPS = 1e-12
MIB = 1024 * 1024
WIDE = 8 * BLK
CHUNKS = 16
NN = (((1,), (0,)), ((), ()))
NT = (((1,), (1,)), ((), ()))
TN = (((0,), (0,)), ((), ()))


def mm(a, b, dims=NN):
    return lax.dot_general(a, b, dims, preferred_element_type=F32)


def split2(a):
    hi = a.astype(BF16)
    lo = (a - hi.astype(F32)).astype(BF16)
    return hi, lo


def split3(a):
    hi = a.astype(BF16)
    rest = a - hi.astype(F32)
    mid = rest.astype(BF16)
    lo = (rest - mid.astype(F32)).astype(BF16)
    return hi, mid, lo


def rows3(a):
    return jnp.concatenate(split3(a), axis=0)


def fold3(a):
    n = a.shape[0] // 3
    return (a[2 * n :] + a[n : 2 * n]) + a[:n]


def rows2(a):
    return jnp.concatenate(split2(a), axis=0)


def fold2(a):
    n = a.shape[0] // 2
    return a[n:] + a[:n]


def self_products(total, r):
    total = fold3(total)
    return (total[:, 2 * r :] + total[:, r : 2 * r]) + total[:, :r]


def times(a, b):
    a_hi, a_mid, a_lo = (v.astype(F32) for v in split3(a))
    b_hi, b_mid, b_lo = split3(b)
    left = jnp.concatenate([a_lo, a_mid, a_hi, a_mid, a_hi, a_hi], axis=1).astype(BF16)
    return mm(left, jnp.concatenate([b_hi, b_mid, b_lo, b_hi, b_mid, b_hi], axis=0))


def eye_like(n):
    return (lax.broadcasted_iota(jnp.int32, (n, n), 0) == lax.broadcasted_iota(jnp.int32, (n, n), 1)).astype(F32)


def gram_schmidt(gram):
    n = gram.shape[0]
    left, weights = gram, eye_like(n)
    row_id = lax.broadcasted_iota(jnp.int32, (n, 1), 0)
    m = 4
    for j in range(0, n, m):
        columns = [jnp.broadcast_to(left[:, i : i + 1], (n, n)) for i in range(j, j + m)]
        rows = [left[i : i + 1, :] for i in range(j, j + m)]
        given = [weights[i : i + 1, :] for i in range(j, j + m)]
        off_left, off_weights = jnp.zeros((n, n), F32), jnp.zeros((n, n), F32)
        for i in range(m):
            at = j + i
            s = jnp.maximum(columns[i][at : at + 1, :], 0.0)
            inverse = 1.0 / (s + EPS)
            c = (2.0 - s * inverse) * inverse
            f = jnp.where(row_id > at, columns[i] * c, 0.0)
            h = f * (2.0 - c * s)
            for later in range(i + 1, m):
                to = j + later
                columns[later] = columns[later] - h * columns[later][at : at + 1, :]
                rows[later] = rows[later] - h[to : to + 1, :] * rows[i]
                given[later] = given[later] - f[to : to + 1, :] * given[i]
            off_left = off_left + h * rows[i]
            off_weights = off_weights + f * given[i]
        left, weights = left - off_left, weights - off_weights
        yield left, weights


def unit_weights(state):
    left, weights = state
    eye = eye_like(left.shape[0])
    s = jnp.maximum(jnp.sum(left * eye, axis=1, keepdims=True), 0.0)
    return weights / jnp.sqrt(s + EPS), eye * (s / (s + EPS))


def comm_kernel(
    geom, act, vg, w, err, rt_in, merged, left_out, r_out, gi,
    rt, actr, vg_v, err_v, uout, uin, vstage, vgx, wbuf, outs, lacc, lf, rc, rxz, ysum, q1, aout, ain, zsum, tz,
    local_sem, send_sem, recv_sem,
):
    nz, nx, nc, ny = geom
    nb = nc * nx * nz
    per = nx * nz
    _, _, tok, part = actr.shape
    d = part * CHUNKS
    half = CHUNKS // 2
    r = rt.shape[0]
    wide = min(WIDE, per * BLK)
    wb = wide // BLK
    pieces = d // wide
    per_piece = per // wb
    dp, y = lax.axis_index("dp"), lax.axis_index("tp")
    c = lax.rem(dp, nc)
    x = lax.rem(lax.div(dp, nc), nx)
    z = lax.div(dp, nc * nx)
    mine = x * nz + z

    def shifted(i, by, n):
        return lax.rem(i + by, n)

    def device(zz, xx, cc, yy):
        return ((zz * nx + xx) * nc + cc, yy)

    y_peers = [(dy, shifted(y, dy, ny)) for dy in range(1, ny)]
    plane = [
        (shifted(x, dx, nx), shifted(z, dz, nz)) for dx in range(nx) for dz in range(nz) if (dx, dz) != (0, 0)
    ]
    cores = [shifted(c, dc, nc) for dc in range(1, nc)]
    up, down, across = shifted(y, 1, ny), shifted(y, ny - 1, ny), shifted(y, 2, ny)

    sent, settled = [], []
    counter = [0, 0]

    def describe(src, dst, to):
        i = counter[0]
        counter[0] += 1
        copy = pltpu.make_async_remote_copy(
            src_ref=src, dst_ref=dst, send_sem=send_sem.at[i], recv_sem=recv_sem.at[i], device_id=to, device_id_type=MESH
        )
        sent.append(copy)
        return copy

    def send(src, dst, to):
        copy = describe(src, dst, to)
        copy.start()
        return copy

    def send_both(one, other):
        one, other = describe(*one), describe(*other)

        @pl.when(c == 0)
        def _():
            one.start()
            other.start()

        @pl.when(c != 0)
        def _():
            other.start()
            one.start()

        return one, other

    def fetch(src, dst):
        i = counter[1]
        counter[1] += 1
        copy = pltpu.make_async_copy(src, dst, local_sem.at[i])
        copy.start()
        return copy

    def wait_all(copies):
        for copy in copies:
            copy.wait_recv()

    def settle(copies):
        for copy in copies:
            copy.wait_send()
        settled.extend(id(copy) for copy in copies)

    def tokens(yy):
        return pl.ds(pl.multiple_of(yy * tok, tok), tok)

    barrier = pltpu.get_barrier_semaphore()
    everyone = (
        [device(z, x, cc, y) for cc in cores]
        + [device(zz, xx, c, y) for xx, zz in plane]
        + [device(z, x, c, yy) for _, yy in y_peers]
    )
    for peer in everyone:
        pl.semaphore_signal(barrier, inc=1, device_id=peer, device_id_type=MESH)

    load_rt = fetch(rt_in, rt)
    load_vg = [fetch(vg.at[tokens(yy)], vg_v.at[i]) for i, yy in enumerate((y, up, across, down))]
    share = d // 4
    load_err = [fetch(err.at[pl.ds(i * share, share)], err_v.at[pl.ds(i * share, share)]) for i in range(4)]
    pl.semaphore_wait(barrier, len(everyone))

    from_down, from_up, from_across = {}, {}, {}

    def cols(i):
        return pl.ds(i * part, part)

    def direct(*numbers):
        for i in numbers:
            j = (i + half) % CHUNKS
            from_down[i], from_up[j] = send_both(
                (act.at[:, cols(i)], actr.at[3, i], device(z, x, c, up)),
                (act.at[:, cols(j)], actr.at[1, j], device(z, x, c, down)),
            )

    def forward(*numbers):
        for i in numbers:
            j = i + half
            from_down[i].wait_recv()
            from_up[j].wait_recv()
            from_across[i], from_across[j] = send_both(
                (actr.at[3, i], actr.at[2, i], device(z, x, c, up)),
                (actr.at[1, j], actr.at[2, j], device(z, x, c, down)),
            )


    recv_vg = [send(vg.at[tokens(up)], vgx.at[0, 3], device(z, x, c, up))]
    recv_vg.append(send(vg.at[tokens(down)], vgx.at[0, 1], device(z, x, c, down)))
    few = tok // 2
    ways = (up, down)
    vg_passing = [
        send(vg.at[pl.ds(pl.multiple_of(across * tok + h * few, few), few)], vstage.at[h], device(z, x, c, ways[h]))
        for h in range(2)
    ]
    direct(0)
    load_act = {
        i: fetch(act.at[:, cols(i)], actr.at[0, i]) for j in range(half) for i in (j, j + half)
    }
    load_vgx = fetch(vg.at[tokens(y)], vgx.at[0, 0])
    load_w = fetch(w.at[c], wbuf.at[:, :, :, 0])

    load_rt.wait()
    rt3 = rows3(rt[...])
    for load in load_vg:
        load.wait()
    for dy in range(ny):
        uout[dy] = fold3(mm(rt3, vg_v[dy], NT))
    recv_u = [send(uout.at[dy], uin.at[dy - 1], device(z, x, c, yy)) for dy, yy in y_peers]

    own_w = w.at[c, x, z]
    w_from_down, w_from_up = send_both(
        (own_w, wbuf.at[x, z, :, 3], device(z, x, c, up)), (own_w, wbuf.at[x, z, :, 1], device(z, x, c, down))
    )
    direct(1, 2)

    def place(h, a, b):
        return (a, b) if h == 0 else (b, a)

    def piece(h, first, second):
        zz, xx = place(h, first, second)
        return wbuf.at[xx, zz, h, 1:ny]

    def neighbour(h, stage, way):
        n = (nz if h == 0 else nx) if stage == 0 else (nx if h == 0 else nz)
        first, second = place(h, z, x)
        if stage == 0:
            first = shifted(first, way % n, n)
        else:
            second = shifted(second, way % n, n)
        zz, xx = place(h, first, second)
        return device(zz, xx, c, y)

    half_here = [(place(h, z, x), place(h, nz, nx)) for h in range(2)]
    stage_one, stage_one_across, stage_two, stage_two_across = {}, {}, {}, {}

    def weights_first():
        for h in range(2):
            (first, second), _ = half_here[h]
            own = piece(h, first, second)
            stage_one[h, 1], stage_one[h, -1] = send_both(
                (own, own, neighbour(h, 0, 1)), (own, own, neighbour(h, 0, -1))
            )

    def weights_across():
        for h in range(2):
            (first, second), (n, _) = half_here[h]
            way = 1 - 2 * h
            stage_one[h, way].wait_recv()
            came = piece(h, shifted(first, -way % n, n), second)
            stage_one_across[h] = send(came, came, neighbour(h, 0, way))

    def weights_second(i):
        for h in range(2):
            (first, second), (n, _) = half_here[h]
            if i in (1, 2):
                way = 3 - 2 * i
                if way != 1 - 2 * h:
                    stage_one[h, way].wait_recv()
                first = shifted(first, -way % n, n)
            elif i == 3:
                stage_one_across[h].wait_recv()
                first = shifted(first, 2, n)
            here = piece(h, first, second)
            stage_two[h, i, 1], stage_two[h, i, -1] = send_both(
                (here, here, neighbour(h, 1, 1)), (here, here, neighbour(h, 1, -1))
            )

    def weights_second_across(i):
        for h in range(2):
            (first, second), (n, m) = half_here[h]
            first = shifted(first, (0, n - 1, 1, 2)[i], n)
            way = (1, -1, 1, -1)[i]
            stage_two[h, i, way].wait_recv()
            came = piece(h, first, shifted(second, -way % m, m))
            stage_two_across[h, i] = send(came, came, neighbour(h, 1, way))

    rt2 = rt3[: 2 * r]

    def columns(p):
        return pl.ds(pl.multiple_of(p * wide, wide), wide)

    def store_left(value, cc, j0):
        for j in range(wb):
            lacc[cc, j0 + j] = value[:, j * BLK : (j + 1) * BLK]

    def load_left(ref, cc, j0):
        return jnp.concatenate([ref[cc, j0 + j] for j in range(wb)], axis=1)

    for load in load_err:
        load.wait()

    def err_left(p, carry):
        hi, lo = split2(err_v[columns(p), :])
        store_left(fold2(mm(rt2, lo, NT) + mm(rt2, hi, NT)), lax.div(p, per_piece), lax.rem(p, per_piece) * wb)
        return carry

    lax.fori_loop(0, pieces, err_left, 0)

    wait_all(recv_u)
    ut = uout[0]
    for dy in range(ny - 1):
        ut = ut + uin[dy]
    ut3 = rows3(ut)
    for load in load_act.values():
        load.wait()

    def own_act(p):
        n = wide // part
        if n >= 1:
            return jnp.concatenate([actr[0, p * n + i] for i in range(n)], axis=1)
        n = part // wide
        inside = pl.ds(pl.multiple_of(lax.rem(p, n) * wide, wide), wide)
        return actr[0, lax.div(p, n), :, inside]

    def act_left(cc):
        def step(i, carry):
            value = fold3(mm(ut3, own_act(cc * per_piece + i)))
            store_left(load_left(lacc, cc, i * wb) + value, cc, i * wb)
            return carry

        lax.fori_loop(0, per_piece, step, 0)

    recv = []
    for cc in cores:
        act_left(cc)
        recv.append(send(lacc.at[cc], rc, device(z, x, cc, y)))
    act_left(c)

    recv_core = recv
    direct(3)
    load_vgx.wait()
    for h in range(2):
        vg_passing[h].wait_recv()
        recv_vg.append(send(vstage.at[h], vgx.at[0, 2, h * few : (h + 1) * few], device(z, x, c, ways[h])))
    wait_all(recv)
    lacc[c] += rc[...]
    recv = [
        send(lacc.at[c, xx * nz + zz], rxz.at[i], device(zz, xx, c, y)) for i, (xx, zz) in enumerate(plane)
    ]
    load_w.wait()
    w_from_down.wait_recv()
    w_halves = [send(wbuf.at[x, z, 0, 3], wbuf.at[x, z, 0, 2], device(z, x, c, up))]
    w_from_up.wait_recv()
    w_halves.append(send(wbuf.at[x, z, 1, 1], wbuf.at[x, z, 1, 2], device(z, x, c, down)))
    direct(4)
    settle(recv_u + recv_core)
    recv_rs = recv
    wait_all(recv)
    total = lacc[c, mine]
    for i in range(len(plane)):
        total = total + rxz[i]
    ysum[y] = total
    own = ysum.at[y]
    recv = [send(own, own, device(z, x, c, yy)) for _, yy in y_peers]
    direct(*range(5, 12))
    wait_all(w_halves)
    weights_first()
    weights_second(0)
    settle(recv_rs)
    wait_all(recv)
    total = ysum[0]
    for yy in range(1, ny):
        total = total + ysum[yy]
    lf[c, mine] = total
    own = lf.at[c, mine]
    recv_y = recv
    recv = [send(own, own, device(zz, xx, c, y)) for xx, zz in plane]
    weights_across()
    weights_second(1)
    weights_second(2)
    settle(recv_y)
    wait_all(recv)
    recv_ag = recv
    own = lf.at[c]
    recv = [send(own, own, device(z, x, cc, y)) for cc in cores]
    weights_second(3)
    weights_second_across(0)
    settle(recv_ag)

    wait_all(recv_vg)
    recv_vgx = [send(vgx.at[0], vgx.at[dc], device(z, x, cc, y)) for dc, cc in enumerate(cores, 1)]
    settle(vg_passing + recv_vg + [w_from_down, w_from_up] + w_halves + list(stage_one.values()))
    wait_all(recv)

    def left_piece(p):
        return rows3(load_left(lf, lax.div(p, per_piece), lax.rem(p, per_piece) * wb))

    def products(p, carry):
        gram, by_act = carry
        block = left_piece(p)
        return gram + mm(block, block, NT), by_act + mm(block[: 2 * r], own_act(p), NT)

    gram, by_act = lax.fori_loop(
        0, pieces, products, (jnp.zeros((3 * r, 3 * r), F32), jnp.zeros((2 * r, tok), F32))
    )
    aout[...] = fold2(by_act)
    early = list(sent)
    recv_a = [send(aout, ain.at[dy - 1], device(z, x, c, yy)) for dy, yy in y_peers]
    direct(*range(12, CHUNKS))
    forward(*range(half))
    weights_second_across(1)
    weights_second_across(2)

    total = jnp.zeros((2 * r, err_v.shape[1]), F32)
    count = nb // (r // 4)
    for i, state in enumerate(gram_schmidt(self_products(gram, r))):
        block = jnp.concatenate([lf[(i * count + j) // per, (i * count + j) % per] for j in range(count)], axis=1)
        hi, lo = split2(err_v[i * count * BLK : (i + 1) * count * BLK, :])
        block = rows2(block)
        total = total + (mm(block, lo) + mm(block, hi))
    total = fold2(total)
    weights, norms = unit_weights(state)

    def apply_first(p, gram):
        block = times(weights, load_left(lf, lax.div(p, per_piece), lax.rem(p, per_piece) * wb))
        q1[p] = block
        block = rows3(block)
        return gram + mm(block, block, NT)

    off = self_products(lax.fori_loop(0, pieces, apply_first, jnp.zeros((3 * r, 3 * r), F32)), r) - norms
    row_id = lax.broadcasted_iota(jnp.int32, (r, r), 0)
    col_id = lax.broadcasted_iota(jnp.int32, (r, r), 1)
    again = jnp.where(col_id < row_id, off, jnp.where(col_id == row_id, 0.5 * off, 0.0))
    weights = weights - times(again, weights)
    scale = math.sqrt(float(d))

    wait_all(recv_a)
    for slot in range(ny):
        total = total + fold3(mm(rows3(aout[...] if slot == 0 else ain[ny - slot - 1]), vg_v[slot]))
    zsum[0] = total
    recv = [send(zsum.at[0], zsum.at[dc], device(z, x, cc, y)) for dc, cc in enumerate(cores, 1)]
    weights_second_across(3)

    def apply_second(p, carry):
        block = q1[p]
        block = block - times(again, block)
        left_out[:, columns(p)] = block * scale
        return carry

    lax.fori_loop(0, pieces, apply_second, 0)
    settle([copy for copy in early if id(copy) not in settled])
    wait_all(recv)
    for dc in range(1, nc):
        total = total + zsum[dc]
    tz[mine] = total
    own = tz.at[mine]
    recv = [send(own, own, device(zz, xx, c, y)) for xx, zz in plane]


    for i in range(4):
        for h in range(2):
            stage_two[h, i, (-1, 1, -1, 1)[i]].wait_recv()
            stage_two_across[h, i].wait_recv()
    wait_all(recv_vgx)

    def input_grad(i, carry):
        total = None
        for slot in range(ny):
            weight = wbuf[lax.div(i, nz), lax.rem(i, nz), :, slot].reshape(BLK, BLK)
            part_sum = mm(vgx[:, slot].reshape(nc * tok, BLK), weight, NT).astype(BF16).astype(F32)
            total = part_sum if total is None else total + part_sum
        total = total.astype(BF16).reshape(nc, tok, BLK)
        gi[:, pl.ds(pl.multiple_of((c * per + i) * BLK, BLK), BLK)] = total[0]
        for dc in range(1, nc):
            outs[dc - 1, :, pl.ds(pl.multiple_of(i * BLK, BLK), BLK)] = total[dc]
        return carry

    lax.fori_loop(0, per, input_grad, 0)
    share_of = gi.at[:, pl.ds(pl.multiple_of(c * per * BLK, BLK), per * BLK)]
    sent_out = [send(outs.at[nc - 1 - dc], share_of, device(z, x, cc, y)) for dc, cc in enumerate(cores, 1)]

    for i in range(CHUNKS):
        if i >= half:
            from_down[i].wait_recv()
        else:
            from_up[i].wait_recv()
    cotangent = vg_v[...].reshape(ny * tok, BLK).astype(F32).T.astype(BF16)

    def merge(j):
        from_across[j].wait_recv()
        at = pl.ds(j * part, part)
        merged[at, :] = err_v[at, :] + mm(cotangent, actr[:, j].reshape(ny * tok, part)).T

    for i in range(half - 2):
        merge(i)
        merge(i + half)

    wait_all(recv)
    total = tz[0]
    for i in range(1, per):
        total = total + tz[i]
    r_out[...] = times(weights, total) / float(nb)
    last = [id(from_across[i + h]) for i in range(half - 2, half) for h in (0, half)]
    settle([copy for copy in sent if id(copy) not in settled + last])

    for i in range(half - 2, half):
        merge(i)
        merge(i + half)

    wait_all(sent_out)
    settle([copy for copy in sent if id(copy) not in settled])
    assert counter == [send_sem.shape[0], local_sem.shape[0]], counter


def error_kernel(merged, left, right, gi, error_out, left_out, right_out, gi_out, error, sem):
    d = merged.shape[0]
    pieces = error.shape[0]
    rows = d // pieces
    copies = [
        pltpu.make_async_copy(a, b, sem.at[pieces + i])
        for i, (a, b) in enumerate([(gi, gi_out), (left, left_out), (right, right_out)])
    ]
    for copy in copies:
        copy.start()
    hi, lo = split2(right[...] / math.sqrt(float(d)))
    right3 = jnp.concatenate([hi, hi, lo], axis=0)
    for i in range(pieces):
        at = pl.ds(i * rows, rows)
        hi, lo = split2(left[:, at])
        error[i] = merged[at, :] - mm(jnp.concatenate([hi, lo, hi], axis=0), right3, TN)
        copies.append(pltpu.make_async_copy(error.at[i], error_out.at[at], sem.at[i]))
        copies[-1].start()
    for copy in copies:
        copy.wait()


def build(geom):
    nz, nx, nc, ny = geom

    def body(act, vg, w, err, right_prev):
        tok, d = act.shape
        kv = vg.shape[1]
        r = right_prev.shape[1]
        nb = nc * nx * nz
        per = nx * nz
        wide = min(WIDE, per * BLK)
        assert d == nb * BLK and kv == BLK and per * BLK % wide == 0
        sends = 3 * (ny - 1) + 6 + 4 + 3 * CHUNKS + 30 + 3 * (per - 1) + 5 * (nc - 1)
        pieces = w.reshape(nc, nx, nz, 2, BLK // 2, kv)
        inputs = [
            pltpu.with_memory_space_constraint(a, pltpu.HBM) for a in (act, vg, pieces, err[0], right_prev.T)
        ]
        hbm = pl.BlockSpec(memory_space=pltpu.HBM)
        vmem = pl.BlockSpec(memory_space=pltpu.VMEM)
        anywhere = pl.BlockSpec(memory_space=pl.ANY)
        results = (((d, kv), F32), ((r, d), F32), ((r, kv), F32), ((tok, d), BF16))
        made = pl.pallas_call(
            functools.partial(comm_kernel, geom),
            out_shape=tuple(pltpu.VMEM(*shape) for shape in results),
            in_specs=[hbm] * 5,
            out_specs=(vmem,) * 4,
            scratch_shapes=[
                pltpu.VMEM((r, kv), F32),
                pltpu.VMEM((ny, CHUNKS, tok, d // CHUNKS), BF16),
                pltpu.VMEM((ny, tok, kv), BF16),
                pltpu.VMEM((d, kv), F32),
                pltpu.VMEM((ny, r, tok), F32),
                pltpu.VMEM((ny - 1, r, tok), F32),
                pltpu.VMEM((2, tok // 2, kv), BF16),
                pltpu.VMEM((nc, ny, tok, kv), BF16),
                pltpu.VMEM((nx, nz, 2, ny, BLK // 2, kv), BF16),
                pltpu.VMEM((max(nc - 1, 1), tok, per * BLK), BF16),
                pltpu.VMEM((nc, per, r, BLK), F32),
                pltpu.VMEM((nc, per, r, BLK), F32),
                pltpu.VMEM((per, r, BLK), F32),
                pltpu.VMEM((per - 1, r, BLK), F32),
                pltpu.VMEM((ny, r, BLK), F32),
                pltpu.VMEM((d // wide, r, wide), F32),
                pltpu.VMEM((r, tok), F32),
                pltpu.VMEM((ny - 1, r, tok), F32),
                pltpu.VMEM((nc, r, kv), F32),
                pltpu.VMEM((per, r, kv), F32),
                pltpu.SemaphoreType.DMA((1 + 1 + 4 + CHUNKS + ny + 1,)),
                pltpu.SemaphoreType.DMA((sends,)),
                pltpu.SemaphoreType.DMA((sends,)),
            ],
            compiler_params=pltpu.CompilerParams(
                collective_id=0, has_side_effects=True, vmem_limit_bytes=44 * MIB
            ),
        )(*inputs)

        pieces = 16
        error_next, left, right, grad_input = pl.pallas_call(
            error_kernel,
            out_shape=tuple(jax.ShapeDtypeStruct(*shape) for shape in results),
            in_specs=[vmem] * 4,
            out_specs=(anywhere,) * 4,
            scratch_shapes=[pltpu.VMEM((pieces, d // pieces, kv), F32), pltpu.SemaphoreType.DMA((pieces + 3,))],
            compiler_params=pltpu.CompilerParams(vmem_limit_bytes=24 * MIB),
        )(*made)
        return (grad_input, error_next[None], left.T, right.T)

    return body


def solution(mesh):
    return jax.shard_map(
        build((4, 4, 2, 4)),
        mesh=mesh,
        in_specs=(
            P(("dp", "tp"), None),
            P("dp", "tp"),
            P(None, "tp"),
            P("dp", None, "tp"),
            P("tp", None),
        ),
        out_specs=(P(("dp", "tp"), None), P("dp", None, "tp"), P(), P("tp", None)),
        check_vma=False,
    )
```

```python
import functools
import math

import jax
import jax.numpy as jnp
from jax import lax
from jax.experimental import pallas as pl
from jax.experimental.pallas import tpu as pltpu
from jax.sharding import PartitionSpec as P

MESH = pl.DeviceIdType.MESH
F32 = jnp.float32
BF16 = jnp.bfloat16
BLK = 256
EPS = 1e-12
MIB = 1024 * 1024
WIDE = 8 * BLK
CHUNKS = 16
NN = (((1,), (0,)), ((), ()))
NT = (((1,), (1,)), ((), ()))
TN = (((0,), (0,)), ((), ()))


def mm(a, b, dims=NN):
    return lax.dot_general(a, b, dims, preferred_element_type=F32)


def split2(a):
    hi = a.astype(BF16)
    lo = (a - hi.astype(F32)).astype(BF16)
    return hi, lo


def split3(a):
    hi = a.astype(BF16)
    rest = a - hi.astype(F32)
    mid = rest.astype(BF16)
    lo = (rest - mid.astype(F32)).astype(BF16)
    return hi, mid, lo


def rows3(a):
    return jnp.concatenate(split3(a), axis=0)


def fold3(a):
    n = a.shape[0] // 3
    return (a[2 * n :] + a[n : 2 * n]) + a[:n]


def rows2(a):
    return jnp.concatenate(split2(a), axis=0)


def fold2(a):
    n = a.shape[0] // 2
    return a[n:] + a[:n]


def self_products(total, r):
    total = fold3(total)
    return (total[:, 2 * r :] + total[:, r : 2 * r]) + total[:, :r]


def times(a, b):
    a_hi, a_mid, a_lo = (v.astype(F32) for v in split3(a))
    b_hi, b_mid, b_lo = split3(b)
    left = jnp.concatenate([a_lo, a_mid, a_hi, a_mid, a_hi, a_hi], axis=1).astype(BF16)
    return mm(left, jnp.concatenate([b_hi, b_mid, b_lo, b_hi, b_mid, b_hi], axis=0))


def eye_like(n):
    return (lax.broadcasted_iota(jnp.int32, (n, n), 0) == lax.broadcasted_iota(jnp.int32, (n, n), 1)).astype(F32)


def gram_schmidt(gram):
    n = gram.shape[0]
    left, weights = gram, eye_like(n)
    row_id = lax.broadcasted_iota(jnp.int32, (n, 1), 0)
    m = 4
    for j in range(0, n, m):
        columns = [jnp.broadcast_to(left[:, i : i + 1], (n, n)) for i in range(j, j + m)]
        rows = [left[i : i + 1, :] for i in range(j, j + m)]
        given = [weights[i : i + 1, :] for i in range(j, j + m)]
        off_left, off_weights = jnp.zeros((n, n), F32), jnp.zeros((n, n), F32)
        for i in range(m):
            at = j + i
            s = jnp.maximum(columns[i][at : at + 1, :], 0.0)
            inverse = 1.0 / (s + EPS)
            c = (2.0 - s * inverse) * inverse
            f = jnp.where(row_id > at, columns[i] * c, 0.0)
            h = f * (2.0 - c * s)
            for later in range(i + 1, m):
                to = j + later
                columns[later] = columns[later] - h * columns[later][at : at + 1, :]
                rows[later] = rows[later] - h[to : to + 1, :] * rows[i]
                given[later] = given[later] - f[to : to + 1, :] * given[i]
            off_left = off_left + h * rows[i]
            off_weights = off_weights + f * given[i]
        left, weights = left - off_left, weights - off_weights
        yield left, weights


def unit_weights(state):
    left, weights = state
    eye = eye_like(left.shape[0])
    s = jnp.maximum(jnp.sum(left * eye, axis=1, keepdims=True), 0.0)
    return weights / jnp.sqrt(s + EPS), eye * (s / (s + EPS))


def comm_kernel(
    geom, act, vg, w, err, rt_in, merged, left_out, r_out, gi,
    rt, actr, vg_v, err_v, uout, uin, vstage, vgx, wbuf, outs, lacc, lf, rc, rxz, ysum, q1, aout, ain, zsum, tz,
    local_sem, send_sem, recv_sem,
):
    nz, nx, nc, ny = geom
    nb = nc * nx * nz
    per = nx * nz
    _, _, tok, part = actr.shape
    d = part * CHUNKS
    half = CHUNKS // 2
    r = rt.shape[0]
    wide = min(WIDE, per * BLK)
    wb = wide // BLK
    pieces = d // wide
    per_piece = per // wb
    dp, y = lax.axis_index("dp"), lax.axis_index("tp")
    c = lax.rem(dp, nc)
    x = lax.rem(lax.div(dp, nc), nx)
    z = lax.div(dp, nc * nx)
    mine = x * nz + z

    def shifted(i, by, n):
        return lax.rem(i + by, n)

    def device(zz, xx, cc, yy):
        return ((zz * nx + xx) * nc + cc, yy)

    y_peers = [(dy, shifted(y, dy, ny)) for dy in range(1, ny)]
    plane = [
        (shifted(x, dx, nx), shifted(z, dz, nz)) for dx in range(nx) for dz in range(nz) if (dx, dz) != (0, 0)
    ]
    cores = [shifted(c, dc, nc) for dc in range(1, nc)]
    up, down, across = shifted(y, 1, ny), shifted(y, ny - 1, ny), shifted(y, 2, ny)

    sent, settled = [], []
    counter = [0, 0]

    def describe(src, dst, to):
        i = counter[0]
        counter[0] += 1
        copy = pltpu.make_async_remote_copy(
            src_ref=src, dst_ref=dst, send_sem=send_sem.at[i], recv_sem=recv_sem.at[i], device_id=to, device_id_type=MESH
        )
        sent.append(copy)
        return copy

    def send(src, dst, to):
        copy = describe(src, dst, to)
        copy.start()
        return copy

    def send_both(one, other):
        one, other = describe(*one), describe(*other)

        @pl.when(c == 0)
        def _():
            one.start()
            other.start()

        @pl.when(c != 0)
        def _():
            other.start()
            one.start()

        return one, other

    def fetch(src, dst):
        i = counter[1]
        counter[1] += 1
        copy = pltpu.make_async_copy(src, dst, local_sem.at[i])
        copy.start()
        return copy

    def wait_all(copies):
        for copy in copies:
            copy.wait_recv()

    def settle(copies):
        for copy in copies:
            copy.wait_send()
        settled.extend(id(copy) for copy in copies)

    def tokens(yy):
        return pl.ds(pl.multiple_of(yy * tok, tok), tok)

    barrier = pltpu.get_barrier_semaphore()
    everyone = (
        [device(z, x, c, yy) for _, yy in y_peers]
        + [device(z, x, cc, y) for cc in cores]
        + [device(zz, xx, c, y) for xx, zz in plane]
    )
    for peer in everyone:
        pl.semaphore_signal(barrier, inc=1, device_id=peer, device_id_type=MESH)

    def cols(i):
        return pl.ds(i * part, part)

    load_rt = fetch(rt_in, rt)
    load_vg = [fetch(vg.at[tokens(yy)], vg_v.at[i]) for i, yy in enumerate((y, up, across, down))]
    share = d // 4
    load_act = {i: fetch(act.at[:, cols(i)], actr.at[0, i]) for j in range(half) for i in (j, j + half)}
    load_err = [fetch(err.at[pl.ds(i * share, share)], err_v.at[pl.ds(i * share, share)]) for i in range(4)]
    pl.semaphore_wait(barrier, len(everyone))

    from_down, from_up, from_across = {}, {}, {}

    def direct(*units):
        for u in units:
            i = 2 * u
            j = (i + half) % CHUNKS
            for n in (i, i + 1, j, j + 1):
                if n in load_act:
                    load_act.pop(n).wait()
            from_down[i], from_up[j] = send_both(
                (actr.at[0, i : i + 2], actr.at[3, i : i + 2], device(z, x, c, up)),
                (actr.at[0, j : j + 2], actr.at[1, j : j + 2], device(z, x, c, down)),
            )

    arrived = set()

    def arrive(copies, i):
        if (id(copies), i) not in arrived:
            arrived.add((id(copies), i))
            copies[i].wait_recv()

    passed_on = [(0, 2), (2, 2), (4, 2), (6, 1), (7, 1)]

    def forward():
        for i, n in passed_on:
            j = i + half
            arrive(from_down, i // 2 * 2)
            arrive(from_up, j // 2 * 2)
            from_across[i], from_across[j] = send_both(
                (actr.at[3, i : i + n], actr.at[2, i : i + n], device(z, x, c, up)),
                (actr.at[1, j : j + n], actr.at[2, j : j + n], device(z, x, c, down)),
            )

    recv_vg = [send(vg.at[tokens(up)], vgx.at[0, 3], device(z, x, c, up))]
    recv_vg.append(send(vg.at[tokens(down)], vgx.at[0, 1], device(z, x, c, down)))
    few = tok // 2
    ways = (up, down)
    vg_passing = [
        send(vg.at[pl.ds(pl.multiple_of(across * tok + h * few, few), few)], vstage.at[h], device(z, x, c, ways[h]))
        for h in range(2)
    ]
    direct(0)
    load_vgx = fetch(vg.at[tokens(y)], vgx.at[0, 0])
    load_w = fetch(w.at[c], wbuf.at[:, :, :, 0])

    load_rt.wait()
    rt3 = rows3(rt[...])
    for load in load_vg:
        load.wait()
    for dy in range(ny):
        uout[dy] = fold3(mm(rt3, vg_v[dy], NT))
    recv_u = [send(uout.at[dy], uin.at[dy - 1], device(z, x, c, yy)) for dy, yy in y_peers]

    own_w = w.at[c, x, z]
    w_from_down, w_from_up = send_both(
        (own_w, wbuf.at[x, z, :, 3], device(z, x, c, up)), (own_w, wbuf.at[x, z, :, 1], device(z, x, c, down))
    )
    direct(1)

    def place(h, a, b):
        return (a, b) if h == 0 else (b, a)

    def piece(h, first, second):
        zz, xx = place(h, first, second)
        return wbuf.at[xx, zz, h, 1:ny]

    def neighbour(h, stage, way):
        n = (nz if h == 0 else nx) if stage == 0 else (nx if h == 0 else nz)
        first, second = place(h, z, x)
        if stage == 0:
            first = shifted(first, way % n, n)
        else:
            second = shifted(second, way % n, n)
        zz, xx = place(h, first, second)
        return device(zz, xx, c, y)

    half_here = [(place(h, z, x), place(h, nz, nx)) for h in range(2)]
    stage_one, stage_one_across, stage_two, stage_two_across = {}, {}, {}, {}

    def weights_first():
        for h in range(2):
            (first, second), _ = half_here[h]
            own = piece(h, first, second)
            stage_one[h, 1], stage_one[h, -1] = send_both(
                (own, own, neighbour(h, 0, 1)), (own, own, neighbour(h, 0, -1))
            )

    def weights_across():
        for h in range(2):
            (first, second), (n, _) = half_here[h]
            way = 1 - 2 * h
            stage_one[h, way].wait_recv()
            came = piece(h, shifted(first, -way % n, n), second)
            stage_one_across[h] = send(came, came, neighbour(h, 0, way))

    def weights_second(i):
        for h in range(2):
            (first, second), (n, _) = half_here[h]
            if i in (1, 2):
                way = 3 - 2 * i
                if way != 1 - 2 * h:
                    stage_one[h, way].wait_recv()
                first = shifted(first, -way % n, n)
            elif i == 3:
                stage_one_across[h].wait_recv()
                first = shifted(first, 2, n)
            here = piece(h, first, second)
            stage_two[h, i, 1], stage_two[h, i, -1] = send_both(
                (here, here, neighbour(h, 1, 1)), (here, here, neighbour(h, 1, -1))
            )

    def weights_second_across(i):
        for h in range(2):
            (first, second), (n, m) = half_here[h]
            first = shifted(first, (0, n - 1, 1, 2)[i], n)
            way = (1, -1, 1, -1)[i]
            stage_two[h, i, way].wait_recv()
            came = piece(h, first, shifted(second, -way % m, m))
            stage_two_across[h, i] = send(came, came, neighbour(h, 1, way))

    rt2 = rt3[: 2 * r]

    def columns(p):
        return pl.ds(pl.multiple_of(p * wide, wide), wide)

    def store_left(value, cc, j0):
        for j in range(wb):
            lacc[cc, j0 + j] = value[:, j * BLK : (j + 1) * BLK]

    def load_left(ref, cc, j0):
        return jnp.concatenate([ref[cc, j0 + j] for j in range(wb)], axis=1)

    for load in load_err:
        load.wait()

    def err_left(p, carry):
        hi, lo = split2(err_v[columns(p), :])
        store_left(fold2(mm(rt2, lo, NT) + mm(rt2, hi, NT)), lax.div(p, per_piece), lax.rem(p, per_piece) * wb)
        return carry

    lax.fori_loop(0, pieces, err_left, 0)

    wait_all(recv_u)
    ut = uout[0]
    for dy in range(ny - 1):
        ut = ut + uin[dy]
    ut3 = rows3(ut)
    for load in load_act.values():
        load.wait()
    load_act.clear()

    def own_act(p):
        n = wide // part
        if n >= 1:
            return jnp.concatenate([actr[0, p * n + i] for i in range(n)], axis=1)
        n = part // wide
        inside = pl.ds(pl.multiple_of(lax.rem(p, n) * wide, wide), wide)
        return actr[0, lax.div(p, n), :, inside]

    def act_left(cc):
        def step(i, carry):
            value = fold3(mm(ut3, own_act(cc * per_piece + i)))
            store_left(load_left(lacc, cc, i * wb) + value, cc, i * wb)
            return carry

        lax.fori_loop(0, per_piece, step, 0)

    recv = []
    for cc in cores:
        act_left(cc)
        recv.append(send(lacc.at[cc], rc, device(z, x, cc, y)))
    act_left(c)

    recv_core = recv
    load_vgx.wait()
    for h in range(2):
        vg_passing[h].wait_recv()
        recv_vg.append(send(vstage.at[h], vgx.at[0, 2, h * few : (h + 1) * few], device(z, x, c, ways[h])))
    wait_all(recv)
    lacc[c] += rc[...]
    recv = [
        send(lacc.at[c, xx * nz + zz], rxz.at[i], device(zz, xx, c, y)) for i, (xx, zz) in enumerate(plane)
    ]
    load_w.wait()
    w_from_down.wait_recv()
    w_halves = [send(wbuf.at[x, z, 0, 3], wbuf.at[x, z, 0, 2], device(z, x, c, up))]
    w_from_up.wait_recv()
    w_halves.append(send(wbuf.at[x, z, 1, 1], wbuf.at[x, z, 1, 2], device(z, x, c, down)))
    settle(recv_u + recv_core)
    recv_rs = recv
    wait_all(recv)
    total = lacc[c, mine]
    for i in range(len(plane)):
        total = total + rxz[i]
    ysum[y] = total
    own = ysum.at[y]
    recv = [send(own, own, device(z, x, c, yy)) for _, yy in y_peers]
    direct(2, 3, 4, 5)
    wait_all(w_halves)
    weights_first()
    weights_second(0)
    settle(recv_rs)
    wait_all(recv)
    total = ysum[0]
    for yy in range(1, ny):
        total = total + ysum[yy]
    lf[c, mine] = total
    own = lf.at[c, mine]
    recv_y = recv
    recv = [send(own, own, device(zz, xx, c, y)) for xx, zz in plane]
    weights_across()
    weights_second(1)
    weights_second(2)
    settle(recv_y)
    wait_all(recv)
    recv_ag = recv
    own = lf.at[c]
    recv = [send(own, own, device(z, x, cc, y)) for cc in cores]
    weights_second(3)
    weights_second_across(0)
    settle(recv_ag)

    wait_all(recv_vg)
    recv_vgx = [send(vgx.at[0], vgx.at[dc], device(z, x, cc, y)) for dc, cc in enumerate(cores, 1)]
    settle(vg_passing + recv_vg + [w_from_down, w_from_up] + w_halves + list(stage_one.values()))
    wait_all(recv)

    def left_piece(p):
        return rows3(load_left(lf, lax.div(p, per_piece), lax.rem(p, per_piece) * wb))

    def products(p, carry):
        gram, by_act = carry
        block = left_piece(p)
        return gram + mm(block, block, NT), by_act + mm(block[: 2 * r], own_act(p), NT)

    gram, by_act = lax.fori_loop(
        0, pieces, products, (jnp.zeros((3 * r, 3 * r), F32), jnp.zeros((2 * r, tok), F32))
    )
    aout[...] = fold2(by_act)
    early = list(sent)
    recv_a = [send(aout, ain.at[dy - 1], device(z, x, c, yy)) for dy, yy in y_peers]
    direct(6, 7)
    forward()
    weights_second_across(1)
    weights_second_across(2)

    total = jnp.zeros((2 * r, err_v.shape[1]), F32)
    count = nb // (r // 4)
    for i, state in enumerate(gram_schmidt(self_products(gram, r))):
        block = jnp.concatenate([lf[(i * count + j) // per, (i * count + j) % per] for j in range(count)], axis=1)
        hi, lo = split2(err_v[i * count * BLK : (i + 1) * count * BLK, :])
        block = rows2(block)
        total = total + (mm(block, lo) + mm(block, hi))
    total = fold2(total)
    weights, norms = unit_weights(state)

    def apply_first(p, gram):
        block = times(weights, load_left(lf, lax.div(p, per_piece), lax.rem(p, per_piece) * wb))
        q1[p] = block
        block = rows3(block)
        return gram + mm(block, block, NT)

    off = self_products(lax.fori_loop(0, pieces, apply_first, jnp.zeros((3 * r, 3 * r), F32)), r) - norms
    row_id = lax.broadcasted_iota(jnp.int32, (r, r), 0)
    col_id = lax.broadcasted_iota(jnp.int32, (r, r), 1)
    again = jnp.where(col_id < row_id, off, jnp.where(col_id == row_id, 0.5 * off, 0.0))
    weights = weights - times(again, weights)
    scale = math.sqrt(float(d))

    wait_all(recv_a)
    for slot in range(ny):
        total = total + fold3(mm(rows3(aout[...] if slot == 0 else ain[ny - slot - 1]), vg_v[slot]))
    zsum[0] = total
    recv = [send(zsum.at[0], zsum.at[dc], device(z, x, cc, y)) for dc, cc in enumerate(cores, 1)]
    weights_second_across(3)

    def apply_second(p, carry):
        block = q1[p]
        block = block - times(again, block)
        left_out[:, columns(p)] = block * scale
        return carry

    lax.fori_loop(0, pieces, apply_second, 0)
    settle([copy for copy in early if id(copy) not in settled])
    wait_all(recv)
    for dc in range(1, nc):
        total = total + zsum[dc]
    tz[mine] = total
    own = tz.at[mine]
    recv = [send(own, own, device(zz, xx, c, y)) for xx, zz in plane]


    for i in range(4):
        for h in range(2):
            stage_two[h, i, (-1, 1, -1, 1)[i]].wait_recv()
            stage_two_across[h, i].wait_recv()
    wait_all(recv_vgx)

    def input_grad(i, carry):
        total = None
        for slot in range(ny):
            weight = wbuf[lax.div(i, nz), lax.rem(i, nz), :, slot].reshape(BLK, BLK)
            part_sum = mm(vgx[:, slot].reshape(nc * tok, BLK), weight, NT).astype(BF16).astype(F32)
            total = part_sum if total is None else total + part_sum
        total = total.astype(BF16).reshape(nc, tok, BLK)
        gi[:, pl.ds(pl.multiple_of((c * per + i) * BLK, BLK), BLK)] = total[0]
        for dc in range(1, nc):
            outs[dc - 1, :, pl.ds(pl.multiple_of(i * BLK, BLK), BLK)] = total[dc]
        return carry

    lax.fori_loop(0, per, input_grad, 0)
    share_of = gi.at[:, pl.ds(pl.multiple_of(c * per * BLK, BLK), per * BLK)]
    sent_out = [send(outs.at[nc - 1 - dc], share_of, device(z, x, cc, y)) for dc, cc in enumerate(cores, 1)]

    for i in range(0, CHUNKS, 2):
        arrive(from_down, i)
        arrive(from_up, i)
    cotangent = vg_v[...].reshape(ny * tok, BLK).astype(F32).T.astype(BF16)

    def merge(i, n):
        for j0 in (i, i + half):
            from_across[j0].wait_recv()
            for j in range(j0, j0 + n):
                at = pl.ds(j * part, part)
                merged[at, :] = err_v[at, :] + mm(cotangent, actr[:, j].reshape(ny * tok, part)).T

    for i, n in passed_on[:-2]:
        merge(i, n)

    wait_all(recv)
    total = tz[0]
    for i in range(1, per):
        total = total + tz[i]
    r_out[...] = times(weights, total) / float(nb)
    last = [id(from_across[i + h]) for i, _ in passed_on[-2:] for h in (0, half)]
    settle([copy for copy in sent if id(copy) not in settled + last])

    for i, n in passed_on[-2:]:
        merge(i, n)

    wait_all(sent_out)
    settle([copy for copy in sent if id(copy) not in settled])
    assert counter == [send_sem.shape[0], local_sem.shape[0]], counter


def error_kernel(merged, left, right, gi, error_out, left_out, right_out, gi_out, error, sem):
    d = merged.shape[0]
    pieces = error.shape[0]
    rows = d // pieces
    copies = [
        pltpu.make_async_copy(a, b, sem.at[pieces + i])
        for i, (a, b) in enumerate([(gi, gi_out), (left, left_out), (right, right_out)])
    ]
    for copy in copies:
        copy.start()
    hi, lo = split2(right[...] / math.sqrt(float(d)))
    right3 = jnp.concatenate([hi, hi, lo], axis=0)
    for i in range(pieces):
        at = pl.ds(i * rows, rows)
        hi, lo = split2(left[:, at])
        error[i] = merged[at, :] - mm(jnp.concatenate([hi, lo, hi], axis=0), right3, TN)
        copies.append(pltpu.make_async_copy(error.at[i], error_out.at[at], sem.at[i]))
        copies[-1].start()
    for copy in copies:
        copy.wait()


def build(geom):
    nz, nx, nc, ny = geom

    def body(act, vg, w, err, right_prev):
        tok, d = act.shape
        kv = vg.shape[1]
        r = right_prev.shape[1]
        nb = nc * nx * nz
        per = nx * nz
        wide = min(WIDE, per * BLK)
        assert d == nb * BLK and kv == BLK and per * BLK % wide == 0
        sends = 3 * (ny - 1) + 6 + 4 + CHUNKS + 10 + 30 + 3 * (per - 1) + 5 * (nc - 1)
        pieces = w.reshape(nc, nx, nz, 2, BLK // 2, kv)
        inputs = [
            pltpu.with_memory_space_constraint(a, pltpu.HBM) for a in (act, vg, pieces, err[0], right_prev.T)
        ]
        hbm = pl.BlockSpec(memory_space=pltpu.HBM)
        vmem = pl.BlockSpec(memory_space=pltpu.VMEM)
        anywhere = pl.BlockSpec(memory_space=pl.ANY)
        results = (((d, kv), F32), ((r, d), F32), ((r, kv), F32), ((tok, d), BF16))
        made = pl.pallas_call(
            functools.partial(comm_kernel, geom),
            out_shape=tuple(pltpu.VMEM(*shape) for shape in results),
            in_specs=[hbm] * 5,
            out_specs=(vmem,) * 4,
            scratch_shapes=[
                pltpu.VMEM((r, kv), F32),
                pltpu.VMEM((ny, CHUNKS, tok, d // CHUNKS), BF16),
                pltpu.VMEM((ny, tok, kv), BF16),
                pltpu.VMEM((d, kv), F32),
                pltpu.VMEM((ny, r, tok), F32),
                pltpu.VMEM((ny - 1, r, tok), F32),
                pltpu.VMEM((2, tok // 2, kv), BF16),
                pltpu.VMEM((nc, ny, tok, kv), BF16),
                pltpu.VMEM((nx, nz, 2, ny, BLK // 2, kv), BF16),
                pltpu.VMEM((max(nc - 1, 1), tok, per * BLK), BF16),
                pltpu.VMEM((nc, per, r, BLK), F32),
                pltpu.VMEM((nc, per, r, BLK), F32),
                pltpu.VMEM((per, r, BLK), F32),
                pltpu.VMEM((per - 1, r, BLK), F32),
                pltpu.VMEM((ny, r, BLK), F32),
                pltpu.VMEM((d // wide, r, wide), F32),
                pltpu.VMEM((r, tok), F32),
                pltpu.VMEM((ny - 1, r, tok), F32),
                pltpu.VMEM((nc, r, kv), F32),
                pltpu.VMEM((per, r, kv), F32),
                pltpu.SemaphoreType.DMA((1 + 1 + 4 + CHUNKS + ny + 1,)),
                pltpu.SemaphoreType.DMA((sends,)),
                pltpu.SemaphoreType.DMA((sends,)),
            ],
            compiler_params=pltpu.CompilerParams(
                collective_id=0, has_side_effects=True, vmem_limit_bytes=44 * MIB
            ),
        )(*inputs)

        pieces = 16
        error_next, left, right, grad_input = pl.pallas_call(
            error_kernel,
            out_shape=tuple(jax.ShapeDtypeStruct(*shape) for shape in results),
            in_specs=[vmem] * 4,
            out_specs=(anywhere,) * 4,
            scratch_shapes=[pltpu.VMEM((pieces, d // pieces, kv), F32), pltpu.SemaphoreType.DMA((pieces + 3,))],
            compiler_params=pltpu.CompilerParams(vmem_limit_bytes=24 * MIB),
        )(*made)
        return (grad_input, error_next[None], left.T, right.T)

    return body


def solution(mesh):
    return jax.shard_map(
        build((4, 4, 2, 4)),
        mesh=mesh,
        in_specs=(
            P(("dp", "tp"), None),
            P("dp", "tp"),
            P(None, "tp"),
            P("dp", None, "tp"),
            P("tp", None),
        ),
        out_specs=(P(("dp", "tp"), None), P("dp", None, "tp"), P(), P("tp", None)),
        check_vma=False,
    )
```

```python
import functools
import math

import jax
import jax.numpy as jnp
from jax import lax
from jax.experimental import pallas as pl
from jax.experimental.pallas import tpu as pltpu
from jax.sharding import PartitionSpec as P

MESH = pl.DeviceIdType.MESH
F32 = jnp.float32
BF16 = jnp.bfloat16
BLK = 256
EPS = 1e-12
MIB = 1024 * 1024
WIDE = 8 * BLK
CHUNKS = 16
NN = (((1,), (0,)), ((), ()))
NT = (((1,), (1,)), ((), ()))
TN = (((0,), (0,)), ((), ()))


def mm(a, b, dims=NN):
    return lax.dot_general(a, b, dims, preferred_element_type=F32)


def split2(a):
    hi = a.astype(BF16)
    lo = (a - hi.astype(F32)).astype(BF16)
    return hi, lo


def split3(a):
    hi = a.astype(BF16)
    rest = a - hi.astype(F32)
    mid = rest.astype(BF16)
    lo = (rest - mid.astype(F32)).astype(BF16)
    return hi, mid, lo


def rows3(a):
    return jnp.concatenate(split3(a), axis=0)


def fold3(a):
    n = a.shape[0] // 3
    return (a[2 * n :] + a[n : 2 * n]) + a[:n]


def rows2(a):
    return jnp.concatenate(split2(a), axis=0)


def fold2(a):
    n = a.shape[0] // 2
    return a[n:] + a[:n]


def self_products(total, r):
    total = fold3(total)
    return (total[:, 2 * r :] + total[:, r : 2 * r]) + total[:, :r]


def times(a, b):
    a_hi, a_mid, a_lo = (v.astype(F32) for v in split3(a))
    b_hi, b_mid, b_lo = split3(b)
    left = jnp.concatenate([a_lo, a_mid, a_hi, a_mid, a_hi, a_hi], axis=1).astype(BF16)
    return mm(left, jnp.concatenate([b_hi, b_mid, b_lo, b_hi, b_mid, b_hi], axis=0))


def eye_like(n):
    return (lax.broadcasted_iota(jnp.int32, (n, n), 0) == lax.broadcasted_iota(jnp.int32, (n, n), 1)).astype(F32)


def gram_schmidt(gram):
    n = gram.shape[0]
    left, weights = gram, eye_like(n)
    row_id = lax.broadcasted_iota(jnp.int32, (n, 1), 0)
    m = 4
    for j in range(0, n, m):
        columns = [jnp.broadcast_to(left[:, i : i + 1], (n, n)) for i in range(j, j + m)]
        rows = [left[i : i + 1, :] for i in range(j, j + m)]
        given = [weights[i : i + 1, :] for i in range(j, j + m)]
        off_left, off_weights = jnp.zeros((n, n), F32), jnp.zeros((n, n), F32)
        for i in range(m):
            at = j + i
            s = jnp.maximum(columns[i][at : at + 1, :], 0.0)
            inverse = 1.0 / (s + EPS)
            c = (2.0 - s * inverse) * inverse
            f = jnp.where(row_id > at, columns[i] * c, 0.0)
            h = f * (2.0 - c * s)
            for later in range(i + 1, m):
                to = j + later
                columns[later] = columns[later] - h * columns[later][at : at + 1, :]
                rows[later] = rows[later] - h[to : to + 1, :] * rows[i]
                given[later] = given[later] - f[to : to + 1, :] * given[i]
            off_left = off_left + h * rows[i]
            off_weights = off_weights + f * given[i]
        left, weights = left - off_left, weights - off_weights
        yield left, weights


def unit_weights(state):
    left, weights = state
    eye = eye_like(left.shape[0])
    s = jnp.maximum(jnp.sum(left * eye, axis=1, keepdims=True), 0.0)
    return weights / jnp.sqrt(s + EPS), eye * (s / (s + EPS))


def comm_kernel(
    geom, act, vg, w, err, rt_in, merged, left_out, r_out, gi,
    rt, actr, vg_v, err_v, uout, uin, vstage, vgx, wbuf, outs, lacc, lf, rc, rxz, ysum, q1, aout, ain, zsum, tz,
    local_sem, send_sem, recv_sem,
):
    nz, nx, nc, ny = geom
    nb = nc * nx * nz
    per = nx * nz
    _, _, tok, part = actr.shape
    d = part * CHUNKS
    half = CHUNKS // 2
    r = rt.shape[0]
    wide = min(WIDE, per * BLK)
    wb = wide // BLK
    pieces = d // wide
    per_piece = per // wb
    dp, y = lax.axis_index("dp"), lax.axis_index("tp")
    c = lax.rem(dp, nc)
    x = lax.rem(lax.div(dp, nc), nx)
    z = lax.div(dp, nc * nx)
    mine = x * nz + z

    def shifted(i, by, n):
        return lax.rem(i + by, n)

    def device(zz, xx, cc, yy):
        return ((zz * nx + xx) * nc + cc, yy)

    y_peers = [(dy, shifted(y, dy, ny)) for dy in range(1, ny)]
    plane = [
        (shifted(x, dx, nx), shifted(z, dz, nz)) for dx in range(nx) for dz in range(nz) if (dx, dz) != (0, 0)
    ]
    cores = [shifted(c, dc, nc) for dc in range(1, nc)]
    up, down, across = shifted(y, 1, ny), shifted(y, ny - 1, ny), shifted(y, 2, ny)

    sent, settled = [], []
    counter = [0, 0]

    def describe(src, dst, to):
        i = counter[0]
        counter[0] += 1
        copy = pltpu.make_async_remote_copy(
            src_ref=src, dst_ref=dst, send_sem=send_sem.at[i], recv_sem=recv_sem.at[i], device_id=to, device_id_type=MESH
        )
        sent.append(copy)
        return copy

    def send(src, dst, to):
        copy = describe(src, dst, to)
        copy.start()
        return copy

    def send_both(one, other):
        one, other = describe(*one), describe(*other)

        @pl.when(c == 0)
        def _():
            one.start()
            other.start()

        @pl.when(c != 0)
        def _():
            other.start()
            one.start()

        return one, other

    def fetch(src, dst):
        i = counter[1]
        counter[1] += 1
        copy = pltpu.make_async_copy(src, dst, local_sem.at[i])
        copy.start()
        return copy

    def wait_all(copies):
        for copy in copies:
            copy.wait_recv()

    def settle(copies):
        for copy in copies:
            copy.wait_send()
        settled.extend(id(copy) for copy in copies)

    def tokens(yy):
        return pl.ds(pl.multiple_of(yy * tok, tok), tok)

    barrier = pltpu.get_barrier_semaphore()
    everyone = (
        [device(z, x, c, yy) for _, yy in y_peers]
        + [device(z, x, cc, y) for cc in cores]
        + [device(zz, xx, c, y) for xx, zz in plane]
    )
    for peer in everyone:
        pl.semaphore_signal(barrier, inc=1, device_id=peer, device_id_type=MESH)

    load_rt = fetch(rt_in, rt)
    load_vg = [fetch(vg.at[tokens(yy)], vg_v.at[i]) for i, yy in enumerate((y, up, across, down))]
    share = d // 4
    load_err = [fetch(err.at[pl.ds(i * share, share)], err_v.at[pl.ds(i * share, share)]) for i in range(4)]
    pl.semaphore_wait(barrier, len(everyone))

    from_down, from_up, from_across = {}, {}, {}

    def cols(i):
        return pl.ds(i * part, part)

    def direct(*numbers):
        for i in numbers:
            j = (i + half) % CHUNKS
            from_down[i], from_up[j] = send_both(
                (act.at[:, cols(i)], actr.at[3, i], device(z, x, c, up)),
                (act.at[:, cols(j)], actr.at[1, j], device(z, x, c, down)),
            )

    def forward(*numbers):
        for i in numbers:
            j = i + half
            from_down[i].wait_recv()
            from_up[j].wait_recv()
            from_across[i], from_across[j] = send_both(
                (actr.at[3, i], actr.at[2, i], device(z, x, c, up)),
                (actr.at[1, j], actr.at[2, j], device(z, x, c, down)),
            )


    recv_vg = [send(vg.at[tokens(up)], vgx.at[0, 3], device(z, x, c, up))]
    recv_vg.append(send(vg.at[tokens(down)], vgx.at[0, 1], device(z, x, c, down)))
    few = tok // 2
    ways = (up, down)
    vg_passing = [
        send(vg.at[pl.ds(pl.multiple_of(across * tok + h * few, few), few)], vstage.at[h], device(z, x, c, ways[h]))
        for h in range(2)
    ]
    direct(0)
    load_act = {
        i: fetch(act.at[:, cols(i)], actr.at[0, i]) for j in range(half) for i in (j, j + half)
    }
    load_vgx = fetch(vg.at[tokens(y)], vgx.at[0, 0])
    load_w = fetch(w.at[c], wbuf.at[:, :, :, 0])

    load_rt.wait()
    rt3 = rows3(rt[...])
    for load in load_vg:
        load.wait()
    for dy in range(ny):
        uout[dy] = fold3(mm(rt3, vg_v[dy], NT))
    recv_u = [send(uout.at[dy], uin.at[dy - 1], device(z, x, c, yy)) for dy, yy in y_peers]

    own_w = w.at[c, x, z]
    w_from_down, w_from_up = send_both(
        (own_w, wbuf.at[x, z, :, 3], device(z, x, c, up)), (own_w, wbuf.at[x, z, :, 1], device(z, x, c, down))
    )
    direct(1, 2)

    def place(h, a, b):
        return (a, b) if h == 0 else (b, a)

    def piece(h, first, second):
        zz, xx = place(h, first, second)
        return wbuf.at[xx, zz, h, 1:ny]

    def neighbour(h, stage, way):
        n = (nz if h == 0 else nx) if stage == 0 else (nx if h == 0 else nz)
        first, second = place(h, z, x)
        if stage == 0:
            first = shifted(first, way % n, n)
        else:
            second = shifted(second, way % n, n)
        zz, xx = place(h, first, second)
        return device(zz, xx, c, y)

    half_here = [(place(h, z, x), place(h, nz, nx)) for h in range(2)]
    stage_one, stage_one_across, stage_two, stage_two_across = {}, {}, {}, {}

    def weights_first():
        for h in range(2):
            (first, second), _ = half_here[h]
            own = piece(h, first, second)
            stage_one[h, 1], stage_one[h, -1] = send_both(
                (own, own, neighbour(h, 0, 1)), (own, own, neighbour(h, 0, -1))
            )

    def weights_across():
        for h in range(2):
            (first, second), (n, _) = half_here[h]
            way = 1 - 2 * h
            stage_one[h, way].wait_recv()
            came = piece(h, shifted(first, -way % n, n), second)
            stage_one_across[h] = send(came, came, neighbour(h, 0, way))

    def weights_second(i):
        for h in range(2):
            (first, second), (n, _) = half_here[h]
            if i in (1, 2):
                way = 3 - 2 * i
                if way != 1 - 2 * h:
                    stage_one[h, way].wait_recv()
                first = shifted(first, -way % n, n)
            elif i == 3:
                stage_one_across[h].wait_recv()
                first = shifted(first, 2, n)
            here = piece(h, first, second)
            stage_two[h, i, 1], stage_two[h, i, -1] = send_both(
                (here, here, neighbour(h, 1, 1)), (here, here, neighbour(h, 1, -1))
            )

    def weights_second_across(i):
        for h in range(2):
            (first, second), (n, m) = half_here[h]
            first = shifted(first, (0, n - 1, 1, 2)[i], n)
            way = (1, -1, 1, -1)[i]
            stage_two[h, i, way].wait_recv()
            came = piece(h, first, shifted(second, -way % m, m))
            stage_two_across[h, i] = send(came, came, neighbour(h, 1, way))

    rt2 = rt3[: 2 * r]

    def columns(p):
        return pl.ds(pl.multiple_of(p * wide, wide), wide)

    def store_left(value, cc, j0):
        for j in range(wb):
            lacc[cc, j0 + j] = value[:, j * BLK : (j + 1) * BLK]

    def load_left(ref, cc, j0):
        return jnp.concatenate([ref[cc, j0 + j] for j in range(wb)], axis=1)

    for load in load_err:
        load.wait()

    def err_left(p, carry):
        hi, lo = split2(err_v[columns(p), :])
        store_left(fold2(mm(rt2, lo, NT) + mm(rt2, hi, NT)), lax.div(p, per_piece), lax.rem(p, per_piece) * wb)
        return carry

    lax.fori_loop(0, pieces, err_left, 0)

    wait_all(recv_u)
    ut = uout[0]
    for dy in range(ny - 1):
        ut = ut + uin[dy]
    ut3 = rows3(ut)
    for load in load_act.values():
        load.wait()

    def own_act(p):
        n = wide // part
        if n >= 1:
            return jnp.concatenate([actr[0, p * n + i] for i in range(n)], axis=1)
        n = part // wide
        inside = pl.ds(pl.multiple_of(lax.rem(p, n) * wide, wide), wide)
        return actr[0, lax.div(p, n), :, inside]

    def act_left(cc):
        def step(i, carry):
            value = fold3(mm(ut3, own_act(cc * per_piece + i)))
            store_left(load_left(lacc, cc, i * wb) + value, cc, i * wb)
            return carry

        lax.fori_loop(0, per_piece, step, 0)

    recv = []
    for cc in cores:
        act_left(cc)
        recv.append(send(lacc.at[cc], rc, device(z, x, cc, y)))
    act_left(c)

    recv_core = recv
    direct(3)
    load_vgx.wait()
    for h in range(2):
        vg_passing[h].wait_recv()
        recv_vg.append(send(vstage.at[h], vgx.at[0, 2, h * few : (h + 1) * few], device(z, x, c, ways[h])))
    wait_all(recv)
    lacc[c] += rc[...]
    recv = [
        send(lacc.at[c, xx * nz + zz], rxz.at[i], device(zz, xx, c, y)) for i, (xx, zz) in enumerate(plane)
    ]
    load_w.wait()
    w_from_down.wait_recv()
    w_halves = [send(wbuf.at[x, z, 0, 3], wbuf.at[x, z, 0, 2], device(z, x, c, up))]
    w_from_up.wait_recv()
    w_halves.append(send(wbuf.at[x, z, 1, 1], wbuf.at[x, z, 1, 2], device(z, x, c, down)))
    direct(4, 5)
    settle(recv_u + recv_core)
    recv_rs = recv
    wait_all(recv)
    total = lacc[c, mine]
    for i in range(len(plane)):
        total = total + rxz[i]
    ysum[y] = total
    own = ysum.at[y]
    recv = [send(own, own, device(z, x, c, yy)) for _, yy in y_peers]
    direct(*range(6, 12))
    wait_all(w_halves)
    weights_first()
    weights_second(0)
    settle(recv_rs)
    wait_all(recv)
    total = ysum[0]
    for yy in range(1, ny):
        total = total + ysum[yy]
    lf[c, mine] = total
    own = lf.at[c, mine]
    recv_y = recv
    recv = [send(own, own, device(zz, xx, c, y)) for xx, zz in plane]
    weights_across()
    weights_second(1)
    weights_second(2)
    settle(recv_y)
    wait_all(recv)
    recv_ag = recv
    own = lf.at[c]
    recv = [send(own, own, device(z, x, cc, y)) for cc in cores]
    weights_second(3)
    weights_second_across(0)
    settle(recv_ag)

    wait_all(recv_vg)
    recv_vgx = [send(vgx.at[0], vgx.at[dc], device(z, x, cc, y)) for dc, cc in enumerate(cores, 1)]
    settle(vg_passing + recv_vg + [w_from_down, w_from_up] + w_halves + list(stage_one.values()))
    wait_all(recv)

    def left_piece(p):
        return rows3(load_left(lf, lax.div(p, per_piece), lax.rem(p, per_piece) * wb))

    def products(p, carry):
        gram, by_act = carry
        block = left_piece(p)
        return gram + mm(block, block, NT), by_act + mm(block[: 2 * r], own_act(p), NT)

    gram, by_act = lax.fori_loop(
        0, pieces, products, (jnp.zeros((3 * r, 3 * r), F32), jnp.zeros((2 * r, tok), F32))
    )
    aout[...] = fold2(by_act)
    early = list(sent)
    recv_a = [send(aout, ain.at[dy - 1], device(z, x, c, yy)) for dy, yy in y_peers]
    direct(*range(12, CHUNKS))
    forward(*range(half))
    weights_second_across(1)
    weights_second_across(2)

    total = jnp.zeros((2 * r, err_v.shape[1]), F32)
    count = nb // (r // 4)
    for i, state in enumerate(gram_schmidt(self_products(gram, r))):
        block = jnp.concatenate([lf[(i * count + j) // per, (i * count + j) % per] for j in range(count)], axis=1)
        hi, lo = split2(err_v[i * count * BLK : (i + 1) * count * BLK, :])
        block = rows2(block)
        total = total + (mm(block, lo) + mm(block, hi))
    total = fold2(total)
    weights, norms = unit_weights(state)

    def apply_first(p, gram):
        block = times(weights, load_left(lf, lax.div(p, per_piece), lax.rem(p, per_piece) * wb))
        q1[p] = block
        block = rows3(block)
        return gram + mm(block, block, NT)

    off = self_products(lax.fori_loop(0, pieces, apply_first, jnp.zeros((3 * r, 3 * r), F32)), r) - norms
    row_id = lax.broadcasted_iota(jnp.int32, (r, r), 0)
    col_id = lax.broadcasted_iota(jnp.int32, (r, r), 1)
    again = jnp.where(col_id < row_id, off, jnp.where(col_id == row_id, 0.5 * off, 0.0))
    weights = weights - times(again, weights)
    scale = math.sqrt(float(d))

    wait_all(recv_a)
    for slot in range(ny):
        total = total + fold3(mm(rows3(aout[...] if slot == 0 else ain[ny - slot - 1]), vg_v[slot]))
    zsum[0] = total
    recv = [send(zsum.at[0], zsum.at[dc], device(z, x, cc, y)) for dc, cc in enumerate(cores, 1)]
    weights_second_across(3)

    def apply_second(p, carry):
        block = q1[p]
        block = block - times(again, block)
        left_out[:, columns(p)] = block * scale
        return carry

    lax.fori_loop(0, pieces, apply_second, 0)
    settle([copy for copy in early if id(copy) not in settled])
    wait_all(recv)
    for dc in range(1, nc):
        total = total + zsum[dc]
    tz[mine] = total
    own = tz.at[mine]
    recv = [send(own, own, device(zz, xx, c, y)) for xx, zz in plane]


    for i in range(4):
        for h in range(2):
            stage_two[h, i, (-1, 1, -1, 1)[i]].wait_recv()
            stage_two_across[h, i].wait_recv()
    wait_all(recv_vgx)

    def input_grad(i, carry):
        total = None
        for slot in range(ny):
            weight = wbuf[lax.div(i, nz), lax.rem(i, nz), :, slot].reshape(BLK, BLK)
            part_sum = mm(vgx[:, slot].reshape(nc * tok, BLK), weight, NT).astype(BF16).astype(F32)
            total = part_sum if total is None else total + part_sum
        total = total.astype(BF16).reshape(nc, tok, BLK)
        gi[:, pl.ds(pl.multiple_of((c * per + i) * BLK, BLK), BLK)] = total[0]
        for dc in range(1, nc):
            outs[dc - 1, :, pl.ds(pl.multiple_of(i * BLK, BLK), BLK)] = total[dc]
        return carry

    lax.fori_loop(0, per, input_grad, 0)
    share_of = gi.at[:, pl.ds(pl.multiple_of(c * per * BLK, BLK), per * BLK)]
    sent_out = [send(outs.at[nc - 1 - dc], share_of, device(z, x, cc, y)) for dc, cc in enumerate(cores, 1)]

    for i in range(CHUNKS):
        if i >= half:
            from_down[i].wait_recv()
        else:
            from_up[i].wait_recv()
    cotangent = vg_v[...].reshape(ny * tok, BLK).astype(F32).T.astype(BF16)

    def merge(j):
        from_across[j].wait_recv()
        at = pl.ds(j * part, part)
        merged[at, :] = err_v[at, :] + mm(cotangent, actr[:, j].reshape(ny * tok, part)).T

    for i in range(half - 2):
        merge(i)
        merge(i + half)

    wait_all(recv)
    total = tz[0]
    for i in range(1, per):
        total = total + tz[i]
    r_out[...] = times(weights, total) / float(nb)
    last = [id(from_across[i + h]) for i in range(half - 2, half) for h in (0, half)]
    settle([copy for copy in sent if id(copy) not in settled + last])

    for i in range(half - 2, half):
        merge(i)
        merge(i + half)

    wait_all(sent_out)
    settle([copy for copy in sent if id(copy) not in settled])
    assert counter == [send_sem.shape[0], local_sem.shape[0]], counter


def error_kernel(merged, left, right, gi, error_out, left_out, right_out, gi_out, error, sem):
    d = merged.shape[0]
    pieces = error.shape[0]
    rows = d // pieces
    copies = [
        pltpu.make_async_copy(a, b, sem.at[pieces + i])
        for i, (a, b) in enumerate([(gi, gi_out), (left, left_out), (right, right_out)])
    ]
    for copy in copies:
        copy.start()
    hi, lo = split2(right[...] / math.sqrt(float(d)))
    right3 = jnp.concatenate([hi, hi, lo], axis=0)
    for i in range(pieces):
        at = pl.ds(i * rows, rows)
        hi, lo = split2(left[:, at])
        error[i] = merged[at, :] - mm(jnp.concatenate([hi, lo, hi], axis=0), right3, TN)
        copies.append(pltpu.make_async_copy(error.at[i], error_out.at[at], sem.at[i]))
        copies[-1].start()
    for copy in copies:
        copy.wait()


def build(geom):
    nz, nx, nc, ny = geom

    def body(act, vg, w, err, right_prev):
        tok, d = act.shape
        kv = vg.shape[1]
        r = right_prev.shape[1]
        nb = nc * nx * nz
        per = nx * nz
        wide = min(WIDE, per * BLK)
        assert d == nb * BLK and kv == BLK and per * BLK % wide == 0
        sends = 3 * (ny - 1) + 6 + 4 + 3 * CHUNKS + 30 + 3 * (per - 1) + 5 * (nc - 1)
        pieces = w.reshape(nc, nx, nz, 2, BLK // 2, kv)
        inputs = [
            pltpu.with_memory_space_constraint(a, pltpu.HBM) for a in (act, vg, pieces, err[0], right_prev.T)
        ]
        hbm = pl.BlockSpec(memory_space=pltpu.HBM)
        vmem = pl.BlockSpec(memory_space=pltpu.VMEM)
        anywhere = pl.BlockSpec(memory_space=pl.ANY)
        results = (((d, kv), F32), ((r, d), F32), ((r, kv), F32), ((tok, d), BF16))
        made = pl.pallas_call(
            functools.partial(comm_kernel, geom),
            out_shape=tuple(pltpu.VMEM(*shape) for shape in results),
            in_specs=[hbm] * 5,
            out_specs=(vmem,) * 4,
            scratch_shapes=[
                pltpu.VMEM((r, kv), F32),
                pltpu.VMEM((ny, CHUNKS, tok, d // CHUNKS), BF16),
                pltpu.VMEM((ny, tok, kv), BF16),
                pltpu.VMEM((d, kv), F32),
                pltpu.VMEM((ny, r, tok), F32),
                pltpu.VMEM((ny - 1, r, tok), F32),
                pltpu.VMEM((2, tok // 2, kv), BF16),
                pltpu.VMEM((nc, ny, tok, kv), BF16),
                pltpu.VMEM((nx, nz, 2, ny, BLK // 2, kv), BF16),
                pltpu.VMEM((max(nc - 1, 1), tok, per * BLK), BF16),
                pltpu.VMEM((nc, per, r, BLK), F32),
                pltpu.VMEM((nc, per, r, BLK), F32),
                pltpu.VMEM((per, r, BLK), F32),
                pltpu.VMEM((per - 1, r, BLK), F32),
                pltpu.VMEM((ny, r, BLK), F32),
                pltpu.VMEM((d // wide, r, wide), F32),
                pltpu.VMEM((r, tok), F32),
                pltpu.VMEM((ny - 1, r, tok), F32),
                pltpu.VMEM((nc, r, kv), F32),
                pltpu.VMEM((per, r, kv), F32),
                pltpu.SemaphoreType.DMA((1 + 1 + 4 + CHUNKS + ny + 1,)),
                pltpu.SemaphoreType.DMA((sends,)),
                pltpu.SemaphoreType.DMA((sends,)),
            ],
            compiler_params=pltpu.CompilerParams(
                collective_id=0, has_side_effects=True, vmem_limit_bytes=44 * MIB
            ),
        )(*inputs)

        pieces = 16
        error_next, left, right, grad_input = pl.pallas_call(
            error_kernel,
            out_shape=tuple(jax.ShapeDtypeStruct(*shape) for shape in results),
            in_specs=[vmem] * 4,
            out_specs=(anywhere,) * 4,
            scratch_shapes=[pltpu.VMEM((pieces, d // pieces, kv), F32), pltpu.SemaphoreType.DMA((pieces + 3,))],
            compiler_params=pltpu.CompilerParams(vmem_limit_bytes=24 * MIB),
        )(*made)
        return (grad_input, error_next[None], left.T, right.T)

    return body


def solution(mesh):
    return jax.shard_map(
        build((4, 4, 2, 4)),
        mesh=mesh,
        in_specs=(
            P(("dp", "tp"), None),
            P("dp", "tp"),
            P(None, "tp"),
            P("dp", None, "tp"),
            P("tp", None),
        ),
        out_specs=(P(("dp", "tp"), None), P("dp", None, "tp"), P(), P("tp", None)),
        check_vma=False,
    )
```

```python
import functools
import math

import jax
import jax.numpy as jnp
from jax import lax
from jax.experimental import pallas as pl
from jax.experimental.pallas import tpu as pltpu
from jax.sharding import PartitionSpec as P

MESH = pl.DeviceIdType.MESH
F32 = jnp.float32
BF16 = jnp.bfloat16
BLK = 256
EPS = 1e-12
MIB = 1024 * 1024
WIDE = 8 * BLK
CHUNKS = 16
NN = (((1,), (0,)), ((), ()))
NT = (((1,), (1,)), ((), ()))
TN = (((0,), (0,)), ((), ()))


def mm(a, b, dims=NN):
    return lax.dot_general(a, b, dims, preferred_element_type=F32)


def split2(a):
    hi = a.astype(BF16)
    lo = (a - hi.astype(F32)).astype(BF16)
    return hi, lo


def split3(a):
    hi = a.astype(BF16)
    rest = a - hi.astype(F32)
    mid = rest.astype(BF16)
    lo = (rest - mid.astype(F32)).astype(BF16)
    return hi, mid, lo


def rows3(a):
    return jnp.concatenate(split3(a), axis=0)


def fold3(a):
    n = a.shape[0] // 3
    return (a[2 * n :] + a[n : 2 * n]) + a[:n]


def rows2(a):
    return jnp.concatenate(split2(a), axis=0)


def fold2(a):
    n = a.shape[0] // 2
    return a[n:] + a[:n]


def self_products(total, r):
    total = fold3(total)
    return (total[:, 2 * r :] + total[:, r : 2 * r]) + total[:, :r]


def times(a, b):
    a_hi, a_mid, a_lo = (v.astype(F32) for v in split3(a))
    b_hi, b_mid, b_lo = split3(b)
    left = jnp.concatenate([a_lo, a_mid, a_hi, a_mid, a_hi, a_hi], axis=1).astype(BF16)
    return mm(left, jnp.concatenate([b_hi, b_mid, b_lo, b_hi, b_mid, b_hi], axis=0))


def eye_like(n):
    return (lax.broadcasted_iota(jnp.int32, (n, n), 0) == lax.broadcasted_iota(jnp.int32, (n, n), 1)).astype(F32)


def gram_schmidt(gram):
    n = gram.shape[0]
    left, weights = gram, eye_like(n)
    row_id = lax.broadcasted_iota(jnp.int32, (n, 1), 0)
    m = 4
    for j in range(0, n, m):
        columns = [jnp.broadcast_to(left[:, i : i + 1], (n, n)) for i in range(j, j + m)]
        rows = [left[i : i + 1, :] for i in range(j, j + m)]
        given = [weights[i : i + 1, :] for i in range(j, j + m)]
        off_left, off_weights = jnp.zeros((n, n), F32), jnp.zeros((n, n), F32)
        for i in range(m):
            at = j + i
            s = jnp.maximum(columns[i][at : at + 1, :], 0.0)
            inverse = 1.0 / (s + EPS)
            c = (2.0 - s * inverse) * inverse
            f = jnp.where(row_id > at, columns[i] * c, 0.0)
            h = f * (2.0 - c * s)
            for later in range(i + 1, m):
                to = j + later
                columns[later] = columns[later] - h * columns[later][at : at + 1, :]
                rows[later] = rows[later] - h[to : to + 1, :] * rows[i]
                given[later] = given[later] - f[to : to + 1, :] * given[i]
            off_left = off_left + h * rows[i]
            off_weights = off_weights + f * given[i]
        left, weights = left - off_left, weights - off_weights
        yield left, weights


def unit_weights(state):
    left, weights = state
    eye = eye_like(left.shape[0])
    s = jnp.maximum(jnp.sum(left * eye, axis=1, keepdims=True), 0.0)
    return weights / jnp.sqrt(s + EPS), eye * (s / (s + EPS))


def comm_kernel(
    geom, act, vg, w, err, rt_in, merged, left_out, r_out, gi,
    rt, actr, vg_v, err_v, uout, uin, vstage, vgx, wbuf, outs, lacc, lf, rc, rxz, ysum, q1, aout, ain, zsum, tz,
    local_sem, send_sem, recv_sem,
):
    nz, nx, nc, ny = geom
    nb = nc * nx * nz
    per = nx * nz
    _, _, tok, part = actr.shape
    d = part * CHUNKS
    half = CHUNKS // 2
    r = rt.shape[0]
    wide = min(WIDE, per * BLK)
    wb = wide // BLK
    pieces = d // wide
    per_piece = per // wb
    dp, y = lax.axis_index("dp"), lax.axis_index("tp")
    c = lax.rem(dp, nc)
    x = lax.rem(lax.div(dp, nc), nx)
    z = lax.div(dp, nc * nx)
    mine = x * nz + z

    def shifted(i, by, n):
        return lax.rem(i + by, n)

    def device(zz, xx, cc, yy):
        return ((zz * nx + xx) * nc + cc, yy)

    y_peers = [(dy, shifted(y, dy, ny)) for dy in range(1, ny)]
    plane = [
        (shifted(x, dx, nx), shifted(z, dz, nz)) for dx in range(nx) for dz in range(nz) if (dx, dz) != (0, 0)
    ]
    cores = [shifted(c, dc, nc) for dc in range(1, nc)]
    up, down, across = shifted(y, 1, ny), shifted(y, ny - 1, ny), shifted(y, 2, ny)

    sent, settled = [], []
    counter = [0, 0]

    def describe(src, dst, to):
        i = counter[0]
        counter[0] += 1
        copy = pltpu.make_async_remote_copy(
            src_ref=src, dst_ref=dst, send_sem=send_sem.at[i], recv_sem=recv_sem.at[i], device_id=to, device_id_type=MESH
        )
        sent.append(copy)
        return copy

    def send(src, dst, to):
        copy = describe(src, dst, to)
        copy.start()
        return copy

    def send_both(one, other):
        one, other = describe(*one), describe(*other)

        @pl.when(c == 0)
        def _():
            one.start()
            other.start()

        @pl.when(c != 0)
        def _():
            other.start()
            one.start()

        return one, other

    def fetch(src, dst):
        i = counter[1]
        counter[1] += 1
        copy = pltpu.make_async_copy(src, dst, local_sem.at[i])
        copy.start()
        return copy

    def wait_all(copies):
        for copy in copies:
            copy.wait_recv()

    def settle(copies):
        for copy in copies:
            copy.wait_send()
        settled.extend(id(copy) for copy in copies)

    def tokens(yy):
        return pl.ds(pl.multiple_of(yy * tok, tok), tok)

    barrier = pltpu.get_barrier_semaphore()
    everyone = (
        [device(z, x, c, yy) for _, yy in y_peers]
        + [device(z, x, cc, y) for cc in cores]
        + [device(zz, xx, c, y) for xx, zz in plane]
    )
    for peer in everyone:
        pl.semaphore_signal(barrier, inc=1, device_id=peer, device_id_type=MESH)

    load_rt = fetch(rt_in, rt)
    load_vg = [fetch(vg.at[tokens(yy)], vg_v.at[i]) for i, yy in enumerate((y, up, across, down))]
    share = d // 4
    load_err = [fetch(err.at[pl.ds(i * share, share)], err_v.at[pl.ds(i * share, share)]) for i in range(4)]
    pl.semaphore_wait(barrier, len(everyone))

    from_down, from_up, from_across = {}, {}, {}

    def cols(i):
        return pl.ds(i * part, part)

    def direct(*numbers):
        for i in numbers:
            j = (i + half) % CHUNKS
            from_down[i], from_up[j] = send_both(
                (act.at[:, cols(i)], actr.at[3, i], device(z, x, c, up)),
                (act.at[:, cols(j)], actr.at[1, j], device(z, x, c, down)),
            )

    passed_on = [(i, 0, part) for i in range(half - 1)]
    passed_on += [(half - 1, 0, part // 2), (half - 1, part // 2, part)]

    def forward():
        for i, lo, hi in passed_on:
            j = i + half
            if lo == 0:
                from_down[i].wait_recv()
                from_up[j].wait_recv()
            from_across[i, lo], from_across[j, lo] = send_both(
                (actr.at[3, i, :, lo:hi], actr.at[2, i, :, lo:hi], device(z, x, c, up)),
                (actr.at[1, j, :, lo:hi], actr.at[2, j, :, lo:hi], device(z, x, c, down)),
            )

    recv_vg = [send(vg.at[tokens(up)], vgx.at[0, 3], device(z, x, c, up))]
    recv_vg.append(send(vg.at[tokens(down)], vgx.at[0, 1], device(z, x, c, down)))
    few = tok // 2
    ways = (up, down)
    vg_passing = [
        send(vg.at[pl.ds(pl.multiple_of(across * tok + h * few, few), few)], vstage.at[h], device(z, x, c, ways[h]))
        for h in range(2)
    ]
    direct(0)
    load_act = {
        i: fetch(act.at[:, cols(i)], actr.at[0, i]) for j in range(half) for i in (j, j + half)
    }
    load_vgx = fetch(vg.at[tokens(y)], vgx.at[0, 0])
    load_w = fetch(w.at[c], wbuf.at[:, :, :, 0])

    load_rt.wait()
    rt3 = rows3(rt[...])
    for load in load_vg:
        load.wait()
    for dy in range(ny):
        uout[dy] = fold3(mm(rt3, vg_v[dy], NT))
    recv_u = [send(uout.at[dy], uin.at[dy - 1], device(z, x, c, yy)) for dy, yy in y_peers]

    own_w = w.at[c, x, z]
    w_from_down, w_from_up = send_both(
        (own_w, wbuf.at[x, z, :, 3], device(z, x, c, up)), (own_w, wbuf.at[x, z, :, 1], device(z, x, c, down))
    )
    direct(1, 2)

    def place(h, a, b):
        return (a, b) if h == 0 else (b, a)

    def piece(h, first, second):
        zz, xx = place(h, first, second)
        return wbuf.at[xx, zz, h, 1:ny]

    def neighbour(h, stage, way):
        n = (nz if h == 0 else nx) if stage == 0 else (nx if h == 0 else nz)
        first, second = place(h, z, x)
        if stage == 0:
            first = shifted(first, way % n, n)
        else:
            second = shifted(second, way % n, n)
        zz, xx = place(h, first, second)
        return device(zz, xx, c, y)

    half_here = [(place(h, z, x), place(h, nz, nx)) for h in range(2)]
    stage_one, stage_one_across, stage_two, stage_two_across = {}, {}, {}, {}

    def weights_first():
        for h in range(2):
            (first, second), _ = half_here[h]
            own = piece(h, first, second)
            stage_one[h, 1], stage_one[h, -1] = send_both(
                (own, own, neighbour(h, 0, 1)), (own, own, neighbour(h, 0, -1))
            )

    def weights_across():
        for h in range(2):
            (first, second), (n, _) = half_here[h]
            way = 1 - 2 * h
            stage_one[h, way].wait_recv()
            came = piece(h, shifted(first, -way % n, n), second)
            stage_one_across[h] = send(came, came, neighbour(h, 0, way))

    def weights_second(i):
        for h in range(2):
            (first, second), (n, _) = half_here[h]
            if i in (1, 2):
                way = 3 - 2 * i
                if way != 1 - 2 * h:
                    stage_one[h, way].wait_recv()
                first = shifted(first, -way % n, n)
            elif i == 3:
                stage_one_across[h].wait_recv()
                first = shifted(first, 2, n)
            here = piece(h, first, second)
            stage_two[h, i, 1], stage_two[h, i, -1] = send_both(
                (here, here, neighbour(h, 1, 1)), (here, here, neighbour(h, 1, -1))
            )

    def weights_second_across(i):
        for h in range(2):
            (first, second), (n, m) = half_here[h]
            first = shifted(first, (0, n - 1, 1, 2)[i], n)
            way = (1, -1, 1, -1)[i]
            stage_two[h, i, way].wait_recv()
            came = piece(h, first, shifted(second, -way % m, m))
            stage_two_across[h, i] = send(came, came, neighbour(h, 1, way))

    rt2 = rt3[: 2 * r]

    def columns(p):
        return pl.ds(pl.multiple_of(p * wide, wide), wide)

    def store_left(value, cc, j0):
        for j in range(wb):
            lacc[cc, j0 + j] = value[:, j * BLK : (j + 1) * BLK]

    def load_left(ref, cc, j0):
        return jnp.concatenate([ref[cc, j0 + j] for j in range(wb)], axis=1)

    for load in load_err:
        load.wait()

    def err_left(p, carry):
        hi, lo = split2(err_v[columns(p), :])
        store_left(fold2(mm(rt2, lo, NT) + mm(rt2, hi, NT)), lax.div(p, per_piece), lax.rem(p, per_piece) * wb)
        return carry

    lax.fori_loop(0, pieces, err_left, 0)

    wait_all(recv_u)
    ut = uout[0]
    for dy in range(ny - 1):
        ut = ut + uin[dy]
    ut3 = rows3(ut)
    for load in load_act.values():
        load.wait()

    def own_act(p):
        n = wide // part
        if n >= 1:
            return jnp.concatenate([actr[0, p * n + i] for i in range(n)], axis=1)
        n = part // wide
        inside = pl.ds(pl.multiple_of(lax.rem(p, n) * wide, wide), wide)
        return actr[0, lax.div(p, n), :, inside]

    def act_left(cc):
        def step(i, carry):
            value = fold3(mm(ut3, own_act(cc * per_piece + i)))
            store_left(load_left(lacc, cc, i * wb) + value, cc, i * wb)
            return carry

        lax.fori_loop(0, per_piece, step, 0)

    recv = []
    for cc in cores:
        act_left(cc)
        recv.append(send(lacc.at[cc], rc, device(z, x, cc, y)))
    act_left(c)

    recv_core = recv
    direct(3)
    load_vgx.wait()
    for h in range(2):
        vg_passing[h].wait_recv()
        recv_vg.append(send(vstage.at[h], vgx.at[0, 2, h * few : (h + 1) * few], device(z, x, c, ways[h])))
    wait_all(recv)
    lacc[c] += rc[...]
    recv = [
        send(lacc.at[c, xx * nz + zz], rxz.at[i], device(zz, xx, c, y)) for i, (xx, zz) in enumerate(plane)
    ]
    load_w.wait()
    w_from_down.wait_recv()
    w_halves = [send(wbuf.at[x, z, 0, 3], wbuf.at[x, z, 0, 2], device(z, x, c, up))]
    w_from_up.wait_recv()
    w_halves.append(send(wbuf.at[x, z, 1, 1], wbuf.at[x, z, 1, 2], device(z, x, c, down)))
    direct(4, 5)
    settle(recv_u + recv_core)
    recv_rs = recv
    wait_all(recv)
    total = lacc[c, mine]
    for i in range(len(plane)):
        total = total + rxz[i]
    ysum[y] = total
    own = ysum.at[y]
    recv = [send(own, own, device(z, x, c, yy)) for _, yy in y_peers]
    direct(*range(6, 12))
    wait_all(w_halves)
    weights_first()
    weights_second(0)
    settle(recv_rs)
    wait_all(recv)
    total = ysum[0]
    for yy in range(1, ny):
        total = total + ysum[yy]
    lf[c, mine] = total
    own = lf.at[c, mine]
    recv_y = recv
    recv = [send(own, own, device(zz, xx, c, y)) for xx, zz in plane]
    weights_across()
    weights_second(1)
    weights_second(2)
    settle(recv_y)
    wait_all(recv)
    recv_ag = recv
    own = lf.at[c]
    recv = [send(own, own, device(z, x, cc, y)) for cc in cores]
    weights_second(3)
    weights_second_across(0)
    settle(recv_ag)

    wait_all(recv_vg)
    recv_vgx = [send(vgx.at[0], vgx.at[dc], device(z, x, cc, y)) for dc, cc in enumerate(cores, 1)]
    settle(vg_passing + recv_vg + [w_from_down, w_from_up] + w_halves + list(stage_one.values()))
    wait_all(recv)

    def left_piece(p):
        return rows3(load_left(lf, lax.div(p, per_piece), lax.rem(p, per_piece) * wb))

    def products(p, carry):
        gram, by_act = carry
        block = left_piece(p)
        return gram + mm(block, block, NT), by_act + mm(block[: 2 * r], own_act(p), NT)

    gram, by_act = lax.fori_loop(
        0, pieces, products, (jnp.zeros((3 * r, 3 * r), F32), jnp.zeros((2 * r, tok), F32))
    )
    aout[...] = fold2(by_act)
    early = list(sent)
    recv_a = [send(aout, ain.at[dy - 1], device(z, x, c, yy)) for dy, yy in y_peers]
    direct(*range(12, CHUNKS))
    forward()
    weights_second_across(1)
    weights_second_across(2)

    total = jnp.zeros((2 * r, err_v.shape[1]), F32)
    count = nb // (r // 4)
    for i, state in enumerate(gram_schmidt(self_products(gram, r))):
        block = jnp.concatenate([lf[(i * count + j) // per, (i * count + j) % per] for j in range(count)], axis=1)
        hi, lo = split2(err_v[i * count * BLK : (i + 1) * count * BLK, :])
        block = rows2(block)
        total = total + (mm(block, lo) + mm(block, hi))
    total = fold2(total)
    weights, norms = unit_weights(state)

    def apply_first(p, gram):
        block = times(weights, load_left(lf, lax.div(p, per_piece), lax.rem(p, per_piece) * wb))
        q1[p] = block
        block = rows3(block)
        return gram + mm(block, block, NT)

    off = self_products(lax.fori_loop(0, pieces, apply_first, jnp.zeros((3 * r, 3 * r), F32)), r) - norms
    row_id = lax.broadcasted_iota(jnp.int32, (r, r), 0)
    col_id = lax.broadcasted_iota(jnp.int32, (r, r), 1)
    again = jnp.where(col_id < row_id, off, jnp.where(col_id == row_id, 0.5 * off, 0.0))
    weights = weights - times(again, weights)
    scale = math.sqrt(float(d))

    wait_all(recv_a)
    for slot in range(ny):
        total = total + fold3(mm(rows3(aout[...] if slot == 0 else ain[ny - slot - 1]), vg_v[slot]))
    zsum[0] = total
    recv = [send(zsum.at[0], zsum.at[dc], device(z, x, cc, y)) for dc, cc in enumerate(cores, 1)]
    weights_second_across(3)

    def apply_second(p, carry):
        block = q1[p]
        block = block - times(again, block)
        left_out[:, columns(p)] = block * scale
        return carry

    lax.fori_loop(0, pieces, apply_second, 0)
    settle([copy for copy in early if id(copy) not in settled])
    wait_all(recv)
    for dc in range(1, nc):
        total = total + zsum[dc]
    tz[mine] = total
    own = tz.at[mine]
    recv = [send(own, own, device(zz, xx, c, y)) for xx, zz in plane]


    for i in range(4):
        for h in range(2):
            stage_two[h, i, (-1, 1, -1, 1)[i]].wait_recv()
            stage_two_across[h, i].wait_recv()
    wait_all(recv_vgx)

    def input_grad(i, carry):
        total = None
        for slot in range(ny):
            weight = wbuf[lax.div(i, nz), lax.rem(i, nz), :, slot].reshape(BLK, BLK)
            part_sum = mm(vgx[:, slot].reshape(nc * tok, BLK), weight, NT).astype(BF16).astype(F32)
            total = part_sum if total is None else total + part_sum
        total = total.astype(BF16).reshape(nc, tok, BLK)
        gi[:, pl.ds(pl.multiple_of((c * per + i) * BLK, BLK), BLK)] = total[0]
        for dc in range(1, nc):
            outs[dc - 1, :, pl.ds(pl.multiple_of(i * BLK, BLK), BLK)] = total[dc]
        return carry

    lax.fori_loop(0, per, input_grad, 0)
    share_of = gi.at[:, pl.ds(pl.multiple_of(c * per * BLK, BLK), per * BLK)]
    sent_out = [send(outs.at[nc - 1 - dc], share_of, device(z, x, cc, y)) for dc, cc in enumerate(cores, 1)]

    for i in range(CHUNKS):
        if i >= half:
            from_down[i].wait_recv()
        else:
            from_up[i].wait_recv()
    cotangent = vg_v[...].reshape(ny * tok, BLK).astype(F32).T.astype(BF16)

    def merge(i, lo, hi):
        for j in (i, i + half):
            from_across[j, lo].wait_recv()
            at = pl.ds(j * part + lo, hi - lo)
            block = mm(cotangent, actr[:, j, :, lo:hi].reshape(ny * tok, hi - lo))
            merged[at, :] = err_v[at, :] + block.T

    for bounds in passed_on[:-3]:
        merge(*bounds)

    wait_all(recv)
    total = tz[0]
    for i in range(1, per):
        total = total + tz[i]
    r_out[...] = times(weights, total) / float(nb)
    last = [id(from_across[i + h, lo]) for i, lo, _ in passed_on[-3:] for h in (0, half)]
    settle([copy for copy in sent if id(copy) not in settled + last])

    for bounds in passed_on[-3:]:
        merge(*bounds)

    wait_all(sent_out)
    settle([copy for copy in sent if id(copy) not in settled])
    assert counter == [send_sem.shape[0], local_sem.shape[0]], counter


def error_kernel(merged, left, right, gi, error_out, left_out, right_out, gi_out, error, sem):
    d = merged.shape[0]
    pieces = error.shape[0]
    rows = d // pieces
    pairs = [(gi.at[i : i + 16], gi_out.at[i : i + 16]) for i in range(0, gi.shape[0], 16)]
    pairs += [(left.at[i : i + 8], left_out.at[i : i + 8]) for i in range(0, left.shape[0], 8)]
    pairs.append((right, right_out))
    copies = [pltpu.make_async_copy(a, b, sem.at[pieces + i]) for i, (a, b) in enumerate(pairs)]
    for copy in copies:
        copy.start()
    hi, lo = split2(right[...] / math.sqrt(float(d)))
    right3 = jnp.concatenate([hi, hi, lo], axis=0)
    for i in range(pieces):
        at = pl.ds(i * rows, rows)
        hi, lo = split2(left[:, at])
        error[i] = merged[at, :] - mm(jnp.concatenate([hi, lo, hi], axis=0), right3, TN)
        copies.append(pltpu.make_async_copy(error.at[i], error_out.at[at], sem.at[i]))
        copies[-1].start()
    for copy in copies:
        copy.wait()


def build(geom):
    nz, nx, nc, ny = geom

    def body(act, vg, w, err, right_prev):
        tok, d = act.shape
        kv = vg.shape[1]
        r = right_prev.shape[1]
        nb = nc * nx * nz
        per = nx * nz
        wide = min(WIDE, per * BLK)
        assert d == nb * BLK and kv == BLK and per * BLK % wide == 0
        sends = 3 * (ny - 1) + 6 + 4 + 3 * CHUNKS + 2 + 30 + 3 * (per - 1) + 5 * (nc - 1)
        pieces = w.reshape(nc, nx, nz, 2, BLK // 2, kv)
        inputs = [
            pltpu.with_memory_space_constraint(a, pltpu.HBM) for a in (act, vg, pieces, err[0], right_prev.T)
        ]
        hbm = pl.BlockSpec(memory_space=pltpu.HBM)
        vmem = pl.BlockSpec(memory_space=pltpu.VMEM)
        anywhere = pl.BlockSpec(memory_space=pl.ANY)
        results = (((d, kv), F32), ((r, d), F32), ((r, kv), F32), ((tok, d), BF16))
        made = pl.pallas_call(
            functools.partial(comm_kernel, geom),
            out_shape=tuple(pltpu.VMEM(*shape) for shape in results),
            in_specs=[hbm] * 5,
            out_specs=(vmem,) * 4,
            scratch_shapes=[
                pltpu.VMEM((r, kv), F32),
                pltpu.VMEM((ny, CHUNKS, tok, d // CHUNKS), BF16),
                pltpu.VMEM((ny, tok, kv), BF16),
                pltpu.VMEM((d, kv), F32),
                pltpu.VMEM((ny, r, tok), F32),
                pltpu.VMEM((ny - 1, r, tok), F32),
                pltpu.VMEM((2, tok // 2, kv), BF16),
                pltpu.VMEM((nc, ny, tok, kv), BF16),
                pltpu.VMEM((nx, nz, 2, ny, BLK // 2, kv), BF16),
                pltpu.VMEM((max(nc - 1, 1), tok, per * BLK), BF16),
                pltpu.VMEM((nc, per, r, BLK), F32),
                pltpu.VMEM((nc, per, r, BLK), F32),
                pltpu.VMEM((per, r, BLK), F32),
                pltpu.VMEM((per - 1, r, BLK), F32),
                pltpu.VMEM((ny, r, BLK), F32),
                pltpu.VMEM((d // wide, r, wide), F32),
                pltpu.VMEM((r, tok), F32),
                pltpu.VMEM((ny - 1, r, tok), F32),
                pltpu.VMEM((nc, r, kv), F32),
                pltpu.VMEM((per, r, kv), F32),
                pltpu.SemaphoreType.DMA((1 + 1 + 4 + CHUNKS + ny + 1,)),
                pltpu.SemaphoreType.DMA((sends,)),
                pltpu.SemaphoreType.DMA((sends,)),
            ],
            compiler_params=pltpu.CompilerParams(
                collective_id=0, has_side_effects=True, vmem_limit_bytes=44 * MIB
            ),
        )(*inputs)

        pieces = 16
        error_next, left, right, grad_input = pl.pallas_call(
            error_kernel,
            out_shape=tuple(jax.ShapeDtypeStruct(*shape) for shape in results),
            in_specs=[vmem] * 4,
            out_specs=(anywhere,) * 4,
            scratch_shapes=[pltpu.VMEM((pieces, d // pieces, kv), F32), pltpu.SemaphoreType.DMA((pieces + tok // 16 + r // 8 + 1,))],
            compiler_params=pltpu.CompilerParams(vmem_limit_bytes=24 * MIB),
        )(*made)
        return (grad_input, error_next[None], left.T, right.T)

    return body


def solution(mesh):
    return jax.shard_map(
        build((4, 4, 2, 4)),
        mesh=mesh,
        in_specs=(
            P(("dp", "tp"), None),
            P("dp", "tp"),
            P(None, "tp"),
            P("dp", None, "tp"),
            P("tp", None),
        ),
        out_specs=(P(("dp", "tp"), None), P("dp", None, "tp"), P(), P("tp", None)),
        check_vma=False,
    )
```

```python
import functools
import math

import jax
import jax.numpy as jnp
from jax import lax
from jax.experimental import pallas as pl
from jax.experimental.pallas import tpu as pltpu
from jax.sharding import PartitionSpec as P

MESH = pl.DeviceIdType.MESH
F32 = jnp.float32
BF16 = jnp.bfloat16
BLK = 256
EPS = 1e-12
MIB = 1024 * 1024
WIDE = 8 * BLK
CHUNKS = 16
NN = (((1,), (0,)), ((), ()))
NT = (((1,), (1,)), ((), ()))
TN = (((0,), (0,)), ((), ()))


def mm(a, b, dims=NN):
    return lax.dot_general(a, b, dims, preferred_element_type=F32)


def split2(a):
    hi = a.astype(BF16)
    lo = (a - hi.astype(F32)).astype(BF16)
    return hi, lo


def split3(a):
    hi = a.astype(BF16)
    rest = a - hi.astype(F32)
    mid = rest.astype(BF16)
    lo = (rest - mid.astype(F32)).astype(BF16)
    return hi, mid, lo


def rows3(a):
    return jnp.concatenate(split3(a), axis=0)


def fold3(a):
    n = a.shape[0] // 3
    return (a[2 * n :] + a[n : 2 * n]) + a[:n]


def rows2(a):
    return jnp.concatenate(split2(a), axis=0)


def fold2(a):
    n = a.shape[0] // 2
    return a[n:] + a[:n]


def self_products(total, r):
    total = fold3(total)
    return (total[:, 2 * r :] + total[:, r : 2 * r]) + total[:, :r]


def times(a, b):
    a_hi, a_mid, a_lo = (v.astype(F32) for v in split3(a))
    b_hi, b_mid, b_lo = split3(b)
    left = jnp.concatenate([a_lo, a_mid, a_hi, a_mid, a_hi, a_hi], axis=1).astype(BF16)
    return mm(left, jnp.concatenate([b_hi, b_mid, b_lo, b_hi, b_mid, b_hi], axis=0))


def eye_like(n):
    return (lax.broadcasted_iota(jnp.int32, (n, n), 0) == lax.broadcasted_iota(jnp.int32, (n, n), 1)).astype(F32)


def gram_schmidt(gram):
    n = gram.shape[0]
    left, weights = gram, eye_like(n)
    row_id = lax.broadcasted_iota(jnp.int32, (n, 1), 0)
    m = 4
    for j in range(0, n, m):
        columns = [jnp.broadcast_to(left[:, i : i + 1], (n, n)) for i in range(j, j + m)]
        rows = [left[i : i + 1, :] for i in range(j, j + m)]
        given = [weights[i : i + 1, :] for i in range(j, j + m)]
        off_left, off_weights = jnp.zeros((n, n), F32), jnp.zeros((n, n), F32)
        for i in range(m):
            at = j + i
            s = jnp.maximum(columns[i][at : at + 1, :], 0.0)
            inverse = 1.0 / (s + EPS)
            c = (2.0 - s * inverse) * inverse
            f = jnp.where(row_id > at, columns[i] * c, 0.0)
            h = f * (2.0 - c * s)
            for later in range(i + 1, m):
                to = j + later
                columns[later] = columns[later] - h * columns[later][at : at + 1, :]
                rows[later] = rows[later] - h[to : to + 1, :] * rows[i]
                given[later] = given[later] - f[to : to + 1, :] * given[i]
            off_left = off_left + h * rows[i]
            off_weights = off_weights + f * given[i]
        left, weights = left - off_left, weights - off_weights
        yield left, weights


def unit_weights(state):
    left, weights = state
    eye = eye_like(left.shape[0])
    s = jnp.maximum(jnp.sum(left * eye, axis=1, keepdims=True), 0.0)
    return weights / jnp.sqrt(s + EPS), eye * (s / (s + EPS))


def comm_kernel(
    geom, act, vg, w, err, rt_in, merged, left_out, r_out, gi,
    rt, actr, vg_v, err_v, uout, uin, vstage, vgx, wbuf, outs, lacc, lf, rc, rxz, ysum, q1, aout, ain, zsum, tz,
    local_sem, send_sem, recv_sem,
):
    nz, nx, nc, ny = geom
    nb = nc * nx * nz
    per = nx * nz
    _, _, tok, part = actr.shape
    d = part * CHUNKS
    half = CHUNKS // 2
    r = rt.shape[0]
    wide = min(WIDE, per * BLK)
    wb = wide // BLK
    pieces = d // wide
    per_piece = per // wb
    dp, y = lax.axis_index("dp"), lax.axis_index("tp")
    c = lax.rem(dp, nc)
    x = lax.rem(lax.div(dp, nc), nx)
    z = lax.div(dp, nc * nx)
    mine = x * nz + z

    def shifted(i, by, n):
        return lax.rem(i + by, n)

    def device(zz, xx, cc, yy):
        return ((zz * nx + xx) * nc + cc, yy)

    y_peers = [(dy, shifted(y, dy, ny)) for dy in range(1, ny)]
    plane = [
        (shifted(x, dx, nx), shifted(z, dz, nz)) for dx in range(nx) for dz in range(nz) if (dx, dz) != (0, 0)
    ]
    cores = [shifted(c, dc, nc) for dc in range(1, nc)]
    up, down, across = shifted(y, 1, ny), shifted(y, ny - 1, ny), shifted(y, 2, ny)

    sent, settled = [], []
    counter = [0, 0]

    def describe(src, dst, to):
        i = counter[0]
        counter[0] += 1
        copy = pltpu.make_async_remote_copy(
            src_ref=src, dst_ref=dst, send_sem=send_sem.at[i], recv_sem=recv_sem.at[i], device_id=to, device_id_type=MESH
        )
        sent.append(copy)
        return copy

    def send(src, dst, to):
        copy = describe(src, dst, to)
        copy.start()
        return copy

    def send_both(one, other):
        one, other = describe(*one), describe(*other)

        @pl.when(c == 0)
        def _():
            one.start()
            other.start()

        @pl.when(c != 0)
        def _():
            other.start()
            one.start()

        return one, other

    def fetch(src, dst):
        i = counter[1]
        counter[1] += 1
        copy = pltpu.make_async_copy(src, dst, local_sem.at[i])
        copy.start()
        return copy

    def wait_all(copies):
        for copy in copies:
            copy.wait_recv()

    def settle(copies):
        for copy in copies:
            copy.wait_send()
        settled.extend(id(copy) for copy in copies)

    def tokens(yy):
        return pl.ds(pl.multiple_of(yy * tok, tok), tok)

    barrier = pltpu.get_barrier_semaphore()
    everyone = (
        [device(z, x, c, yy) for _, yy in y_peers]
        + [device(z, x, cc, y) for cc in cores]
        + [device(zz, xx, c, y) for xx, zz in plane]
    )
    for peer in everyone:
        pl.semaphore_signal(barrier, inc=1, device_id=peer, device_id_type=MESH)

    load_rt = fetch(rt_in, rt)
    load_vg = [fetch(vg.at[tokens(yy)], vg_v.at[i]) for i, yy in enumerate((y, up, across, down))]
    share = d // 4
    load_err = [fetch(err.at[pl.ds(i * share, share)], err_v.at[pl.ds(i * share, share)]) for i in range(4)]
    pl.semaphore_wait(barrier, len(everyone))

    from_down, from_up, from_across = {}, {}, {}

    def cols(i):
        return pl.ds(i * part, part)

    def direct(*numbers):
        for i in numbers:
            j = (i + half) % CHUNKS
            from_down[i], from_up[j] = send_both(
                (act.at[:, cols(i)], actr.at[3, i], device(z, x, c, up)),
                (act.at[:, cols(j)], actr.at[1, j], device(z, x, c, down)),
            )

    def forward(*numbers):
        for i in numbers:
            j = i + half
            from_down[i].wait_recv()
            from_up[j].wait_recv()
            from_across[i], from_across[j] = send_both(
                (actr.at[3, i], actr.at[2, i], device(z, x, c, up)),
                (actr.at[1, j], actr.at[2, j], device(z, x, c, down)),
            )


    recv_vg = [send(vg.at[tokens(up)], vgx.at[0, 3], device(z, x, c, up))]
    recv_vg.append(send(vg.at[tokens(down)], vgx.at[0, 1], device(z, x, c, down)))
    few = tok // 2
    ways = (up, down)
    vg_passing = [
        send(vg.at[pl.ds(pl.multiple_of(across * tok + h * few, few), few)], vstage.at[h], device(z, x, c, ways[h]))
        for h in range(2)
    ]
    direct(0)
    load_act = {
        i: fetch(act.at[:, cols(i)], actr.at[0, i]) for j in range(half) for i in (j, j + half)
    }
    load_vgx = fetch(vg.at[tokens(y)], vgx.at[0, 0])
    load_w = fetch(w.at[c], wbuf.at[:, :, :, 0])

    load_rt.wait()
    rt3 = rows3(rt[...])
    for load in load_vg:
        load.wait()
    for dy in range(ny):
        uout[dy] = fold3(mm(rt3, vg_v[dy], NT))
    recv_u = [send(uout.at[dy], uin.at[dy - 1], device(z, x, c, yy)) for dy, yy in y_peers]

    own_w = w.at[c, x, z]
    w_from_down, w_from_up = send_both(
        (own_w, wbuf.at[x, z, :, 3], device(z, x, c, up)), (own_w, wbuf.at[x, z, :, 1], device(z, x, c, down))
    )
    direct(1, 2)

    def place(h, a, b):
        return (a, b) if h == 0 else (b, a)

    def piece(h, first, second):
        zz, xx = place(h, first, second)
        return wbuf.at[xx, zz, h, 1:ny]

    def neighbour(h, stage, way):
        n = (nz if h == 0 else nx) if stage == 0 else (nx if h == 0 else nz)
        first, second = place(h, z, x)
        if stage == 0:
            first = shifted(first, way % n, n)
        else:
            second = shifted(second, way % n, n)
        zz, xx = place(h, first, second)
        return device(zz, xx, c, y)

    half_here = [(place(h, z, x), place(h, nz, nx)) for h in range(2)]
    stage_one, stage_one_across, stage_two, stage_two_across = {}, {}, {}, {}

    def weights_first():
        for h in range(2):
            (first, second), _ = half_here[h]
            own = piece(h, first, second)
            stage_one[h, 1], stage_one[h, -1] = send_both(
                (own, own, neighbour(h, 0, 1)), (own, own, neighbour(h, 0, -1))
            )

    def weights_across():
        for h in range(2):
            (first, second), (n, _) = half_here[h]
            way = 1 - 2 * h
            stage_one[h, way].wait_recv()
            came = piece(h, shifted(first, -way % n, n), second)
            stage_one_across[h] = send(came, came, neighbour(h, 0, way))

    def weights_second(i):
        for h in range(2):
            (first, second), (n, _) = half_here[h]
            if i in (1, 2):
                way = 3 - 2 * i
                if way != 1 - 2 * h:
                    stage_one[h, way].wait_recv()
                first = shifted(first, -way % n, n)
            elif i == 3:
                stage_one_across[h].wait_recv()
                first = shifted(first, 2, n)
            here = piece(h, first, second)
            stage_two[h, i, 1], stage_two[h, i, -1] = send_both(
                (here, here, neighbour(h, 1, 1)), (here, here, neighbour(h, 1, -1))
            )

    def weights_second_across(i):
        for h in range(2):
            (first, second), (n, m) = half_here[h]
            first = shifted(first, (0, n - 1, 1, 2)[i], n)
            way = (1, -1, 1, -1)[i]
            stage_two[h, i, way].wait_recv()
            came = piece(h, first, shifted(second, -way % m, m))
            stage_two_across[h, i] = send(came, came, neighbour(h, 1, way))

    rt2 = rt3[: 2 * r]

    def columns(p):
        return pl.ds(pl.multiple_of(p * wide, wide), wide)

    def store_left(value, cc, j0):
        for j in range(wb):
            lacc[cc, j0 + j] = value[:, j * BLK : (j + 1) * BLK]

    def load_left(ref, cc, j0):
        return jnp.concatenate([ref[cc, j0 + j] for j in range(wb)], axis=1)

    for load in load_err:
        load.wait()

    def err_left(p, carry):
        hi, lo = split2(err_v[columns(p), :])
        store_left(fold2(mm(rt2, lo, NT) + mm(rt2, hi, NT)), lax.div(p, per_piece), lax.rem(p, per_piece) * wb)
        return carry

    lax.fori_loop(0, pieces, err_left, 0)

    wait_all(recv_u)
    ut = uout[0]
    for dy in range(ny - 1):
        ut = ut + uin[dy]
    ut3 = rows3(ut)
    for load in load_act.values():
        load.wait()

    def own_act(p):
        n = wide // part
        if n >= 1:
            return jnp.concatenate([actr[0, p * n + i] for i in range(n)], axis=1)
        n = part // wide
        inside = pl.ds(pl.multiple_of(lax.rem(p, n) * wide, wide), wide)
        return actr[0, lax.div(p, n), :, inside]

    def act_left(cc):
        def step(i, carry):
            value = fold3(mm(ut3, own_act(cc * per_piece + i)))
            store_left(load_left(lacc, cc, i * wb) + value, cc, i * wb)
            return carry

        lax.fori_loop(0, per_piece, step, 0)

    recv = []
    for cc in cores:
        act_left(cc)
        recv.append(send(lacc.at[cc], rc, device(z, x, cc, y)))
    act_left(c)

    recv_core = recv
    direct(3)
    load_vgx.wait()
    for h in range(2):
        vg_passing[h].wait_recv()
        recv_vg.append(send(vstage.at[h], vgx.at[0, 2, h * few : (h + 1) * few], device(z, x, c, ways[h])))
    wait_all(recv)
    lacc[c] += rc[...]
    recv = [
        send(lacc.at[c, xx * nz + zz], rxz.at[i], device(zz, xx, c, y)) for i, (xx, zz) in enumerate(plane)
    ]
    load_w.wait()
    w_from_down.wait_recv()
    w_halves = [send(wbuf.at[x, z, 0, 3], wbuf.at[x, z, 0, 2], device(z, x, c, up))]
    w_from_up.wait_recv()
    w_halves.append(send(wbuf.at[x, z, 1, 1], wbuf.at[x, z, 1, 2], device(z, x, c, down)))
    direct(4, 5, 6)
    settle(recv_u + recv_core)
    recv_rs = recv
    wait_all(recv)
    total = lacc[c, mine]
    for i in range(len(plane)):
        total = total + rxz[i]
    ysum[y] = total
    own = ysum.at[y]
    recv = [send(own, own, device(z, x, c, yy)) for _, yy in y_peers]
    direct(*range(7, 12))
    wait_all(w_halves)
    weights_first()
    weights_second(0)
    settle(recv_rs)
    wait_all(recv)
    total = ysum[0]
    for yy in range(1, ny):
        total = total + ysum[yy]
    lf[c, mine] = total
    own = lf.at[c, mine]
    recv_y = recv
    recv = [send(own, own, device(zz, xx, c, y)) for xx, zz in plane]
    weights_across()
    weights_second(1)
    weights_second(2)
    settle(recv_y)
    wait_all(recv)
    recv_ag = recv
    own = lf.at[c]
    recv = [send(own, own, device(z, x, cc, y)) for cc in cores]
    weights_second(3)
    weights_second_across(0)
    settle(recv_ag)

    wait_all(recv_vg)
    recv_vgx = [send(vgx.at[0], vgx.at[dc], device(z, x, cc, y)) for dc, cc in enumerate(cores, 1)]
    settle(vg_passing + recv_vg + [w_from_down, w_from_up] + w_halves + list(stage_one.values()))
    wait_all(recv)

    def left_piece(p):
        return rows3(load_left(lf, lax.div(p, per_piece), lax.rem(p, per_piece) * wb))

    def products(p, carry):
        gram, by_act = carry
        block = left_piece(p)
        return gram + mm(block, block, NT), by_act + mm(block[: 2 * r], own_act(p), NT)

    gram, by_act = lax.fori_loop(
        0, pieces, products, (jnp.zeros((3 * r, 3 * r), F32), jnp.zeros((2 * r, tok), F32))
    )
    aout[...] = fold2(by_act)
    early = list(sent)
    recv_a = [send(aout, ain.at[dy - 1], device(z, x, c, yy)) for dy, yy in y_peers]
    direct(*range(12, CHUNKS))
    forward(*range(half))
    weights_second_across(1)
    weights_second_across(2)

    total = jnp.zeros((2 * r, err_v.shape[1]), F32)
    count = nb // (r // 4)
    for i, state in enumerate(gram_schmidt(self_products(gram, r))):
        block = jnp.concatenate([lf[(i * count + j) // per, (i * count + j) % per] for j in range(count)], axis=1)
        hi, lo = split2(err_v[i * count * BLK : (i + 1) * count * BLK, :])
        block = rows2(block)
        total = total + (mm(block, lo) + mm(block, hi))
    total = fold2(total)
    weights, norms = unit_weights(state)

    def apply_first(p, gram):
        block = times(weights, load_left(lf, lax.div(p, per_piece), lax.rem(p, per_piece) * wb))
        q1[p] = block
        block = rows3(block)
        return gram + mm(block, block, NT)

    off = self_products(lax.fori_loop(0, pieces, apply_first, jnp.zeros((3 * r, 3 * r), F32)), r) - norms
    row_id = lax.broadcasted_iota(jnp.int32, (r, r), 0)
    col_id = lax.broadcasted_iota(jnp.int32, (r, r), 1)
    again = jnp.where(col_id < row_id, off, jnp.where(col_id == row_id, 0.5 * off, 0.0))
    weights = weights - times(again, weights)
    scale = math.sqrt(float(d))

    wait_all(recv_a)
    for slot in range(ny):
        total = total + fold3(mm(rows3(aout[...] if slot == 0 else ain[ny - slot - 1]), vg_v[slot]))
    zsum[0] = total
    recv = [send(zsum.at[0], zsum.at[dc], device(z, x, cc, y)) for dc, cc in enumerate(cores, 1)]
    weights_second_across(3)

    def apply_second(p, carry):
        block = q1[p]
        block = block - times(again, block)
        left_out[:, columns(p)] = block * scale
        return carry

    lax.fori_loop(0, pieces, apply_second, 0)
    settle([copy for copy in early if id(copy) not in settled])
    wait_all(recv)
    for dc in range(1, nc):
        total = total + zsum[dc]
    tz[mine] = total
    own = tz.at[mine]
    recv = [send(own, own, device(zz, xx, c, y)) for xx, zz in plane]


    for i in range(4):
        for h in range(2):
            stage_two[h, i, (-1, 1, -1, 1)[i]].wait_recv()
            stage_two_across[h, i].wait_recv()
    wait_all(recv_vgx)

    def input_grad(i, carry):
        total = None
        for slot in range(ny):
            weight = wbuf[lax.div(i, nz), lax.rem(i, nz), :, slot].reshape(BLK, BLK)
            part_sum = mm(vgx[:, slot].reshape(nc * tok, BLK), weight, NT).astype(BF16).astype(F32)
            total = part_sum if total is None else total + part_sum
        total = total.astype(BF16).reshape(nc, tok, BLK)
        gi[:, pl.ds(pl.multiple_of((c * per + i) * BLK, BLK), BLK)] = total[0]
        for dc in range(1, nc):
            outs[dc - 1, :, pl.ds(pl.multiple_of(i * BLK, BLK), BLK)] = total[dc]
        return carry

    lax.fori_loop(0, per, input_grad, 0)
    share_of = gi.at[:, pl.ds(pl.multiple_of(c * per * BLK, BLK), per * BLK)]
    sent_out = [send(outs.at[nc - 1 - dc], share_of, device(z, x, cc, y)) for dc, cc in enumerate(cores, 1)]

    for i in range(CHUNKS):
        if i >= half:
            from_down[i].wait_recv()
        else:
            from_up[i].wait_recv()
    cotangent = vg_v[...].reshape(ny * tok, BLK).astype(F32).T.astype(BF16)

    def merge(j):
        from_across[j].wait_recv()
        at = pl.ds(j * part, part)
        merged[at, :] = err_v[at, :] + mm(cotangent, actr[:, j].reshape(ny * tok, part)).T

    for i in range(half - 2):
        merge(i)
        merge(i + half)

    wait_all(recv)
    total = tz[0]
    for i in range(1, per):
        total = total + tz[i]
    r_out[...] = times(weights, total) / float(nb)
    last = [id(from_across[i + h]) for i in range(half - 2, half) for h in (0, half)]
    settle([copy for copy in sent if id(copy) not in settled + last])

    for i in range(half - 2, half):
        merge(i)
        merge(i + half)

    wait_all(sent_out)
    settle([copy for copy in sent if id(copy) not in settled])
    assert counter == [send_sem.shape[0], local_sem.shape[0]], counter


def error_kernel(merged, left, right, gi, error_out, left_out, right_out, gi_out, error, sem):
    d = merged.shape[0]
    pieces = error.shape[0]
    rows = d // pieces
    copies = [
        pltpu.make_async_copy(a, b, sem.at[pieces + i])
        for i, (a, b) in enumerate([(gi, gi_out), (left, left_out), (right, right_out)])
    ]
    for copy in copies:
        copy.start()
    hi, lo = split2(right[...] / math.sqrt(float(d)))
    right3 = jnp.concatenate([hi, hi, lo], axis=0)
    for i in range(pieces):
        at = pl.ds(i * rows, rows)
        hi, lo = split2(left[:, at])
        error[i] = merged[at, :] - mm(jnp.concatenate([hi, lo, hi], axis=0), right3, TN)
        copies.append(pltpu.make_async_copy(error.at[i], error_out.at[at], sem.at[i]))
        copies[-1].start()
    for copy in copies:
        copy.wait()


def build(geom):
    nz, nx, nc, ny = geom

    def body(act, vg, w, err, right_prev):
        tok, d = act.shape
        kv = vg.shape[1]
        r = right_prev.shape[1]
        nb = nc * nx * nz
        per = nx * nz
        wide = min(WIDE, per * BLK)
        assert d == nb * BLK and kv == BLK and per * BLK % wide == 0
        sends = 3 * (ny - 1) + 6 + 4 + 3 * CHUNKS + 30 + 3 * (per - 1) + 5 * (nc - 1)
        pieces = w.reshape(nc, nx, nz, 2, BLK // 2, kv)
        inputs = [
            pltpu.with_memory_space_constraint(a, pltpu.HBM) for a in (act, vg, pieces, err[0], right_prev.T)
        ]
        hbm = pl.BlockSpec(memory_space=pltpu.HBM)
        vmem = pl.BlockSpec(memory_space=pltpu.VMEM)
        anywhere = pl.BlockSpec(memory_space=pl.ANY)
        results = (((d, kv), F32), ((r, d), F32), ((r, kv), F32), ((tok, d), BF16))
        made = pl.pallas_call(
            functools.partial(comm_kernel, geom),
            out_shape=tuple(pltpu.VMEM(*shape) for shape in results),
            in_specs=[hbm] * 5,
            out_specs=(vmem,) * 4,
            scratch_shapes=[
                pltpu.VMEM((r, kv), F32),
                pltpu.VMEM((ny, CHUNKS, tok, d // CHUNKS), BF16),
                pltpu.VMEM((ny, tok, kv), BF16),
                pltpu.VMEM((d, kv), F32),
                pltpu.VMEM((ny, r, tok), F32),
                pltpu.VMEM((ny - 1, r, tok), F32),
                pltpu.VMEM((2, tok // 2, kv), BF16),
                pltpu.VMEM((nc, ny, tok, kv), BF16),
                pltpu.VMEM((nx, nz, 2, ny, BLK // 2, kv), BF16),
                pltpu.VMEM((max(nc - 1, 1), tok, per * BLK), BF16),
                pltpu.VMEM((nc, per, r, BLK), F32),
                pltpu.VMEM((nc, per, r, BLK), F32),
                pltpu.VMEM((per, r, BLK), F32),
                pltpu.VMEM((per - 1, r, BLK), F32),
                pltpu.VMEM((ny, r, BLK), F32),
                pltpu.VMEM((d // wide, r, wide), F32),
                pltpu.VMEM((r, tok), F32),
                pltpu.VMEM((ny - 1, r, tok), F32),
                pltpu.VMEM((nc, r, kv), F32),
                pltpu.VMEM((per, r, kv), F32),
                pltpu.SemaphoreType.DMA((1 + 1 + 4 + CHUNKS + ny + 1,)),
                pltpu.SemaphoreType.DMA((sends,)),
                pltpu.SemaphoreType.DMA((sends,)),
            ],
            compiler_params=pltpu.CompilerParams(
                collective_id=0, has_side_effects=True, vmem_limit_bytes=44 * MIB
            ),
        )(*inputs)

        pieces = 16
        error_next, left, right, grad_input = pl.pallas_call(
            error_kernel,
            out_shape=tuple(jax.ShapeDtypeStruct(*shape) for shape in results),
            in_specs=[vmem] * 4,
            out_specs=(anywhere,) * 4,
            scratch_shapes=[pltpu.VMEM((pieces, d // pieces, kv), F32), pltpu.SemaphoreType.DMA((pieces + 3,))],
            compiler_params=pltpu.CompilerParams(vmem_limit_bytes=24 * MIB),
        )(*made)
        return (grad_input, error_next[None], left.T, right.T)

    return body


def solution(mesh):
    return jax.shard_map(
        build((4, 4, 2, 4)),
        mesh=mesh,
        in_specs=(
            P(("dp", "tp"), None),
            P("dp", "tp"),
            P(None, "tp"),
            P("dp", None, "tp"),
            P("tp", None),
        ),
        out_specs=(P(("dp", "tp"), None), P("dp", None, "tp"), P(), P("tp", None)),
        check_vma=False,
    )
```
